32 devices in a mesh: wide: 16 (over z, x, core), narrow: 2 (over y).
Axes of the slice: x: 2, y: 2, z: 4, core: 2. Of those that a mesh axis runs over, the one named last changes fastest.
Arguments:
- layer_in: bfloat16 [16, 1280, 768], P('wide', 'narrow'), may hold values from -6 to 6
- pre_gain: float32 [768], replicated, may hold values from 0.5 to 1.5
- w_heads: bfloat16 [768, 24, 130], P(None, 'narrow'), may hold values from -0.21875 to 0.21875
- w_bc: bfloat16 [768, 256], replicated, may hold values from -0.21875 to 0.21875
- conv_x: float32 [7, 24, 64], P(None, 'narrow'), may hold values from -2 to 2
- conv_bc: float32 [7, 256], replicated, may hold values from -2 to 2
- dt_bias: float32 [24, 2], P('narrow'), may hold values from -7 to -3
- a_log: float32 [24], P('narrow'), may hold values from -1 to 1.5
- skip_d: float32 [24], P('narrow'), may hold values from 0.5 to 1.5
- norm_gain: float32 [24, 64], P('narrow'), may hold values from 0.5 to 1.5
- w_out: bfloat16 [24, 64, 768], P('narrow'), may hold values from -0.15625 to 0.15625
- cotangent: bfloat16 [16, 1280, 768], P('wide', 'narrow'), may hold values from -6 to 6
- starts: int32 [16, 4], P('wide'), may hold values from 0 to 1279, as said below
- live: int32 [16, 1280], P('wide'), may hold values from 0 to 1, as said below
Outputs:
- out: bfloat16 [16, 1280, 768], P('wide', 'narrow')
- grad_input: float32 [16, 1280, 768], P('wide', 'narrow')
- grad_pre_gain: float32 [768], P('wide')
- grad_w_heads: float32 [768, 24, 130], P('wide', 'narrow')
- grad_w_bc: float32 [768, 256], P('wide')
- grad_conv_x: float32 [7, 24, 64], P(None, 'narrow', 'wide')
- grad_conv_bc: float32 [7, 256], P(None, 'wide')
- grad_dt_bias: float32 [24, 2], P('narrow')
- grad_a_log: float32 [24], P('narrow')
- grad_skip_d: float32 [24], P('narrow')
- grad_norm_gain: float32 [24, 64], P('narrow', 'wide')
- grad_w_out: float32 [24, 64, 768], P('narrow', None, 'wide')
The draws below stay inside these ranges and needn't reach their ends.
Inputs may be any that keep to these rules, and one draw needn't show every extreme that they name: Per row the starts are increasing and the first is 0; in every row the second document starts below 160 and the third at or beyond 1280 - 1280 / 16; in some row the last document starts at the row's last position. In every row the live positions are a prefix of the row, of 1200 or more positions.
All inputs are finite; a program needn't handle non-finite values.
Results may differ from the reference program's by a relative error of at most 0.0088.
Values may be sent and summed in bfloat16 or wider, within the bound.
A program may use at most 384 MiB of HBM per device.

```python
import jax
import jax.numpy as jnp
from jax import lax

D = 768
H = 24
HD = 64
N = 64
K = 7
DI = 1536
BLOCK = 128
SEQ_LEN = 1280
ROWS = 16


def draw_starts(key, part):
    key = jax.random.fold_in(key, 11)
    key_one, key_two, key_three = jax.random.split(key, 3)
    first = jax.random.randint(key_one, (ROWS, 1), 1, max(2, SEQ_LEN // 8))
    second = jax.random.randint(key_two, (ROWS, 1), SEQ_LEN - max(2, SEQ_LEN // 16), SEQ_LEN - 1)
    spread = jax.random.randint(key_three, (ROWS, 1), 0, 1 << 20)
    third = second + 1 + spread % (SEQ_LEN - 1 - second)
    row_index = jnp.arange(ROWS, dtype=jnp.int32)[:, None]
    third = jnp.where(row_index == ROWS - 1, SEQ_LEN - 1, third)
    zeros = jnp.zeros((ROWS, 1), jnp.int32)
    return jnp.concatenate([zeros, first, second, third], axis=1).astype(jnp.int32)


def draw_live(key, part):
    key = jax.random.fold_in(key, 23)
    cut = jax.random.randint(key, (ROWS, 1), 0, SEQ_LEN // 16 + 1)
    where_at = jnp.arange(SEQ_LEN, dtype=jnp.int32)[None, :]
    return (where_at < SEQ_LEN - cut).astype(jnp.int32)


def block_levels(key, dims, shards, least, largest):
    level = 1.0
    for dim, shards_of in shards:
        heights = jax.random.uniform(jax.random.fold_in(jax.random.fold_in(key, 6), dim), (shards_of,), jnp.float32, least / len(shards), largest / len(shards))
        level = level * jnp.repeat(jnp.exp(heights), dims[dim] // shards_of).reshape((-1,) + (1,) * (len(dims) - 1 - dim))
    return level


def bell_draw(own_key, extent, scale, most, cuts=(), held_as=jnp.bfloat16):
    factor_of = block_levels(own_key, extent, cuts, -0.22, 0.18) if cuts else 1.0
    array = jax.random.normal(own_key, extent, jnp.float32) * scale * factor_of
    return jnp.minimum(jnp.maximum(array, -most), most).astype(held_as)


def setup_inputs(seed: int = 0) -> dict:
    seeds = jax.random.split(jax.random.key(seed), 15)
    return {
        "layer_in": bell_draw(seeds[0], (ROWS, SEQ_LEN, D), 1.0, 6.0, ((0, 16), (1, 2))),
        "pre_gain": jnp.clip(1.0 + 0.1 * jax.random.normal(seeds[1], (D,), jnp.float32), 0.5, 1.5),
        "w_heads": bell_draw(seeds[2], (D, H, 2 * HD + 2), D ** -0.5, 0.21875, ((1, 2),)),
        "w_bc": bell_draw(seeds[3], (D, 4 * N), D ** -0.5, 0.21875),
        "conv_x": bell_draw(seeds[4], (K, H, HD), K ** -0.5, 2.0, ((1, 2),), jnp.float32),
        "conv_bc": bell_draw(seeds[5], (K, 4 * N), K ** -0.5, 2.0, (), jnp.float32),
        "dt_bias": jnp.clip(-7.0 + 4.0 * jax.random.uniform(seeds[6], (H, 2), jnp.float32) ** block_levels(seeds[6], (H, 2), ((0, 2),), -0.2, 0.2), -7.0, -3.0),
        "a_log": jnp.clip(-1.0 + 2.5 * jax.random.uniform(seeds[7], (H,), jnp.float32) ** block_levels(seeds[7], (H,), ((0, 2),), -0.2, 0.2), -1.0, 1.5),
        "skip_d": jnp.clip(0.5 + 1.0 * jax.random.uniform(seeds[8], (H,), jnp.float32) ** block_levels(seeds[8], (H,), ((0, 2),), -0.2, 0.2), 0.5, 1.5),
        "norm_gain": jnp.clip(1.0 + 0.1 * jax.random.normal(seeds[9], (H, HD), jnp.float32), 0.5, 1.5),
        "w_out": bell_draw(seeds[10], (H, HD, D), DI ** -0.5, 0.15625, ((0, 2),)),
        "cotangent": bell_draw(seeds[11], (ROWS, SEQ_LEN, D), 1.0, 6.0, ((0, 16), (1, 2))),
        "starts": draw_starts(jax.random.fold_in(seeds[14], 71), 0),
        "live": draw_live(jax.random.fold_in(seeds[14], 71), 0),
    }


EPS = 1e-05
HIGH = lax.Precision.HIGHEST

@jax.custom_vjp
def low(v):
    return lax.optimization_barrier(v.astype(jnp.bfloat16)).astype(jnp.float32)

@jax.custom_vjp
def low_back(v):
    return v

def low_keep(v):
    return (low(v), None)

def low_pass(kept, grad):
    return (grad,)

def back_keep(v):
    return (v, None)

def back_low(kept, grad):
    return (low(grad),)
low.defvjp(low_keep, low_pass)
low_back.defvjp(back_keep, back_low)

def segment_ids(starts):
    where_at = jnp.arange(SEQ_LEN, dtype=jnp.int32)
    hits = (starts[:, :, None] <= where_at[None, None, :]).astype(jnp.int32)
    return (lax.optimization_barrier(jnp.sum(hits, axis=1)) - 1).astype(jnp.int32)

def conv_doc(values, taps, seg):
    half = (taps.shape[0] - 1) // 2
    length = values.shape[1]
    padded = jnp.pad(values, ((0, 0), (half, half), (0, 0)))
    seg_pad = jnp.pad(seg, ((0, 0), (half, half)), constant_values=-1)
    total = jnp.zeros_like(values)
    for offset in range(taps.shape[0]):
        same = (seg_pad[:, offset:offset + length] == seg).astype(values.dtype)
        total = total + taps[offset] * padded[:, offset:offset + length] * same[:, :, None]
    return total

def ssd_forward(xc, steps, decays, bmat, cmat, seg, prec):
    rows, length, heads, hdim = xc.shape
    blocks = length // BLOCK
    xb = xc.reshape(rows, blocks, BLOCK, heads, hdim)
    stepb = steps.reshape(rows, blocks, BLOCK, heads)
    cum = jnp.cumsum(decays.reshape(rows, blocks, BLOCK, heads), axis=2)
    bb = bmat.reshape(rows, blocks, BLOCK, -1)
    cb = cmat.reshape(rows, blocks, BLOCK, -1)
    sb = seg.reshape(rows, blocks, BLOCK)
    order = jnp.arange(BLOCK, dtype=jnp.int32)
    causal = order[:, None] >= order[None, :]
    same = ((sb[:, :, :, None] == sb[:, :, None, :]) & causal)[..., None]
    diff = cum[:, :, :, None, :] - cum[:, :, None, :, :]
    weights = jnp.where(same, jnp.exp(jnp.where(same, diff, 0.0)), 0.0)
    inner = jnp.einsum('rbtn,rbsn->rbts', cb, bb, precision=prec)
    mix = weights * inner[..., None] * stepb[:, :, None, :, :]
    intra = jnp.einsum('rbtsh,rbshp->rbthp', mix, xb, precision=prec)
    last = sb[:, :, -1]
    cum_end = cum[:, :, -1, :]
    to_end = (sb == last[:, :, None]).astype(cum.dtype)[..., None] * jnp.exp(cum_end[:, :, None, :] - cum) * stepb
    states = jnp.einsum('rbshp,rbsn->rbhpn', to_end[..., None] * xb, bb, precision=prec)
    decay_end = jnp.exp(cum_end)

    def carry_step(carry, item):
        state, seg_prev = carry
        block_state, block_last, block_decay = item
        keep = (block_last == seg_prev).astype(state.dtype)[:, None, None, None]
        fresh = keep * block_decay[:, :, None, None] * state + block_state
        return ((fresh, block_last), (state, seg_prev))
    init = (jnp.zeros((rows, heads, hdim, bb.shape[-1]), xc.dtype), jnp.full((rows,), -1, jnp.int32))
    items = (jnp.moveaxis(states, 1, 0), jnp.moveaxis(last, 1, 0), jnp.moveaxis(decay_end, 1, 0))
    _, (before, seg_before) = lax.scan(carry_step, init, items)
    before = jnp.moveaxis(before, 0, 1)
    seg_before = jnp.moveaxis(seg_before, 0, 1)
    enter = (sb == seg_before[:, :, None]).astype(cum.dtype)[..., None] * jnp.exp(cum)
    inter = jnp.einsum('rbtn,rbhpn->rbthp', cb, before, precision=prec) * enter[..., None]
    return (intra + inter).reshape(rows, length, heads, hdim)

def mixer(proj, bcproj, conv_x, conv_bc, dt_bias, a_log, skip_d, seg, mask, rounder, prec):
    rows, length, heads, width = proj.shape
    hdim = (width - 2) // 2
    state = bcproj.shape[-1] // 4
    gate = proj[..., :hdim]
    values = proj[..., hdim:2 * hdim] * mask[:, :, None, None]
    mixed_x = conv_doc(values.reshape(rows, length, heads * hdim), conv_x.reshape(conv_x.shape[0], heads * hdim), seg)
    xc = rounder(jax.nn.silu(mixed_x)).reshape(rows, length, heads, hdim)
    maps = rounder(jax.nn.silu(conv_doc(bcproj * mask[:, :, None], conv_bc, seg)))
    b_fwd = maps[..., :state]
    c_fwd = maps[..., state:2 * state]
    b_bwd = maps[..., 2 * state:3 * state]
    c_bwd = maps[..., 3 * state:]
    rate = -jnp.exp(a_log)
    dt_fwd = jax.nn.softplus(proj[..., 2 * hdim] + dt_bias[:, 0]) * mask[:, :, None]
    dt_bwd = jax.nn.softplus(proj[..., 2 * hdim + 1] + dt_bias[:, 1]) * mask[:, :, None]
    out_fwd = ssd_forward(xc, dt_fwd, dt_fwd * rate, b_fwd, c_fwd, seg, prec)

    def flip(v):
        return jnp.flip(v, axis=1)
    out_bwd = flip(ssd_forward(flip(xc), flip(dt_bwd), flip(dt_bwd * rate), flip(b_bwd), flip(c_bwd), flip(seg), prec))
    keep_prev = (seg[:, 1:] == seg[:, :-1]).astype(xc.dtype)[:, :, None, None]
    shifted_fwd = jnp.pad(out_fwd[:, :-1] * keep_prev, ((0, 0), (1, 0), (0, 0), (0, 0)))
    shifted_bwd = jnp.pad(out_bwd[:, 1:] * keep_prev, ((0, 0), (0, 1), (0, 0), (0, 0)))
    return (shifted_fwd + shifted_bwd + skip_d[:, None] * xc, gate)

def layer_rows(x, pre_gain, w_heads, w_bc, conv_x, conv_bc, dt_bias, a_log, skip_d, norm_gain, w_out, seg, mask):
    scale = lax.rsqrt(lax.optimization_barrier(jnp.mean(x * x, axis=-1, keepdims=True)) + EPS)
    normed = low(x * scale * pre_gain)
    proj = low_back(jnp.einsum('rld,dhc->rlhc', normed, w_heads, precision=HIGH))
    bcproj = jnp.einsum('rld,dc->rlc', normed, w_bc, precision=HIGH)
    ymix, gate = mixer(proj, bcproj, conv_x, conv_bc, dt_bias, a_log, skip_d, seg, mask, low, HIGH)
    rows, length, heads, hdim = ymix.shape
    gated = (ymix * jax.nn.silu(gate)).reshape(rows, length, heads * hdim)
    inv = lax.rsqrt(lax.optimization_barrier(jnp.mean(gated * gated, axis=-1, keepdims=True)) + EPS)
    hn = low(gated * inv * norm_gain.reshape(-1))
    return x + jnp.einsum('rlc,cd->rld', hn, w_out.reshape(heads * hdim, -1), precision=HIGH)

def reference(layer_in, pre_gain, w_heads, w_bc, conv_x, conv_bc, dt_bias, a_log, skip_d, norm_gain, w_out, cotangent, starts, live):
    seg = segment_ids(starts)
    mask = live.astype(jnp.float32)
    params = tuple((v.astype(jnp.float32) for v in (pre_gain, w_heads, w_bc, conv_x, conv_bc, dt_bias, a_log, skip_d, norm_gain, w_out)))

    def whole(x, *weights):

        def step(carry, row):
            x_row, seg_row, mask_row = row
            result = jax.checkpoint(layer_rows)(x_row[None], *weights, seg_row[None], mask_row[None])
            return (carry, result[0])
        return lax.scan(step, 0, (x, seg, mask))[1]
    out, pull = jax.vjp(whole, layer_in.astype(jnp.float32), *params)
    grads = pull(cotangent.astype(jnp.float32))
    return (out.astype(jnp.bfloat16), grads[0], grads[1], grads[2], grads[3], grads[4], grads[5], grads[6], grads[7], grads[8], grads[9], grads[10])
```

```python
import functools

import jax
import jax.numpy as jnp
from jax import lax
from jax.experimental import pallas as pl
from jax.experimental.pallas import tpu as pltpu
from jax.sharding import PartitionSpec as P

H = 24
HD = 64
BLOCK = 128
SEQ_LEN = 1280


EPS = 1e-05
HIGH = lax.Precision.HIGHEST


def rounded(value):
    return value + lax.stop_gradient(value.astype(jnp.bfloat16).astype(jnp.float32) - value)


def segment_ids(starts):
    where_at = jnp.arange(SEQ_LEN, dtype=jnp.int32)
    hits = (starts[:, :, None] <= where_at[None, None, :]).astype(jnp.int32)
    return jnp.sum(hits, axis=1) - 1


def conv_doc(values, taps, seg):
    half = (taps.shape[0] - 1) // 2
    length = values.shape[1]
    padded = jnp.pad(values, ((0, 0), (half, half), (0, 0)))
    seg_pad = jnp.pad(seg, ((0, 0), (half, half)), constant_values=-1)
    total = jnp.zeros_like(values)
    for offset in range(taps.shape[0]):
        same = (seg_pad[:, offset : offset + length] == seg).astype(values.dtype)
        total = total + taps[offset] * padded[:, offset : offset + length] * same[:, :, None]
    return total


def ssd_forward(xc, steps, decays, bmat, cmat, seg, prec):
    rows, length, heads, hdim = xc.shape
    blocks = length // BLOCK
    xb = xc.reshape(rows, blocks, BLOCK, heads, hdim)
    stepb = steps.reshape(rows, blocks, BLOCK, heads)
    cum = jnp.cumsum(decays.reshape(rows, blocks, BLOCK, heads), axis=2)
    bb = bmat.reshape(rows, blocks, BLOCK, -1)
    cb = cmat.reshape(rows, blocks, BLOCK, -1)
    sb = seg.reshape(rows, blocks, BLOCK)
    order = jnp.arange(BLOCK, dtype=jnp.int32)
    causal = order[:, None] >= order[None, :]
    same = ((sb[:, :, :, None] == sb[:, :, None, :]) & causal)[..., None]
    diff = cum[:, :, :, None, :] - cum[:, :, None, :, :]
    weights = jnp.where(same, jnp.exp(jnp.where(same, diff, 0.0)), 0.0)
    inner = jnp.einsum("rbtn,rbsn->rbts", cb, bb, precision=prec)
    mix = weights * inner[..., None] * stepb[:, :, None, :, :]
    intra = jnp.einsum("rbtsh,rbshp->rbthp", mix, xb, precision=prec)
    last = sb[:, :, -1]
    cum_end = cum[:, :, -1, :]
    to_end = (
        (sb == last[:, :, None]).astype(cum.dtype)[..., None]
        * jnp.exp(cum_end[:, :, None, :] - cum)
        * stepb
    )
    states = jnp.einsum("rbshp,rbsn->rbhpn", to_end[..., None] * xb, bb, precision=prec)
    decay_end = jnp.exp(cum_end)

    def carry_step(carry, item):
        state, seg_prev = carry
        block_state, block_last, block_decay = item
        keep = (block_last == seg_prev).astype(state.dtype)[:, None, None, None]
        fresh = keep * block_decay[:, :, None, None] * state + block_state
        return ((fresh, block_last), (state, seg_prev))

    init = (
        jnp.zeros((rows, heads, hdim, bb.shape[-1]), xc.dtype),
        jnp.full((rows,), -1, jnp.int32),
    )
    items = (jnp.moveaxis(states, 1, 0), jnp.moveaxis(last, 1, 0), jnp.moveaxis(decay_end, 1, 0))
    _, (before, seg_before) = lax.scan(carry_step, init, items)
    before = jnp.moveaxis(before, 0, 1)
    seg_before = jnp.moveaxis(seg_before, 0, 1)
    enter = (sb == seg_before[:, :, None]).astype(cum.dtype)[..., None] * jnp.exp(cum)
    inter = jnp.einsum("rbtn,rbhpn->rbthp", cb, before, precision=prec) * enter[..., None]
    return (intra + inter).reshape(rows, length, heads, hdim)


def mixer(proj, bcproj, conv_x, conv_bc, dt_bias, a_log, skip_d, seg, mask, rounder, prec):
    rows, length, heads, width = proj.shape
    hdim = (width - 2) // 2
    state = bcproj.shape[-1] // 4
    gate = proj[..., :hdim]
    values = proj[..., hdim : 2 * hdim] * mask[:, :, None, None]
    mixed_x = conv_doc(
        values.reshape(rows, length, heads * hdim),
        conv_x.reshape(conv_x.shape[0], heads * hdim),
        seg,
    )
    xc = rounder(jax.nn.silu(mixed_x)).reshape(rows, length, heads, hdim)
    maps = rounder(jax.nn.silu(conv_doc(bcproj * mask[:, :, None], conv_bc, seg)))
    b_fwd = maps[..., :state]
    c_fwd = maps[..., state : 2 * state]
    b_bwd = maps[..., 2 * state : 3 * state]
    c_bwd = maps[..., 3 * state :]
    rate = -jnp.exp(a_log)
    dt_fwd = jax.nn.softplus(proj[..., 2 * hdim] + dt_bias[:, 0]) * mask[:, :, None]
    dt_bwd = jax.nn.softplus(proj[..., 2 * hdim + 1] + dt_bias[:, 1]) * mask[:, :, None]
    out_fwd = ssd_forward(xc, dt_fwd, dt_fwd * rate, b_fwd, c_fwd, seg, prec)

    def flip(v):
        return jnp.flip(v, axis=1)

    out_bwd = flip(
        ssd_forward(
            flip(xc), flip(dt_bwd), flip(dt_bwd * rate), flip(b_bwd), flip(c_bwd), flip(seg), prec
        )
    )
    keep_prev = (seg[:, 1:] == seg[:, :-1]).astype(xc.dtype)[:, :, None, None]
    shifted_fwd = jnp.pad(out_fwd[:, :-1] * keep_prev, ((0, 0), (1, 0), (0, 0), (0, 0)))
    shifted_bwd = jnp.pad(out_bwd[:, 1:] * keep_prev, ((0, 0), (0, 1), (0, 0), (0, 0)))
    return (shifted_fwd + shifted_bwd + skip_d[:, None] * xc, gate)


def shards(
    layer_in,
    pre_gain,
    w_heads,
    w_bc,
    conv_x,
    conv_bc,
    dt_bias,
    a_log,
    skip_d,
    norm_gain,
    w_out,
    cotangent,
    starts,
    live,
):
    seg = segment_ids(starts)
    mask = live.astype(jnp.float32)
    x_here = layer_in.astype(jnp.float32)
    scale = lax.rsqrt(jnp.mean(x_here * x_here, axis=-1, keepdims=True) + EPS)
    normed_here = (x_here * scale * pre_gain).astype(jnp.bfloat16)
    normed = lax.all_gather(normed_here, "narrow", axis=1, tiled=True)
    proj = jnp.einsum("rld,dhc->rlhc", normed, w_heads, preferred_element_type=jnp.float32)
    bcproj = jnp.einsum("rld,dc->rlc", normed, w_bc, preferred_element_type=jnp.float32)

    def mix_local(proj_in, bc_in, taps_x, taps_bc, bias_in, log_rate, diag_in):
        return mixer(
            proj_in, bc_in, taps_x, taps_bc, bias_in, log_rate, diag_in, seg, mask, rounded, HIGH
        )

    (ymix, gate), pull_mix = jax.vjp(
        mix_local, proj, bcproj, conv_x, conv_bc, dt_bias, a_log, skip_d
    )
    rows, length, heads, hdim = ymix.shape
    sigma = jax.nn.sigmoid(gate)
    act = gate * sigma
    gated = (ymix * act).reshape(rows, length, heads * hdim)
    squares = lax.psum(jnp.sum(gated * gated, axis=-1), "narrow")
    inv = lax.rsqrt(squares / (H * HD) + EPS)[..., None]
    gain_flat = norm_gain.reshape(-1)
    normalized = gated * inv
    hn = (normalized * gain_flat).astype(jnp.bfloat16)
    w_flat = w_out.reshape(heads * hdim, -1)
    partial_value = jnp.einsum("rlc,cd->rld", hn, w_flat, preferred_element_type=jnp.float32)
    branch = lax.psum_scatter(partial_value, "narrow", scatter_dimension=1, tiled=True)
    out = (x_here + branch).astype(jnp.bfloat16)
    grad_out = lax.all_gather(cotangent, "narrow", axis=1, tiled=True)
    g_w_out = jnp.einsum("rlc,rld->cd", hn, grad_out, preferred_element_type=jnp.float32)
    g_hn = jnp.einsum("rld,cd->rlc", grad_out, w_flat, preferred_element_type=jnp.float32)
    g_gain = jnp.sum(g_hn * normalized, axis=(0, 1))
    weighted = g_hn * gain_flat
    cross = lax.psum(jnp.sum(weighted * gated, axis=-1), "narrow")
    g_gated = inv * weighted - gated * (inv * inv * inv) * (cross / (H * HD))[..., None]
    g_gated = g_gated.reshape(rows, length, heads, hdim)
    g_ymix = g_gated * act
    g_gate = g_gated * ymix * (sigma * (1.0 + gate * (1.0 - sigma)))
    g_proj, g_bcproj, g_conv_x, g_conv_bc, g_dt_bias, g_a_log, g_skip = pull_mix((g_ymix, g_gate))
    g_proj_low = g_proj.astype(jnp.bfloat16)
    g_w_heads = jnp.einsum("rld,rlhc->dhc", normed, g_proj_low, preferred_element_type=jnp.float32)
    g_w_bc = jnp.einsum(
        "rld,rlc->dc", normed, g_bcproj, precision=HIGH, preferred_element_type=jnp.float32
    )
    g_normed = jnp.einsum("rlhc,dhc->rld", g_proj_low, w_heads, preferred_element_type=jnp.float32)
    g_normed = g_normed + jnp.einsum(
        "rlc,dc->rld", g_bcproj, w_bc, precision=HIGH, preferred_element_type=jnp.float32
    )
    g_normed_here = lax.psum_scatter(g_normed, "narrow", scatter_dimension=1, tiled=True)
    weighted_in = g_normed_here * pre_gain
    g_pre = jnp.sum(g_normed_here * x_here * scale, axis=(0, 1))
    g_x = scale * weighted_in - x_here * (scale * scale * scale) * jnp.mean(
        weighted_in * x_here, axis=-1, keepdims=True
    )
    grad_input = cotangent.astype(jnp.float32) + g_x
    g_pre, g_w_bc, g_conv_bc = lax.psum((g_pre, g_w_bc, g_conv_bc), "narrow")
    reduced = (
        lax.psum_scatter(g_w_heads, "wide", scatter_dimension=0, tiled=True),
        lax.psum_scatter(g_w_out.reshape(heads, hdim, -1), "wide", scatter_dimension=2, tiled=True),
        lax.psum_scatter(g_conv_x, "wide", scatter_dimension=2, tiled=True),
        lax.psum_scatter(g_gain.reshape(heads, hdim), "wide", scatter_dimension=1, tiled=True),
        lax.psum_scatter(g_pre, "wide", scatter_dimension=0, tiled=True),
        lax.psum_scatter(g_w_bc, "wide", scatter_dimension=0, tiled=True),
        lax.psum_scatter(g_conv_bc, "wide", scatter_dimension=1, tiled=True),
    )
    share_pre, share_bc, share_conv = (reduced[4], reduced[5], reduced[6])
    head_bias, head_rate, head_diag = lax.psum((g_dt_bias, g_a_log, g_skip), "wide")
    return (
        out,
        grad_input,
        share_pre,
        reduced[0],
        share_bc,
        reduced[2],
        share_conv,
        head_bias,
        head_rate,
        head_diag,
        reduced[3],
        reduced[1],
    )


HALO = 16
F32 = jnp.float32
BF16 = jnp.bfloat16
LOGZERO = -1e30
VMEM_LIMIT = 56 * 2**20


def mm(a, b, dims=((1,), (0,)), precision=None):
    return lax.dot_general(a, b, (dims, ((), ())), precision=precision, preferred_element_type=F32)


def nt(a, b):
    return mm(a, b, ((1,), (1,)))


def tn(a, b):
    return mm(a, b, ((0,), (0,)))


def seg_at(info, pos):
    seg = jnp.full(pos.shape, -1, jnp.int32)
    for j in range(4):
        seg = seg + (pos >= info[j]).astype(jnp.int32)
    return jnp.where(pos >= info[6], 99, seg)


def iota(shape, dim):
    return lax.broadcasted_iota(jnp.int32, shape, dim)


def silu_parts(v):
    sg = 1.0 / (1.0 + jnp.exp(-v))
    return v * sg, sg * (1.0 + v * (1.0 - sg))


def conv_taps(src, seg_src, taps, first, rows):
    seg0 = seg_src[first : first + rows, :]
    total = src[first : first + rows, :] * taps[3:4, :]
    for k in (0, 1, 2, 4, 5, 6):
        lo = first + k - 3
        same = seg_src[lo : lo + rows, :] == seg0
        total = total + jnp.where(same, src[lo : lo + rows, :], 0.0) * taps[k : k + 1, :]
    return total


def front_kernel(
    length, hl, starts, live_ref, x_in, edge, gain, wdt_a, wdt_b, wbc_ref, taps_ref, small_a, small_b,
    info, taps_o, gain_o, skip_o, wdt, wbc, taps, normed_o, rs_o, bcm_o, dsl_o, b_o, bk_o, bkt_o, c_o, ce_o, cet_o, g_o, gt_o,
    colt_o, rows_o, coltt_o, rowst_o, et_o, wt_o, dpt_o, dt_o, sig_o, seg_s, maps_s, cum_s, x_s,
):
    nb = length // BLOCK
    ext = length + 2 * HALO
    dm = x_in.shape[1]
    n = lax.axis_index("narrow")
    for i in range(4):
        info[i] = starts[0, i]
    count = jnp.sum(live_ref[...].astype(F32)).astype(jnp.int32)
    off = n * length
    info[4] = count
    info[5] = off
    info[6] = live_ref.shape[1]
    info[7] = n
    ch = small_a.shape[1]
    taps_o[:, 0:ch] = small_a[0:8, :]
    taps_o[:, ch : 2 * ch] = small_b[0:8, :]
    gain_o[:, 0:ch] = small_a[8:16, :]
    gain_o[:, ch : 2 * ch] = small_b[8:16, :]
    skip_o[:, 0:ch] = small_a[16:24, :]
    skip_o[:, ch : 2 * ch] = small_b[16:24, :]
    src = iota((2 * hl, 128), 0)
    dst = iota((2 * hl, 128), 1)
    place = (src % 2) * 64 + src // 2
    one = jnp.float32(1.0)
    at_a = jnp.where(dst == place, one, 0.0).astype(BF16)
    at_b = jnp.where(dst == place + hl, one, 0.0).astype(BF16)
    wdt[...] = (mm(wdt_a[...], at_a) + mm(wdt_b[...], at_b)).astype(BF16)
    wbc[...] = pack_columns(wbc_ref[...])
    taps[...] = pack_columns(taps_ref[...])

    bias = small_a[24:25, 0:128] + pltpu.roll(small_b[24:25, 0:128], hl, 1)
    alog = small_a[25:26, 0:128] + pltpu.roll(small_b[25:26, 0:128], hl, 1)
    zero_edge = jnp.zeros((HALO, dm), BF16)
    x_s[0:HALO, :] = jnp.where(n == 1, edge[...], zero_edge)
    x_s[HALO : HALO + length, :] = x_in[...]
    x_s[HALO + length : ext, :] = jnp.where(n == 1, zero_edge, edge[...])
    x = x_s[...].astype(F32)
    rs = lax.rsqrt(jnp.mean(x * x, axis=1, keepdims=True) + EPS)
    normed = (x * rs * gain[...]).astype(BF16)
    normed_o[...] = normed
    rs_o[...] = rs[HALO : HALO + length, :]
    pos256 = iota((ext, 256), 0) + (off - HALO)
    seg_s[...] = seg_at(info, pos256)
    live = pos256 < count
    bcm_o[...] = jnp.where(live, mm(normed, wbc[...]), 0.0)
    crows = length + HALO
    cfirst = HALO // 2
    mix = conv_taps(bcm_o, seg_s, taps, cfirst, crows)
    maps, dsl = silu_parts(mix)
    dsl_o[...] = jnp.zeros_like(dsl_o)
    dsl_o[cfirst : cfirst + crows, :] = dsl
    maps_s[...] = jnp.zeros_like(maps_s)
    maps_s[cfirst : cfirst + crows, :] = maps.astype(BF16).astype(F32)
    own = slice(HALO, HALO + length)
    segx = seg_s[own, 0:128]
    lane = iota((length, 128), 1)
    fwd = lane < 64
    segp = seg_s[HALO - 1 : HALO - 1 + length, 0:128]
    segn = seg_s[HALO + 1 : HALO + 1 + length, 0:128]
    bmap = maps_s[own, 0:128]
    cprev = jnp.where(segp == segx, maps_s[HALO - 1 : HALO - 1 + length, 128:256], 0.0)
    cnext = jnp.where(segn == segx, maps_s[HALO + 1 : HALO + 1 + length, 128:256], 0.0)
    cmap = jnp.where(fwd, cprev, cnext)
    b_o[...] = bmap.astype(BF16)
    c_o[...] = cmap.astype(BF16)
    raw = mm(normed[own, :], wdt[...]) + bias
    softp = jnp.maximum(raw, 0.0) + jnp.log(1.0 + jnp.exp(-jnp.abs(raw)))
    softp = jnp.where(raw < -15.0, jnp.exp(jnp.minimum(raw, 0.0)), softp)
    pos128 = iota((length, 128), 0) + off
    m = pos128 < count
    dt = jnp.where(m, softp, 0.0)
    sg = jnp.where(m, 1.0 / (1.0 + jnp.exp(-raw)), 0.0)
    ratio = jnp.where(m, jnp.where(raw < -15.0, 1.0, sg / jnp.maximum(softp, 1e-30)), 0.0)
    rate = -jnp.exp(alog)
    a = dt * rate
    dt_o[...] = a
    sig_o[:, 0:128] = sg * rate
    sig_o[:, 128:256] = ratio
    tri = (iota((BLOCK, BLOCK), 0) >= iota((BLOCK, BLOCK), 1)).astype(F32)
    logdt = jnp.maximum(jnp.log(dt), LOGZERO)
    sub = iota((BLOCK, BLOCK), 0)
    ln = iota((BLOCK, BLOCK), 1)
    fwdb = ln < 64
    cum_s[...] = jnp.zeros_like(cum_s)
    dvals, ends = [], []
    for b in range(nb):
        blk = slice(b * BLOCK, (b + 1) * BLOCK)
        ab = a[blk, :]
        cum = mm(tri, ab, precision=HIGH)
        cx = cum - ab
        end = cum[BLOCK - 1 : BLOCK, :]
        colt = jnp.where(fwdb, cx, end - cum)
        rows = jnp.where(fwdb, logdt[blk, :] - cum, cx + logdt[blk, :] - end)
        colt_o[blk, :] = colt
        rows_o[blk, :] = rows
        coltt = colt.T
        coltt_o[b] = coltt
        et_o[b] = jnp.exp(coltt)
        rowst_o[b] = rows.T
        wt_o[b] = jnp.exp(jnp.minimum(rows + end, 60.0)).T
        first_pos = off + b * BLOCK
        sp = seg_at(info, sub + first_pos)
        st = seg_at(info, ln + first_pos)
        before = seg_at(info, sub * 0 + (first_pos - 1))
        begin = seg_at(info, sub * 0 + first_pos)
        last = seg_at(info, sub * 0 + (first_pos + BLOCK - 1))
        after = seg_at(info, sub * 0 + (first_pos + BLOCK))
        enter = jnp.where(fwdb, (sp == before).astype(F32), (sp == after).astype(F32))
        keep = jnp.where(fwdb, (sp == last).astype(F32), (sp == begin).astype(F32))
        ce = cmap[blk, :] * enter
        bk = bmap[blk, :] * keep
        ce_o[blk, :] = ce
        bk_o[blk, :] = bk
        cet_o[b] = ce.T
        bkt_o[b] = bk.T
        chain = jnp.where(fwdb[0:1, :], (last == before).astype(F32)[0:1, :], (begin == after).astype(F32)[0:1, :])
        dvals.append(jnp.exp(end) * chain)
        ends.append(end)
        cb = cmap[blk, :].astype(BF16)
        bb = bmap[blk, :].astype(BF16)
        zero = jnp.zeros_like(bb)
        same = sp == st
        low = same & (sub > ln)
        high = same & (sub < ln)
        bf = jnp.where(fwdb, bb, zero)
        br = jnp.where(fwdb, zero, bb)
        g_o[b] = jnp.where(low, nt(cb, bf), jnp.where(high, nt(cb, br), 0.0))
        gt_o[b] = jnp.where(high, nt(bf, cb), jnp.where(low, nt(br, cb), 0.0))
    ones = jnp.ones((1, 128), F32)
    prefix, suffix = [ones], [ones]
    for b in range(nb):
        prefix.append(prefix[-1] * dvals[b])
        suffix.append(suffix[-1] * dvals[nb - 1 - b])
    suffix = suffix[::-1]
    f1 = fwdb[0:1, :]
    for b in range(nb):
        cum_s[b : b + 1, :] = dvals[b]
        cum_s[48 + b : 49 + b, :] = ends[b]
    for i in range(nb + 1):
        cum_s[16 + i : 17 + i, :] = jnp.where(f1, prefix[i], suffix[i])
        cum_s[32 + i : 33 + i, :] = jnp.where(f1, suffix[i], prefix[i])
    dpt_o[...] = cum_s[...].T


def pair_rows(dpt, j, base, i, half):
    lane = iota((1, 128), 1)
    one = dpt[pl.ds(half * 64 + 2 * j, 1), :][:, base + i : base + i + 1]
    two = dpt[pl.ds(half * 64 + 2 * j + 1, 1), :][:, base + i : base + i + 1]
    return jnp.where(lane < 64, one, two)


def assemble(dst, pieces):
    quarter = dst.shape[0] // 4
    q = lax.axis_index("wide") % 4
    cbit = q % 2
    xbit = q // 2
    places = (q, (1 - xbit) * 2 + cbit, xbit * 2 + 1 - cbit, (1 - xbit) * 2 + 1 - cbit)
    for place, piece in zip(places, pieces):
        dst[pl.ds(pl.multiple_of(place * quarter, quarter), quarter), :] = piece[...]


def vals_kernel(
    length, other, info, normed, *refs,
):
    nb = length // BLOCK
    ext = length + 2 * HALO
    j = pl.program_id(0)
    step = j
    if other:
        p0, p1, p2, p3, taps, wt, bkt, dpt = refs[:8]
        xc_o, vm_o, ds_o, s_o, bnd_o, wvo_o, vm_s, seg_s, wall_s = refs[13:]
        j = j + pl.num_programs(0)

        @pl.when(step == 0)
        def _():
            assemble(wvo_o, (p0, p1, p2, p3))
            for i in range(wall_s.shape[0]):
                wall_s[i] = wvo_o[:, i * 128 : (i + 1) * 128]

        wv = wall_s[step]
    else:
        wv_ref, taps, wt, bkt, dpt, xc_o, vm_o, ds_o, s_o, bnd_o, vm_s, seg_s = refs
        wv = wv_ref[...]
    off, count = info[5], info[4]

    @pl.when(step == 0)
    def _():
        seg_s[...] = seg_at(info, iota((ext, 128), 0) + (off - HALO))

    live = iota((ext, 128), 0) + (off - HALO) < count
    vm = jnp.where(live, mm(normed[...], wv), 0.0)
    vm_s[...] = vm
    vm_o[...] = vm.astype(BF16)
    mix = conv_taps(vm_s, seg_s, taps, HALO, length)
    act, ds = silu_parts(mix)
    xc = act.astype(BF16)
    xc_o[...] = xc
    ds_o[...] = ds.astype(BF16)
    lane = iota((BLOCK, 128), 1)
    top = iota((BLOCK, 128), 0) < 64
    loc = []
    for b in range(nb):
        blk = slice(b * BLOCK, (b + 1) * BLOCK)
        got = []
        for i in range(2):
            h = 2 * j + i
            w = jnp.where(top, wt[b, pl.ds(h, 1), :], wt[b, pl.ds(64 + h, 1), :])
            got.append(mm((bkt[b] * w).astype(BF16), xc[blk, :]))
        loc.append(jnp.where(lane < 64, got[0], got[1]))
    state = jnp.zeros((64, 128), F32)
    s_o[0, 0, 0:64, :] = state.astype(BF16)
    for b in range(nb):
        state = pair_rows(dpt, j, 0, b, 0) * state + loc[b][0:64, :]
        s_o[0, b + 1, 0:64, :] = state.astype(BF16)
    end_f = state
    state = jnp.zeros((64, 128), F32)
    s_o[0, nb, 64:128, :] = state.astype(BF16)
    for b in range(nb - 1, -1, -1):
        state = pair_rows(dpt, j, 0, b, 1) * state + loc[b][64:128, :]
        s_o[0, b, 64:128, :] = state.astype(BF16)
    bnd_o[0] = jnp.where(info[7] == 0, end_f, state).astype(BF16)


def scan_kernel(length, info, xc_ref, s_ref, s0_ref, dpt, colt, rowst, ce, g, skip, y_o, st_o):
    nb = length // BLOCK
    j = pl.program_id(0)
    right = (info[7] == 1).astype(F32)
    s0 = s0_ref[0].astype(F32)
    lane = iota((BLOCK, 128), 1)
    first = lane < 64
    low = iota((BLOCK, BLOCK), 0) > lane
    for i in range(nb + 1):
        f = s_ref[0, i, 0:64, :].astype(F32) + pair_rows(dpt, j, 16, i, 0) * (s0 * right)
        r = s_ref[0, i, 64:128, :].astype(F32) + pair_rows(dpt, j, 16, i, 1) * (s0 * (1.0 - right))
        st_o[0, i, 0:64, :] = f.astype(BF16)
        st_o[0, i, 64:128, :] = r.astype(BF16)
    for b in range(nb):
        blk = slice(b * BLOCK, (b + 1) * BLOCK)
        xb = xc_ref[blk, :]
        rhs = jnp.concatenate([xb, st_o[0, b, 0:64, :], st_o[0, b + 1, 64:128, :]], axis=0)
        got = []
        for i in range(2):
            h = 2 * j + i
            mine = pltpu.roll(colt[blk, :], 128 - h, 1)
            cf = jnp.broadcast_to(mine[:, 0:1], (BLOCK, 128))
            cb = jnp.broadcast_to(mine[:, 64:65], (BLOCK, 128))
            diff = jnp.where(low, cf + rowst[b, pl.ds(h, 1), :], cb + rowst[b, pl.ds(64 + h, 1), :])
            mix = jnp.exp(jnp.minimum(diff, 60.0)) * g[b]
            ct = ce[blk, :] * jnp.exp(jnp.where(first, cf, cb))
            lhs = jnp.concatenate([mix.astype(BF16), ct.astype(BF16)], axis=1)
            got.append(mm(lhs, rhs))
        y = jnp.where(first, got[0], got[1]) + skip[0:1, :] * xb.astype(F32)
        y_o[blk, :] = y.astype(BF16)


def by_core(v, keep, send):
    share = v.shape[0] // 16
    cbit = lax.axis_index("wide") % 2
    v = v.astype(BF16).reshape(8, 2, share, v.shape[1])
    keep[...] = jnp.where(cbit == 0, v[:, 0], v[:, 1]).reshape(8 * share, v.shape[3])
    send[...] = jnp.where(cbit == 0, v[:, 1], v[:, 0]).reshape(8 * share, v.shape[3])


def gate_kernel(
    tiles, x_ref, g_ref, normed, y_ref, wout_a, wg_a, p0, p1, p2, p3, gain,
    out_o, gy_o, keep_o, send_o, ggate_o, ggain_o, wgo_o, hn_s, other_s,
):
    i = pl.program_id(0)
    dm = x_ref.shape[1]

    @pl.when(i == 0)
    def _():
        assemble(other_s, (p0, p1, p2, p3))
        wgo_o[...] = other_s[:, dm:]

    wout = (wout_a[...], other_s[:, 0:dm])

    chans = y_ref.shape[1]
    half = chans // 2
    y = y_ref[...].astype(F32)
    nrows = normed[pl.ds(pl.multiple_of(i * BLOCK + HALO, HALO), BLOCK), :]
    gate = jnp.concatenate([mm(nrows, wg_a[...]), mm(nrows, other_s[:, dm:])], axis=1)
    act, dact = silu_parts(gate)
    gated = y * act
    inv = lax.rsqrt(jnp.sum(gated * gated, axis=1, keepdims=True) * (1.0 / chans) + EPS)
    nrm = gated * inv
    gainv = gain[0:1, :]
    hn = (nrm * gainv).astype(BF16)
    rows = pl.ds(pl.multiple_of(i * BLOCK, BLOCK), BLOCK)
    hn_s[rows, :] = hn
    branch = mm(hn[:, 0:half], wout[0]) + mm(hn[:, half:], wout[1])
    out_o[...] = (x_ref[rows, :].astype(F32) + branch).astype(BF16)
    g = g_ref[rows, :]
    ghn = jnp.concatenate([nt(g, wout[0]), nt(g, wout[1])], axis=1)

    @pl.when(i == 0)
    def _():
        ggain_o[...] = jnp.zeros_like(ggain_o)

    ggain_o[0:1, :] += jnp.sum(ghn * nrm, axis=0, keepdims=True)
    wgt = ghn * gainv
    cross = jnp.sum(wgt * gated, axis=1, keepdims=True) * (1.0 / chans)
    ggated = inv * wgt - gated * (inv * inv * inv * cross)
    gy_o[...] = (ggated * act).astype(BF16)
    ggate_o[rows, :] = (ggated * y * dact).astype(BF16)

    @pl.when(i == tiles - 1)
    def _():
        length = g_ref.shape[0]
        gt = g_ref[...].T
        nt_ = normed[HALO : HALO + length, :].T
        for k in range(2):
            for p in range(half // 256):
                cols = slice(k * half + p * 256, k * half + (p + 1) * 256)
                dst = slice(p * 256, (p + 1) * 256)
                dst2 = slice(half + p * 256, half + (p + 1) * 256)
                by_core(mm(gt, hn_s[:, cols]), keep_o.at[k, :, dst], send_o.at[k, :, dst])
                by_core(mm(nt_, ggate_o[:, cols]), keep_o.at[k, :, dst2], send_o.at[k, :, dst2])


def gstate_kernel(length, info, gy_ref, et, cet, dpt, gs_o, bnd_o):
    nb = length // BLOCK
    j = pl.program_id(0)
    lane = iota((BLOCK, 128), 1)
    top = iota((BLOCK, 128), 0) < 64
    loc = []
    for b in range(nb):
        blk = slice(b * BLOCK, (b + 1) * BLOCK)
        gy = gy_ref[blk, :]
        got = []
        for i in range(2):
            h = 2 * j + i
            e = jnp.where(top, et[b, pl.ds(h, 1), :], et[b, pl.ds(64 + h, 1), :])
            got.append(mm((cet[b] * e).astype(BF16), gy))
        loc.append(jnp.where(lane < 64, got[0], got[1]))
    state = jnp.zeros((64, 128), F32)
    gs_o[0, nb, 0:64, :] = state.astype(BF16)
    for b in range(nb - 1, -1, -1):
        state = pair_rows(dpt, j, 0, b, 0) * state + loc[b][0:64, :]
        gs_o[0, b, 0:64, :] = state.astype(BF16)
    end_f = state
    state = jnp.zeros((64, 128), F32)
    gs_o[0, 0, 64:128, :] = state.astype(BF16)
    for b in range(nb):
        state = pair_rows(dpt, j, 0, b, 1) * state + loc[b][64:128, :]
        gs_o[0, b + 1, 64:128, :] = state.astype(BF16)
    bnd_o[0] = jnp.where(info[7] == 1, end_f, state).astype(BF16)


def gscan_kernel(
    length, info, xc_ref, ds_ref, gy_ref, st_ref, gs_ref, gs0_ref, dpt, rows_ref, coltt, et, gt, bk, cet, skip,
    gmix_o, ggt_o, gb_o, gct_o, k_o, r_o, phi_o, gskip_o, gst_s,
):
    nb = length // BLOCK
    j = pl.program_id(0)
    right = (info[7] == 1).astype(F32)
    s0 = gs0_ref[0].astype(F32)
    sub = iota((BLOCK, BLOCK), 0)
    lane = iota((BLOCK, 128), 1)
    first = lane < 64
    later = lane > sub
    top = sub < 64

    @pl.when(j == 0)
    def _():
        ggt_o[...] = jnp.zeros_like(ggt_o)
        gb_o[...] = jnp.zeros_like(gb_o)
        gct_o[...] = jnp.zeros_like(gct_o)
        k_o[...] = jnp.zeros_like(k_o)
        r_o[...] = jnp.zeros_like(r_o)

    phi_o[...] = jnp.zeros_like(phi_o)
    for i in range(nb + 1):
        f = gs_ref[0, i, 0:64, :].astype(F32) + pair_rows(dpt, j, 32, i, 0) * (s0 * (1.0 - right))
        r = gs_ref[0, i, 64:128, :].astype(F32) + pair_rows(dpt, j, 32, i, 1) * (s0 * right)
        f = f.astype(BF16)
        r = r.astype(BF16)
        gst_s[i, 0:64, :] = f
        gst_s[i, 64:128, :] = r
        if i > 0:
            phi_o[i - 1 : i, :] = jnp.sum(f.astype(F32) * st_ref[0, i, 0:64, :].astype(F32), axis=0, keepdims=True)
        if i < nb:
            phi_o[8 + i : 9 + i, :] = jnp.sum(
                r.astype(F32) * st_ref[0, i, 64:128, :].astype(F32), axis=0, keepdims=True
            )
    gskip = jnp.zeros((1, 128), F32)
    for b in range(nb):
        blk = slice(b * BLOCK, (b + 1) * BLOCK)
        xb = xc_ref[blk, :]
        gy = gy_ref[blk, :]
        gyf = gy.astype(F32)
        gskip = gskip + jnp.sum(gyf * xb.astype(F32), axis=0, keepdims=True)
        rhs = jnp.concatenate([gy, gst_s[b + 1, 0:64, :], gst_s[b, 64:128, :]], axis=0)
        left = jnp.concatenate([xb, st_ref[0, b, 0:64, :], st_ref[0, b + 1, 64:128, :]], axis=0)
        lane2 = iota((2 * BLOCK, 128), 1)
        got = []
        for i in range(2):
            h = 2 * j + i
            mine = pltpu.roll(rows_ref[blk, :], 128 - h, 1)
            cf = jnp.broadcast_to(mine[:, 0:1], (BLOCK, 128))
            cb = jnp.broadcast_to(mine[:, 64:65], (BLOCK, 128))
            diff = jnp.where(later, cf + coltt[b, pl.ds(h, 1), :], cb + coltt[b, pl.ds(64 + h, 1), :])
            et_m = jnp.exp(jnp.minimum(diff, 60.0))
            mt = et_m * gt[b]
            endf = dpt[pl.ds(h, 1), :][:, 48 + b : 49 + b]
            endb = dpt[pl.ds(64 + h, 1), :][:, 48 + b : 49 + b]
            w = jnp.exp(jnp.minimum(jnp.where(first, cf + endf, cb + endb), 60.0))
            bt = bk[blk, :] * w
            lhs_b = jnp.where((lane2 < 64) == (i == 0), left, jnp.zeros_like(left))
            big = nt(lhs_b, rhs)
            gmt = big[0:BLOCK, 0:BLOCK]
            gbt = big[0:BLOCK, BLOCK:]
            gctt = big[BLOCK:, 0:BLOCK]
            ge = gmt * et_m
            ggt_o[b] += ge
            q = gmt * mt
            qf = jnp.where(later, q, 0.0)
            qb = q - qf
            e = jnp.where(top, et[b, pl.ds(h, 1), :], et[b, pl.ds(64 + h, 1), :])
            gce = gctt * e
            gct_o[b] += gce
            ct = gce * cet[b]
            r_o[b, pl.ds(h, 1), :] = jnp.sum(qf, axis=0, keepdims=True) + jnp.sum(ct[0:64, :], axis=0, keepdims=True)
            r_o[b, pl.ds(64 + h, 1), :] = jnp.sum(qb, axis=0, keepdims=True) + jnp.sum(
                ct[64:128, :], axis=0, keepdims=True
            )
            gb_o[b] += gbt * w
            u = gbt * bt
            kf = jnp.sum(qf + jnp.where(first, u, 0.0), axis=1, keepdims=True)
            kb = jnp.sum(qb + jnp.where(first, 0.0, u), axis=1, keepdims=True)
            k_o[blk, :] += jnp.where(lane == h, kf, jnp.where(lane == 64 + h, kb, 0.0))
            lhs = jnp.concatenate([mt.astype(BF16), bt.astype(BF16)], axis=1)
            got.append(mm(lhs, rhs))
        gx = jnp.where(first, got[0], got[1]) + skip[0:1, :] * gyf
        gmix_o[blk, :] = (gx * ds_ref[blk, :].astype(F32)).astype(BF16)
    gskip_o[...] = jnp.broadcast_to(gskip, (8, 128))


def join_kernel(
    length, heads, info, ggt, gb, gct, k_ref, r_ref, phi, b_ref, c_ref, bk, dsl, a_ref, sig,
    gmb_o, gv_o, small_o, gc_s, gm_s,
):
    nb = length // BLOCK
    off = info[5]
    chans = phi.shape[1]
    sub = iota((BLOCK, BLOCK), 0)
    lane = iota((BLOCK, 128), 1)
    first = lane < 64
    low = sub > lane
    high = sub < lane
    upper_strict = high.astype(F32)
    upper = (sub <= lane).astype(F32)
    lower_strict = low.astype(F32)
    lower = (sub >= lane).astype(F32)
    owner = iota((chans, 128), 0) // 64
    to_f = (owner == iota((chans, 128), 1)).astype(F32)
    to_b = (owner + 64 == iota((chans, 128), 1)).astype(F32)
    phi_f = mm(phi[0:8, :], to_f, precision=HIGH)
    phi_b = mm(phi[8:16, :], to_b, precision=HIGH)
    gc_s[...] = jnp.zeros_like(gc_s)
    gm_s[...] = jnp.zeros_like(gm_s)
    sum_bias = jnp.zeros((1, 128), F32)
    sum_rate = jnp.zeros((1, 128), F32)
    for b in range(nb):
        blk = slice(b * BLOCK, (b + 1) * BLOCK)
        ext = slice(HALO + b * BLOCK, HALO + (b + 1) * BLOCK)
        first_pos = off + b * BLOCK
        sp = seg_at(info, sub + first_pos)
        st = seg_at(info, lane + first_pos)
        before = seg_at(info, sub * 0 + (first_pos - 1))
        begin = seg_at(info, sub * 0 + first_pos)
        last = seg_at(info, sub * 0 + (first_pos + BLOCK - 1))
        after = seg_at(info, sub * 0 + (first_pos + BLOCK))
        enter = jnp.where(first, (sp == before).astype(F32), (sp == after).astype(F32))
        keep = jnp.where(first, (sp == last).astype(F32), (sp == begin).astype(F32))
        same = sp == st
        gg = ggt[b]
        gf = jnp.where(same & high, gg, 0.0).astype(BF16)
        gr = jnp.where(same & low, gg, 0.0).astype(BF16)
        cm = c_ref[blk, :]
        bm = b_ref[blk, :]
        gm_s[ext, 0:128] = jnp.where(first, mm(gf, cm), mm(gr, cm)) + gb[b] * keep
        gc_s[ext, :] = jnp.where(first, tn(gf, bm), tn(gr, bm)) + gct[b].T * enter
        kb = k_ref[blk, :]
        rb = r_ref[b].T
        ga_f = mm(upper_strict, rb, precision=HIGH) - mm(upper, kb, precision=HIGH) + phi_f[b : b + 1, :]
        ga_b = mm(lower_strict, rb, precision=HIGH) - mm(lower, kb, precision=HIGH) + phi_b[b : b + 1, :]
        ga = jnp.where(first, ga_f, ga_b)
        gv = kb * sig[blk, 128:256] + ga * sig[blk, 0:128]
        gv_o[blk, :] = gv.astype(BF16)
        sum_bias = sum_bias + jnp.sum(gv, axis=0, keepdims=True)
        sum_rate = sum_rate + jnp.sum(ga * a_ref[blk, :], axis=0, keepdims=True)
    small_o[...] = jnp.zeros_like(small_o)
    small_o[0:1, :] = sum_bias
    small_o[1:2, :] = sum_rate
    small_o[8:9, :] = pltpu.roll(sum_bias, 128 - heads // 2, 1)
    small_o[9:10, :] = pltpu.roll(sum_rate, 128 - heads // 2, 1)
    mid = length + HALO
    lo = HALO // 2
    pos = iota((mid, 128), 0) + (off - HALO + lo)
    seg0 = seg_at(info, pos)
    segn = seg_at(info, pos + 1)
    segp = seg_at(info, pos - 1)
    from_next = jnp.where(seg0 == segn, gc_s[lo + 1 : lo + 1 + mid, :], 0.0)
    from_prev = jnp.where(seg0 == segp, gc_s[lo - 1 : lo - 1 + mid, :], 0.0)
    gm_s[lo : lo + mid, 128:256] = jnp.where(iota((mid, 128), 1) < 64, from_next, from_prev)
    gmb_o[...] = gm_s[...] * dsl[...]


def back_kernel(
    length, steps, info, gmix, edge, vm, wv_a, wg_a, wv_b, wg_b, ggate, normed, taps, gmb, edge_bc, bcm, taps_bc, gv, wdt, wbc, x_ref, g_ref, rs, pre,
    keep_o, send_o, gtaps_o, keepbc_o, sendbc_o, gtapsbc_o, gin_o, gpre_o, acc_s, ext_s, vm_s, seg_s,
):
    j = pl.program_id(0)
    ext = length + 2 * HALO
    off, count = info[5], info[4]
    own = slice(HALO, HALO + length)

    @pl.when(j == 0)
    def _():
        seg_s[...] = seg_at(info, iota((ext, 128), 0) + (off - HALO))
        ext_s[...] = jnp.zeros_like(ext_s)

    seg0 = seg_s[own, :]
    live = iota((length, 128), 0) + off < count

    def back_conv(grad, data, tap, gtap):
        total = grad[own, :] * tap[3:4, :]
        mine = grad[own, :]
        gtap[3:4, :] = jnp.sum(mine * data[own, :], axis=0, keepdims=True)
        for k in (0, 1, 2, 4, 5, 6):
            lo = HALO + 3 - k
            same = seg_s[lo : lo + length, :] == seg0
            total = total + jnp.where(same, grad[lo : lo + length, :], 0.0) * tap[k : k + 1, :]
            up = HALO + k - 3
            same = seg_s[up : up + length, :] == seg0
            gtap[k : k + 1, :] = jnp.sum(
                jnp.where(same, data[up : up + length, :], 0.0) * mine, axis=0, keepdims=True
            )
        gtap[7:8, :] = jnp.zeros((1, 128), F32)
        return jnp.where(live, total, 0.0)

    @pl.when(j == 0)
    def _():
        no = normed[own, :]
        both = []
        for k in range(2):
            cols = slice(k * 128, (k + 1) * 128)
            ext_s[...] = gmb[:, cols]
            lo = HALO // 2
            hi = length + lo
            got = edge_bc[:, cols]
            ext_s[lo : lo + HALO, :] += jnp.where(info[7] == 1, got, 0.0)
            ext_s[hi : hi + HALO, :] += jnp.where(info[7] == 1, 0.0, got)
            vm_s[...] = bcm[:, cols]
            gbc = back_conv(ext_s, vm_s, taps_bc.at[:, cols], gtapsbc_o.at[:, cols])
            both.append(gbc.astype(BF16))
        gbc = jnp.concatenate(both + [gv[...]], axis=1)
        gw = tn(no, gbc)
        by_core(gw, keepbc_o.at[0], sendbc_o.at[0])
        turned = pltpu.roll(gw[:, 256:], 128 - steps, 1)
        by_core(jnp.concatenate([gw[:, 0:256], turned], axis=1), keepbc_o.at[1], sendbc_o.at[1])
        acc_s[...] = nt(gbc[:, 0:256], wbc[...]) + nt(gv[...], wdt[...])

    ext_s[own, :] = gmix[...].astype(F32)
    halo = edge[...].astype(F32)
    right = info[7] == 1
    ext_s[0:HALO, :] = jnp.where(right, halo, 0.0)
    ext_s[HALO + length : ext, :] = jnp.where(right, 0.0, halo)
    vm_s[...] = vm[...].astype(F32)
    gvals = back_conv(ext_s, vm_s, taps, gtaps_o).astype(BF16)
    by_core(tn(normed[own, :], gvals), keep_o.at[0], send_o.at[0])
    both = jnp.concatenate([gvals, ggate[...]], axis=1)
    mine = j < steps // 2
    weights = jnp.concatenate(
        [jnp.where(mine, wv_a[...], wv_b[...]), jnp.where(mine, wg_a[...], wg_b[...])], axis=1
    )
    acc_s[...] += nt(both, weights)

    @pl.when(j == steps - 1)
    def _():
        x = x_ref[...].astype(F32)
        gn = acc_s[...]
        r = rs[...]
        wp = gn * pre[...]
        mean = jnp.mean(wp * x, axis=1, keepdims=True)
        gin_o[...] = g_ref[...].astype(F32) + r * wp - x * (r * r * r * mean)
        gpre_o[...] = jnp.broadcast_to(jnp.sum(gn * x * r, axis=0, keepdims=True), gpre_o.shape)


def whole(shape, grid):
    zeros = (0,) * len(shape)
    if grid:
        return pl.BlockSpec(shape, lambda j: zeros)
    return pl.BlockSpec(shape, lambda: zeros)


def columns(rows, first=0):
    return pl.BlockSpec((rows, 128), lambda j: (0, first + j))


SMEM = pl.BlockSpec(memory_space=pltpu.SMEM)
VMEM = pl.BlockSpec(memory_space=pltpu.VMEM)
ANY = pl.BlockSpec(memory_space=pl.ANY)


def sds(shape, dtype):
    return jax.ShapeDtypeStruct(shape, dtype)


def params(grid):
    if grid:
        return pltpu.CompilerParams(vmem_limit_bytes=VMEM_LIMIT, dimension_semantics=("arbitrary",))
    return pltpu.CompilerParams(vmem_limit_bytes=VMEM_LIMIT)


def cost(us):
    return pl.CostEstimate(flops=int(us * 1.1e9), bytes_accessed=int(us * 1e6), transcendentals=0)


def pack_columns(v):
    n = v.shape[-1] // 4
    return jnp.concatenate([v[..., 0:n], v[..., 2 * n : 3 * n], v[..., n : 2 * n], v[..., 3 * n :]], axis=-1)


def small_kernel(hl, conv, gain, dtb, alog, skip, out_o):
    ch = out_o.shape[1]
    out_o[...] = jnp.zeros_like(out_o)
    lane = iota((1, 128), 1)
    wide_lane = iota((1, ch), 1)
    bias = jnp.zeros((1, 128), F32)
    rate = jnp.zeros((1, 128), F32)
    diag = jnp.zeros((1, ch), F32)
    for h in range(hl):
        cols = slice(h * HD, (h + 1) * HD)
        out_o[0:7, cols] = conv[:, h, :]
        out_o[8:9, cols] = gain[h : h + 1, :]
        bias = jnp.where(lane == h, dtb[h, 0], jnp.where(lane == 64 + h, dtb[h, 1], bias))
        rate = jnp.where((lane == h) | (lane == 64 + h), alog[h], rate)
        diag = jnp.where(wide_lane // HD == h, skip[h], diag)
    out_o[16:17, :] = diag
    out_o[24:25, 0:128] = bias
    out_o[25:26, 0:128] = rate


def swap(v):
    return lax.ppermute(v, "narrow", [(0, 1), (1, 0)])


def flip(v, bit, wide):
    return lax.ppermute(v, "wide", [(i, i ^ bit) for i in range(wide)])


def cross(v, bit, wide):
    pairs = [(i * 2 + k, (i ^ bit) * 2 + 1 - k) for i in range(wide) for k in range(2)]
    return lax.ppermute(v, ("wide", "narrow"), pairs)


def pick(v, dim, index):
    return lax.dynamic_index_in_dim(v, index, dim, keepdims=False)


def total(*parts):
    acc = parts[0].astype(F32)
    for v in parts[1:]:
        acc = acc + v.astype(F32)
    return acc


def split_positions(
    wide, layer_in, pre_gain, w_heads, w_bc, conv_x, conv_bc, dt_bias, a_log, skip_d, norm_gain, w_out, cotangent, starts, live
):
    n = lax.axis_index("narrow")
    w = lax.axis_index("wide")
    left = n == 0
    _, length, dm = layer_in.shape
    hl = w_heads.shape[1]
    heads = 2 * hl
    ch = hl * HD
    chans = 2 * ch
    pairs = heads // 2
    hp = pairs // 2
    nb = length // BLOCK
    ext = length + 2 * HALO
    share = dm // wide
    x = layer_in[0]
    g = cotangent[0]
    xbit = (w // 2) % 2
    zbits = w // 4

    edge = swap(jnp.where(left, x[length - HALO :], x[:HALO]))
    small_own = pl.pallas_call(
        functools.partial(small_kernel, hl),
        out_shape=sds((32, ch), F32),
        in_specs=[VMEM, VMEM, SMEM, SMEM, SMEM],
        out_specs=VMEM,
        name="small",
    )(conv_x, norm_gain, dt_bias, a_log, skip_d)
    small_other = swap(small_own)
    wdt = w_heads[:, :, 2 * HD :].reshape(dm, 2 * hl)
    wdt_other = swap(wdt)

    quarter = dm // 4
    q = w % 4

    def gather(own):
        p0 = swap(lax.dynamic_slice(own, (q * quarter, 0), (quarter, own.shape[1])))
        p1 = flip(p0, 2, wide)
        return p0, p1, flip(p0, 1, wide), flip(p1, 1, wide)

    wv = w_heads[:, :, HD : 2 * HD].reshape(dm, ch)
    wg = w_heads[:, :, :HD].reshape(dm, ch)
    wo = w_out.reshape(ch, dm)
    wv_pieces = gather(wv)
    wog_pieces = gather(jnp.concatenate([wo, wg], axis=1))

    pos = (length, 128)
    sq = (nb, BLOCK, BLOCK)
    front_shapes = [
        ((8, chans), F32), ((8, chans), F32), ((8, chans), F32), ((dm, 128), BF16), ((dm, 256), BF16), ((7, 256), F32),
        ((ext, dm), BF16), ((length, 1), F32), ((ext, 256), F32), ((ext, 256), F32), (pos, BF16), (pos, F32), (sq, F32),
        (pos, BF16), (pos, F32), (sq, F32), (sq, F32), (sq, F32), (pos, F32), (pos, F32), (sq, F32), (sq, F32),
        (sq, F32), (sq, F32), ((128, 128), F32), (pos, F32), ((length, 256), F32),
    ]
    (
        info, taps, gain, skip, wdt_all, wbc, taps_bc, normed, rs, bcm, dsl, bmap, bk, bkt, cmap, ce, cet, gmat, gmat_t,
        colt, rows, coltt, rowst, et, wt, dpt, a_dt, sig,
    ) = pl.pallas_call(
        functools.partial(front_kernel, length, hl),
        out_shape=[sds((8,), jnp.int32)] + [sds(*v) for v in front_shapes],
        in_specs=[SMEM] + [VMEM] * 10,
        out_specs=[SMEM] + [VMEM] * len(front_shapes),
        scratch_shapes=[
            pltpu.VMEM((ext, 256), jnp.int32), pltpu.VMEM((ext, 256), F32), pltpu.VMEM((128, 128), F32),
            pltpu.VMEM((ext, dm), BF16),
        ],
        compiler_params=params(False),
        cost_estimate=cost(8),
        name="front",
    )(starts, live, x, edge, pre_gain.reshape(1, dm), wdt, wdt_other, w_bc, conv_bc, small_own, small_other)

    state_spec = pl.BlockSpec((1, nb + 1, 128, 128), lambda j: (j, 0, 0, 0))
    bnd_spec = pl.BlockSpec((1, 64, 128), lambda j: (j, 0, 0))
    far_spec = pl.BlockSpec((1, 64, 128), lambda j: ((j + hp) % pairs, 0, 0))
    state_shape = sds((pairs, nb + 1, 128, 128), BF16)
    bnd_shape = sds((pairs, 64, 128), BF16)
    act_shape = sds((length, chans), BF16)
    own_spec = pl.BlockSpec((dm, 128), lambda j: (0, jnp.minimum(j, hp - 1)))
    other_spec = pl.BlockSpec((dm, 128), lambda j: (0, jnp.maximum(j - hp, 0)))

    def vals(other, weights, before):
        first = hp if other else 0
        extra = [sds((dm, ch), BF16)] if other else []
        specs = [SMEM, whole((ext, dm), 1)]
        if other:
            specs += [whole((quarter, ch), 1)] * 4
        else:
            specs += [columns(dm)]
        specs += [columns(8, first), whole(sq, 1), whole(sq, 1), whole((128, 128), 1)] + [ANY] * len(before)
        scratch = [pltpu.VMEM((ext, 128), F32), pltpu.VMEM((ext, 128), jnp.int32)]
        if other:
            scratch.append(pltpu.VMEM((hp, dm, 128), BF16))
        return pl.pallas_call(
            functools.partial(vals_kernel, length, other),
            grid=(hp,),
            out_shape=[act_shape, sds((ext, chans), BF16), act_shape, state_shape, bnd_shape] + extra,
            in_specs=specs,
            out_specs=[
                columns(length, first), columns(ext, first), columns(length, first),
                pl.BlockSpec((1, nb + 1, 128, 128), lambda j: (j + first, 0, 0, 0)),
                pl.BlockSpec((1, 64, 128), lambda j: (j + first, 0, 0)),
            ] + [whole((dm, ch), 1)] * other,
            scratch_shapes=scratch,
            input_output_aliases={len(specs) - len(before) + i: i for i in range(len(before))},
            compiler_params=params(True),
            cost_estimate=cost(8),
            name="vals_other" if other else "vals_own",
        )(info, normed, *weights, taps, wt, bkt, dpt, *before)

    own_vals = vals(False, (wv,), ())
    xc, vm, ds, s_loc, bnd, wv_other = vals(True, wv_pieces, own_vals)

    y, s_true = pl.pallas_call(
        functools.partial(scan_kernel, length),
        grid=(pairs,),
        out_shape=[act_shape, state_shape],
        in_specs=[
            SMEM, columns(length), state_spec, far_spec, whole((128, 128), 1), whole(pos, 1), whole(sq, 1), whole(pos, 1),
            whole(sq, 1), columns(8),
        ],
        out_specs=[columns(length), state_spec],
        compiler_params=params(True),
        cost_estimate=cost(19),
        name="scan",
    )(info, xc, s_loc, swap(bnd), dpt, colt, rowst, ce, gmat, skip)

    tile_spec = pl.BlockSpec((BLOCK, chans), lambda i: (i, 0))
    gw_shape = (2, dm // 2, dm + ch)
    out, gy, keep_a, send_a, ggate, ggain, wg_other = pl.pallas_call(
        functools.partial(gate_kernel, nb),
        grid=(nb,),
        out_shape=[
            sds((length, dm), BF16), act_shape, sds(gw_shape, BF16), sds(gw_shape, BF16), act_shape, sds((8, chans), F32),
            sds((dm, ch), BF16),
        ],
        in_specs=[
            whole((length, dm), 1), whole((length, dm), 1), whole((ext, dm), 1), tile_spec, whole((ch, dm), 1),
            whole((dm, ch), 1),
        ] + [whole((quarter, dm + ch), 1)] * 4 + [whole((8, chans), 1)],
        out_specs=[
            pl.BlockSpec((BLOCK, dm), lambda i: (i, 0)), tile_spec, whole(gw_shape, 1), whole(gw_shape, 1),
            whole((length, chans), 1), whole((8, chans), 1), whole((dm, ch), 1),
        ],
        scratch_shapes=[pltpu.VMEM((length, chans), BF16), pltpu.VMEM((dm, dm + ch), BF16)],
        compiler_params=params(True),
        cost_estimate=cost(22),
        name="gated",
    )(x, g, normed, y, wo, wg, *wog_pieces, gain)

    def meet(keep, got):
        cols = keep.shape[-1]
        keep = keep.reshape(2, wide // 4, 2, share, cols)
        got = got.reshape(2, wide // 4, 2, share, cols)

        def piece(half, xx):
            return total(pick(keep[half], 1, xx), pick(got[half], 1, xx)).astype(BF16)

        return piece(0, xbit), piece(0, 1 - xbit), piece(1, xbit), piece(1, 1 - xbit)

    def plane(mine, to_x, to_y, to_d):
        return total(mine, flip(to_x, 2, wide), swap(to_y), cross(to_d, 2, wide)).astype(mine.dtype)

    def depth(v):
        parts = [pick(v, 0, zbits)]
        for k in (1, 2, 3):
            parts.append(flip(pick(v, 0, zbits ^ k), 4 * k, wide))
        return total(*parts)

    a_pieces = meet(keep_a, flip(send_a, 1, wide))

    gs_loc, gbnd = pl.pallas_call(
        functools.partial(gstate_kernel, length),
        grid=(pairs,),
        out_shape=[state_shape, bnd_shape],
        in_specs=[SMEM, columns(length), whole(sq, 1), whole(sq, 1), whole((128, 128), 1)],
        out_specs=[state_spec, bnd_spec],
        compiler_params=params(True),
        cost_estimate=cost(9),
        name="gstate",
    )(info, gy, et, cet, dpt)

    gs_loc, gbnd, *a_pieces = lax.optimization_barrier((gs_loc, gbnd, *a_pieces))
    a_plane = plane(*a_pieces)

    gmix, ggt, gb, gct, ksum, rsum, phi, gskip = pl.pallas_call(
        functools.partial(gscan_kernel, length),
        grid=(pairs,),
        out_shape=[
            act_shape, sds(sq, F32), sds(sq, F32), sds(sq, F32), sds(pos, F32), sds(sq, F32), sds((16, chans), F32),
            sds((8, chans), F32),
        ],
        in_specs=[
            SMEM, columns(length), columns(length), columns(length), state_spec, state_spec, far_spec, whole((128, 128), 1),
            whole(pos, 1), whole(sq, 1), whole(sq, 1), whole(sq, 1), whole(pos, 1), whole(sq, 1), columns(8),
        ],
        out_specs=[
            columns(length), whole(sq, 1), whole(sq, 1), whole(sq, 1), whole(pos, 1), whole(sq, 1), columns(16), columns(8),
        ],
        scratch_shapes=[pltpu.VMEM((nb + 1, 128, 128), BF16)],
        compiler_params=params(True),
        cost_estimate=cost(35),
        name="gscan",
    )(info, xc, ds, gy, s_true, gs_loc, swap(gbnd), dpt, rows, coltt, et, gmat_t, bk, cet, skip)

    gmix, ggt, a_plane = lax.optimization_barrier((gmix, ggt, a_plane))
    wa = depth(a_plane)
    edge_x = swap(jnp.where(left, gmix[length - HALO :], gmix[:HALO]))

    gmb, gv, small = pl.pallas_call(
        functools.partial(join_kernel, length, heads),
        out_shape=[sds((ext, 256), F32), sds(pos, BF16), sds((16, 128), F32)],
        in_specs=[SMEM] + [VMEM] * 12,
        out_specs=[VMEM] * 3,
        scratch_shapes=[pltpu.VMEM((ext, 128), F32), pltpu.VMEM((ext, 256), F32)],
        compiler_params=params(False),
        cost_estimate=cost(6),
        name="join",
    )(info, ggt, gb, gct, ksum, rsum, phi, bmap, cmap, bk, dsl, a_dt, sig)

    lo = HALO // 2
    edge_bc = swap(jnp.where(left, gmb[length + lo : length + lo + HALO], gmb[lo : lo + HALO]))

    keep_b, send_b, gtaps, keep_bc, send_bc, gtaps_bc, grad_in, gpre = pl.pallas_call(
        functools.partial(back_kernel, length, pairs),
        grid=(pairs,),
        out_shape=[
            sds((2, dm // 2, ch), BF16), sds((2, dm // 2, ch), BF16), sds((8, chans), F32), sds((2, dm // 2, 384), BF16),
            sds((2, dm // 2, 384), BF16), sds((8, 256), F32), sds((length, dm), F32), sds((8, dm), F32),
        ],
        in_specs=[
            SMEM, columns(length), pl.BlockSpec((HALO, 128), lambda j: (0, (j + hp) % pairs)), columns(ext), own_spec, own_spec,
            other_spec, other_spec, columns(length), whole((ext, dm), 1), columns(8), whole((ext, 256), 1),
            whole((HALO, 256), 1), whole((ext, 256), 1), whole((7, 256), 1), whole(pos, 1), whole((dm, 128), 1),
            whole((dm, 256), 1), whole((length, dm), 1), whole((length, dm), 1), whole((length, 1), 1), whole((1, dm), 1),
        ],
        out_specs=[
            pl.BlockSpec((1, dm // 2, 128), lambda j: (j // hp, 0, j % hp)),
            pl.BlockSpec((1, dm // 2, 128), lambda j: (j // hp, 0, j % hp)), columns(8), whole((2, dm // 2, 384), 1),
            whole((2, dm // 2, 384), 1), whole((8, 256), 1), whole((length, dm), 1), whole((8, dm), 1),
        ],
        scratch_shapes=[
            pltpu.VMEM((length, dm), F32), pltpu.VMEM((ext, 128), F32), pltpu.VMEM((ext, 128), F32),
            pltpu.VMEM((ext, 128), jnp.int32),
        ],
        compiler_params=params(True),
        cost_estimate=cost(24),
        name="back",
    )(
        info, gmix, edge_x, vm, wv, wg, wv_other, wg_other, ggate, normed, taps, gmb, edge_bc, bcm, taps_bc, gv, wdt_all, wbc,
        x, g, rs, pre_gain.reshape(1, dm),
    )

    keep_b, send_b, wa = lax.optimization_barrier((keep_b, send_b, wa))

    keep_bb = jnp.concatenate([keep_b, keep_bc], axis=2)
    send_bb = jnp.concatenate([send_b, send_bc], axis=2)
    wb = depth(plane(*meet(keep_bb, flip(send_bb, 1, wide))))

    small = jnp.pad(small, ((0, 0), (0, ch - 128)))
    common = jnp.concatenate([gpre, jnp.pad(gtaps_bc, ((0, 0), (0, dm - 256)))], axis=0)
    own_rows = jnp.concatenate([gtaps[:, :ch], ggain[:, :ch], gskip[:, :ch], small[:8], common], axis=0)
    far_rows = jnp.concatenate([gtaps[:, ch:], ggain[:, ch:], gskip[:, ch:], small[8:], common], axis=0)
    tiny = jnp.stack([own_rows, far_rows])
    tiny = tiny + flip(tiny, 1, wide)
    tiny = plane(tiny[0], tiny[0], tiny[1], tiny[1])
    tiny = total(tiny, *[flip(tiny, 4 * k, wide) for k in (1, 2, 3)])

    def part(v, dim):
        size = v.shape[dim] // wide
        return lax.dynamic_slice_in_dim(v, w * size, size, dim)

    gate_part = wa[:, dm:].reshape(share, hl, HD)
    vals_part = wb[:, :ch].reshape(share, hl, HD)
    bc_part = pack_columns(wb[:, ch : ch + 256])
    dt_cols = wb[:, ch + 256 :]
    dt_part = jnp.stack([dt_cols[:, 0:hl], dt_cols[:, 64 : 64 + hl]], axis=2)
    g_w_heads = jnp.concatenate([gate_part, vals_part, dt_part], axis=2)
    g_w_out = jnp.transpose(wa[:, :dm].reshape(share, hl, HD), (1, 2, 0))
    return (
        out[None],
        grad_in[None],
        part(tiny[32], 0),
        g_w_heads,
        bc_part,
        part(tiny[0:7].reshape(7, hl, HD), 2),
        part(pack_columns(tiny[40:47, :256]), 1),
        jnp.stack([tiny[24, 0:hl], tiny[24, 64 : 64 + hl]], axis=1),
        tiny[25, 0:hl] + tiny[25, 64 : 64 + hl],
        jnp.sum(tiny[16].reshape(hl, HD), axis=1),
        part(tiny[8].reshape(hl, HD), 1),
        g_w_out,
    )


def solution(mesh):
    body = shards
    if mesh.shape["narrow"] == 2 and mesh.shape["wide"] == 16:
        body = functools.partial(split_positions, mesh.shape["wide"])
    return jax.shard_map(
        body,
        mesh=mesh,
        in_specs=(
            P("wide", "narrow", None),
            P(),
            P(None, "narrow", None),
            P(),
            P(None, "narrow", None),
            P(),
            P("narrow", None),
            P("narrow"),
            P("narrow"),
            P("narrow", None),
            P("narrow", None, None),
            P("wide", "narrow", None),
            P("wide", None),
            P("wide", None),
        ),
        out_specs=(
            P("wide", "narrow", None),
            P("wide", "narrow", None),
            P("wide"),
            P("wide", "narrow", None),
            P("wide", None),
            P(None, "narrow", "wide"),
            P(None, "wide"),
            P("narrow", None),
            P("narrow"),
            P("narrow"),
            P("narrow", "wide"),
            P("narrow", None, "wide"),
        ),
        check_vma=False,
    )
```

```python
import functools

import jax
import jax.numpy as jnp
from jax import lax
from jax.experimental import pallas as pl
from jax.experimental.pallas import tpu as pltpu
from jax.sharding import PartitionSpec as P

H = 24
HD = 64
BLOCK = 128
SEQ_LEN = 1280


EPS = 1e-05
HIGH = lax.Precision.HIGHEST


def rounded(value):
    return value + lax.stop_gradient(value.astype(jnp.bfloat16).astype(jnp.float32) - value)


def segment_ids(starts):
    where_at = jnp.arange(SEQ_LEN, dtype=jnp.int32)
    hits = (starts[:, :, None] <= where_at[None, None, :]).astype(jnp.int32)
    return jnp.sum(hits, axis=1) - 1


def conv_doc(values, taps, seg):
    half = (taps.shape[0] - 1) // 2
    length = values.shape[1]
    padded = jnp.pad(values, ((0, 0), (half, half), (0, 0)))
    seg_pad = jnp.pad(seg, ((0, 0), (half, half)), constant_values=-1)
    total = jnp.zeros_like(values)
    for offset in range(taps.shape[0]):
        same = (seg_pad[:, offset : offset + length] == seg).astype(values.dtype)
        total = total + taps[offset] * padded[:, offset : offset + length] * same[:, :, None]
    return total


def ssd_forward(xc, steps, decays, bmat, cmat, seg, prec):
    rows, length, heads, hdim = xc.shape
    blocks = length // BLOCK
    xb = xc.reshape(rows, blocks, BLOCK, heads, hdim)
    stepb = steps.reshape(rows, blocks, BLOCK, heads)
    cum = jnp.cumsum(decays.reshape(rows, blocks, BLOCK, heads), axis=2)
    bb = bmat.reshape(rows, blocks, BLOCK, -1)
    cb = cmat.reshape(rows, blocks, BLOCK, -1)
    sb = seg.reshape(rows, blocks, BLOCK)
    order = jnp.arange(BLOCK, dtype=jnp.int32)
    causal = order[:, None] >= order[None, :]
    same = ((sb[:, :, :, None] == sb[:, :, None, :]) & causal)[..., None]
    diff = cum[:, :, :, None, :] - cum[:, :, None, :, :]
    weights = jnp.where(same, jnp.exp(jnp.where(same, diff, 0.0)), 0.0)
    inner = jnp.einsum("rbtn,rbsn->rbts", cb, bb, precision=prec)
    mix = weights * inner[..., None] * stepb[:, :, None, :, :]
    intra = jnp.einsum("rbtsh,rbshp->rbthp", mix, xb, precision=prec)
    last = sb[:, :, -1]
    cum_end = cum[:, :, -1, :]
    to_end = (
        (sb == last[:, :, None]).astype(cum.dtype)[..., None]
        * jnp.exp(cum_end[:, :, None, :] - cum)
        * stepb
    )
    states = jnp.einsum("rbshp,rbsn->rbhpn", to_end[..., None] * xb, bb, precision=prec)
    decay_end = jnp.exp(cum_end)

    def carry_step(carry, item):
        state, seg_prev = carry
        block_state, block_last, block_decay = item
        keep = (block_last == seg_prev).astype(state.dtype)[:, None, None, None]
        fresh = keep * block_decay[:, :, None, None] * state + block_state
        return ((fresh, block_last), (state, seg_prev))

    init = (
        jnp.zeros((rows, heads, hdim, bb.shape[-1]), xc.dtype),
        jnp.full((rows,), -1, jnp.int32),
    )
    items = (jnp.moveaxis(states, 1, 0), jnp.moveaxis(last, 1, 0), jnp.moveaxis(decay_end, 1, 0))
    _, (before, seg_before) = lax.scan(carry_step, init, items)
    before = jnp.moveaxis(before, 0, 1)
    seg_before = jnp.moveaxis(seg_before, 0, 1)
    enter = (sb == seg_before[:, :, None]).astype(cum.dtype)[..., None] * jnp.exp(cum)
    inter = jnp.einsum("rbtn,rbhpn->rbthp", cb, before, precision=prec) * enter[..., None]
    return (intra + inter).reshape(rows, length, heads, hdim)


def mixer(proj, bcproj, conv_x, conv_bc, dt_bias, a_log, skip_d, seg, mask, rounder, prec):
    rows, length, heads, width = proj.shape
    hdim = (width - 2) // 2
    state = bcproj.shape[-1] // 4
    gate = proj[..., :hdim]
    values = proj[..., hdim : 2 * hdim] * mask[:, :, None, None]
    mixed_x = conv_doc(
        values.reshape(rows, length, heads * hdim),
        conv_x.reshape(conv_x.shape[0], heads * hdim),
        seg,
    )
    xc = rounder(jax.nn.silu(mixed_x)).reshape(rows, length, heads, hdim)
    maps = rounder(jax.nn.silu(conv_doc(bcproj * mask[:, :, None], conv_bc, seg)))
    b_fwd = maps[..., :state]
    c_fwd = maps[..., state : 2 * state]
    b_bwd = maps[..., 2 * state : 3 * state]
    c_bwd = maps[..., 3 * state :]
    rate = -jnp.exp(a_log)
    dt_fwd = jax.nn.softplus(proj[..., 2 * hdim] + dt_bias[:, 0]) * mask[:, :, None]
    dt_bwd = jax.nn.softplus(proj[..., 2 * hdim + 1] + dt_bias[:, 1]) * mask[:, :, None]
    out_fwd = ssd_forward(xc, dt_fwd, dt_fwd * rate, b_fwd, c_fwd, seg, prec)

    def flip(v):
        return jnp.flip(v, axis=1)

    out_bwd = flip(
        ssd_forward(
            flip(xc), flip(dt_bwd), flip(dt_bwd * rate), flip(b_bwd), flip(c_bwd), flip(seg), prec
        )
    )
    keep_prev = (seg[:, 1:] == seg[:, :-1]).astype(xc.dtype)[:, :, None, None]
    shifted_fwd = jnp.pad(out_fwd[:, :-1] * keep_prev, ((0, 0), (1, 0), (0, 0), (0, 0)))
    shifted_bwd = jnp.pad(out_bwd[:, 1:] * keep_prev, ((0, 0), (0, 1), (0, 0), (0, 0)))
    return (shifted_fwd + shifted_bwd + skip_d[:, None] * xc, gate)


def shards(
    layer_in,
    pre_gain,
    w_heads,
    w_bc,
    conv_x,
    conv_bc,
    dt_bias,
    a_log,
    skip_d,
    norm_gain,
    w_out,
    cotangent,
    starts,
    live,
):
    seg = segment_ids(starts)
    mask = live.astype(jnp.float32)
    x_here = layer_in.astype(jnp.float32)
    scale = lax.rsqrt(jnp.mean(x_here * x_here, axis=-1, keepdims=True) + EPS)
    normed_here = (x_here * scale * pre_gain).astype(jnp.bfloat16)
    normed = lax.all_gather(normed_here, "narrow", axis=1, tiled=True)
    proj = jnp.einsum("rld,dhc->rlhc", normed, w_heads, preferred_element_type=jnp.float32)
    bcproj = jnp.einsum("rld,dc->rlc", normed, w_bc, preferred_element_type=jnp.float32)

    def mix_local(proj_in, bc_in, taps_x, taps_bc, bias_in, log_rate, diag_in):
        return mixer(
            proj_in, bc_in, taps_x, taps_bc, bias_in, log_rate, diag_in, seg, mask, rounded, HIGH
        )

    (ymix, gate), pull_mix = jax.vjp(
        mix_local, proj, bcproj, conv_x, conv_bc, dt_bias, a_log, skip_d
    )
    rows, length, heads, hdim = ymix.shape
    sigma = jax.nn.sigmoid(gate)
    act = gate * sigma
    gated = (ymix * act).reshape(rows, length, heads * hdim)
    squares = lax.psum(jnp.sum(gated * gated, axis=-1), "narrow")
    inv = lax.rsqrt(squares / (H * HD) + EPS)[..., None]
    gain_flat = norm_gain.reshape(-1)
    normalized = gated * inv
    hn = (normalized * gain_flat).astype(jnp.bfloat16)
    w_flat = w_out.reshape(heads * hdim, -1)
    partial_value = jnp.einsum("rlc,cd->rld", hn, w_flat, preferred_element_type=jnp.float32)
    branch = lax.psum_scatter(partial_value, "narrow", scatter_dimension=1, tiled=True)
    out = (x_here + branch).astype(jnp.bfloat16)
    grad_out = lax.all_gather(cotangent, "narrow", axis=1, tiled=True)
    g_w_out = jnp.einsum("rlc,rld->cd", hn, grad_out, preferred_element_type=jnp.float32)
    g_hn = jnp.einsum("rld,cd->rlc", grad_out, w_flat, preferred_element_type=jnp.float32)
    g_gain = jnp.sum(g_hn * normalized, axis=(0, 1))
    weighted = g_hn * gain_flat
    cross = lax.psum(jnp.sum(weighted * gated, axis=-1), "narrow")
    g_gated = inv * weighted - gated * (inv * inv * inv) * (cross / (H * HD))[..., None]
    g_gated = g_gated.reshape(rows, length, heads, hdim)
    g_ymix = g_gated * act
    g_gate = g_gated * ymix * (sigma * (1.0 + gate * (1.0 - sigma)))
    g_proj, g_bcproj, g_conv_x, g_conv_bc, g_dt_bias, g_a_log, g_skip = pull_mix((g_ymix, g_gate))
    g_proj_low = g_proj.astype(jnp.bfloat16)
    g_w_heads = jnp.einsum("rld,rlhc->dhc", normed, g_proj_low, preferred_element_type=jnp.float32)
    g_w_bc = jnp.einsum(
        "rld,rlc->dc", normed, g_bcproj, precision=HIGH, preferred_element_type=jnp.float32
    )
    g_normed = jnp.einsum("rlhc,dhc->rld", g_proj_low, w_heads, preferred_element_type=jnp.float32)
    g_normed = g_normed + jnp.einsum(
        "rlc,dc->rld", g_bcproj, w_bc, precision=HIGH, preferred_element_type=jnp.float32
    )
    g_normed_here = lax.psum_scatter(g_normed, "narrow", scatter_dimension=1, tiled=True)
    weighted_in = g_normed_here * pre_gain
    g_pre = jnp.sum(g_normed_here * x_here * scale, axis=(0, 1))
    g_x = scale * weighted_in - x_here * (scale * scale * scale) * jnp.mean(
        weighted_in * x_here, axis=-1, keepdims=True
    )
    grad_input = cotangent.astype(jnp.float32) + g_x
    g_pre, g_w_bc, g_conv_bc = lax.psum((g_pre, g_w_bc, g_conv_bc), "narrow")
    reduced = (
        lax.psum_scatter(g_w_heads, "wide", scatter_dimension=0, tiled=True),
        lax.psum_scatter(g_w_out.reshape(heads, hdim, -1), "wide", scatter_dimension=2, tiled=True),
        lax.psum_scatter(g_conv_x, "wide", scatter_dimension=2, tiled=True),
        lax.psum_scatter(g_gain.reshape(heads, hdim), "wide", scatter_dimension=1, tiled=True),
        lax.psum_scatter(g_pre, "wide", scatter_dimension=0, tiled=True),
        lax.psum_scatter(g_w_bc, "wide", scatter_dimension=0, tiled=True),
        lax.psum_scatter(g_conv_bc, "wide", scatter_dimension=1, tiled=True),
    )
    share_pre, share_bc, share_conv = (reduced[4], reduced[5], reduced[6])
    head_bias, head_rate, head_diag = lax.psum((g_dt_bias, g_a_log, g_skip), "wide")
    return (
        out,
        grad_input,
        share_pre,
        reduced[0],
        share_bc,
        reduced[2],
        share_conv,
        head_bias,
        head_rate,
        head_diag,
        reduced[3],
        reduced[1],
    )


HALO = 16
F32 = jnp.float32
BF16 = jnp.bfloat16
LOGZERO = -1e30
VMEM_LIMIT = 56 * 2**20


def mm(a, b, dims=((1,), (0,)), precision=None):
    return lax.dot_general(a, b, (dims, ((), ())), precision=precision, preferred_element_type=F32)


def nt(a, b):
    return mm(a, b, ((1,), (1,)))


def tn(a, b):
    return mm(a, b, ((0,), (0,)))


def seg_at(info, pos):
    seg = jnp.full(pos.shape, -1, jnp.int32)
    for j in range(4):
        seg = seg + (pos >= info[j]).astype(jnp.int32)
    return jnp.where(pos >= info[6], 99, seg)


def iota(shape, dim):
    return lax.broadcasted_iota(jnp.int32, shape, dim)


def silu_parts(v):
    sg = 1.0 / (1.0 + jnp.exp(-v))
    return v * sg, sg * (1.0 + v * (1.0 - sg))


def conv_taps(src, seg_src, taps, first, rows):
    seg0 = seg_src[first : first + rows, :]
    total = src[first : first + rows, :] * taps[3:4, :]
    for k in (0, 1, 2, 4, 5, 6):
        lo = first + k - 3
        same = seg_src[lo : lo + rows, :] == seg0
        total = total + jnp.where(same, src[lo : lo + rows, :], 0.0) * taps[k : k + 1, :]
    return total


def front_kernel(
    length, hl, starts, live_ref, x_in, edge, gain, wdt_a, wdt_b, wbc_ref, taps_ref, small_a, small_b,
    info, taps_o, gain_o, skip_o, wdt, wbc, taps, normed_o, rs_o, bcm_o, dsl_o, b_o, bk_o, bkt_o, c_o, ce_o, cet_o, g_o, gt_o,
    colt_o, rows_o, coltt_o, rowst_o, et_o, wt_o, dpt_o, dt_o, sig_o, seg_s, maps_s, cum_s, x_s,
):
    nb = length // BLOCK
    ext = length + 2 * HALO
    dm = x_in.shape[1]
    n = lax.axis_index("narrow")
    for i in range(4):
        info[i] = starts[0, i]
    count = jnp.sum(live_ref[...].astype(F32)).astype(jnp.int32)
    off = n * length
    info[4] = count
    info[5] = off
    info[6] = live_ref.shape[1]
    info[7] = n
    ch = small_a.shape[1]
    taps_o[:, 0:ch] = small_a[0:8, :]
    taps_o[:, ch : 2 * ch] = small_b[0:8, :]
    gain_o[:, 0:ch] = small_a[8:16, :]
    gain_o[:, ch : 2 * ch] = small_b[8:16, :]
    skip_o[:, 0:ch] = small_a[16:24, :]
    skip_o[:, ch : 2 * ch] = small_b[16:24, :]
    src = iota((2 * hl, 128), 0)
    dst = iota((2 * hl, 128), 1)
    place = (src % 2) * 64 + src // 2
    one = jnp.float32(1.0)
    at_a = jnp.where(dst == place, one, 0.0).astype(BF16)
    at_b = jnp.where(dst == place + hl, one, 0.0).astype(BF16)
    wdt[...] = (mm(wdt_a[...], at_a) + mm(wdt_b[...], at_b)).astype(BF16)
    wbc[...] = pack_columns(wbc_ref[...])
    taps[...] = pack_columns(taps_ref[...])

    bias = small_a[24:25, 0:128] + pltpu.roll(small_b[24:25, 0:128], hl, 1)
    alog = small_a[25:26, 0:128] + pltpu.roll(small_b[25:26, 0:128], hl, 1)
    zero_edge = jnp.zeros((HALO, dm), BF16)
    x_s[0:HALO, :] = jnp.where(n == 1, edge[...], zero_edge)
    x_s[HALO : HALO + length, :] = x_in[...]
    x_s[HALO + length : ext, :] = jnp.where(n == 1, zero_edge, edge[...])
    x = x_s[...].astype(F32)
    rs = lax.rsqrt(jnp.mean(x * x, axis=1, keepdims=True) + EPS)
    normed = (x * rs * gain[...]).astype(BF16)
    normed_o[...] = normed
    rs_o[...] = rs[HALO : HALO + length, :]
    pos256 = iota((ext, 256), 0) + (off - HALO)
    seg_s[...] = seg_at(info, pos256)
    live = pos256 < count
    bcm_o[...] = jnp.where(live, mm(normed, wbc[...]), 0.0)
    crows = length + HALO
    cfirst = HALO // 2
    mix = conv_taps(bcm_o, seg_s, taps, cfirst, crows)
    maps, dsl = silu_parts(mix)
    dsl_o[...] = jnp.zeros_like(dsl_o)
    dsl_o[cfirst : cfirst + crows, :] = dsl
    maps_s[...] = jnp.zeros_like(maps_s)
    maps_s[cfirst : cfirst + crows, :] = maps.astype(BF16).astype(F32)
    own = slice(HALO, HALO + length)
    segx = seg_s[own, 0:128]
    lane = iota((length, 128), 1)
    fwd = lane < 64
    segp = seg_s[HALO - 1 : HALO - 1 + length, 0:128]
    segn = seg_s[HALO + 1 : HALO + 1 + length, 0:128]
    bmap = maps_s[own, 0:128]
    cprev = jnp.where(segp == segx, maps_s[HALO - 1 : HALO - 1 + length, 128:256], 0.0)
    cnext = jnp.where(segn == segx, maps_s[HALO + 1 : HALO + 1 + length, 128:256], 0.0)
    cmap = jnp.where(fwd, cprev, cnext)
    b_o[...] = bmap.astype(BF16)
    c_o[...] = cmap.astype(BF16)
    raw = mm(normed[own, :], wdt[...]) + bias
    softp = jnp.maximum(raw, 0.0) + jnp.log(1.0 + jnp.exp(-jnp.abs(raw)))
    softp = jnp.where(raw < -15.0, jnp.exp(jnp.minimum(raw, 0.0)), softp)
    pos128 = iota((length, 128), 0) + off
    m = pos128 < count
    dt = jnp.where(m, softp, 0.0)
    sg = jnp.where(m, 1.0 / (1.0 + jnp.exp(-raw)), 0.0)
    ratio = jnp.where(m, jnp.where(raw < -15.0, 1.0, sg / jnp.maximum(softp, 1e-30)), 0.0)
    rate = -jnp.exp(alog)
    a = dt * rate
    dt_o[...] = a
    sig_o[:, 0:128] = sg * rate
    sig_o[:, 128:256] = ratio
    tri = (iota((BLOCK, BLOCK), 0) >= iota((BLOCK, BLOCK), 1)).astype(F32)
    logdt = jnp.maximum(jnp.log(dt), LOGZERO)
    sub = iota((BLOCK, BLOCK), 0)
    ln = iota((BLOCK, BLOCK), 1)
    fwdb = ln < 64
    cum_s[...] = jnp.zeros_like(cum_s)
    dvals, ends = [], []
    for b in range(nb):
        blk = slice(b * BLOCK, (b + 1) * BLOCK)
        ab = a[blk, :]
        cum = mm(tri, ab, precision=HIGH)
        cx = cum - ab
        end = cum[BLOCK - 1 : BLOCK, :]
        colt = jnp.where(fwdb, cx, end - cum)
        rows = jnp.where(fwdb, logdt[blk, :] - cum, cx + logdt[blk, :] - end)
        colt_o[blk, :] = colt
        rows_o[blk, :] = rows
        coltt = colt.T
        coltt_o[b] = coltt
        et_o[b] = jnp.exp(coltt)
        rowst_o[b] = rows.T
        wt_o[b] = jnp.exp(jnp.minimum(rows + end, 60.0)).T
        first_pos = off + b * BLOCK
        sp = seg_at(info, sub + first_pos)
        st = seg_at(info, ln + first_pos)
        before = seg_at(info, sub * 0 + (first_pos - 1))
        begin = seg_at(info, sub * 0 + first_pos)
        last = seg_at(info, sub * 0 + (first_pos + BLOCK - 1))
        after = seg_at(info, sub * 0 + (first_pos + BLOCK))
        enter = jnp.where(fwdb, (sp == before).astype(F32), (sp == after).astype(F32))
        keep = jnp.where(fwdb, (sp == last).astype(F32), (sp == begin).astype(F32))
        ce = cmap[blk, :] * enter
        bk = bmap[blk, :] * keep
        ce_o[blk, :] = ce
        bk_o[blk, :] = bk
        cet_o[b] = ce.T
        bkt_o[b] = bk.T
        chain = jnp.where(fwdb[0:1, :], (last == before).astype(F32)[0:1, :], (begin == after).astype(F32)[0:1, :])
        dvals.append(jnp.exp(end) * chain)
        ends.append(end)
        cb = cmap[blk, :].astype(BF16)
        bb = bmap[blk, :].astype(BF16)
        zero = jnp.zeros_like(bb)
        same = sp == st
        low = same & (sub > ln)
        high = same & (sub < ln)
        bf = jnp.where(fwdb, bb, zero)
        br = jnp.where(fwdb, zero, bb)
        g_o[b] = jnp.where(low, nt(cb, bf), jnp.where(high, nt(cb, br), 0.0))
        gt_o[b] = jnp.where(high, nt(bf, cb), jnp.where(low, nt(br, cb), 0.0))
    ones = jnp.ones((1, 128), F32)
    prefix, suffix = [ones], [ones]
    for b in range(nb):
        prefix.append(prefix[-1] * dvals[b])
        suffix.append(suffix[-1] * dvals[nb - 1 - b])
    suffix = suffix[::-1]
    f1 = fwdb[0:1, :]
    for b in range(nb):
        cum_s[b : b + 1, :] = dvals[b]
        cum_s[48 + b : 49 + b, :] = ends[b]
    for i in range(nb + 1):
        cum_s[16 + i : 17 + i, :] = jnp.where(f1, prefix[i], suffix[i])
        cum_s[32 + i : 33 + i, :] = jnp.where(f1, suffix[i], prefix[i])
    dpt_o[...] = cum_s[...].T


def pair_rows(dpt, j, base, i, half):
    lane = iota((1, 128), 1)
    one = dpt[pl.ds(half * 64 + 2 * j, 1), :][:, base + i : base + i + 1]
    two = dpt[pl.ds(half * 64 + 2 * j + 1, 1), :][:, base + i : base + i + 1]
    return jnp.where(lane < 64, one, two)


def assemble(dst, pieces):
    quarter = dst.shape[0] // 4
    q = lax.axis_index("wide") % 4
    cbit = q % 2
    xbit = q // 2
    places = (q, (1 - xbit) * 2 + cbit, xbit * 2 + 1 - cbit, (1 - xbit) * 2 + 1 - cbit)
    for place, piece in zip(places, pieces):
        dst[pl.ds(pl.multiple_of(place * quarter, quarter), quarter), :] = piece[...]


def vals_kernel(
    length, other, info, normed, *refs,
):
    nb = length // BLOCK
    ext = length + 2 * HALO
    j = pl.program_id(0)
    step = j
    if other:
        p0, p1, p2, p3, taps, wt, bkt, dpt = refs[:8]
        xc_o, vm_o, ds_o, s_o, bnd_o, wvo_o, vm_s, seg_s, wall_s = refs[13:]
        j = j + pl.num_programs(0)

        @pl.when(step == 0)
        def _():
            assemble(wvo_o, (p0, p1, p2, p3))
            for i in range(wall_s.shape[0]):
                wall_s[i] = wvo_o[:, i * 128 : (i + 1) * 128]

        wv = wall_s[step]
    else:
        wv_ref, taps, wt, bkt, dpt, xc_o, vm_o, ds_o, s_o, bnd_o, vm_s, seg_s = refs
        wv = wv_ref[...]
    off, count = info[5], info[4]

    @pl.when(step == 0)
    def _():
        seg_s[...] = seg_at(info, iota((ext, 128), 0) + (off - HALO))

    live = iota((ext, 128), 0) + (off - HALO) < count
    vm = jnp.where(live, mm(normed[...], wv), 0.0)
    vm_s[...] = vm
    vm_o[...] = vm.astype(BF16)
    mix = conv_taps(vm_s, seg_s, taps, HALO, length)
    act, ds = silu_parts(mix)
    xc = act.astype(BF16)
    xc_o[...] = xc
    ds_o[...] = ds.astype(BF16)
    lane = iota((BLOCK, 128), 1)
    top = iota((BLOCK, 128), 0) < 64
    loc = []
    for b in range(nb):
        blk = slice(b * BLOCK, (b + 1) * BLOCK)
        got = []
        for i in range(2):
            h = 2 * j + i
            w = jnp.where(top, wt[b, pl.ds(h, 1), :], wt[b, pl.ds(64 + h, 1), :])
            got.append((bkt[b] * w).astype(BF16))
        got = mm(jnp.concatenate(got, axis=0), xc[blk, :])
        loc.append(jnp.where(lane < 64, got[0:BLOCK, :], got[BLOCK:, :]))
    state = jnp.zeros((64, 128), F32)
    s_o[0, 0, 0:64, :] = state.astype(BF16)
    for b in range(nb):
        state = pair_rows(dpt, j, 0, b, 0) * state + loc[b][0:64, :]
        s_o[0, b + 1, 0:64, :] = state.astype(BF16)
    end_f = state
    state = jnp.zeros((64, 128), F32)
    s_o[0, nb, 64:128, :] = state.astype(BF16)
    for b in range(nb - 1, -1, -1):
        state = pair_rows(dpt, j, 0, b, 1) * state + loc[b][64:128, :]
        s_o[0, b, 64:128, :] = state.astype(BF16)
    bnd_o[0] = jnp.where(info[7] == 0, end_f, state).astype(BF16)


def scan_kernel(length, info, xc_ref, s_ref, s0_ref, dpt, colt, rowst, ce, g, skip, y_o, st_o):
    nb = length // BLOCK
    j = pl.program_id(0)
    right = (info[7] == 1).astype(F32)
    s0 = s0_ref[0].astype(F32)
    lane = iota((BLOCK, 128), 1)
    first = lane < 64
    low = iota((BLOCK, BLOCK), 0) > lane
    for i in range(nb + 1):
        f = s_ref[0, i, 0:64, :].astype(F32) + pair_rows(dpt, j, 16, i, 0) * (s0 * right)
        r = s_ref[0, i, 64:128, :].astype(F32) + pair_rows(dpt, j, 16, i, 1) * (s0 * (1.0 - right))
        st_o[0, i, 0:64, :] = f.astype(BF16)
        st_o[0, i, 64:128, :] = r.astype(BF16)
    for b in range(nb):
        blk = slice(b * BLOCK, (b + 1) * BLOCK)
        xb = xc_ref[blk, :]
        rhs = jnp.concatenate([xb, st_o[0, b, 0:64, :], st_o[0, b + 1, 64:128, :]], axis=0)
        got = []
        for i in range(2):
            h = 2 * j + i
            mine = pltpu.roll(colt[blk, :], 128 - h, 1)
            cf = jnp.broadcast_to(mine[:, 0:1], (BLOCK, 128))
            cb = jnp.broadcast_to(mine[:, 64:65], (BLOCK, 128))
            diff = jnp.where(low, cf + rowst[b, pl.ds(h, 1), :], cb + rowst[b, pl.ds(64 + h, 1), :])
            mix = jnp.exp(jnp.minimum(diff, 60.0)) * g[b]
            ct = ce[blk, :] * jnp.exp(jnp.where(first, cf, cb))
            lhs = jnp.concatenate([mix.astype(BF16), ct.astype(BF16)], axis=1)
            got.append(lhs)
        got = mm(jnp.concatenate(got, axis=0), rhs)
        y = jnp.where(first, got[0:BLOCK, :], got[BLOCK:, :]) + skip[0:1, :] * xb.astype(F32)
        y_o[blk, :] = y.astype(BF16)


def by_core(v, keep, send):
    share = v.shape[0] // 16
    cbit = lax.axis_index("wide") % 2
    v = v.astype(BF16).reshape(8, 2, share, v.shape[1])
    keep[...] = jnp.where(cbit == 0, v[:, 0], v[:, 1]).reshape(8 * share, v.shape[3])
    send[...] = jnp.where(cbit == 0, v[:, 1], v[:, 0]).reshape(8 * share, v.shape[3])


def gate_kernel(
    tiles, x_ref, g_ref, normed, y_ref, wout_a, wg_a, p0, p1, p2, p3, gain,
    out_o, gy_o, keep_o, send_o, ggate_o, ggain_o, wgo_o, hn_s, other_s,
):
    i = pl.program_id(0)
    dm = x_ref.shape[1]

    @pl.when(i == 0)
    def _():
        assemble(other_s, (p0, p1, p2, p3))
        wgo_o[...] = other_s[:, dm:]

    wout = (wout_a[...], other_s[:, 0:dm])

    chans = y_ref.shape[1]
    half = chans // 2
    y = y_ref[...].astype(F32)
    nrows = normed[pl.ds(pl.multiple_of(i * BLOCK + HALO, HALO), BLOCK), :]
    gate = jnp.concatenate([mm(nrows, wg_a[...]), mm(nrows, other_s[:, dm:])], axis=1)
    act, dact = silu_parts(gate)
    gated = y * act
    inv = lax.rsqrt(jnp.sum(gated * gated, axis=1, keepdims=True) * (1.0 / chans) + EPS)
    nrm = gated * inv
    gainv = gain[0:1, :]
    hn = (nrm * gainv).astype(BF16)
    rows = pl.ds(pl.multiple_of(i * BLOCK, BLOCK), BLOCK)
    hn_s[rows, :] = hn
    branch = mm(hn[:, 0:half], wout[0]) + mm(hn[:, half:], wout[1])
    out_o[...] = (x_ref[rows, :].astype(F32) + branch).astype(BF16)
    g = g_ref[rows, :]
    ghn = jnp.concatenate([nt(g, wout[0]), nt(g, wout[1])], axis=1)

    @pl.when(i == 0)
    def _():
        ggain_o[...] = jnp.zeros_like(ggain_o)

    ggain_o[0:1, :] += jnp.sum(ghn * nrm, axis=0, keepdims=True)
    wgt = ghn * gainv
    cross = jnp.sum(wgt * gated, axis=1, keepdims=True) * (1.0 / chans)
    ggated = inv * wgt - gated * (inv * inv * inv * cross)
    gy_o[...] = (ggated * act).astype(BF16)
    ggate_o[rows, :] = (ggated * y * dact).astype(BF16)

    @pl.when(i == tiles - 1)
    def _():
        length = g_ref.shape[0]
        gt = g_ref[...].T
        nt_ = normed[HALO : HALO + length, :].T
        for k in range(2):
            for p in range(half // 256):
                cols = slice(k * half + p * 256, k * half + (p + 1) * 256)
                dst = slice(p * 256, (p + 1) * 256)
                dst2 = slice(half + p * 256, half + (p + 1) * 256)
                by_core(mm(gt, hn_s[:, cols]), keep_o.at[k, :, dst], send_o.at[k, :, dst])
                by_core(mm(nt_, ggate_o[:, cols]), keep_o.at[k, :, dst2], send_o.at[k, :, dst2])


def gstate_kernel(length, info, gy_ref, et, cet, dpt, gs_o, bnd_o):
    nb = length // BLOCK
    j = pl.program_id(0)
    lane = iota((BLOCK, 128), 1)
    top = iota((BLOCK, 128), 0) < 64
    loc = []
    for b in range(nb):
        blk = slice(b * BLOCK, (b + 1) * BLOCK)
        gy = gy_ref[blk, :]
        got = []
        for i in range(2):
            h = 2 * j + i
            e = jnp.where(top, et[b, pl.ds(h, 1), :], et[b, pl.ds(64 + h, 1), :])
            got.append((cet[b] * e).astype(BF16))
        got = mm(jnp.concatenate(got, axis=0), gy)
        loc.append(jnp.where(lane < 64, got[0:BLOCK, :], got[BLOCK:, :]))
    state = jnp.zeros((64, 128), F32)
    gs_o[0, nb, 0:64, :] = state.astype(BF16)
    for b in range(nb - 1, -1, -1):
        state = pair_rows(dpt, j, 0, b, 0) * state + loc[b][0:64, :]
        gs_o[0, b, 0:64, :] = state.astype(BF16)
    end_f = state
    state = jnp.zeros((64, 128), F32)
    gs_o[0, 0, 64:128, :] = state.astype(BF16)
    for b in range(nb):
        state = pair_rows(dpt, j, 0, b, 1) * state + loc[b][64:128, :]
        gs_o[0, b + 1, 64:128, :] = state.astype(BF16)
    bnd_o[0] = jnp.where(info[7] == 1, end_f, state).astype(BF16)


def gscan_kernel(
    length, info, xc_ref, ds_ref, gy_ref, st_ref, gs_ref, gs0_ref, dpt, rows_ref, coltt, et, gt, bk, cet, skip,
    gmix_o, ggt_o, gb_o, gct_o, k_o, r_o, phi_o, gskip_o, gst_s,
):
    nb = length // BLOCK
    j = pl.program_id(0)
    right = (info[7] == 1).astype(F32)
    s0 = gs0_ref[0].astype(F32)
    sub = iota((BLOCK, BLOCK), 0)
    lane = iota((BLOCK, 128), 1)
    first = lane < 64
    later = lane > sub
    top = sub < 64

    @pl.when(j == 0)
    def _():
        ggt_o[...] = jnp.zeros_like(ggt_o)
        gb_o[...] = jnp.zeros_like(gb_o)
        gct_o[...] = jnp.zeros_like(gct_o)
        k_o[...] = jnp.zeros_like(k_o)
        r_o[...] = jnp.zeros_like(r_o)

    phi_o[...] = jnp.zeros_like(phi_o)
    for i in range(nb + 1):
        f = gs_ref[0, i, 0:64, :].astype(F32) + pair_rows(dpt, j, 32, i, 0) * (s0 * (1.0 - right))
        r = gs_ref[0, i, 64:128, :].astype(F32) + pair_rows(dpt, j, 32, i, 1) * (s0 * right)
        f = f.astype(BF16)
        r = r.astype(BF16)
        gst_s[i, 0:64, :] = f
        gst_s[i, 64:128, :] = r
        if i > 0:
            phi_o[i - 1 : i, :] = jnp.sum(f.astype(F32) * st_ref[0, i, 0:64, :].astype(F32), axis=0, keepdims=True)
        if i < nb:
            phi_o[8 + i : 9 + i, :] = jnp.sum(
                r.astype(F32) * st_ref[0, i, 64:128, :].astype(F32), axis=0, keepdims=True
            )
    gskip = jnp.zeros((1, 128), F32)
    for b in range(nb):
        blk = slice(b * BLOCK, (b + 1) * BLOCK)
        xb = xc_ref[blk, :]
        gy = gy_ref[blk, :]
        gyf = gy.astype(F32)
        gskip = gskip + jnp.sum(gyf * xb.astype(F32), axis=0, keepdims=True)
        rhs = jnp.concatenate([gy, gst_s[b + 1, 0:64, :], gst_s[b, 64:128, :]], axis=0)
        left = jnp.concatenate([xb, st_ref[0, b, 0:64, :], st_ref[0, b + 1, 64:128, :]], axis=0)
        first2 = iota((2 * BLOCK, 128), 1) < 64
        none = jnp.zeros_like(left)
        big2 = nt(jnp.concatenate([jnp.where(first2, left, none), jnp.where(first2, none, left)], axis=0), rhs)
        got = []
        sum_ge, sum_gct, sum_gb = [], [], []
        for i in range(2):
            h = 2 * j + i
            mine = pltpu.roll(rows_ref[blk, :], 128 - h, 1)
            cf = jnp.broadcast_to(mine[:, 0:1], (BLOCK, 128))
            cb = jnp.broadcast_to(mine[:, 64:65], (BLOCK, 128))
            diff = jnp.where(later, cf + coltt[b, pl.ds(h, 1), :], cb + coltt[b, pl.ds(64 + h, 1), :])
            et_m = jnp.exp(jnp.minimum(diff, 60.0))
            mt = et_m * gt[b]
            endf = dpt[pl.ds(h, 1), :][:, 48 + b : 49 + b]
            endb = dpt[pl.ds(64 + h, 1), :][:, 48 + b : 49 + b]
            w = jnp.exp(jnp.minimum(jnp.where(first, cf, cb) + jnp.where(first[0:1, :], endf, endb), 60.0))
            bt = bk[blk, :] * w
            big = big2[2 * BLOCK * i : 2 * BLOCK * (i + 1), :]
            gmt = big[0:BLOCK, 0:BLOCK]
            gbt = big[0:BLOCK, BLOCK:]
            gctt = big[BLOCK:, 0:BLOCK]
            ge = gmt * et_m
            sum_ge.append(ge)
            q = gmt * mt
            qf = jnp.where(later, q, 0.0)
            e = jnp.where(top, et[b, pl.ds(h, 1), :], et[b, pl.ds(64 + h, 1), :])
            gce = gctt * e
            sum_gct.append(gce)
            ct = gce * cet[b]
            rf = jnp.sum(qf, axis=0, keepdims=True)
            rall = jnp.sum(q, axis=0, keepdims=True)
            r_o[b, pl.ds(h, 1), :] = rf + jnp.sum(ct[0:64, :], axis=0, keepdims=True)
            r_o[b, pl.ds(64 + h, 1), :] = rall - rf + jnp.sum(ct[64:128, :], axis=0, keepdims=True)
            gbw = gbt * w
            sum_gb.append(gbw)
            u = gbw * bk[blk, :]
            kf = jnp.sum(qf + jnp.where(first, u, 0.0), axis=1, keepdims=True)
            kb = jnp.sum(q + u, axis=1, keepdims=True) - kf
            k_o[blk, :] += jnp.where(lane == h, kf, jnp.where(lane == 64 + h, kb, 0.0))
            lhs = jnp.concatenate([mt.astype(BF16), bt.astype(BF16)], axis=1)
            got.append(lhs)
        ggt_o[b] += sum_ge[0] + sum_ge[1]
        gct_o[b] += sum_gct[0] + sum_gct[1]
        gb_o[b] += sum_gb[0] + sum_gb[1]
        got = mm(jnp.concatenate(got, axis=0), rhs)
        gx = jnp.where(first, got[0:BLOCK, :], got[BLOCK:, :]) + skip[0:1, :] * gyf
        gmix_o[blk, :] = (gx * ds_ref[blk, :].astype(F32)).astype(BF16)
    gskip_o[...] = jnp.broadcast_to(gskip, (8, 128))


def join_kernel(
    length, heads, info, ggt, gb, gct, k_ref, r_ref, phi, b_ref, c_ref, bk, dsl, a_ref, sig,
    gmb_o, gv_o, small_o, gc_s, gm_s,
):
    nb = length // BLOCK
    off = info[5]
    chans = phi.shape[1]
    sub = iota((BLOCK, BLOCK), 0)
    lane = iota((BLOCK, 128), 1)
    first = lane < 64
    low = sub > lane
    high = sub < lane
    upper_strict = high.astype(F32)
    upper = (sub <= lane).astype(F32)
    lower_strict = low.astype(F32)
    lower = (sub >= lane).astype(F32)
    owner = iota((chans, 128), 0) // 64
    to_f = (owner == iota((chans, 128), 1)).astype(F32)
    to_b = (owner + 64 == iota((chans, 128), 1)).astype(F32)
    phi_f = mm(phi[0:8, :], to_f, precision=HIGH)
    phi_b = mm(phi[8:16, :], to_b, precision=HIGH)
    gc_s[...] = jnp.zeros_like(gc_s)
    gm_s[...] = jnp.zeros_like(gm_s)
    sum_bias = jnp.zeros((1, 128), F32)
    sum_rate = jnp.zeros((1, 128), F32)
    for b in range(nb):
        blk = slice(b * BLOCK, (b + 1) * BLOCK)
        ext = slice(HALO + b * BLOCK, HALO + (b + 1) * BLOCK)
        first_pos = off + b * BLOCK
        sp = seg_at(info, sub + first_pos)
        st = seg_at(info, lane + first_pos)
        before = seg_at(info, sub * 0 + (first_pos - 1))
        begin = seg_at(info, sub * 0 + first_pos)
        last = seg_at(info, sub * 0 + (first_pos + BLOCK - 1))
        after = seg_at(info, sub * 0 + (first_pos + BLOCK))
        enter = jnp.where(first, (sp == before).astype(F32), (sp == after).astype(F32))
        keep = jnp.where(first, (sp == last).astype(F32), (sp == begin).astype(F32))
        same = sp == st
        gg = ggt[b]
        gf = jnp.where(same & high, gg, 0.0).astype(BF16)
        gr = jnp.where(same & low, gg, 0.0).astype(BF16)
        cm = c_ref[blk, :]
        bm = b_ref[blk, :]
        gm_s[ext, 0:128] = jnp.where(first, mm(gf, cm), mm(gr, cm)) + gb[b] * keep
        gc_s[ext, :] = jnp.where(first, tn(gf, bm), tn(gr, bm)) + gct[b].T * enter
        kb = k_ref[blk, :]
        rb = r_ref[b].T
        ga_f = mm(upper_strict, rb, precision=HIGH) - mm(upper, kb, precision=HIGH) + phi_f[b : b + 1, :]
        ga_b = mm(lower_strict, rb, precision=HIGH) - mm(lower, kb, precision=HIGH) + phi_b[b : b + 1, :]
        ga = jnp.where(first, ga_f, ga_b)
        gv = kb * sig[blk, 128:256] + ga * sig[blk, 0:128]
        gv_o[blk, :] = gv.astype(BF16)
        sum_bias = sum_bias + jnp.sum(gv, axis=0, keepdims=True)
        sum_rate = sum_rate + jnp.sum(ga * a_ref[blk, :], axis=0, keepdims=True)
    small_o[...] = jnp.zeros_like(small_o)
    small_o[0:1, :] = sum_bias
    small_o[1:2, :] = sum_rate
    small_o[8:9, :] = pltpu.roll(sum_bias, 128 - heads // 2, 1)
    small_o[9:10, :] = pltpu.roll(sum_rate, 128 - heads // 2, 1)
    mid = length + HALO
    lo = HALO // 2
    pos = iota((mid, 128), 0) + (off - HALO + lo)
    seg0 = seg_at(info, pos)
    segn = seg_at(info, pos + 1)
    segp = seg_at(info, pos - 1)
    from_next = jnp.where(seg0 == segn, gc_s[lo + 1 : lo + 1 + mid, :], 0.0)
    from_prev = jnp.where(seg0 == segp, gc_s[lo - 1 : lo - 1 + mid, :], 0.0)
    gm_s[lo : lo + mid, 128:256] = jnp.where(iota((mid, 128), 1) < 64, from_next, from_prev)
    gmb_o[...] = gm_s[...] * dsl[...]


def back_kernel(
    length, steps, info, gmix, edge, vm, wv_a, wg_a, wv_b, wg_b, ggate, normed, taps, gmb, edge_bc, bcm, taps_bc, gv, wdt, wbc, x_ref, g_ref, rs, pre, ggain, gskip, small,
    keep_o, send_o, tiny_o, gin_o, acc_s, ext_s, vm_s, seg_s,
):
    j = pl.program_id(0)
    ext = length + 2 * HALO
    off, count = info[5], info[4]
    own = slice(HALO, HALO + length)

    @pl.when(j == 0)
    def _():
        seg_s[...] = seg_at(info, iota((ext, 128), 0) + (off - HALO))
        ext_s[...] = jnp.zeros_like(ext_s)

    seg0 = seg_s[own, :]
    live = iota((length, 128), 0) + off < count

    def back_conv(grad, data, tap):
        total = grad[own, :] * tap[3:4, :]
        mine = grad[own, :]
        gtap = [None] * 7
        gtap[3] = jnp.sum(mine * data[own, :], axis=0, keepdims=True)
        for k in (0, 1, 2, 4, 5, 6):
            lo = HALO + 3 - k
            same = seg_s[lo : lo + length, :] == seg0
            total = total + jnp.where(same, grad[lo : lo + length, :], 0.0) * tap[k : k + 1, :]
            up = HALO + k - 3
            same = seg_s[up : up + length, :] == seg0
            gtap[k] = jnp.sum(
                jnp.where(same, data[up : up + length, :], 0.0) * mine, axis=0, keepdims=True
            )
        return jnp.where(live, total, 0.0), gtap

    @pl.when(j == 0)
    def _():
        no = normed[own, :]
        both = []
        tiny_o[...] = jnp.zeros_like(tiny_o)
        for half in range(2):
            tiny_o[half, 10:11, 0:128] = small[8 * half : 8 * half + 1, :]
            tiny_o[half, 10:11, 128:256] = small[8 * half + 1 : 8 * half + 2, :]
        for k in range(2):
            cols = slice(k * 128, (k + 1) * 128)
            ext_s[...] = gmb[:, cols]
            lo = HALO // 2
            hi = length + lo
            got = edge_bc[:, cols]
            ext_s[lo : lo + HALO, :] += jnp.where(info[7] == 1, got, 0.0)
            ext_s[hi : hi + HALO, :] += jnp.where(info[7] == 1, 0.0, got)
            vm_s[...] = bcm[:, cols]
            gbc, gtap = back_conv(ext_s, vm_s, taps_bc.at[:, cols])
            for t in range(7):
                at = (t % 3) * 256 + k * 128
                for half in range(2):
                    tiny_o[half, 11 + t // 3 : 12 + t // 3, at : at + 128] = gtap[t]
            both.append(gbc.astype(BF16))
        gbc = jnp.concatenate(both + [gv[...]], axis=1)
        gw = tn(no, gbc)
        ch = keep_o.shape[2] - 384
        by_core(gw, keep_o.at[0, :, ch:], send_o.at[0, :, ch:])
        turned = pltpu.roll(gw[:, 256:], 128 - steps, 1)
        by_core(jnp.concatenate([gw[:, 0:256], turned], axis=1), keep_o.at[1, :, ch:], send_o.at[1, :, ch:])
        acc_s[...] = nt(gbc[:, 0:256], wbc[...]) + nt(gv[...], wdt[...])

    ext_s[own, :] = gmix[...].astype(F32)
    halo = edge[...].astype(F32)
    right = info[7] == 1
    ext_s[0:HALO, :] = jnp.where(right, halo, 0.0)
    ext_s[HALO + length : ext, :] = jnp.where(right, 0.0, halo)
    vm_s[...] = vm[...].astype(F32)
    gvals, gtap = back_conv(ext_s, vm_s, taps)
    gvals = gvals.astype(BF16)
    half = j // (steps // 2)
    here = pl.ds(pl.multiple_of((j % (steps // 2)) * 128, 128), 128)
    by_core(tn(normed[own, :], gvals), keep_o.at[half, :, here], send_o.at[half, :, here])
    for t in range(7):
        tiny_o[half, t : t + 1, here] = gtap[t]
    tiny_o[half, 7:8, here] = ggain[0:1, :]
    tiny_o[half, 8:9, here] = gskip[0:1, :]
    both = jnp.concatenate([gvals, ggate[...]], axis=1)
    mine = j < steps // 2
    weights = jnp.concatenate(
        [jnp.where(mine, wv_a[...], wv_b[...]), jnp.where(mine, wg_a[...], wg_b[...])], axis=1
    )
    acc_s[...] += nt(both, weights)

    @pl.when(j == steps - 1)
    def _():
        x = x_ref[...].astype(F32)
        gn = acc_s[...]
        r = rs[...]
        wp = gn * pre[...]
        mean = jnp.mean(wp * x, axis=1, keepdims=True)
        gin_o[...] = g_ref[...].astype(F32) + r * wp - x * (r * r * r * mean)
        gpre = jnp.sum(gn * x * r, axis=0, keepdims=True)
        for half in range(2):
            tiny_o[half, 9:10, 0 : gpre.shape[1]] = gpre


def collect_kernel(
    keep, send, tiny, out_o, tiny_o,
    core_s, mine_s, piece_s, got_s, zsend_s, zgot_s, tcore_s, tsum_s, tgot_s, tz_s, tzgot_s,
    core_out, core_in, plane_out, plane_in, z_out, z_in,
):
    w = lax.axis_index("wide")
    n = lax.axis_index("narrow")
    c, xx, z = w % 2, (w // 2) % 2, w // 4
    share = out_o.shape[0]
    core = (w + 1 - 2 * c, n)
    over_x = (w + 2 - 4 * xx, n)
    over_y = (w, 1 - n)
    over_d = (w + 2 - 4 * xx, 1 - n)
    steps = (2, 1, 3)
    over_z = [(((z + d) % 4) * 4 + w % 4, n) for d in steps]
    mesh_ids = pl.DeviceIdType.MESH
    barrier = pltpu.get_barrier_semaphore()
    for other in [core, over_x, over_y, over_d] + over_z:
        pl.semaphore_signal(barrier, inc=1, device_id=other, device_id_type=mesh_ids)
    pl.semaphore_wait(barrier, 7)

    def copy(src, dst, out_sem, in_sem, other):
        got = pltpu.make_async_remote_copy(
            src_ref=src, dst_ref=dst, send_sem=out_sem, recv_sem=in_sem, device_id=other, device_id_type=mesh_ids
        )
        got.start()
        return got

    rows = [pl.ds(pl.multiple_of(((z + d) % 4) * (2 * share), 2 * share), 2 * share) for d in steps + (0,)]
    first = [copy(tiny, tcore_s, core_out.at[4], core_in.at[4], core)]
    for i in range(4):
        first.append(copy(send.at[:, rows[i], :], core_s.at[i], core_out.at[i], core_in.at[i], core))
    ways = (over_x, over_y, over_d)
    first[0].wait()
    tsum_s[...] = tiny[...] + tcore_s[...]
    second = [[]]
    for k, other in enumerate(ways):
        half = 0 if k == 0 else 1
        second[0].append(copy(tsum_s.at[half], tgot_s.at[k], plane_out.at[4, k], plane_in.at[4, k], other))
    for i in range(4):
        first[i + 1].wait()
        both = keep[:, rows[i], :].astype(F32) + core_s[i].astype(F32)
        low, high = both[:, 0:share, :], both[:, share:, :]
        near = jnp.where(xx == 0, low, high)
        far = jnp.where(xx == 0, high, low)
        mine_s[i] = near[0]
        piece_s[i, 0] = far[0].astype(BF16)
        piece_s[i, 1] = near[1].astype(BF16)
        piece_s[i, 2] = far[1].astype(BF16)
        second.append(
            [copy(piece_s.at[i, k], got_s.at[i, k], plane_out.at[i, k], plane_in.at[i, k], ways[k]) for k in range(3)]
        )
    for one in second[0]:
        one.wait()
    tsum = tsum_s[0] + tgot_s[0] + tgot_s[1] + tgot_s[2]
    tz_s[...] = tsum
    third = [copy(tz_s, tzgot_s.at[k], z_out.at[1, k], z_in.at[1, k], over_z[k]) for k in range(3)]
    total = None
    for i in range(4):
        for one in second[i + 1]:
            one.wait()
        total = mine_s[i] + got_s[i, 0].astype(F32) + got_s[i, 1].astype(F32) + got_s[i, 2].astype(F32)
        if i < 3:
            zsend_s[i] = total.astype(BF16)
            third.append(copy(zsend_s.at[i], zgot_s.at[i], z_out.at[0, i], z_in.at[0, i], over_z[i]))
    for one in third:
        one.wait()
    out_o[...] = total + zgot_s[0].astype(F32) + zgot_s[1].astype(F32) + zgot_s[2].astype(F32)
    tiny_o[...] = tsum + tzgot_s[0] + tzgot_s[1] + tzgot_s[2]


def whole(shape, grid):
    zeros = (0,) * len(shape)
    if grid:
        return pl.BlockSpec(shape, lambda j: zeros)
    return pl.BlockSpec(shape, lambda: zeros)


def columns(rows, first=0):
    return pl.BlockSpec((rows, 128), lambda j: (0, first + j))


SMEM = pl.BlockSpec(memory_space=pltpu.SMEM)
VMEM = pl.BlockSpec(memory_space=pltpu.VMEM)
ANY = pl.BlockSpec(memory_space=pl.ANY)


def sds(shape, dtype):
    return jax.ShapeDtypeStruct(shape, dtype)


def params(grid):
    if grid:
        return pltpu.CompilerParams(vmem_limit_bytes=VMEM_LIMIT, dimension_semantics=("arbitrary",))
    return pltpu.CompilerParams(vmem_limit_bytes=VMEM_LIMIT)


def cost(us):
    return pl.CostEstimate(flops=int(us * 1.1e9), bytes_accessed=int(us * 1e6), transcendentals=0)


def pack_columns(v):
    n = v.shape[-1] // 4
    return jnp.concatenate([v[..., 0:n], v[..., 2 * n : 3 * n], v[..., n : 2 * n], v[..., 3 * n :]], axis=-1)


def small_kernel(hl, conv, gain, dtb, alog, skip, out_o):
    ch = out_o.shape[1]
    out_o[...] = jnp.zeros_like(out_o)
    lane = iota((1, 128), 1)
    wide_lane = iota((1, ch), 1)
    bias = jnp.zeros((1, 128), F32)
    rate = jnp.zeros((1, 128), F32)
    diag = jnp.zeros((1, ch), F32)
    for h in range(hl):
        cols = slice(h * HD, (h + 1) * HD)
        out_o[0:7, cols] = conv[:, h, :]
        out_o[8:9, cols] = gain[h : h + 1, :]
        bias = jnp.where(lane == h, dtb[h, 0], jnp.where(lane == 64 + h, dtb[h, 1], bias))
        rate = jnp.where((lane == h) | (lane == 64 + h), alog[h], rate)
        diag = jnp.where(wide_lane // HD == h, skip[h], diag)
    out_o[16:17, :] = diag
    out_o[24:25, 0:128] = bias
    out_o[25:26, 0:128] = rate


def swap(v):
    return lax.ppermute(v, "narrow", [(0, 1), (1, 0)])


def flip(v, bit, wide):
    return lax.ppermute(v, "wide", [(i, i ^ bit) for i in range(wide)])


def cross(v, bit, wide):
    pairs = [(i * 2 + k, (i ^ bit) * 2 + 1 - k) for i in range(wide) for k in range(2)]
    return lax.ppermute(v, ("wide", "narrow"), pairs)


def pick(v, dim, index):
    return lax.dynamic_index_in_dim(v, index, dim, keepdims=False)


def total(*parts):
    acc = parts[0].astype(F32)
    for v in parts[1:]:
        acc = acc + v.astype(F32)
    return acc


def split_positions(
    wide, layer_in, pre_gain, w_heads, w_bc, conv_x, conv_bc, dt_bias, a_log, skip_d, norm_gain, w_out, cotangent, starts, live
):
    n = lax.axis_index("narrow")
    w = lax.axis_index("wide")
    left = n == 0
    _, length, dm = layer_in.shape
    hl = w_heads.shape[1]
    heads = 2 * hl
    ch = hl * HD
    chans = 2 * ch
    pairs = heads // 2
    hp = pairs // 2
    nb = length // BLOCK
    ext = length + 2 * HALO
    share = dm // wide
    x = layer_in[0]
    g = cotangent[0]
    xbit = (w // 2) % 2
    zbits = w // 4

    edge = swap(jnp.where(left, x[length - HALO :], x[:HALO]))
    small_own = pl.pallas_call(
        functools.partial(small_kernel, hl),
        out_shape=sds((32, ch), F32),
        in_specs=[VMEM, VMEM, SMEM, SMEM, SMEM],
        out_specs=VMEM,
        name="small",
    )(conv_x, norm_gain, dt_bias, a_log, skip_d)
    small_other = swap(small_own)
    wdt = w_heads[:, :, 2 * HD :].reshape(dm, 2 * hl)
    wdt_other = swap(wdt)

    quarter = dm // 4
    q = w % 4

    def gather(own):
        p0 = swap(lax.dynamic_slice(own, (q * quarter, 0), (quarter, own.shape[1])))
        p1 = flip(p0, 2, wide)
        return p0, p1, flip(p0, 1, wide), flip(p1, 1, wide)

    wv = w_heads[:, :, HD : 2 * HD].reshape(dm, ch)
    wg = w_heads[:, :, :HD].reshape(dm, ch)
    wo = w_out.reshape(ch, dm)
    wv_pieces = gather(wv)
    wog_pieces = gather(jnp.concatenate([wo, wg], axis=1))

    pos = (length, 128)
    sq = (nb, BLOCK, BLOCK)
    front_shapes = [
        ((8, chans), F32), ((8, chans), F32), ((8, chans), F32), ((dm, 128), BF16), ((dm, 256), BF16), ((7, 256), F32),
        ((ext, dm), BF16), ((length, 1), F32), ((ext, 256), F32), ((ext, 256), F32), (pos, BF16), (pos, F32), (sq, F32),
        (pos, BF16), (pos, F32), (sq, F32), (sq, F32), (sq, F32), (pos, F32), (pos, F32), (sq, F32), (sq, F32),
        (sq, F32), (sq, F32), ((128, 128), F32), (pos, F32), ((length, 256), F32),
    ]
    (
        info, taps, gain, skip, wdt_all, wbc, taps_bc, normed, rs, bcm, dsl, bmap, bk, bkt, cmap, ce, cet, gmat, gmat_t,
        colt, rows, coltt, rowst, et, wt, dpt, a_dt, sig,
    ) = pl.pallas_call(
        functools.partial(front_kernel, length, hl),
        out_shape=[sds((8,), jnp.int32)] + [sds(*v) for v in front_shapes],
        in_specs=[SMEM] + [VMEM] * 10,
        out_specs=[SMEM] + [VMEM] * len(front_shapes),
        scratch_shapes=[
            pltpu.VMEM((ext, 256), jnp.int32), pltpu.VMEM((ext, 256), F32), pltpu.VMEM((128, 128), F32),
            pltpu.VMEM((ext, dm), BF16),
        ],
        compiler_params=params(False),
        cost_estimate=cost(8),
        name="front",
    )(starts, live, x, edge, pre_gain.reshape(1, dm), wdt, wdt_other, w_bc, conv_bc, small_own, small_other)

    state_spec = pl.BlockSpec((1, nb + 1, 128, 128), lambda j: (j, 0, 0, 0))
    bnd_spec = pl.BlockSpec((1, 64, 128), lambda j: (j, 0, 0))
    far_spec = pl.BlockSpec((1, 64, 128), lambda j: ((j + hp) % pairs, 0, 0))
    state_shape = sds((pairs, nb + 1, 128, 128), BF16)
    bnd_shape = sds((pairs, 64, 128), BF16)
    act_shape = sds((length, chans), BF16)
    own_spec = pl.BlockSpec((dm, 128), lambda j: (0, jnp.minimum(j, hp - 1)))
    other_spec = pl.BlockSpec((dm, 128), lambda j: (0, jnp.maximum(j - hp, 0)))

    def vals(other, weights, before):
        first = hp if other else 0
        extra = [sds((dm, ch), BF16)] if other else []
        specs = [SMEM, whole((ext, dm), 1)]
        if other:
            specs += [whole((quarter, ch), 1)] * 4
        else:
            specs += [columns(dm)]
        specs += [columns(8, first), whole(sq, 1), whole(sq, 1), whole((128, 128), 1)] + [ANY] * len(before)
        scratch = [pltpu.VMEM((ext, 128), F32), pltpu.VMEM((ext, 128), jnp.int32)]
        if other:
            scratch.append(pltpu.VMEM((hp, dm, 128), BF16))
        return pl.pallas_call(
            functools.partial(vals_kernel, length, other),
            grid=(hp,),
            out_shape=[act_shape, sds((ext, chans), BF16), act_shape, state_shape, bnd_shape] + extra,
            in_specs=specs,
            out_specs=[
                columns(length, first), columns(ext, first), columns(length, first),
                pl.BlockSpec((1, nb + 1, 128, 128), lambda j: (j + first, 0, 0, 0)),
                pl.BlockSpec((1, 64, 128), lambda j: (j + first, 0, 0)),
            ] + [whole((dm, ch), 1)] * other,
            scratch_shapes=scratch,
            input_output_aliases={len(specs) - len(before) + i: i for i in range(len(before))},
            compiler_params=params(True),
            cost_estimate=cost(8),
            name="vals_other" if other else "vals_own",
        )(info, normed, *weights, taps, wt, bkt, dpt, *before)

    own_vals = vals(False, (wv,), ())
    xc, vm, ds, s_loc, bnd, wv_other = vals(True, wv_pieces, own_vals)

    y, s_true = pl.pallas_call(
        functools.partial(scan_kernel, length),
        grid=(pairs,),
        out_shape=[act_shape, state_shape],
        in_specs=[
            SMEM, columns(length), state_spec, far_spec, whole((128, 128), 1), whole(pos, 1), whole(sq, 1), whole(pos, 1),
            whole(sq, 1), columns(8),
        ],
        out_specs=[columns(length), state_spec],
        compiler_params=params(True),
        cost_estimate=cost(19),
        name="scan",
    )(info, xc, s_loc, swap(bnd), dpt, colt, rowst, ce, gmat, skip)

    tile_spec = pl.BlockSpec((BLOCK, chans), lambda i: (i, 0))
    gw_shape = (2, dm // 2, dm + ch)
    out, gy, keep_a, send_a, ggate, ggain, wg_other = pl.pallas_call(
        functools.partial(gate_kernel, nb),
        grid=(nb,),
        out_shape=[
            sds((length, dm), BF16), act_shape, sds(gw_shape, BF16), sds(gw_shape, BF16), act_shape, sds((8, chans), F32),
            sds((dm, ch), BF16),
        ],
        in_specs=[
            whole((length, dm), 1), whole((length, dm), 1), whole((ext, dm), 1), tile_spec, whole((ch, dm), 1),
            whole((dm, ch), 1),
        ] + [whole((quarter, dm + ch), 1)] * 4 + [whole((8, chans), 1)],
        out_specs=[
            pl.BlockSpec((BLOCK, dm), lambda i: (i, 0)), tile_spec, whole(gw_shape, 1), whole(gw_shape, 1),
            whole((length, chans), 1), whole((8, chans), 1), whole((dm, ch), 1),
        ],
        scratch_shapes=[pltpu.VMEM((length, chans), BF16), pltpu.VMEM((dm, dm + ch), BF16)],
        compiler_params=params(True),
        cost_estimate=cost(22),
        name="gated",
    )(x, g, normed, y, wo, wg, *wog_pieces, gain)

    def meet(keep, got):
        cols = keep.shape[-1]
        keep = keep.reshape(2, wide // 4, 2, share, cols)
        got = got.reshape(2, wide // 4, 2, share, cols)

        def piece(half, xx):
            return total(pick(keep[half], 1, xx), pick(got[half], 1, xx)).astype(BF16)

        return piece(0, xbit), piece(0, 1 - xbit), piece(1, xbit), piece(1, 1 - xbit)

    def plane(mine, to_x, to_y, to_d):
        return total(mine, flip(to_x, 2, wide), swap(to_y), cross(to_d, 2, wide)).astype(mine.dtype)

    def depth(v):
        parts = [pick(v, 0, zbits)]
        for k in (1, 2, 3):
            parts.append(flip(pick(v, 0, zbits ^ k), 4 * k, wide))
        return total(*parts)

    a_pieces = meet(keep_a, flip(send_a, 1, wide))

    gs_loc, gbnd = pl.pallas_call(
        functools.partial(gstate_kernel, length),
        grid=(pairs,),
        out_shape=[state_shape, bnd_shape],
        in_specs=[SMEM, columns(length), whole(sq, 1), whole(sq, 1), whole((128, 128), 1)],
        out_specs=[state_spec, bnd_spec],
        compiler_params=params(True),
        cost_estimate=cost(9),
        name="gstate",
    )(info, gy, et, cet, dpt)

    gs_loc, gbnd, *a_pieces = lax.optimization_barrier((gs_loc, gbnd, *a_pieces))
    a_plane = plane(*a_pieces)

    gmix, ggt, gb, gct, ksum, rsum, phi, gskip = pl.pallas_call(
        functools.partial(gscan_kernel, length),
        grid=(pairs,),
        out_shape=[
            act_shape, sds(sq, F32), sds(sq, F32), sds(sq, F32), sds(pos, F32), sds(sq, F32), sds((16, chans), F32),
            sds((8, chans), F32),
        ],
        in_specs=[
            SMEM, columns(length), columns(length), columns(length), state_spec, state_spec, far_spec, whole((128, 128), 1),
            whole(pos, 1), whole(sq, 1), whole(sq, 1), whole(sq, 1), whole(pos, 1), whole(sq, 1), columns(8),
        ],
        out_specs=[
            columns(length), whole(sq, 1), whole(sq, 1), whole(sq, 1), whole(pos, 1), whole(sq, 1), columns(16), columns(8),
        ],
        scratch_shapes=[pltpu.VMEM((nb + 1, 128, 128), BF16)],
        compiler_params=params(True),
        cost_estimate=cost(35),
        name="gscan",
    )(info, xc, ds, gy, s_true, gs_loc, swap(gbnd), dpt, rows, coltt, et, gmat_t, bk, cet, skip)

    gmix, ggt, a_plane = lax.optimization_barrier((gmix, ggt, a_plane))
    wa = depth(a_plane)
    edge_x = swap(jnp.where(left, gmix[length - HALO :], gmix[:HALO]))

    gmb, gv, small = pl.pallas_call(
        functools.partial(join_kernel, length, heads),
        out_shape=[sds((ext, 256), F32), sds(pos, BF16), sds((16, 128), F32)],
        in_specs=[SMEM] + [VMEM] * 12,
        out_specs=[VMEM] * 3,
        scratch_shapes=[pltpu.VMEM((ext, 128), F32), pltpu.VMEM((ext, 256), F32)],
        compiler_params=params(False),
        cost_estimate=cost(6),
        name="join",
    )(info, ggt, gb, gct, ksum, rsum, phi, bmap, cmap, bk, dsl, a_dt, sig)

    lo = HALO // 2
    edge_bc = swap(jnp.where(left, gmb[length + lo : length + lo + HALO], gmb[lo : lo + HALO]))

    keep_b, send_b, tiny, grad_in = pl.pallas_call(
        functools.partial(back_kernel, length, pairs),
        grid=(pairs,),
        out_shape=[
            sds((2, dm // 2, ch + 384), BF16), sds((2, dm // 2, ch + 384), BF16), sds((2, 16, ch), F32), sds((length, dm), F32),
        ],
        in_specs=[
            SMEM, columns(length), pl.BlockSpec((HALO, 128), lambda j: (0, (j + hp) % pairs)), columns(ext), own_spec, own_spec,
            other_spec, other_spec, columns(length), whole((ext, dm), 1), columns(8), whole((ext, 256), 1),
            whole((HALO, 256), 1), whole((ext, 256), 1), whole((7, 256), 1), whole(pos, 1), whole((dm, 128), 1),
            whole((dm, 256), 1), whole((length, dm), 1), whole((length, dm), 1), whole((length, 1), 1), whole((1, dm), 1),
            columns(8), columns(8), whole((16, 128), 1),
        ],
        out_specs=[
            whole((2, dm // 2, ch + 384), 1), whole((2, dm // 2, ch + 384), 1), whole((2, 16, ch), 1), whole((length, dm), 1),
        ],
        scratch_shapes=[
            pltpu.VMEM((length, dm), F32), pltpu.VMEM((ext, 128), F32), pltpu.VMEM((ext, 128), F32),
            pltpu.VMEM((ext, 128), jnp.int32),
        ],
        compiler_params=params(True),
        cost_estimate=cost(24),
        name="back",
    )(
        info, gmix, edge_x, vm, wv, wg, wv_other, wg_other, ggate, normed, taps, gmb, edge_bc, bcm, taps_bc, gv, wdt_all, wbc,
        x, g, rs, pre_gain.reshape(1, dm), ggain, gskip, small,
    )

    keep_b, send_b, wa = lax.optimization_barrier((keep_b, send_b, wa))

    cols = ch + 384
    wb, tiny = pl.pallas_call(
        collect_kernel,
        out_shape=[sds((share, cols), F32), sds((16, ch), F32)],
        in_specs=[VMEM] * 3,
        out_specs=[VMEM] * 2,
        scratch_shapes=[
            pltpu.VMEM((4, 2, 2 * share, cols), BF16),
            pltpu.VMEM((4, share, cols), F32),
            pltpu.VMEM((4, 3, share, cols), BF16),
            pltpu.VMEM((4, 3, share, cols), BF16),
            pltpu.VMEM((3, share, cols), BF16),
            pltpu.VMEM((3, share, cols), BF16),
            pltpu.VMEM((2, 16, ch), F32),
            pltpu.VMEM((2, 16, ch), F32),
            pltpu.VMEM((3, 16, ch), F32),
            pltpu.VMEM((16, ch), F32),
            pltpu.VMEM((3, 16, ch), F32),
            pltpu.SemaphoreType.DMA((5,)),
            pltpu.SemaphoreType.DMA((5,)),
            pltpu.SemaphoreType.DMA((5, 3)),
            pltpu.SemaphoreType.DMA((5, 3)),
            pltpu.SemaphoreType.DMA((2, 3)),
            pltpu.SemaphoreType.DMA((2, 3)),
        ],
        compiler_params=pltpu.CompilerParams(collective_id=0, has_side_effects=True, vmem_limit_bytes=VMEM_LIMIT),
        name="collect",
    )(keep_b, send_b, tiny)

    def part(v, dim):
        size = v.shape[dim] // wide
        return lax.dynamic_slice_in_dim(v, w * size, size, dim)

    gate_part = wa[:, dm:].reshape(share, hl, HD)
    vals_part = wb[:, :ch].reshape(share, hl, HD)
    bc_part = pack_columns(wb[:, ch : ch + 256])
    dt_cols = wb[:, ch + 256 :]
    dt_part = jnp.stack([dt_cols[:, 0:hl], dt_cols[:, 64 : 64 + hl]], axis=2)
    g_w_heads = jnp.concatenate([gate_part, vals_part, dt_part], axis=2)
    g_w_out = jnp.transpose(wa[:, :dm].reshape(share, hl, HD), (1, 2, 0))
    taps_rows = tiny[11:14].reshape(3, 3, 256).reshape(9, 256)[:7]
    return (
        out[None],
        grad_in[None],
        part(tiny[9], 0),
        g_w_heads,
        bc_part,
        part(tiny[0:7].reshape(7, hl, HD), 2),
        part(pack_columns(taps_rows), 1),
        jnp.stack([tiny[10, 0:hl], tiny[10, 64 : 64 + hl]], axis=1),
        tiny[10, 128 : 128 + hl] + tiny[10, 192 : 192 + hl],
        jnp.sum(tiny[8].reshape(hl, HD), axis=1),
        part(tiny[7].reshape(hl, HD), 1),
        g_w_out,
    )


def solution(mesh):
    body = shards
    if mesh.shape["narrow"] == 2 and mesh.shape["wide"] == 16:
        body = functools.partial(split_positions, mesh.shape["wide"])
    return jax.shard_map(
        body,
        mesh=mesh,
        in_specs=(
            P("wide", "narrow", None),
            P(),
            P(None, "narrow", None),
            P(),
            P(None, "narrow", None),
            P(),
            P("narrow", None),
            P("narrow"),
            P("narrow"),
            P("narrow", None),
            P("narrow", None, None),
            P("wide", "narrow", None),
            P("wide", None),
            P("wide", None),
        ),
        out_specs=(
            P("wide", "narrow", None),
            P("wide", "narrow", None),
            P("wide"),
            P("wide", "narrow", None),
            P("wide", None),
            P(None, "narrow", "wide"),
            P(None, "wide"),
            P("narrow", None),
            P("narrow"),
            P("narrow"),
            P("narrow", "wide"),
            P("narrow", None, "wide"),
        ),
        check_vma=False,
    )
```

```python
import functools

import jax
import jax.numpy as jnp
from jax import lax
from jax.experimental import pallas as pl
from jax.experimental.pallas import tpu as pltpu
from jax.sharding import PartitionSpec as P

H = 24
HD = 64
BLOCK = 128
SEQ_LEN = 1280


EPS = 1e-05
HIGH = lax.Precision.HIGHEST


def rounded(value):
    return value + lax.stop_gradient(value.astype(jnp.bfloat16).astype(jnp.float32) - value)


def segment_ids(starts):
    where_at = jnp.arange(SEQ_LEN, dtype=jnp.int32)
    hits = (starts[:, :, None] <= where_at[None, None, :]).astype(jnp.int32)
    return jnp.sum(hits, axis=1) - 1


def conv_doc(values, taps, seg):
    half = (taps.shape[0] - 1) // 2
    length = values.shape[1]
    padded = jnp.pad(values, ((0, 0), (half, half), (0, 0)))
    seg_pad = jnp.pad(seg, ((0, 0), (half, half)), constant_values=-1)
    total = jnp.zeros_like(values)
    for offset in range(taps.shape[0]):
        same = (seg_pad[:, offset : offset + length] == seg).astype(values.dtype)
        total = total + taps[offset] * padded[:, offset : offset + length] * same[:, :, None]
    return total


def ssd_forward(xc, steps, decays, bmat, cmat, seg, prec):
    rows, length, heads, hdim = xc.shape
    blocks = length // BLOCK
    xb = xc.reshape(rows, blocks, BLOCK, heads, hdim)
    stepb = steps.reshape(rows, blocks, BLOCK, heads)
    cum = jnp.cumsum(decays.reshape(rows, blocks, BLOCK, heads), axis=2)
    bb = bmat.reshape(rows, blocks, BLOCK, -1)
    cb = cmat.reshape(rows, blocks, BLOCK, -1)
    sb = seg.reshape(rows, blocks, BLOCK)
    order = jnp.arange(BLOCK, dtype=jnp.int32)
    causal = order[:, None] >= order[None, :]
    same = ((sb[:, :, :, None] == sb[:, :, None, :]) & causal)[..., None]
    diff = cum[:, :, :, None, :] - cum[:, :, None, :, :]
    weights = jnp.where(same, jnp.exp(jnp.where(same, diff, 0.0)), 0.0)
    inner = jnp.einsum("rbtn,rbsn->rbts", cb, bb, precision=prec)
    mix = weights * inner[..., None] * stepb[:, :, None, :, :]
    intra = jnp.einsum("rbtsh,rbshp->rbthp", mix, xb, precision=prec)
    last = sb[:, :, -1]
    cum_end = cum[:, :, -1, :]
    to_end = (
        (sb == last[:, :, None]).astype(cum.dtype)[..., None]
        * jnp.exp(cum_end[:, :, None, :] - cum)
        * stepb
    )
    states = jnp.einsum("rbshp,rbsn->rbhpn", to_end[..., None] * xb, bb, precision=prec)
    decay_end = jnp.exp(cum_end)

    def carry_step(carry, item):
        state, seg_prev = carry
        block_state, block_last, block_decay = item
        keep = (block_last == seg_prev).astype(state.dtype)[:, None, None, None]
        fresh = keep * block_decay[:, :, None, None] * state + block_state
        return ((fresh, block_last), (state, seg_prev))

    init = (
        jnp.zeros((rows, heads, hdim, bb.shape[-1]), xc.dtype),
        jnp.full((rows,), -1, jnp.int32),
    )
    items = (jnp.moveaxis(states, 1, 0), jnp.moveaxis(last, 1, 0), jnp.moveaxis(decay_end, 1, 0))
    _, (before, seg_before) = lax.scan(carry_step, init, items)
    before = jnp.moveaxis(before, 0, 1)
    seg_before = jnp.moveaxis(seg_before, 0, 1)
    enter = (sb == seg_before[:, :, None]).astype(cum.dtype)[..., None] * jnp.exp(cum)
    inter = jnp.einsum("rbtn,rbhpn->rbthp", cb, before, precision=prec) * enter[..., None]
    return (intra + inter).reshape(rows, length, heads, hdim)


def mixer(proj, bcproj, conv_x, conv_bc, dt_bias, a_log, skip_d, seg, mask, rounder, prec):
    rows, length, heads, width = proj.shape
    hdim = (width - 2) // 2
    state = bcproj.shape[-1] // 4
    gate = proj[..., :hdim]
    values = proj[..., hdim : 2 * hdim] * mask[:, :, None, None]
    mixed_x = conv_doc(
        values.reshape(rows, length, heads * hdim),
        conv_x.reshape(conv_x.shape[0], heads * hdim),
        seg,
    )
    xc = rounder(jax.nn.silu(mixed_x)).reshape(rows, length, heads, hdim)
    maps = rounder(jax.nn.silu(conv_doc(bcproj * mask[:, :, None], conv_bc, seg)))
    b_fwd = maps[..., :state]
    c_fwd = maps[..., state : 2 * state]
    b_bwd = maps[..., 2 * state : 3 * state]
    c_bwd = maps[..., 3 * state :]
    rate = -jnp.exp(a_log)
    dt_fwd = jax.nn.softplus(proj[..., 2 * hdim] + dt_bias[:, 0]) * mask[:, :, None]
    dt_bwd = jax.nn.softplus(proj[..., 2 * hdim + 1] + dt_bias[:, 1]) * mask[:, :, None]
    out_fwd = ssd_forward(xc, dt_fwd, dt_fwd * rate, b_fwd, c_fwd, seg, prec)

    def flip(v):
        return jnp.flip(v, axis=1)

    out_bwd = flip(
        ssd_forward(
            flip(xc), flip(dt_bwd), flip(dt_bwd * rate), flip(b_bwd), flip(c_bwd), flip(seg), prec
        )
    )
    keep_prev = (seg[:, 1:] == seg[:, :-1]).astype(xc.dtype)[:, :, None, None]
    shifted_fwd = jnp.pad(out_fwd[:, :-1] * keep_prev, ((0, 0), (1, 0), (0, 0), (0, 0)))
    shifted_bwd = jnp.pad(out_bwd[:, 1:] * keep_prev, ((0, 0), (0, 1), (0, 0), (0, 0)))
    return (shifted_fwd + shifted_bwd + skip_d[:, None] * xc, gate)


def shards(
    layer_in,
    pre_gain,
    w_heads,
    w_bc,
    conv_x,
    conv_bc,
    dt_bias,
    a_log,
    skip_d,
    norm_gain,
    w_out,
    cotangent,
    starts,
    live,
):
    seg = segment_ids(starts)
    mask = live.astype(jnp.float32)
    x_here = layer_in.astype(jnp.float32)
    scale = lax.rsqrt(jnp.mean(x_here * x_here, axis=-1, keepdims=True) + EPS)
    normed_here = (x_here * scale * pre_gain).astype(jnp.bfloat16)
    normed = lax.all_gather(normed_here, "narrow", axis=1, tiled=True)
    proj = jnp.einsum("rld,dhc->rlhc", normed, w_heads, preferred_element_type=jnp.float32)
    bcproj = jnp.einsum("rld,dc->rlc", normed, w_bc, preferred_element_type=jnp.float32)

    def mix_local(proj_in, bc_in, taps_x, taps_bc, bias_in, log_rate, diag_in):
        return mixer(
            proj_in, bc_in, taps_x, taps_bc, bias_in, log_rate, diag_in, seg, mask, rounded, HIGH
        )

    (ymix, gate), pull_mix = jax.vjp(
        mix_local, proj, bcproj, conv_x, conv_bc, dt_bias, a_log, skip_d
    )
    rows, length, heads, hdim = ymix.shape
    sigma = jax.nn.sigmoid(gate)
    act = gate * sigma
    gated = (ymix * act).reshape(rows, length, heads * hdim)
    squares = lax.psum(jnp.sum(gated * gated, axis=-1), "narrow")
    inv = lax.rsqrt(squares / (H * HD) + EPS)[..., None]
    gain_flat = norm_gain.reshape(-1)
    normalized = gated * inv
    hn = (normalized * gain_flat).astype(jnp.bfloat16)
    w_flat = w_out.reshape(heads * hdim, -1)
    partial_value = jnp.einsum("rlc,cd->rld", hn, w_flat, preferred_element_type=jnp.float32)
    branch = lax.psum_scatter(partial_value, "narrow", scatter_dimension=1, tiled=True)
    out = (x_here + branch).astype(jnp.bfloat16)
    grad_out = lax.all_gather(cotangent, "narrow", axis=1, tiled=True)
    g_w_out = jnp.einsum("rlc,rld->cd", hn, grad_out, preferred_element_type=jnp.float32)
    g_hn = jnp.einsum("rld,cd->rlc", grad_out, w_flat, preferred_element_type=jnp.float32)
    g_gain = jnp.sum(g_hn * normalized, axis=(0, 1))
    weighted = g_hn * gain_flat
    cross = lax.psum(jnp.sum(weighted * gated, axis=-1), "narrow")
    g_gated = inv * weighted - gated * (inv * inv * inv) * (cross / (H * HD))[..., None]
    g_gated = g_gated.reshape(rows, length, heads, hdim)
    g_ymix = g_gated * act
    g_gate = g_gated * ymix * (sigma * (1.0 + gate * (1.0 - sigma)))
    g_proj, g_bcproj, g_conv_x, g_conv_bc, g_dt_bias, g_a_log, g_skip = pull_mix((g_ymix, g_gate))
    g_proj_low = g_proj.astype(jnp.bfloat16)
    g_w_heads = jnp.einsum("rld,rlhc->dhc", normed, g_proj_low, preferred_element_type=jnp.float32)
    g_w_bc = jnp.einsum(
        "rld,rlc->dc", normed, g_bcproj, precision=HIGH, preferred_element_type=jnp.float32
    )
    g_normed = jnp.einsum("rlhc,dhc->rld", g_proj_low, w_heads, preferred_element_type=jnp.float32)
    g_normed = g_normed + jnp.einsum(
        "rlc,dc->rld", g_bcproj, w_bc, precision=HIGH, preferred_element_type=jnp.float32
    )
    g_normed_here = lax.psum_scatter(g_normed, "narrow", scatter_dimension=1, tiled=True)
    weighted_in = g_normed_here * pre_gain
    g_pre = jnp.sum(g_normed_here * x_here * scale, axis=(0, 1))
    g_x = scale * weighted_in - x_here * (scale * scale * scale) * jnp.mean(
        weighted_in * x_here, axis=-1, keepdims=True
    )
    grad_input = cotangent.astype(jnp.float32) + g_x
    g_pre, g_w_bc, g_conv_bc = lax.psum((g_pre, g_w_bc, g_conv_bc), "narrow")
    reduced = (
        lax.psum_scatter(g_w_heads, "wide", scatter_dimension=0, tiled=True),
        lax.psum_scatter(g_w_out.reshape(heads, hdim, -1), "wide", scatter_dimension=2, tiled=True),
        lax.psum_scatter(g_conv_x, "wide", scatter_dimension=2, tiled=True),
        lax.psum_scatter(g_gain.reshape(heads, hdim), "wide", scatter_dimension=1, tiled=True),
        lax.psum_scatter(g_pre, "wide", scatter_dimension=0, tiled=True),
        lax.psum_scatter(g_w_bc, "wide", scatter_dimension=0, tiled=True),
        lax.psum_scatter(g_conv_bc, "wide", scatter_dimension=1, tiled=True),
    )
    share_pre, share_bc, share_conv = (reduced[4], reduced[5], reduced[6])
    head_bias, head_rate, head_diag = lax.psum((g_dt_bias, g_a_log, g_skip), "wide")
    return (
        out,
        grad_input,
        share_pre,
        reduced[0],
        share_bc,
        reduced[2],
        share_conv,
        head_bias,
        head_rate,
        head_diag,
        reduced[3],
        reduced[1],
    )


HALO = 16
F32 = jnp.float32
BF16 = jnp.bfloat16
LOGZERO = -1e30


def mm(a, b, dims=((1,), (0,)), precision=None):
    return lax.dot_general(a, b, (dims, ((), ())), precision=precision, preferred_element_type=F32)


def nt(a, b):
    return mm(a, b, ((1,), (1,)))


def tn(a, b):
    return mm(a, b, ((0,), (0,)))


def seg_at(info, pos):
    seg = jnp.full(pos.shape, -1, jnp.int32)
    for j in range(4):
        seg = seg + (pos >= info[j]).astype(jnp.int32)
    return jnp.where(pos >= info[6], 99, seg)


def iota(shape, dim):
    return lax.broadcasted_iota(jnp.int32, shape, dim)


def silu_parts(v):
    sg = 0.5 * jnp.tanh(0.5 * v) + 0.5
    act = v * sg
    return act, sg + act * (1.0 - sg)


def thirds(v):
    hi = v.astype(BF16).astype(F32)
    rest = v - hi
    mid = rest.astype(BF16).astype(F32)
    return hi, mid, rest - mid


def column_terms(values):
    sub = iota((16, 128), 0)
    v = jnp.ones((16, 128), F32)
    for k, value in enumerate(values):
        v = jnp.where((sub >= 3 * k) & (sub < 3 * k + 3), value, v)
    hi, mid, low = thirds(v)
    part = sub % 3
    out = jnp.where(part == 0, hi, jnp.where(part == 1, mid, low))
    return jnp.where(sub < 3 * len(values), out, 1.0).astype(BF16)


def row_base(count, places):
    sub = iota((16, 384), 0)
    lane = iota((16, 384), 1)
    out = jnp.zeros((16, 384), F32)
    for k, spans in enumerate(places):
        for lo, hi in spans:
            out = jnp.where((sub >= 3 * k) & (sub < 3 * k + 3) & (lane >= lo) & (lane < hi), 1.0, out)
    return out


def row_terms(count, base, one, two):
    sub = iota((16, 128), 0)
    part = sub - 3 * count
    made = []
    for k, value in enumerate((one, two)):
        hi, mid, low = thirds(jnp.broadcast_to(value, (16, 128)))
        here = base[:, 128 * k : 128 * (k + 1)]
        made.append(
            jnp.where(part == 0, hi, jnp.where(part == 1, mid, jnp.where(part == 2, low, here))).astype(BF16)
        )
    return jnp.concatenate(made + [base[:, 256:].astype(BF16)], axis=1)


def conv_taps(src, seg_src, taps, first, rows):
    seg0 = seg_src[first : first + rows, :]
    total = src[first : first + rows, :] * taps[3:4, :]
    for k in (0, 1, 2, 4, 5, 6):
        lo = first + k - 3
        same = seg_src[lo : lo + rows, :] == seg0
        total = total + jnp.where(same, src[lo : lo + rows, :], 0.0) * taps[k : k + 1, :]
    return total


def front_kernel(
    length, hl, starts, live_ref, x_in, gain, wbc_ref, taps_ref, small_a, small_b,
    info, taps_o, gain_o, skip_o, wdt, wbc, taps, normed_o, rs_o, bcm_o, dsl_o, maps_o, ta_o, tb_o, tc_o, dpt_o, sig_o, seg_s, maps_s, cum_s, x_s,
):
    nb = length // BLOCK
    ext = length + 2 * HALO
    dm = x_in.shape[1]
    n = lax.axis_index("narrow")
    for i in range(4):
        info[i] = starts[0, i]
    count = jnp.sum(live_ref[...].astype(F32)).astype(jnp.int32)
    off = n * length
    info[4] = count
    info[5] = off
    info[6] = live_ref.shape[1]
    info[7] = n
    ch = small_a.shape[1]
    for k, small in enumerate((small_a, small_b)):
        cols = slice(k * ch, (k + 1) * ch)
        taps_o[:, cols] = small[0:8, :]
        gain_o[:, cols] = jnp.broadcast_to(small[7:8, :], (8, ch))
        skip_o[:, cols] = jnp.broadcast_to(small[8:9, :], (8, ch))
    dst = iota((128, 2 * hl), 0)
    src = iota((128, 2 * hl), 1)
    place = (src % 2) * 64 + src // 2
    at_a = jnp.where(dst == place, 1.0, 0.0).astype(BF16)
    at_b = jnp.where(dst == place + hl, 1.0, 0.0).astype(BF16)
    own_steps = small_a[16 : 16 + 2 * hl, :].astype(BF16)
    far_steps = small_b[16 : 16 + 2 * hl, :].astype(BF16)
    wdt[...] = (mm(at_a, own_steps) + mm(at_b, far_steps)).astype(BF16)
    wbc[...] = pack_columns(wbc_ref[...])
    taps[...] = pack_columns(taps_ref[...])

    bias = small_a[9:10, 0:128] + pltpu.roll(small_b[9:10, 0:128], hl, 1)
    alog = small_a[9:10, 128:256] + pltpu.roll(small_b[9:10, 128:256], hl, 1)
    edge = small_b[16 + 2 * hl : 24 + 2 * hl, :]
    zero_edge = jnp.zeros((8, dm), F32)
    before = jnp.concatenate([zero_edge, jnp.where(n == 1, edge, 0.0)], axis=0)
    behind = jnp.concatenate([jnp.where(n == 1, 0.0, edge), zero_edge], axis=0)
    x_s[0:HALO, :] = before.astype(BF16)
    x_s[HALO : HALO + length, :] = x_in[...]
    x_s[HALO + length : ext, :] = behind.astype(BF16)
    x = x_s[...].astype(F32)
    rs = lax.rsqrt(jnp.mean(x * x, axis=1, keepdims=True) + EPS)
    normed = (x * rs * gain[...]).astype(BF16)
    normed_o[...] = normed
    rs_o[...] = rs[HALO : HALO + length, :]
    pos256 = iota((ext, 256), 0) + (off - HALO)
    seg_s[...] = seg_at(info, pos256)
    live = pos256 < count
    bcm_o[...] = jnp.where(live, mm(normed, wbc[...]), 0.0)
    crows = length + HALO
    cfirst = HALO // 2
    mix = conv_taps(bcm_o, seg_s, taps, cfirst, crows)
    maps, dsl = silu_parts(mix)
    dsl_o[...] = jnp.zeros_like(dsl_o)
    dsl_o[cfirst : cfirst + crows, :] = dsl
    maps_s[...] = jnp.zeros_like(maps_s)
    maps_s[cfirst : cfirst + crows, :] = maps.astype(BF16).astype(F32)
    own = slice(HALO, HALO + length)
    segx = seg_s[own, 0:128]
    lane = iota((length, 128), 1)
    fwd = lane < 64
    segp = seg_s[HALO - 1 : HALO - 1 + length, 0:128]
    segn = seg_s[HALO + 1 : HALO + 1 + length, 0:128]
    bmap = maps_s[own, 0:128]
    cprev = jnp.where(segp == segx, maps_s[HALO - 1 : HALO - 1 + length, 128:256], 0.0)
    cnext = jnp.where(segn == segx, maps_s[HALO + 1 : HALO + 1 + length, 128:256], 0.0)
    cmap = jnp.where(fwd, cprev, cnext)
    maps_o[:, 0:128] = bmap.astype(BF16)
    maps_o[:, 128:256] = cmap.astype(BF16)
    raw = nt(normed[own, :], wdt[...]) + bias
    softp = jnp.maximum(raw, 0.0) + jnp.log(1.0 + jnp.exp(-jnp.abs(raw)))
    softp = jnp.where(raw < -15.0, jnp.exp(jnp.minimum(raw, 0.0)), softp)
    pos128 = iota((length, 128), 0) + off
    m = pos128 < count
    dt = jnp.where(m, softp, 0.0)
    sg = jnp.where(m, 1.0 / (1.0 + jnp.exp(-raw)), 0.0)
    ratio = jnp.where(m, jnp.where(raw < -15.0, 1.0, sg / jnp.maximum(softp, 1e-30)), 0.0)
    rate = -jnp.exp(alog)
    a = dt * rate
    sig_o[:, 256:384] = a
    sig_o[:, 0:128] = sg * rate
    sig_o[:, 128:256] = ratio
    tri = (iota((BLOCK, BLOCK), 0) >= iota((BLOCK, BLOCK), 1)).astype(F32)
    logdt = jnp.maximum(jnp.log(dt), LOGZERO)
    sub = iota((BLOCK, BLOCK), 0)
    ln = iota((BLOCK, BLOCK), 1)
    fwdb = ln < 64
    cum_s[...] = jnp.zeros_like(cum_s)
    dvals, ends = [], []
    for b in range(nb):
        blk = slice(b * BLOCK, (b + 1) * BLOCK)
        ab = a[blk, :]
        cum = mm(tri, ab, precision=HIGH)
        cx = cum - ab
        end = cum[BLOCK - 1 : BLOCK, :]
        colt = jnp.where(fwdb, cx, end - cum)
        rows = jnp.where(fwdb, logdt[blk, :] - cum, cx + logdt[blk, :] - end)
        tb_o[0, b] = colt.T
        tb_o[1, b] = rows.T
        ta_o[0, b] = jnp.minimum(rows + end, 60.0).T
        first_pos = off + b * BLOCK
        sp = seg_at(info, sub + first_pos)
        st = seg_at(info, ln + first_pos)
        before = seg_at(info, sub * 0 + (first_pos - 1))
        begin = seg_at(info, sub * 0 + first_pos)
        last = seg_at(info, sub * 0 + (first_pos + BLOCK - 1))
        after = seg_at(info, sub * 0 + (first_pos + BLOCK))
        enter = jnp.where(fwdb, (sp == before).astype(F32), (sp == after).astype(F32))
        keep = jnp.where(fwdb, (sp == last).astype(F32), (sp == begin).astype(F32))
        ce = cmap[blk, :] * enter
        bk = bmap[blk, :] * keep
        tb_o[3, b] = ce
        tc_o[1, b] = bk
        tc_o[2, b] = ce.T
        ta_o[1, b] = bk.T
        chain = jnp.where(fwdb[0:1, :], (last == before).astype(F32)[0:1, :], (begin == after).astype(F32)[0:1, :])
        dvals.append(jnp.exp(end) * chain)
        ends.append(end)
        cb = cmap[blk, :].astype(BF16)
        bb = bmap[blk, :].astype(BF16)
        zero = jnp.zeros_like(bb)
        same = sp == st
        low = same & (sub > ln)
        high = same & (sub < ln)
        bf = jnp.where(fwdb, bb, zero)
        br = jnp.where(fwdb, zero, bb)
        tb_o[2, b] = jnp.where(low, nt(cb, bf), jnp.where(high, nt(cb, br), 0.0))
        tc_o[0, b] = jnp.where(high, nt(bf, cb), jnp.where(low, nt(br, cb), 0.0))
    ones = jnp.ones((1, 128), F32)
    prefix, suffix = [ones], [ones]
    for b in range(nb):
        prefix.append(prefix[-1] * dvals[b])
        suffix.append(suffix[-1] * dvals[nb - 1 - b])
    suffix = suffix[::-1]
    f1 = fwdb[0:1, :]
    for b in range(nb):
        cum_s[b : b + 1, :] = dvals[b]
        cum_s[48 + b : 49 + b, :] = ends[b]
    for i in range(nb + 1):
        cum_s[16 + i : 17 + i, :] = jnp.where(f1, prefix[i], suffix[i])
        cum_s[32 + i : 33 + i, :] = jnp.where(f1, suffix[i], prefix[i])
    dpt_o[...] = cum_s[...].T


def pair_rows(dpt, j, base, i, half):
    lane = iota((1, 128), 1)
    one = dpt[pl.ds(half * 64 + 2 * j, 1), :][:, base + i : base + i + 1]
    two = dpt[pl.ds(half * 64 + 2 * j + 1, 1), :][:, base + i : base + i + 1]
    return jnp.where(lane < 64, one, two)


def assemble(dst, pieces):
    quarter = dst.shape[0] // 4
    q = lax.axis_index("wide") % 4
    cbit = q % 2
    xbit = q // 2
    places = (q, (1 - xbit) * 2 + cbit, xbit * 2 + 1 - cbit, (1 - xbit) * 2 + 1 - cbit)
    for place, piece in zip(places, pieces):
        dst[pl.ds(pl.multiple_of(place * quarter, quarter), quarter), :] = piece[...]


def vals_kernel(
    length, other, info, normed, *refs,
):
    nb = length // BLOCK
    ext = length + 2 * HALO
    j = pl.program_id(0)
    step = j
    if other:
        p0, p1, p2, p3, taps, ta, dpt = refs[:7]
        xc_o, vm_o, ds_o, s_o, bnd_o, wvo_o, vm_s, seg_s, wall_s = refs[11:]
        j = j + pl.num_programs(0)

        @pl.when(step == 0)
        def _():
            assemble(wvo_o, (p0, p1, p2, p3))
            for i in range(wall_s.shape[0]):
                wall_s[i] = wvo_o[:, i * 128 : (i + 1) * 128]

        wv = wall_s[step]
    else:
        wv_ref, taps, ta, dpt, xc_o, vm_o, ds_o, s_o, bnd_o, vm_s, seg_s = refs
        wv = wv_ref[...]
    off, count = info[5], info[4]

    @pl.when(step == 0)
    def _():
        seg_s[...] = seg_at(info, iota((ext, 128), 0) + (off - HALO))

    live = iota((ext, 128), 0) + (off - HALO) < count
    vm = jnp.where(live, mm(normed[...], wv), 0.0)
    vm_s[...] = vm
    vm_o[...] = vm.astype(BF16)
    mix = conv_taps(vm_s, seg_s, taps, HALO, length)
    act, ds = silu_parts(mix)
    xc = act.astype(BF16)
    xc_o[...] = xc
    ds_o[...] = ds.astype(BF16)
    lane = iota((BLOCK, 128), 1)
    top = iota((BLOCK, 128), 0) < 64
    loc = []
    for b in range(nb):
        blk = slice(b * BLOCK, (b + 1) * BLOCK)
        got = []
        for i in range(2):
            h = 2 * j + i
            w = jnp.exp(jnp.where(top, ta[0, b, pl.ds(h, 1), :], ta[0, b, pl.ds(64 + h, 1), :]))
            got.append((ta[1, b] * w).astype(BF16))
        got = mm(jnp.concatenate(got, axis=0), xc[blk, :])
        loc.append(jnp.where(lane < 64, got[0:BLOCK, :], got[BLOCK:, :]))
    state = jnp.zeros((64, 128), F32)
    s_o[0, 0, 0:64, :] = state.astype(BF16)
    for b in range(nb):
        state = pair_rows(dpt, j, 0, b, 0) * state + loc[b][0:64, :]
        s_o[0, b + 1, 0:64, :] = state.astype(BF16)
    end_f = state
    state = jnp.zeros((64, 128), F32)
    s_o[0, nb, 64:128, :] = state.astype(BF16)
    for b in range(nb - 1, -1, -1):
        state = pair_rows(dpt, j, 0, b, 1) * state + loc[b][64:128, :]
        s_o[0, b, 64:128, :] = state.astype(BF16)
    bnd_o[0] = jnp.where(info[7] == 0, end_f, state).astype(BF16)


def scan_kernel(length, first_pair, info, xc_ref, s_ref, s0_ref, dpt, tb, skip, *refs):
    nb = length // BLOCK
    y_o, st_o = refs[-2:]
    j = pl.program_id(0) + first_pair
    right = (info[7] == 1).astype(F32)
    s0 = s0_ref[0].astype(F32)
    lane = iota((BLOCK, 128), 1)
    first = lane < 64
    low = iota((BLOCK, BLOCK), 0) > lane
    base = row_base(2, [[(0, 128), (256, 320)], [(128, 256), (320, 384)]])
    for i in range(nb + 1):
        f = s_ref[0, i, 0:64, :].astype(F32) + pair_rows(dpt, j, 16, i, 0) * (s0 * right)
        r = s_ref[0, i, 64:128, :].astype(F32) + pair_rows(dpt, j, 16, i, 1) * (s0 * (1.0 - right))
        st_o[0, i, 0:64, :] = f.astype(BF16)
        st_o[0, i, 64:128, :] = r.astype(BF16)
    for b in range(nb):
        blk = slice(b * BLOCK, (b + 1) * BLOCK)
        xb = xc_ref[blk, :]
        rhs = jnp.concatenate([xb, st_o[0, b, 0:64, :], st_o[0, b + 1, 64:128, :]], axis=0)
        got = []
        for i in range(2):
            h = 2 * j + i
            terms = column_terms([tb[0, b, pl.ds(h, 1), :], tb[0, b, pl.ds(64 + h, 1), :]])
            expo = tn(terms, row_terms(2, base, tb[1, b, pl.ds(h, 1), :], tb[1, b, pl.ds(64 + h, 1), :]))
            diff = jnp.where(low, expo[:, 0:128], expo[:, 128:256])
            mix = jnp.exp(jnp.minimum(diff, 60.0)) * tb[2, b]
            ct = tb[3, b] * jnp.exp(expo[:, 256:])
            lhs = jnp.concatenate([mix.astype(BF16), ct.astype(BF16)], axis=1)
            got.append(lhs)
        got = mm(jnp.concatenate(got, axis=0), rhs)
        y = jnp.where(first, got[0:BLOCK, :], got[BLOCK:, :]) + skip[0:1, :] * xb.astype(F32)
        y_o[blk, :] = y.astype(BF16)


def by_core(v, keep, send):
    share = v.shape[0] // 16
    cbit = lax.axis_index("wide") % 2
    v = v.astype(BF16).reshape(8, 2, share, v.shape[1])
    keep[...] = jnp.where(cbit == 0, v[:, 0], v[:, 1]).reshape(8 * share, v.shape[3])
    send[...] = jnp.where(cbit == 0, v[:, 1], v[:, 0]).reshape(8 * share, v.shape[3])


def gate_kernel(
    tiles, x_ref, g_ref, normed, y_ref, wout_a, wg_a, p0, p1, p2, p3, gain,
    out_o, gy_o, keep_o, send_o, ggate_o, ggain_o, wgo_o, hn_s, other_s, gated_s, act_s, dact_s, ghn_s,
):
    dm = x_ref.shape[1]
    chans = y_ref.shape[1]
    half = chans // 2
    step = 256
    assemble(other_s, (p0, p1, p2, p3))
    wgo_o[...] = other_s[:, dm:]
    ggain_o[...] = jnp.zeros_like(ggain_o)

    @pl.loop(0, tiles)
    def _(i):
        start = pl.multiple_of(i * BLOCK, BLOCK)
        rows = pl.ds(start, BLOCK)
        nrows = normed[pl.ds(pl.multiple_of(start + HALO, HALO), BLOCK), :]
        squares = jnp.zeros((BLOCK, 128), F32)
        for lo in range(0, chans, step):
            wg = wg_a[:, lo : lo + step] if lo < half else other_s[:, dm + lo - half : dm + lo - half + step]
            gates = mm(nrows, wg)
            for at in range(0, step, 128):
                cols = slice(lo + at, lo + at + 128)
                act, dact = silu_parts(gates[:, at : at + 128])
                gated = y_ref[rows, cols].astype(F32) * act
                squares = squares + gated * gated
                gated_s[:, cols] = gated
                act_s[:, cols] = act
                dact_s[:, cols] = dact
        inv = lax.rsqrt(jnp.sum(squares, axis=1, keepdims=True) * (1.0 / chans) + EPS)
        inv = jnp.broadcast_to(inv, (BLOCK, 128))
        g = g_ref[rows, :]
        across = jnp.zeros((BLOCK, 128), F32)
        for lo in range(0, chans, step):
            wo = wout_a[lo : lo + step, :] if lo < half else other_s[lo - half : lo - half + step, 0:dm]
            ghns = nt(g, wo)
            for at in range(0, step, 128):
                cols = slice(lo + at, lo + at + 128)
                gainv = gain[0:1, cols]
                gated = gated_s[:, cols]
                nrm = gated * inv
                hn_s[rows, cols] = (nrm * gainv).astype(BF16)
                ghn = ghns[:, at : at + 128]
                ggain_o[0:1, cols] += jnp.sum(ghn * nrm, axis=0, keepdims=True)
                wgt = ghn * gainv
                ghn_s[:, cols] = wgt
                across = across + wgt * gated
        cross = jnp.sum(across, axis=1, keepdims=True) * (1.0 / chans)
        cross = jnp.broadcast_to(cross, (BLOCK, 128)) * (inv * inv * inv)
        hn = hn_s[rows, :]
        branch = mm(hn[:, 0:half], wout_a[...]) + mm(hn[:, half:], other_s[:, 0:dm])
        out_o[rows, :] = (x_ref[rows, :].astype(F32) + branch).astype(BF16)
        for lo in range(0, chans, 128):
            cols = slice(lo, lo + 128)
            ggated = inv * ghn_s[:, cols] - gated_s[:, cols] * cross
            gy_o[rows, cols] = (ggated * act_s[:, cols]).astype(BF16)
            ggate_o[rows, cols] = (ggated * y_ref[rows, cols].astype(F32) * dact_s[:, cols]).astype(BF16)

    length = g_ref.shape[0]
    gt = g_ref[...].T
    nt_ = normed[HALO : HALO + length, :].T
    for k in range(2):
        for p in range(half // 256):
            cols = slice(k * half + p * 256, k * half + (p + 1) * 256)
            dst = slice(p * 256, (p + 1) * 256)
            dst2 = slice(half + p * 256, half + (p + 1) * 256)
            by_core(mm(gt, hn_s[:, cols]), keep_o.at[k, :, dst], send_o.at[k, :, dst])
            by_core(mm(nt_, ggate_o[:, cols]), keep_o.at[k, :, dst2], send_o.at[k, :, dst2])


def gstate_kernel(length, first_pair, info, gy_ref, coltt, cet, dpt, *refs):
    nb = length // BLOCK
    gs_o, bnd_o = refs[-2:]
    j = pl.program_id(0) + first_pair
    lane = iota((BLOCK, 128), 1)
    top = iota((BLOCK, 128), 0) < 64
    loc = []
    for b in range(nb):
        blk = slice(b * BLOCK, (b + 1) * BLOCK)
        gy = gy_ref[blk, :]
        got = []
        for i in range(2):
            h = 2 * j + i
            e = jnp.exp(jnp.where(top, coltt[b, pl.ds(h, 1), :], coltt[b, pl.ds(64 + h, 1), :]))
            got.append((cet[b] * e).astype(BF16))
        got = mm(jnp.concatenate(got, axis=0), gy)
        loc.append(jnp.where(lane < 64, got[0:BLOCK, :], got[BLOCK:, :]))
    state = jnp.zeros((64, 128), F32)
    gs_o[0, nb, 0:64, :] = state.astype(BF16)
    for b in range(nb - 1, -1, -1):
        state = pair_rows(dpt, j, 0, b, 0) * state + loc[b][0:64, :]
        gs_o[0, b, 0:64, :] = state.astype(BF16)
    end_f = state
    state = jnp.zeros((64, 128), F32)
    gs_o[0, 0, 64:128, :] = state.astype(BF16)
    for b in range(nb):
        state = pair_rows(dpt, j, 0, b, 1) * state + loc[b][64:128, :]
        gs_o[0, b + 1, 64:128, :] = state.astype(BF16)
    bnd_o[0] = jnp.where(info[7] == 1, end_f, state).astype(BF16)


def gscan_kernel(
    length, first_pair, info, xc_ref, ds_ref, gy_ref, st_ref, gs_ref, gs0_ref, dpt, rowst, wt, coltt, tc, skip,
    *refs,
):
    nb = length // BLOCK
    gmix_o, ggt_o, gb_o, gct_o, k_o, r_o, phi_o, gskip_o, edge_o, gst_s = refs[-10:]
    step = pl.program_id(0)
    j = step + first_pair
    right = (info[7] == 1).astype(F32)
    s0 = gs0_ref[0].astype(F32)
    sub = iota((BLOCK, BLOCK), 0)
    lane = iota((BLOCK, 128), 1)
    first = lane < 64
    later = lane > sub
    top = sub < 64

    @pl.when(step == 0)
    def _():
        for k, acc in enumerate((ggt_o, gb_o, gct_o, k_o, r_o)):
            acc[...] = jnp.zeros_like(acc) if first_pair else refs[3 + k][...]

    base = row_base(4, [[(0, 128)], [(128, 256)], [(256, 320)], [(320, 384)]])

    phi_o[...] = jnp.zeros_like(phi_o)
    for i in range(nb + 1):
        f = gs_ref[0, i, 0:64, :].astype(F32) + pair_rows(dpt, j, 32, i, 0) * (s0 * (1.0 - right))
        r = gs_ref[0, i, 64:128, :].astype(F32) + pair_rows(dpt, j, 32, i, 1) * (s0 * right)
        f = f.astype(BF16)
        r = r.astype(BF16)
        gst_s[i, 0:64, :] = f
        gst_s[i, 64:128, :] = r
        if i > 0:
            phi_o[i - 1 : i, :] = jnp.sum(f.astype(F32) * st_ref[0, i, 0:64, :].astype(F32), axis=0, keepdims=True)
        if i < nb:
            phi_o[8 + i : 9 + i, :] = jnp.sum(
                r.astype(F32) * st_ref[0, i, 64:128, :].astype(F32), axis=0, keepdims=True
            )
    gskip = jnp.zeros((1, 128), F32)
    for b in range(nb):
        blk = slice(b * BLOCK, (b + 1) * BLOCK)
        xb = xc_ref[blk, :]
        gy = gy_ref[blk, :]
        gyf = gy.astype(F32)
        gskip = gskip + jnp.sum(gyf * xb.astype(F32), axis=0, keepdims=True)
        rhs = jnp.concatenate([gy, gst_s[b + 1, 0:64, :], gst_s[b, 64:128, :]], axis=0)
        left = jnp.concatenate([xb, st_ref[0, b, 0:64, :], st_ref[0, b + 1, 64:128, :]], axis=0)
        first2 = iota((2 * BLOCK, 128), 1) < 64
        none = jnp.zeros_like(left)
        big2 = nt(jnp.concatenate([jnp.where(first2, left, none), jnp.where(first2, none, left)], axis=0), rhs)
        got = []
        sum_ge, sum_gct, sum_gb, kparts = [], [], [], []
        for i in range(2):
            h = 2 * j + i
            terms = column_terms([v[b, pl.ds(at + h, 1), :] for v in (rowst, wt) for at in (0, 64)])
            expo = tn(terms, row_terms(4, base, coltt[b, pl.ds(h, 1), :], coltt[b, pl.ds(64 + h, 1), :]))
            diff = jnp.where(later, expo[:, 0:128], expo[:, 128:256])
            et_m = jnp.exp(jnp.minimum(diff, 60.0))
            mt = et_m * tc[0, b]
            w = jnp.exp(expo[:, 256:])
            bt = tc[1, b] * w
            big = big2[2 * BLOCK * i : 2 * BLOCK * (i + 1), :]
            gmt = big[0:BLOCK, 0:BLOCK]
            gbt = big[0:BLOCK, BLOCK:]
            gctt = big[BLOCK:, 0:BLOCK]
            ge = gmt * et_m
            sum_ge.append(ge)
            q = gmt * mt
            qf = jnp.where(later, q, 0.0)
            e = jnp.exp(jnp.where(top, coltt[b, pl.ds(h, 1), :], coltt[b, pl.ds(64 + h, 1), :]))
            gce = gctt * e
            sum_gct.append(gce)
            ct = gce * tc[2, b]
            rf = jnp.sum(qf, axis=0, keepdims=True)
            rall = jnp.sum(q, axis=0, keepdims=True)
            r_o[b, pl.ds(h, 1), :] = rf + jnp.sum(ct[0:64, :], axis=0, keepdims=True)
            r_o[b, pl.ds(64 + h, 1), :] = rall - rf + jnp.sum(ct[64:128, :], axis=0, keepdims=True)
            gbw = gbt * w
            sum_gb.append(gbw)
            u = gbw * tc[1, b]
            kf = jnp.sum(qf + jnp.where(first, u, 0.0), axis=1, keepdims=True)
            kb = jnp.sum(q + u, axis=1, keepdims=True) - kf
            kparts += [kf, kb]
            lhs = jnp.concatenate([mt.astype(BF16), bt.astype(BF16)], axis=1)
            got.append(lhs)
        ggt_o[b] += sum_ge[0] + sum_ge[1]
        gct_o[b] += sum_gct[0] + sum_gct[1]
        gb_o[b] += sum_gb[0] + sum_gb[1]
        two = jnp.where(lane % 64 == 0, jnp.where(first, kparts[0], kparts[1]), jnp.where(first, kparts[2], kparts[3]))
        k_o[blk, :] += pltpu.roll(jnp.where(lane % 64 < 2, two, 0.0), 2 * j, 1)
        got = mm(jnp.concatenate(got, axis=0), rhs)
        gx = jnp.where(first, got[0:BLOCK, :], got[BLOCK:, :]) + skip[0:1, :] * gyf
        gmix = (gx * ds_ref[blk, :].astype(F32)).astype(BF16)
        gmix_o[blk, :] = gmix
        if b == 0:
            edge_o[...] = gmix[0:HALO, :]
        if b == nb - 1:
            edge_o[...] = jnp.where(info[7] == 0, gmix[BLOCK - HALO :, :], edge_o[...])
    gskip_o[...] = jnp.broadcast_to(gskip, (8, 128))


def join_kernel(
    length, heads, info, ggt, gb, gct, k_ref, r_ref, phi, maps, dsl, sig,
    gmb_o, gv_o, small_o, edge_o, gc_s, gm_s,
):
    nb = length // BLOCK
    off = info[5]
    chans = phi.shape[1]
    sub = iota((BLOCK, BLOCK), 0)
    lane = iota((BLOCK, 128), 1)
    first = lane < 64
    low = sub > lane
    high = sub < lane
    upper_strict = high.astype(F32)
    upper = (sub <= lane).astype(F32)
    lower_strict = low.astype(F32)
    lower = (sub >= lane).astype(F32)
    owner = iota((chans, 128), 0) // 64
    to_f = (owner == iota((chans, 128), 1)).astype(F32)
    to_b = (owner + 64 == iota((chans, 128), 1)).astype(F32)
    phi_f = mm(phi[0:8, :], to_f, precision=HIGH)
    phi_b = mm(phi[8:16, :], to_b, precision=HIGH)
    gc_s[...] = jnp.zeros_like(gc_s)
    gm_s[...] = jnp.zeros_like(gm_s)
    sum_bias = jnp.zeros((1, 128), F32)
    sum_rate = jnp.zeros((1, 128), F32)
    for b in range(nb):
        blk = slice(b * BLOCK, (b + 1) * BLOCK)
        ext = slice(HALO + b * BLOCK, HALO + (b + 1) * BLOCK)
        first_pos = off + b * BLOCK
        sp = seg_at(info, sub + first_pos)
        st = seg_at(info, lane + first_pos)
        before = seg_at(info, sub * 0 + (first_pos - 1))
        begin = seg_at(info, sub * 0 + first_pos)
        last = seg_at(info, sub * 0 + (first_pos + BLOCK - 1))
        after = seg_at(info, sub * 0 + (first_pos + BLOCK))
        enter = jnp.where(first, (sp == before).astype(F32), (sp == after).astype(F32))
        keep = jnp.where(first, (sp == last).astype(F32), (sp == begin).astype(F32))
        same = sp == st
        gg = ggt[b]
        gf = jnp.where(same & high, gg, 0.0).astype(BF16)
        gr = jnp.where(same & low, gg, 0.0).astype(BF16)
        cm = maps[blk, 128:256]
        bm = maps[blk, 0:128]
        gm_s[ext, 0:128] = jnp.where(first, mm(gf, cm), mm(gr, cm)) + gb[b] * keep
        gc_s[ext, :] = jnp.where(first, tn(gf, bm), tn(gr, bm)) + gct[b].T * enter
        kb = k_ref[blk, :]
        rb = r_ref[b].T
        ga_f = mm(upper_strict, rb, precision=HIGH) - mm(upper, kb, precision=HIGH) + phi_f[b : b + 1, :]
        ga_b = mm(lower_strict, rb, precision=HIGH) - mm(lower, kb, precision=HIGH) + phi_b[b : b + 1, :]
        ga = jnp.where(first, ga_f, ga_b)
        gv = kb * sig[blk, 128:256] + ga * sig[blk, 0:128]
        gv_o[blk, :] = gv.astype(BF16)
        sum_bias = sum_bias + jnp.sum(gv, axis=0, keepdims=True)
        sum_rate = sum_rate + jnp.sum(ga * sig[blk, 256:384], axis=0, keepdims=True)
    small_o[...] = jnp.zeros_like(small_o)
    small_o[0:1, :] = sum_bias
    small_o[1:2, :] = sum_rate
    small_o[8:9, :] = pltpu.roll(sum_bias, 128 - heads // 2, 1)
    small_o[9:10, :] = pltpu.roll(sum_rate, 128 - heads // 2, 1)
    mid = length + HALO
    lo = HALO // 2
    pos = iota((mid, 128), 0) + (off - HALO + lo)
    seg0 = seg_at(info, pos)
    segn = seg_at(info, pos + 1)
    segp = seg_at(info, pos - 1)
    from_next = jnp.where(seg0 == segn, gc_s[lo + 1 : lo + 1 + mid, :], 0.0)
    from_prev = jnp.where(seg0 == segp, gc_s[lo - 1 : lo - 1 + mid, :], 0.0)
    gm_s[lo : lo + mid, 128:256] = jnp.where(iota((mid, 128), 1) < 64, from_next, from_prev)
    gmb_o[...] = gm_s[...] * dsl[...]
    lo = HALO // 2
    edge_o[...] = jnp.where(
        info[7] == 0, gmb_o[length + lo : length + lo + HALO, :], gmb_o[lo : lo + HALO, :]
    )


def back_conv(length, seg_s, live, grad, data, tap):
    own = slice(HALO, HALO + length)
    seg0 = seg_s[own, :]
    mine = grad[own, :]
    total = mine * tap[3:4, :]
    gtap = [None] * 7
    gtap[3] = jnp.sum(mine * data[own, :], axis=0, keepdims=True)
    for k in (0, 1, 2, 4, 5, 6):
        lo = HALO + 3 - k
        same = seg_s[lo : lo + length, :] == seg0
        total = total + jnp.where(same, grad[lo : lo + length, :], 0.0) * tap[k : k + 1, :]
        up = HALO + k - 3
        same = seg_s[up : up + length, :] == seg0
        gtap[k] = jnp.sum(jnp.where(same, data[up : up + length, :], 0.0) * mine, axis=0, keepdims=True)
    return jnp.where(live, total, 0.0), gtap


def back_kernel(
    length, steps, info, gmix, edge_a, edge_b, vm, wv_a, wg_a, wv_b, wg_b, ggate, normed, taps, ggain, gskip,
    keep_o, send_o, tiny_o, acc_o, ext_s, vm_s, seg_s,
):
    j = pl.program_id(0)
    ext = length + 2 * HALO
    off, count = info[5], info[4]
    own = slice(HALO, HALO + length)

    @pl.when(j == 0)
    def _():
        seg_s[...] = seg_at(info, iota((ext, 128), 0) + (off - HALO))
        tiny_o[...] = jnp.zeros_like(tiny_o)
        acc_o[...] = jnp.zeros_like(acc_o)

    live = iota((length, 128), 0) + off < count
    near = j < steps // 2
    ext_s[own, :] = gmix[...].astype(F32)
    halo = jnp.where(near, edge_a[...].astype(F32), edge_b[...].astype(F32))
    right = info[7] == 1
    ext_s[0:HALO, :] = jnp.where(right, halo, 0.0)
    ext_s[HALO + length : ext, :] = jnp.where(right, 0.0, halo)
    vm_s[...] = vm[...].astype(F32)
    gvals, gtap = back_conv(length, seg_s, live, ext_s, vm_s, taps)
    gvals = gvals.astype(BF16)
    half = j // (steps // 2)
    here = pl.ds(pl.multiple_of((j % (steps // 2)) * 128, 128), 128)
    by_core(tn(normed[own, :], gvals), keep_o.at[half, :, here], send_o.at[half, :, here])
    for t in range(7):
        tiny_o[half, t : t + 1, here] = gtap[t]
    tiny_o[half, 7:8, here] = ggain[0:1, :]
    tiny_o[half, 8:9, here] = gskip[0:1, :]
    both = jnp.concatenate([gvals, ggate[...]], axis=1)
    weights = jnp.concatenate(
        [jnp.where(near, wv_a[...], wv_b[...]), jnp.where(near, wg_a[...], wg_b[...])], axis=1
    )
    acc_o[...] += nt(both, weights)


def last_kernel(
    length, hl, info, acc, normed, gmb, edge, bcm, taps_bc, gv, wdt, wbc, x_ref, g_ref, rs, pre, small, tiny,
    keep_o, send_o, tiny_o, gin_o, ext_s, vm_s, seg_s,
):
    ext = length + 2 * HALO
    off, count = info[5], info[4]
    own = slice(HALO, HALO + length)
    seg_s[...] = seg_at(info, iota((ext, 128), 0) + (off - HALO))
    live = iota((length, 128), 0) + off < count
    tiny_o[...] = tiny[...]
    for half in range(2):
        tiny_o[half, 10:11, 0:128] = small[8 * half : 8 * half + 1, :]
        tiny_o[half, 10:11, 128:256] = small[8 * half + 1 : 8 * half + 2, :]
    both = []
    for k in range(2):
        cols = slice(k * 128, (k + 1) * 128)
        ext_s[...] = gmb[:, cols]
        lo = HALO // 2
        hi = length + lo
        got = edge[:, cols]
        ext_s[lo : lo + HALO, :] += jnp.where(info[7] == 1, got, 0.0)
        ext_s[hi : hi + HALO, :] += jnp.where(info[7] == 1, 0.0, got)
        vm_s[...] = bcm[:, cols]
        gbc, gtap = back_conv(length, seg_s, live, ext_s, vm_s, taps_bc.at[:, cols])
        for t in range(7):
            at = (t % 3) * 256 + k * 128
            for half in range(2):
                tiny_o[half, 11 + t // 3 : 12 + t // 3, at : at + 128] = gtap[t]
        both.append(gbc.astype(BF16))
    gbc = jnp.concatenate(both + [gv[...]], axis=1)
    gw = tn(normed[own, :], gbc)
    by_core(gw, keep_o.at[0], send_o.at[0])
    turned = pltpu.roll(gw[:, 256:], 128 - hl, 1)
    by_core(jnp.concatenate([gw[:, 0:256], turned], axis=1), keep_o.at[1], send_o.at[1])
    gn = acc[...] + nt(gbc[:, 0:256], wbc[...]) + mm(gv[...], wdt[...])
    x = x_ref[...].astype(F32)
    r = rs[...]
    wp = gn * pre[...]
    mean = jnp.mean(wp * x, axis=1, keepdims=True)
    gin_o[...] = g_ref[...].astype(F32) + r * wp - x * (r * r * r * mean)
    gpre = jnp.sum(gn * x * r, axis=0, keepdims=True)
    for half in range(2):
        tiny_o[half, 9:10, 0 : gpre.shape[1]] = gpre


def finish_kernel(hl, tiny, conv_o, convbc_o, pre_o, bias_o, rate_o, skip_o, gain_o):
    ch = tiny.shape[1]
    w = lax.axis_index("wide")
    share = pre_o.shape[1]
    lanes = gain_o.shape[1]
    src = iota((ch, 128), 0)
    dst = iota((ch, 128), 1)
    rows = tiny[...]
    by_head = ((src == (dst // lanes) * HD + lanes * w + dst % lanes) & (dst < hl * lanes)).astype(F32)
    got = mm(rows, by_head, precision=HIGH)
    for h in range(hl):
        conv_o[:, h, :] = got[0:7, h * lanes : (h + 1) * lanes]
        gain_o[h : h + 1, :] = got[7:8, h * lanes : (h + 1) * lanes]
    chosen = ((src == share * w + dst) & (dst < share)).astype(F32)
    pre_o[...] = mm(rows[8:16, :], chosen, precision=HIGH)[1:2, 0:share]
    per = (src // HD == dst).astype(F32)
    skip_o[...] = mm(rows[8:16, :], per, precision=HIGH)[0:1, 0:hl]
    size = convbc_o.shape[1]
    group = (size * w) // 64
    start = ((group % 2) * 2 + group // 2) * 64 + (size * w) % 64
    src = iota((256, 128), 0)
    dst = iota((256, 128), 1)
    chosen = ((src == start + dst) & (dst < size)).astype(F32)
    for k in range(3):
        part = mm(rows[8:16, 256 * k : 256 * (k + 1)], chosen, precision=HIGH)
        for r in range(3):
            if 3 * r + k < 7:
                convbc_o[3 * r + k : 3 * r + k + 1, :] = part[3 + r : 4 + r, 0:size]
    both = rows[10:11, 0:128]
    turned = jnp.broadcast_to(both, (128, 128)).T
    bias_o[:, 0:1] = turned[0:hl, 0:1]
    bias_o[:, 1:2] = turned[64 : 64 + hl, 0:1]
    rate = rows[10:11, 128:256]
    rate_o[...] = (rate + pltpu.roll(rate, 64, 1))[:, 0:hl]


def collect_kernel(
    keep, got_v, keep_bc, send_bc, tiny, out_o, tiny_o,
    core_s, mine_s, piece_s, got_s, zsend_s, zgot_s, tcore_s, tsum_s, tgot_s, tz_s, tzgot_s,
    core_out, core_in, plane_out, plane_in, z_out, z_in,
):
    w = lax.axis_index("wide")
    n = lax.axis_index("narrow")
    c, xx, z = w % 2, (w // 2) % 2, w // 4
    share = out_o.shape[0]
    core = (w + 1 - 2 * c, n)
    over_x = (w + 2 - 4 * xx, n)
    over_y = (w, 1 - n)
    over_d = (w + 2 - 4 * xx, 1 - n)
    steps = (2, 1, 3)
    over_z = [(((z + d) % 4) * 4 + w % 4, n) for d in steps]
    mesh_ids = pl.DeviceIdType.MESH
    barrier = pltpu.get_barrier_semaphore()
    for other in [core, over_x, over_y, over_d] + over_z:
        pl.semaphore_signal(barrier, inc=1, device_id=other, device_id_type=mesh_ids)
    pl.semaphore_wait(barrier, 7)

    def copy(src, dst, out_sem, in_sem, other):
        got = pltpu.make_async_remote_copy(
            src_ref=src, dst_ref=dst, send_sem=out_sem, recv_sem=in_sem, device_id=other, device_id_type=mesh_ids
        )
        got.start()
        return got

    rows = [pl.ds(pl.multiple_of(((z + d) % 4) * (2 * share), 2 * share), 2 * share) for d in steps + (0,)]
    first = [copy(tiny, tcore_s, core_out.at[4], core_in.at[4], core)]
    for i in range(4):
        first.append(copy(send_bc.at[:, rows[i], :], core_s.at[i], core_out.at[i], core_in.at[i], core))
    ways = (over_x, over_y, over_d)
    first[0].wait()
    tsum_s[...] = tiny[...] + tcore_s[...]
    second = [[]]
    for k, other in enumerate(ways):
        half = 0 if k == 0 else 1
        second[0].append(copy(tsum_s.at[half], tgot_s.at[k], plane_out.at[4, k], plane_in.at[4, k], other))
    for i in range(4):
        first[i + 1].wait()
        chv = keep.shape[2]
        for cols, both in (
            (slice(0, chv), keep[:, rows[i], :].astype(F32) + got_v[:, rows[i], :].astype(F32)),
            (slice(chv, out_o.shape[1]), keep_bc[:, rows[i], :].astype(F32) + core_s[i].astype(F32)),
        ):
            low, high = both[:, 0:share, :], both[:, share:, :]
            near = jnp.where(xx == 0, low, high)
            far = jnp.where(xx == 0, high, low)
            mine_s[i, :, cols] = near[0]
            piece_s[i, 0, :, cols] = far[0].astype(BF16)
            piece_s[i, 1, :, cols] = near[1].astype(BF16)
            piece_s[i, 2, :, cols] = far[1].astype(BF16)
        second.append(
            [copy(piece_s.at[i, k], got_s.at[i, k], plane_out.at[i, k], plane_in.at[i, k], ways[k]) for k in range(3)]
        )
    for one in second[0]:
        one.wait()
    tsum = tsum_s[0] + tgot_s[0] + tgot_s[1] + tgot_s[2]
    tz_s[...] = tsum
    third = [copy(tz_s, tzgot_s.at[k], z_out.at[1, k], z_in.at[1, k], over_z[k]) for k in range(3)]
    total = None
    for i in range(4):
        for one in second[i + 1]:
            one.wait()
        total = mine_s[i] + got_s[i, 0].astype(F32) + got_s[i, 1].astype(F32) + got_s[i, 2].astype(F32)
        if i < 3:
            zsend_s[i] = total.astype(BF16)
            third.append(copy(zsend_s.at[i], zgot_s.at[i], z_out.at[0, i], z_in.at[0, i], over_z[i]))
    for one in third:
        one.wait()
    out_o[...] = total + zgot_s[0].astype(F32) + zgot_s[1].astype(F32) + zgot_s[2].astype(F32)
    tiny_o[...] = tsum + tzgot_s[0] + tzgot_s[1] + tzgot_s[2]


def whole(shape, grid):
    zeros = (0,) * len(shape)
    if grid:
        return pl.BlockSpec(shape, lambda j: zeros)
    return pl.BlockSpec(shape, lambda: zeros)


def columns(rows, first=0):
    return pl.BlockSpec((rows, 128), lambda j: (0, first + j))


SMEM = pl.BlockSpec(memory_space=pltpu.SMEM)
VMEM = pl.BlockSpec(memory_space=pltpu.VMEM)
ANY = pl.BlockSpec(memory_space=pl.ANY)


def sds(shape, dtype):
    return jax.ShapeDtypeStruct(shape, dtype)


def params(grid, mib):
    if grid:
        return pltpu.CompilerParams(vmem_limit_bytes=mib * 2**20, dimension_semantics=("arbitrary",))
    return pltpu.CompilerParams(vmem_limit_bytes=mib * 2**20)


def cost(us):
    return pl.CostEstimate(flops=int(us * 1.1e9), bytes_accessed=int(us * 1e6), transcendentals=0)


def pack_columns(v):
    n = v.shape[-1] // 4
    return jnp.concatenate([v[..., 0:n], v[..., 2 * n : 3 * n], v[..., n : 2 * n], v[..., 3 * n :]], axis=-1)


def small_kernel(hl, conv, gain, dtb, alog, skip, wdt, x_ref, out_o):
    ch = out_o.shape[1]
    length = x_ref.shape[0]
    lane = iota((1, 128), 1)
    wide_lane = iota((1, ch), 1)
    bias = jnp.zeros((1, 128), F32)
    rate = jnp.zeros((1, 128), F32)
    diag = jnp.zeros((1, ch), F32)
    out_o[0:16, :] = jnp.zeros((16, ch), F32)
    for h in range(hl):
        cols = slice(h * HD, (h + 1) * HD)
        out_o[0:7, cols] = conv[:, h, :]
        out_o[7:8, cols] = gain[h : h + 1, :]
        bias = jnp.where(lane == h, dtb[h, 0], jnp.where(lane == 64 + h, dtb[h, 1], bias))
        rate = jnp.where((lane == h) | (lane == 64 + h), alog[h], rate)
        diag = jnp.where(wide_lane // HD == h, skip[h], diag)
    out_o[8:9, :] = diag
    out_o[9:10, 0:128] = bias
    out_o[9:10, 128:256] = rate
    pick_row = (iota((2 * hl, 2 * hl), 0) == iota((2 * hl, 2 * hl), 1)).astype(F32).astype(BF16)
    out_o[16 : 16 + 2 * hl, :] = nt(pick_row, wdt[...])
    n = lax.axis_index("narrow")
    start, end = x_ref[0:HALO, :].astype(F32), x_ref[length - HALO :, :].astype(F32)
    out_o[16 + 2 * hl :, :] = jnp.where(n == 0, end[8:16, :], start[0:8, :])


def swap(v):
    return lax.ppermute(v, "narrow", [(0, 1), (1, 0)])


def flip(v, bit, wide):
    return lax.ppermute(v, "wide", [(i, i ^ bit) for i in range(wide)])


def cross(v, bit, wide):
    pairs = [(i * 2 + k, (i ^ bit) * 2 + 1 - k) for i in range(wide) for k in range(2)]
    return lax.ppermute(v, ("wide", "narrow"), pairs)


def pick(v, dim, index):
    return lax.dynamic_index_in_dim(v, index, dim, keepdims=False)


def total(*parts):
    acc = parts[0].astype(F32)
    for v in parts[1:]:
        acc = acc + v.astype(F32)
    return acc


def split_positions(
    wide, layer_in, pre_gain, w_heads, w_bc, conv_x, conv_bc, dt_bias, a_log, skip_d, norm_gain, w_out, cotangent, starts, live
):
    n = lax.axis_index("narrow")
    w = lax.axis_index("wide")
    left = n == 0
    _, length, dm = layer_in.shape
    hl = w_heads.shape[1]
    heads = 2 * hl
    ch = hl * HD
    chans = 2 * ch
    pairs = heads // 2
    hp = pairs // 2
    nb = length // BLOCK
    ext = length + 2 * HALO
    share = dm // wide
    x = layer_in[0]
    g = cotangent[0]
    xbit = (w // 2) % 2
    zbits = w // 4

    wdt = w_heads[:, :, 2 * HD :].reshape(dm, 2 * hl)
    small_own = pl.pallas_call(
        functools.partial(small_kernel, hl),
        out_shape=sds((24 + 2 * hl, ch), F32),
        in_specs=[VMEM, VMEM, SMEM, SMEM, SMEM, VMEM, VMEM],
        out_specs=VMEM,
        cost_estimate=cost(2),
        name="small",
    )(conv_x, norm_gain, dt_bias, a_log, skip_d, wdt, x)
    small_other = swap(small_own)

    quarter = dm // 4
    q = w % 4

    def gather(own):
        p0 = swap(lax.dynamic_slice(own, (q * quarter, 0), (quarter, own.shape[1])))
        p1 = flip(p0, 2, wide)
        return p0, p1, flip(p0, 1, wide), flip(p1, 1, wide)

    wv = w_heads[:, :, HD : 2 * HD].reshape(dm, ch)
    wg = w_heads[:, :, :HD].reshape(dm, ch)
    wo = w_out.reshape(ch, dm)
    wv_pieces = gather(wv)
    wog_pieces = gather(jnp.concatenate([wo, wg], axis=1))

    pos = (length, 128)
    sq = (nb, BLOCK, BLOCK)
    front_shapes = [
        ((8, chans), F32), ((8, chans), F32), ((8, chans), F32), ((128, dm), BF16), ((dm, 256), BF16), ((7, 256), F32),
        ((ext, dm), BF16), ((length, 1), F32), ((ext, 256), F32), ((ext, 256), F32), ((length, 256), BF16),
        ((2,) + sq, F32), ((4,) + sq, F32), ((3,) + sq, F32), ((128, 128), F32), ((length, 384), F32),
    ]
    (
        info, taps, gain, skip, wdt_all, wbc, taps_bc, normed, rs, bcm, dsl, maps, tab_a, tab_b, tab_c, dpt, sig,
    ) = pl.pallas_call(
        functools.partial(front_kernel, length, hl),
        out_shape=[sds((8,), jnp.int32)] + [sds(*v) for v in front_shapes],
        in_specs=[SMEM] + [VMEM] * 7,
        out_specs=[SMEM] + [VMEM] * len(front_shapes),
        scratch_shapes=[
            pltpu.VMEM((ext, 256), jnp.int32), pltpu.VMEM((ext, 256), F32), pltpu.VMEM((128, 128), F32),
            pltpu.VMEM((ext, dm), BF16),
        ],
        compiler_params=params(False, 16),
        cost_estimate=cost(8),
        name="front",
    )(starts, live, x, pre_gain.reshape(1, dm), w_bc, conv_bc, small_own, small_other)

    def states(first):
        return pl.BlockSpec((1, nb + 1, 128, 128), lambda j: (j + first, 0, 0, 0))

    bnd_spec = pl.BlockSpec((1, 64, 128), lambda j: (j, 0, 0))
    state_shape = sds((pairs, nb + 1, 128, 128), BF16)
    bnd_shape = sds((hp, 64, 128), BF16)
    act_shape = sds((length, chans), BF16)
    own_spec = pl.BlockSpec((dm, 128), lambda j: (0, jnp.minimum(j, hp - 1)))
    other_spec = pl.BlockSpec((dm, 128), lambda j: (0, jnp.maximum(j - hp, 0)))

    def vals(other, weights, before):
        first = hp if other else 0
        extra = [sds((dm, ch), BF16)] if other else []
        specs = [SMEM, whole((ext, dm), 1)]
        if other:
            specs += [whole((quarter, ch), 1)] * 4
        else:
            specs += [columns(dm)]
        specs += [columns(8, first), whole((2,) + sq, 1), whole((128, 128), 1)] + [ANY] * len(before)
        scratch = [pltpu.VMEM((ext, 128), F32), pltpu.VMEM((ext, 128), jnp.int32)]
        if other:
            scratch.append(pltpu.VMEM((hp, dm, 128), BF16))
        return pl.pallas_call(
            functools.partial(vals_kernel, length, other),
            grid=(hp,),
            out_shape=[act_shape, sds((ext, chans), BF16), act_shape, state_shape, bnd_shape] + extra,
            in_specs=specs,
            out_specs=[
                columns(length, first), columns(ext, first), columns(length, first),
                states(first), bnd_spec,
            ] + [whole((dm, ch), 1)] * other,
            scratch_shapes=scratch,
            input_output_aliases={len(specs) - len(before) + i: i for i in range(len(before))},
            compiler_params=params(True, 14),
            cost_estimate=cost(9),
            name="vals_other" if other else "vals_own",
        )(info, normed, *weights, taps, tab_a, dpt, *before)

    *own_vals, bnd_own = vals(False, (wv,), ())
    xc, vm, ds, s_loc, bnd_other, wv_other = vals(True, wv_pieces, own_vals)

    def aliases(specs, before):
        return {len(specs) - len(before) + i: i for i in range(len(before))}

    def scan(first, s0, before):
        specs = [
            SMEM, columns(length, first), states(first), bnd_spec, whole((128, 128), 1), whole((4,) + sq, 1), columns(8, first),
        ] + [ANY] * len(before)
        return pl.pallas_call(
            functools.partial(scan_kernel, length, first),
            grid=(hp,),
            out_shape=[act_shape, state_shape],
            in_specs=specs,
            out_specs=[columns(length, first), states(first)],
            input_output_aliases=aliases(specs, before),
            compiler_params=params(True, 8),
            cost_estimate=cost(10),
            name="scan_other" if first else "scan_own",
        )(info, xc, s_loc, s0, dpt, tab_b, skip, *before)

    y, s_true = scan(0, swap(bnd_other), scan(hp, swap(bnd_own), ()))

    gw_shape = (2, dm // 2, dm + ch)
    out, gy, keep_a, send_a, ggate, ggain, wg_other = pl.pallas_call(
        functools.partial(gate_kernel, nb),
        out_shape=[
            sds((length, dm), BF16), act_shape, sds(gw_shape, BF16), sds(gw_shape, BF16), act_shape, sds((8, chans), F32),
            sds((dm, ch), BF16),
        ],
        in_specs=[VMEM] * 11,
        out_specs=[VMEM] * 7,
        scratch_shapes=[pltpu.VMEM((length, chans), BF16), pltpu.VMEM((dm, dm + ch), BF16)]
        + [pltpu.VMEM((BLOCK, chans), F32)] * 4,
        compiler_params=params(False, 28),
        cost_estimate=cost(22),
        name="gated",
    )(x, g, normed, y, wo, wg, *wog_pieces, gain)

    def meet(keep, got):
        cols = keep.shape[-1]
        keep = keep.reshape(2, wide // 4, 2, share, cols)
        got = got.reshape(2, wide // 4, 2, share, cols)

        def piece(half, xx):
            return total(pick(keep[half], 1, xx), pick(got[half], 1, xx)).astype(BF16)

        return piece(0, xbit), piece(0, 1 - xbit), piece(1, xbit), piece(1, 1 - xbit)

    def plane(mine, to_x, to_y, to_d):
        return total(mine, flip(to_x, 2, wide), swap(to_y), cross(to_d, 2, wide)).astype(mine.dtype)

    def depth(v):
        parts = [pick(v, 0, zbits)]
        for k in (1, 2, 3):
            parts.append(flip(pick(v, 0, zbits ^ k), 4 * k, wide))
        return total(*parts)

    a_pieces = meet(keep_a, flip(send_a, 1, wide))

    def table(k):
        return pl.BlockSpec((None,) + sq, lambda j: (k, 0, 0, 0))

    def gstate(first, before):
        specs = [SMEM, columns(length, first), table(0), table(2), whole((128, 128), 1)] + [ANY] * len(before)
        return pl.pallas_call(
            functools.partial(gstate_kernel, length, first),
            grid=(hp,),
            out_shape=[state_shape, bnd_shape],
            in_specs=specs,
            out_specs=[states(first), bnd_spec],
            input_output_aliases=aliases(specs, before),
            compiler_params=params(True, 6),
            cost_estimate=cost(5),
            name="gstate_other" if first else "gstate_own",
        )(info, gy, tab_b, tab_c, dpt, *before)

    gs_loc, gbnd_own = gstate(0, ())
    gs_loc, gbnd_other = gstate(hp, (gs_loc,))

    gs_loc, gbnd_other, *a_pieces = lax.optimization_barrier((gs_loc, gbnd_other, *a_pieces))
    a_plane = plane(*a_pieces)

    def gscan(first, gs0, before):
        sums = [whole(sq, 1), whole(sq, 1), whole(sq, 1), whole(pos, 1), whole(sq, 1)]
        specs = [
            SMEM, columns(length, first), columns(length, first), columns(length, first), states(first), states(first),
            bnd_spec, whole((128, 128), 1), table(1), table(0), table(0), whole((3,) + sq, 1), columns(8, first),
        ]
        at = len(specs)
        if before:
            specs += [ANY] * 3 + sums
        return pl.pallas_call(
            functools.partial(gscan_kernel, length, first),
            grid=(hp,),
            out_shape=[
                act_shape, sds(sq, F32), sds(sq, F32), sds(sq, F32), sds(pos, F32), sds(sq, F32), sds((16, chans), F32),
                sds((8, chans), F32), sds((HALO, ch), BF16),
            ],
            in_specs=specs,
            out_specs=[columns(length, first)] + sums + [columns(16, first), columns(8, first), columns(HALO)],
            scratch_shapes=[pltpu.VMEM((nb + 1, 128, 128), BF16)],
            input_output_aliases={at: 0, at + 1: 6, at + 2: 7} if before else {},
            compiler_params=params(True, 14),
            cost_estimate=cost(17),
            name="gscan_other" if first else "gscan_own",
        )(info, xc, ds, gy, s_true, gs_loc, gs0, dpt, tab_b, tab_a, tab_b, tab_c, skip, *before)

    gmix, ggt, gb, gct, ksum, rsum, phi, gskip, edge_other = gscan(hp, swap(gbnd_own), ())
    gmix, ggt, gb, gct, ksum, rsum, phi, gskip, edge_own = gscan(
        0, swap(gbnd_other), (gmix, phi, gskip, ggt, gb, gct, ksum, rsum)
    )

    gmix, ggt, a_plane = lax.optimization_barrier((gmix, ggt, a_plane))
    wa = depth(a_plane)

    gmb, gv, small, edge_bc = pl.pallas_call(
        functools.partial(join_kernel, length, heads),
        out_shape=[sds((ext, 256), F32), sds(pos, BF16), sds((16, 128), F32), sds((HALO, 256), F32)],
        in_specs=[SMEM] + [VMEM] * 9,
        out_specs=[VMEM] * 4,
        scratch_shapes=[pltpu.VMEM((ext, 128), F32), pltpu.VMEM((ext, 256), F32)],
        compiler_params=params(False, 10),
        cost_estimate=cost(6),
        name="join",
    )(info, ggt, gb, gct, ksum, rsum, phi, maps, dsl, sig)

    edge_a, edge_b = swap(edge_other), swap(edge_own)
    edge_bc = swap(edge_bc)
    edge_at_a = pl.BlockSpec((HALO, 128), lambda j: (0, jnp.minimum(j, hp - 1)))
    edge_at_b = pl.BlockSpec((HALO, 128), lambda j: (0, jnp.maximum(j - hp, 0)))

    sum_shape = (2, dm // 2, ch)
    keep_v, send_v, tiny, acc = pl.pallas_call(
        functools.partial(back_kernel, length, pairs),
        grid=(pairs,),
        out_shape=[sds(sum_shape, BF16), sds(sum_shape, BF16), sds((2, 16, ch), F32), sds((length, dm), F32)],
        in_specs=[
            SMEM, columns(length), edge_at_a, edge_at_b, columns(ext), own_spec, own_spec, other_spec, other_spec,
            columns(length), whole((ext, dm), 1), columns(8), columns(8), columns(8),
        ],
        out_specs=[whole(sum_shape, 1), whole(sum_shape, 1), whole((2, 16, ch), 1), whole((length, dm), 1)],
        scratch_shapes=[pltpu.VMEM((ext, 128), F32), pltpu.VMEM((ext, 128), F32), pltpu.VMEM((ext, 128), jnp.int32)],
        compiler_params=params(True, 20),
        cost_estimate=cost(22),
        name="back",
    )(info, gmix, edge_a, edge_b, vm, wv, wg, wv_other, wg_other, ggate, normed, taps, ggain, gskip)

    got_v = flip(send_v, 1, wide)
    keep_bc, send_bc, tiny, grad_in = pl.pallas_call(
        functools.partial(last_kernel, length, hl),
        out_shape=[
            sds((2, dm // 2, 384), BF16), sds((2, dm // 2, 384), BF16), sds((2, 16, ch), F32), sds((length, dm), F32),
        ],
        in_specs=[SMEM] + [VMEM] * 15,
        out_specs=[VMEM] * 4,
        scratch_shapes=[pltpu.VMEM((ext, 128), F32), pltpu.VMEM((ext, 128), F32), pltpu.VMEM((ext, 128), jnp.int32)],
        compiler_params=params(False, 16),
        cost_estimate=cost(6),
        name="last",
    )(
        info, acc, normed, gmb, edge_bc, bcm, taps_bc, gv, wdt_all, wbc, x, g, rs, pre_gain.reshape(1, dm), small, tiny,
    )
    keep_bc, got_v, wa = lax.optimization_barrier((keep_bc, got_v, wa))

    cols = ch + 384
    wb, tiny = pl.pallas_call(
        collect_kernel,
        out_shape=[sds((share, cols), F32), sds((16, ch), F32)],
        in_specs=[VMEM] * 5,
        out_specs=[VMEM] * 2,
        scratch_shapes=[
            pltpu.VMEM((4, 2, 2 * share, 384), BF16),
            pltpu.VMEM((4, share, cols), F32),
            pltpu.VMEM((4, 3, share, cols), BF16),
            pltpu.VMEM((4, 3, share, cols), BF16),
            pltpu.VMEM((3, share, cols), BF16),
            pltpu.VMEM((3, share, cols), BF16),
            pltpu.VMEM((2, 16, ch), F32),
            pltpu.VMEM((2, 16, ch), F32),
            pltpu.VMEM((3, 16, ch), F32),
            pltpu.VMEM((16, ch), F32),
            pltpu.VMEM((3, 16, ch), F32),
            pltpu.SemaphoreType.DMA((5,)),
            pltpu.SemaphoreType.DMA((5,)),
            pltpu.SemaphoreType.DMA((5, 3)),
            pltpu.SemaphoreType.DMA((5, 3)),
            pltpu.SemaphoreType.DMA((2, 3)),
            pltpu.SemaphoreType.DMA((2, 3)),
        ],
        compiler_params=pltpu.CompilerParams(collective_id=0, has_side_effects=True, vmem_limit_bytes=16 * 2**20),
        name="collect",
    )(keep_v, got_v, keep_bc, send_bc, tiny)

    g_conv_x, g_conv_bc, g_pre, g_bias, g_rate, g_skip, g_gain = pl.pallas_call(
        functools.partial(finish_kernel, hl),
        out_shape=[
            sds((7, hl, HD // wide), F32), sds((7, 256 // wide), F32), sds((1, share), F32), sds((hl, 2), F32),
            sds((1, hl), F32), sds((1, hl), F32), sds((hl, HD // wide), F32),
        ],
        in_specs=[VMEM],
        out_specs=[VMEM] * 7,
        name="finish",
    )(tiny)

    gate_part = wa[:, dm:].reshape(share, hl, HD)
    vals_part = wb[:, :ch].reshape(share, hl, HD)
    bc_part = pack_columns(wb[:, ch : ch + 256])
    dt_cols = wb[:, ch + 256 :]
    dt_part = jnp.stack([dt_cols[:, 0:hl], dt_cols[:, 64 : 64 + hl]], axis=2)
    g_w_heads = jnp.concatenate([gate_part, vals_part, dt_part], axis=2)
    g_w_out = jnp.transpose(wa[:, :dm].reshape(share, hl, HD), (1, 2, 0))
    return (
        out[None],
        grad_in[None],
        g_pre[0],
        g_w_heads,
        bc_part,
        g_conv_x,
        g_conv_bc,
        g_bias,
        g_rate[0],
        g_skip[0],
        g_gain,
        g_w_out,
    )


def solution(mesh):
    body = shards
    if mesh.shape["narrow"] == 2 and mesh.shape["wide"] == 16:
        body = functools.partial(split_positions, mesh.shape["wide"])
    return jax.shard_map(
        body,
        mesh=mesh,
        in_specs=(
            P("wide", "narrow", None),
            P(),
            P(None, "narrow", None),
            P(),
            P(None, "narrow", None),
            P(),
            P("narrow", None),
            P("narrow"),
            P("narrow"),
            P("narrow", None),
            P("narrow", None, None),
            P("wide", "narrow", None),
            P("wide", None),
            P("wide", None),
        ),
        out_specs=(
            P("wide", "narrow", None),
            P("wide", "narrow", None),
            P("wide"),
            P("wide", "narrow", None),
            P("wide", None),
            P(None, "narrow", "wide"),
            P(None, "wide"),
            P("narrow", None),
            P("narrow"),
            P("narrow"),
            P("narrow", "wide"),
            P("narrow", None, "wide"),
        ),
        check_vma=False,
    )
```

```python
import functools

import jax
import jax.numpy as jnp
from jax import lax
from jax.experimental import pallas as pl
from jax.experimental.pallas import tpu as pltpu
from jax.sharding import PartitionSpec as P

H = 24
HD = 64
BLOCK = 128
SEQ_LEN = 1280


EPS = 1e-05
HIGH = lax.Precision.HIGHEST


def rounded(value):
    return value + lax.stop_gradient(value.astype(jnp.bfloat16).astype(jnp.float32) - value)


def segment_ids(starts):
    where_at = jnp.arange(SEQ_LEN, dtype=jnp.int32)
    hits = (starts[:, :, None] <= where_at[None, None, :]).astype(jnp.int32)
    return jnp.sum(hits, axis=1) - 1


def conv_doc(values, taps, seg):
    half = (taps.shape[0] - 1) // 2
    length = values.shape[1]
    padded = jnp.pad(values, ((0, 0), (half, half), (0, 0)))
    seg_pad = jnp.pad(seg, ((0, 0), (half, half)), constant_values=-1)
    total = jnp.zeros_like(values)
    for offset in range(taps.shape[0]):
        same = (seg_pad[:, offset : offset + length] == seg).astype(values.dtype)
        total = total + taps[offset] * padded[:, offset : offset + length] * same[:, :, None]
    return total


def ssd_forward(xc, steps, decays, bmat, cmat, seg, prec):
    rows, length, heads, hdim = xc.shape
    blocks = length // BLOCK
    xb = xc.reshape(rows, blocks, BLOCK, heads, hdim)
    stepb = steps.reshape(rows, blocks, BLOCK, heads)
    cum = jnp.cumsum(decays.reshape(rows, blocks, BLOCK, heads), axis=2)
    bb = bmat.reshape(rows, blocks, BLOCK, -1)
    cb = cmat.reshape(rows, blocks, BLOCK, -1)
    sb = seg.reshape(rows, blocks, BLOCK)
    order = jnp.arange(BLOCK, dtype=jnp.int32)
    causal = order[:, None] >= order[None, :]
    same = ((sb[:, :, :, None] == sb[:, :, None, :]) & causal)[..., None]
    diff = cum[:, :, :, None, :] - cum[:, :, None, :, :]
    weights = jnp.where(same, jnp.exp(jnp.where(same, diff, 0.0)), 0.0)
    inner = jnp.einsum("rbtn,rbsn->rbts", cb, bb, precision=prec)
    mix = weights * inner[..., None] * stepb[:, :, None, :, :]
    intra = jnp.einsum("rbtsh,rbshp->rbthp", mix, xb, precision=prec)
    last = sb[:, :, -1]
    cum_end = cum[:, :, -1, :]
    to_end = (
        (sb == last[:, :, None]).astype(cum.dtype)[..., None]
        * jnp.exp(cum_end[:, :, None, :] - cum)
        * stepb
    )
    states = jnp.einsum("rbshp,rbsn->rbhpn", to_end[..., None] * xb, bb, precision=prec)
    decay_end = jnp.exp(cum_end)

    def carry_step(carry, item):
        state, seg_prev = carry
        block_state, block_last, block_decay = item
        keep = (block_last == seg_prev).astype(state.dtype)[:, None, None, None]
        fresh = keep * block_decay[:, :, None, None] * state + block_state
        return ((fresh, block_last), (state, seg_prev))

    init = (
        jnp.zeros((rows, heads, hdim, bb.shape[-1]), xc.dtype),
        jnp.full((rows,), -1, jnp.int32),
    )
    items = (jnp.moveaxis(states, 1, 0), jnp.moveaxis(last, 1, 0), jnp.moveaxis(decay_end, 1, 0))
    _, (before, seg_before) = lax.scan(carry_step, init, items)
    before = jnp.moveaxis(before, 0, 1)
    seg_before = jnp.moveaxis(seg_before, 0, 1)
    enter = (sb == seg_before[:, :, None]).astype(cum.dtype)[..., None] * jnp.exp(cum)
    inter = jnp.einsum("rbtn,rbhpn->rbthp", cb, before, precision=prec) * enter[..., None]
    return (intra + inter).reshape(rows, length, heads, hdim)


def mixer(proj, bcproj, conv_x, conv_bc, dt_bias, a_log, skip_d, seg, mask, rounder, prec):
    rows, length, heads, width = proj.shape
    hdim = (width - 2) // 2
    state = bcproj.shape[-1] // 4
    gate = proj[..., :hdim]
    values = proj[..., hdim : 2 * hdim] * mask[:, :, None, None]
    mixed_x = conv_doc(
        values.reshape(rows, length, heads * hdim),
        conv_x.reshape(conv_x.shape[0], heads * hdim),
        seg,
    )
    xc = rounder(jax.nn.silu(mixed_x)).reshape(rows, length, heads, hdim)
    maps = rounder(jax.nn.silu(conv_doc(bcproj * mask[:, :, None], conv_bc, seg)))
    b_fwd = maps[..., :state]
    c_fwd = maps[..., state : 2 * state]
    b_bwd = maps[..., 2 * state : 3 * state]
    c_bwd = maps[..., 3 * state :]
    rate = -jnp.exp(a_log)
    dt_fwd = jax.nn.softplus(proj[..., 2 * hdim] + dt_bias[:, 0]) * mask[:, :, None]
    dt_bwd = jax.nn.softplus(proj[..., 2 * hdim + 1] + dt_bias[:, 1]) * mask[:, :, None]
    out_fwd = ssd_forward(xc, dt_fwd, dt_fwd * rate, b_fwd, c_fwd, seg, prec)

    def flip(v):
        return jnp.flip(v, axis=1)

    out_bwd = flip(
        ssd_forward(
            flip(xc), flip(dt_bwd), flip(dt_bwd * rate), flip(b_bwd), flip(c_bwd), flip(seg), prec
        )
    )
    keep_prev = (seg[:, 1:] == seg[:, :-1]).astype(xc.dtype)[:, :, None, None]
    shifted_fwd = jnp.pad(out_fwd[:, :-1] * keep_prev, ((0, 0), (1, 0), (0, 0), (0, 0)))
    shifted_bwd = jnp.pad(out_bwd[:, 1:] * keep_prev, ((0, 0), (0, 1), (0, 0), (0, 0)))
    return (shifted_fwd + shifted_bwd + skip_d[:, None] * xc, gate)


def shards(
    layer_in,
    pre_gain,
    w_heads,
    w_bc,
    conv_x,
    conv_bc,
    dt_bias,
    a_log,
    skip_d,
    norm_gain,
    w_out,
    cotangent,
    starts,
    live,
):
    seg = segment_ids(starts)
    mask = live.astype(jnp.float32)
    x_here = layer_in.astype(jnp.float32)
    scale = lax.rsqrt(jnp.mean(x_here * x_here, axis=-1, keepdims=True) + EPS)
    normed_here = (x_here * scale * pre_gain).astype(jnp.bfloat16)
    normed = lax.all_gather(normed_here, "narrow", axis=1, tiled=True)
    proj = jnp.einsum("rld,dhc->rlhc", normed, w_heads, preferred_element_type=jnp.float32)
    bcproj = jnp.einsum("rld,dc->rlc", normed, w_bc, preferred_element_type=jnp.float32)

    def mix_local(proj_in, bc_in, taps_x, taps_bc, bias_in, log_rate, diag_in):
        return mixer(
            proj_in, bc_in, taps_x, taps_bc, bias_in, log_rate, diag_in, seg, mask, rounded, HIGH
        )

    (ymix, gate), pull_mix = jax.vjp(
        mix_local, proj, bcproj, conv_x, conv_bc, dt_bias, a_log, skip_d
    )
    rows, length, heads, hdim = ymix.shape
    sigma = jax.nn.sigmoid(gate)
    act = gate * sigma
    gated = (ymix * act).reshape(rows, length, heads * hdim)
    squares = lax.psum(jnp.sum(gated * gated, axis=-1), "narrow")
    inv = lax.rsqrt(squares / (H * HD) + EPS)[..., None]
    gain_flat = norm_gain.reshape(-1)
    normalized = gated * inv
    hn = (normalized * gain_flat).astype(jnp.bfloat16)
    w_flat = w_out.reshape(heads * hdim, -1)
    partial_value = jnp.einsum("rlc,cd->rld", hn, w_flat, preferred_element_type=jnp.float32)
    branch = lax.psum_scatter(partial_value, "narrow", scatter_dimension=1, tiled=True)
    out = (x_here + branch).astype(jnp.bfloat16)
    grad_out = lax.all_gather(cotangent, "narrow", axis=1, tiled=True)
    g_w_out = jnp.einsum("rlc,rld->cd", hn, grad_out, preferred_element_type=jnp.float32)
    g_hn = jnp.einsum("rld,cd->rlc", grad_out, w_flat, preferred_element_type=jnp.float32)
    g_gain = jnp.sum(g_hn * normalized, axis=(0, 1))
    weighted = g_hn * gain_flat
    cross = lax.psum(jnp.sum(weighted * gated, axis=-1), "narrow")
    g_gated = inv * weighted - gated * (inv * inv * inv) * (cross / (H * HD))[..., None]
    g_gated = g_gated.reshape(rows, length, heads, hdim)
    g_ymix = g_gated * act
    g_gate = g_gated * ymix * (sigma * (1.0 + gate * (1.0 - sigma)))
    g_proj, g_bcproj, g_conv_x, g_conv_bc, g_dt_bias, g_a_log, g_skip = pull_mix((g_ymix, g_gate))
    g_proj_low = g_proj.astype(jnp.bfloat16)
    g_w_heads = jnp.einsum("rld,rlhc->dhc", normed, g_proj_low, preferred_element_type=jnp.float32)
    g_w_bc = jnp.einsum(
        "rld,rlc->dc", normed, g_bcproj, precision=HIGH, preferred_element_type=jnp.float32
    )
    g_normed = jnp.einsum("rlhc,dhc->rld", g_proj_low, w_heads, preferred_element_type=jnp.float32)
    g_normed = g_normed + jnp.einsum(
        "rlc,dc->rld", g_bcproj, w_bc, precision=HIGH, preferred_element_type=jnp.float32
    )
    g_normed_here = lax.psum_scatter(g_normed, "narrow", scatter_dimension=1, tiled=True)
    weighted_in = g_normed_here * pre_gain
    g_pre = jnp.sum(g_normed_here * x_here * scale, axis=(0, 1))
    g_x = scale * weighted_in - x_here * (scale * scale * scale) * jnp.mean(
        weighted_in * x_here, axis=-1, keepdims=True
    )
    grad_input = cotangent.astype(jnp.float32) + g_x
    g_pre, g_w_bc, g_conv_bc = lax.psum((g_pre, g_w_bc, g_conv_bc), "narrow")
    reduced = (
        lax.psum_scatter(g_w_heads, "wide", scatter_dimension=0, tiled=True),
        lax.psum_scatter(g_w_out.reshape(heads, hdim, -1), "wide", scatter_dimension=2, tiled=True),
        lax.psum_scatter(g_conv_x, "wide", scatter_dimension=2, tiled=True),
        lax.psum_scatter(g_gain.reshape(heads, hdim), "wide", scatter_dimension=1, tiled=True),
        lax.psum_scatter(g_pre, "wide", scatter_dimension=0, tiled=True),
        lax.psum_scatter(g_w_bc, "wide", scatter_dimension=0, tiled=True),
        lax.psum_scatter(g_conv_bc, "wide", scatter_dimension=1, tiled=True),
    )
    share_pre, share_bc, share_conv = (reduced[4], reduced[5], reduced[6])
    head_bias, head_rate, head_diag = lax.psum((g_dt_bias, g_a_log, g_skip), "wide")
    return (
        out,
        grad_input,
        share_pre,
        reduced[0],
        share_bc,
        reduced[2],
        share_conv,
        head_bias,
        head_rate,
        head_diag,
        reduced[3],
        reduced[1],
    )


HALO = 16
F32 = jnp.float32
BF16 = jnp.bfloat16
LOGZERO = -1e30


def mm(a, b, dims=((1,), (0,)), precision=None):
    return lax.dot_general(a, b, (dims, ((), ())), precision=precision, preferred_element_type=F32)


def nt(a, b):
    return mm(a, b, ((1,), (1,)))


def tn(a, b):
    return mm(a, b, ((0,), (0,)))


def seg_at(info, pos):
    seg = jnp.full(pos.shape, -1, jnp.int32)
    for j in range(4):
        seg = seg + (pos >= info[j]).astype(jnp.int32)
    return jnp.where(pos >= info[6], 99, seg)


def iota(shape, dim):
    return lax.broadcasted_iota(jnp.int32, shape, dim)


def silu_parts(v):
    sg = 0.5 * jnp.tanh(0.5 * v) + 0.5
    act = v * sg
    return act, sg + act * (1.0 - sg)


def thirds(v):
    hi = v.astype(BF16).astype(F32)
    rest = v - hi
    mid = rest.astype(BF16).astype(F32)
    return hi, mid, rest - mid


def column_terms(values):
    sub = iota((16, 128), 0)
    v = jnp.ones((16, 128), F32)
    for k, value in enumerate(values):
        v = jnp.where((sub >= 3 * k) & (sub < 3 * k + 3), value, v)
    hi, mid, low = thirds(v)
    part = sub % 3
    out = jnp.where(part == 0, hi, jnp.where(part == 1, mid, low))
    return jnp.where(sub < 3 * len(values), out, 1.0).astype(BF16)


def row_base(count, places):
    sub = iota((16, 384), 0)
    lane = iota((16, 384), 1)
    out = jnp.zeros((16, 384), F32)
    for k, spans in enumerate(places):
        for lo, hi in spans:
            out = jnp.where((sub >= 3 * k) & (sub < 3 * k + 3) & (lane >= lo) & (lane < hi), 1.0, out)
    return out


def row_terms(count, base, one, two):
    sub = iota((16, 128), 0)
    part = sub - 3 * count
    made = []
    for k, value in enumerate((one, two)):
        hi, mid, low = thirds(jnp.broadcast_to(value, (16, 128)))
        here = base[:, 128 * k : 128 * (k + 1)]
        made.append(
            jnp.where(part == 0, hi, jnp.where(part == 1, mid, jnp.where(part == 2, low, here))).astype(BF16)
        )
    return jnp.concatenate(made + [base[:, 256:].astype(BF16)], axis=1)


def conv_taps(src, seg_src, taps, first, rows):
    seg0 = seg_src[first : first + rows, :]
    total = src[first : first + rows, :] * taps[3:4, :]
    for k in (0, 1, 2, 4, 5, 6):
        lo = first + k - 3
        same = seg_src[lo : lo + rows, :] == seg0
        total = total + jnp.where(same, src[lo : lo + rows, :], 0.0) * taps[k : k + 1, :]
    return total


def front_kernel(
    length, hl, starts, live_ref, x_in, gain, wbc_ref, taps_ref, small_a, small_b,
    info, taps_o, gain_o, skip_o, wdt, wbc, taps, normed_o, rs_o, bcm_o, dsl_o, maps_o, ta_o, tb_o, tc_o, dpt_o, sig_o, seg_s, maps_s, cum_s, x_s,
):
    nb = length // BLOCK
    ext = length + 2 * HALO
    dm = x_in.shape[1]
    n = lax.axis_index("narrow")
    for i in range(4):
        info[i] = starts[0, i]
    count = jnp.sum(live_ref[...].astype(F32)).astype(jnp.int32)
    off = n * length
    info[4] = count
    info[5] = off
    info[6] = live_ref.shape[1]
    info[7] = n
    ch = small_a.shape[1]
    for k, small in enumerate((small_a, small_b)):
        cols = slice(k * ch, (k + 1) * ch)
        taps_o[:, cols] = small[0:8, :]
        gain_o[:, cols] = jnp.broadcast_to(small[7:8, :], (8, ch))
        skip_o[:, cols] = jnp.broadcast_to(small[8:9, :], (8, ch))
    dst = iota((128, 2 * hl), 0)
    src = iota((128, 2 * hl), 1)
    place = (src % 2) * 64 + src // 2
    at_a = jnp.where(dst == place, 1.0, 0.0).astype(BF16)
    at_b = jnp.where(dst == place + hl, 1.0, 0.0).astype(BF16)
    own_steps = small_a[16 : 16 + 2 * hl, :].astype(BF16)
    far_steps = small_b[16 : 16 + 2 * hl, :].astype(BF16)
    wdt[...] = (mm(at_a, own_steps) + mm(at_b, far_steps)).astype(BF16)
    wbc[...] = pack_columns(wbc_ref[...])
    taps[...] = pack_columns(taps_ref[...])

    bias = small_a[9:10, 0:128] + pltpu.roll(small_b[9:10, 0:128], hl, 1)
    alog = small_a[9:10, 128:256] + pltpu.roll(small_b[9:10, 128:256], hl, 1)
    edge = small_b[16 + 2 * hl : 24 + 2 * hl, :]
    zero_edge = jnp.zeros((8, dm), F32)
    before = jnp.concatenate([zero_edge, jnp.where(n == 1, edge, 0.0)], axis=0)
    behind = jnp.concatenate([jnp.where(n == 1, 0.0, edge), zero_edge], axis=0)
    x_s[0:HALO, :] = before.astype(BF16)
    x_s[HALO : HALO + length, :] = x_in[...]
    x_s[HALO + length : ext, :] = behind.astype(BF16)
    x = x_s[...].astype(F32)
    rs = lax.rsqrt(jnp.mean(x * x, axis=1, keepdims=True) + EPS)
    normed = (x * rs * gain[...]).astype(BF16)
    normed_o[...] = normed
    rs_o[...] = rs[HALO : HALO + length, :]
    pos256 = iota((ext, 256), 0) + (off - HALO)
    seg_s[...] = seg_at(info, pos256)
    live = pos256 < count
    bcm_o[...] = jnp.where(live, mm(normed, wbc[...]), 0.0)
    crows = length + HALO
    cfirst = HALO // 2
    mix = conv_taps(bcm_o, seg_s, taps, cfirst, crows)
    maps, dsl = silu_parts(mix)
    dsl_o[...] = jnp.zeros_like(dsl_o)
    dsl_o[cfirst : cfirst + crows, :] = dsl
    maps_s[...] = jnp.zeros_like(maps_s)
    maps_s[cfirst : cfirst + crows, :] = maps.astype(BF16).astype(F32)
    own = slice(HALO, HALO + length)
    segx = seg_s[own, 0:128]
    lane = iota((length, 128), 1)
    fwd = lane < 64
    segp = seg_s[HALO - 1 : HALO - 1 + length, 0:128]
    segn = seg_s[HALO + 1 : HALO + 1 + length, 0:128]
    bmap = maps_s[own, 0:128]
    cprev = jnp.where(segp == segx, maps_s[HALO - 1 : HALO - 1 + length, 128:256], 0.0)
    cnext = jnp.where(segn == segx, maps_s[HALO + 1 : HALO + 1 + length, 128:256], 0.0)
    cmap = jnp.where(fwd, cprev, cnext)
    maps_o[:, 0:128] = bmap.astype(BF16)
    maps_o[:, 128:256] = cmap.astype(BF16)
    raw = nt(normed[own, :], wdt[...]) + bias
    softp = jnp.maximum(raw, 0.0) + jnp.log(1.0 + jnp.exp(-jnp.abs(raw)))
    softp = jnp.where(raw < -15.0, jnp.exp(jnp.minimum(raw, 0.0)), softp)
    pos128 = iota((length, 128), 0) + off
    m = pos128 < count
    dt = jnp.where(m, softp, 0.0)
    sg = jnp.where(m, 1.0 / (1.0 + jnp.exp(-raw)), 0.0)
    ratio = jnp.where(m, jnp.where(raw < -15.0, 1.0, sg / jnp.maximum(softp, 1e-30)), 0.0)
    rate = -jnp.exp(alog)
    a = dt * rate
    sig_o[:, 256:384] = a
    sig_o[:, 0:128] = sg * rate
    sig_o[:, 128:256] = ratio
    tri = (iota((BLOCK, BLOCK), 0) >= iota((BLOCK, BLOCK), 1)).astype(F32)
    logdt = jnp.maximum(jnp.log(dt), LOGZERO)
    sub = iota((BLOCK, BLOCK), 0)
    ln = iota((BLOCK, BLOCK), 1)
    fwdb = ln < 64
    cum_s[...] = jnp.zeros_like(cum_s)
    dvals, ends = [], []
    for b in range(nb):
        blk = slice(b * BLOCK, (b + 1) * BLOCK)
        ab = a[blk, :]
        cum = mm(tri, ab, precision=HIGH)
        cx = cum - ab
        end = cum[BLOCK - 1 : BLOCK, :]
        colt = jnp.where(fwdb, cx, end - cum)
        rows = jnp.where(fwdb, logdt[blk, :] - cum, cx + logdt[blk, :] - end)
        tb_o[0, b] = colt.T
        tb_o[1, b] = rows.T
        ta_o[0, b] = jnp.minimum(rows + end, 60.0).T
        first_pos = off + b * BLOCK
        sp = seg_at(info, sub + first_pos)
        st = seg_at(info, ln + first_pos)
        before = seg_at(info, sub * 0 + (first_pos - 1))
        begin = seg_at(info, sub * 0 + first_pos)
        last = seg_at(info, sub * 0 + (first_pos + BLOCK - 1))
        after = seg_at(info, sub * 0 + (first_pos + BLOCK))
        enter = jnp.where(fwdb, (sp == before).astype(F32), (sp == after).astype(F32))
        keep = jnp.where(fwdb, (sp == last).astype(F32), (sp == begin).astype(F32))
        ce = cmap[blk, :] * enter
        bk = bmap[blk, :] * keep
        tb_o[3, b] = ce
        tc_o[1, b] = bk
        tc_o[2, b] = ce.T
        ta_o[1, b] = bk.T
        chain = jnp.where(fwdb[0:1, :], (last == before).astype(F32)[0:1, :], (begin == after).astype(F32)[0:1, :])
        dvals.append(jnp.exp(end) * chain)
        ends.append(end)
        cb = cmap[blk, :].astype(BF16)
        bb = bmap[blk, :].astype(BF16)
        zero = jnp.zeros_like(bb)
        same = sp == st
        low = same & (sub > ln)
        high = same & (sub < ln)
        bf = jnp.where(fwdb, bb, zero)
        br = jnp.where(fwdb, zero, bb)
        tb_o[2, b] = jnp.where(low, nt(cb, bf), jnp.where(high, nt(cb, br), 0.0))
        tc_o[0, b] = jnp.where(high, nt(bf, cb), jnp.where(low, nt(br, cb), 0.0))
    ones = jnp.ones((1, 128), F32)
    prefix, suffix = [ones], [ones]
    for b in range(nb):
        prefix.append(prefix[-1] * dvals[b])
        suffix.append(suffix[-1] * dvals[nb - 1 - b])
    suffix = suffix[::-1]
    f1 = fwdb[0:1, :]
    for b in range(nb):
        cum_s[b : b + 1, :] = dvals[b]
        cum_s[48 + b : 49 + b, :] = ends[b]
    for i in range(nb + 1):
        cum_s[16 + i : 17 + i, :] = jnp.where(f1, prefix[i], suffix[i])
        cum_s[32 + i : 33 + i, :] = jnp.where(f1, suffix[i], prefix[i])
    dpt_o[...] = cum_s[...].T


def pair_rows(dpt, j, base, i, half):
    lane = iota((1, 128), 1)
    one = dpt[pl.ds(half * 64 + 2 * j, 1), :][:, base + i : base + i + 1]
    two = dpt[pl.ds(half * 64 + 2 * j + 1, 1), :][:, base + i : base + i + 1]
    return jnp.where(lane < 64, one, two)


def assemble(dst, pieces):
    quarter = dst.shape[0] // 4
    q = lax.axis_index("wide") % 4
    cbit = q % 2
    xbit = q // 2
    places = (q, (1 - xbit) * 2 + cbit, xbit * 2 + 1 - cbit, (1 - xbit) * 2 + 1 - cbit)
    for place, piece in zip(places, pieces):
        dst[pl.ds(pl.multiple_of(place * quarter, quarter), quarter), :] = piece[...]


def vals_kernel(length, other, info, normed, *refs):
    nb = length // BLOCK
    ext = length + 2 * HALO
    step = pl.program_id(0)
    first = step
    if other:
        p0, p1, p2, p3, taps, ta, dpt = refs[:7]
        xc_o, vm_o, ds_o, s_o, bnd_o, wvo_o, vm_a, vm_b, seg_s = refs[11:]
        first = step + pl.num_programs(0)

        @pl.when(step == 0)
        def _():
            assemble(wvo_o, (p0, p1, p2, p3))

        wv = wvo_o[pl.ds(pl.multiple_of(step * 256, 256), 256), :]
    else:
        w_ref, taps, ta, dpt, xc_o, vm_o, ds_o, s_o, bnd_o, vm_a, vm_b, seg_s = refs
        wv = jnp.concatenate([w_ref[h, HD : 2 * HD, :] for h in range(4)], axis=0)
    off, count = info[5], info[4]

    @pl.when(step == 0)
    def _():
        seg_s[...] = seg_at(info, iota((ext, 128), 0) + (off - HALO))

    live = iota((ext, 128), 0) + (off - HALO) < count
    both = nt(normed[...], wv)
    lane = iota((BLOCK, 128), 1)
    top = iota((BLOCK, 128), 0) < 64
    for p, vm_s in enumerate((vm_a, vm_b)):
        j = 2 * first + p
        here = slice(128 * p, 128 * (p + 1))
        vm = jnp.where(live, both[:, here], 0.0)
        vm_s[...] = vm
        vm_o[:, here] = vm.astype(BF16)
        act, ds = silu_parts(conv_taps(vm_s, seg_s, taps[:, here], HALO, length))
        xc = act.astype(BF16)
        xc_o[:, here] = xc
        ds_o[:, here] = ds.astype(BF16)
        loc = []
        for b in range(nb):
            blk = slice(b * BLOCK, (b + 1) * BLOCK)
            got = []
            for i in range(2):
                h = 2 * j + i
                w = jnp.where(top, jnp.exp(ta[0, b, pl.ds(h, 1), :]), jnp.exp(ta[0, b, pl.ds(64 + h, 1), :]))
                got.append((ta[1, b] * w).astype(BF16))
            got = mm(jnp.concatenate(got, axis=0), xc[blk, :])
            loc.append(jnp.where(lane < 64, got[0:BLOCK, :], got[BLOCK:, :]))
        state = jnp.zeros((64, 128), F32)
        s_o[p, 0, 0:64, :] = state.astype(BF16)
        for b in range(nb):
            state = pair_rows(dpt, j, 0, b, 0) * state + loc[b][0:64, :]
            s_o[p, b + 1, 0:64, :] = state.astype(BF16)
        end_f = state
        state = jnp.zeros((64, 128), F32)
        s_o[p, nb, 64:128, :] = state.astype(BF16)
        for b in range(nb - 1, -1, -1):
            state = pair_rows(dpt, j, 0, b, 1) * state + loc[b][64:128, :]
            s_o[p, b, 64:128, :] = state.astype(BF16)
        bnd_o[p] = jnp.where(info[7] == 0, end_f, state).astype(BF16)


def scan_kernel(length, first_pair, info, xc_ref, s_ref, s0_ref, dpt, tb, skip, *refs):
    nb = length // BLOCK
    y_o, st_o = refs[-2:]
    j = pl.program_id(0) + first_pair
    right = (info[7] == 1).astype(F32)
    s0 = s0_ref[0].astype(F32)
    lane = iota((BLOCK, 128), 1)
    first = lane < 64
    low = iota((BLOCK, BLOCK), 0) > lane
    base = row_base(2, [[(0, 128), (256, 320)], [(128, 256), (320, 384)]])
    for i in range(nb + 1):
        f = s_ref[0, i, 0:64, :].astype(F32) + pair_rows(dpt, j, 16, i, 0) * (s0 * right)
        r = s_ref[0, i, 64:128, :].astype(F32) + pair_rows(dpt, j, 16, i, 1) * (s0 * (1.0 - right))
        st_o[0, i, 0:64, :] = f.astype(BF16)
        st_o[0, i, 64:128, :] = r.astype(BF16)
    for b in range(nb):
        blk = slice(b * BLOCK, (b + 1) * BLOCK)
        xb = xc_ref[blk, :]
        rhs = jnp.concatenate([xb, st_o[0, b, 0:64, :], st_o[0, b + 1, 64:128, :]], axis=0)
        got = []
        for i in range(2):
            h = 2 * j + i
            terms = column_terms([tb[0, b, pl.ds(h, 1), :], tb[0, b, pl.ds(64 + h, 1), :]])
            expo = tn(terms, row_terms(2, base, tb[1, b, pl.ds(h, 1), :], tb[1, b, pl.ds(64 + h, 1), :]))
            diff = jnp.where(low, expo[:, 0:128], expo[:, 128:256])
            mix = jnp.exp(jnp.minimum(diff, 60.0)) * tb[2, b]
            ct = tb[3, b] * jnp.exp(expo[:, 256:])
            lhs = jnp.concatenate([mix.astype(BF16), ct.astype(BF16)], axis=1)
            got.append(lhs)
        got = mm(jnp.concatenate(got, axis=0), rhs)
        y = jnp.where(first, got[0:BLOCK, :], got[BLOCK:, :]) + skip[0:1, :] * xb.astype(F32)
        y_o[blk, :] = y.astype(BF16)


def by_core(v, keep, send):
    share = v.shape[0] // 16
    cbit = lax.axis_index("wide") % 2
    v = v.astype(BF16).reshape(8, 2, share, v.shape[1])
    keep[...] = jnp.where(cbit == 0, v[:, 0], v[:, 1]).reshape(8 * share, v.shape[3])
    send[...] = jnp.where(cbit == 0, v[:, 1], v[:, 0]).reshape(8 * share, v.shape[3])


def gate_kernel(
    tiles, x_ref, g_ref, normed, y_ref, wout_a, w_ref, p0, p1, p2, p3, gain,
    out_o, gy_o, keep_o, send_o, ggate_o, ggain_o, wgo_o, hn_s, other_s, gated_s, act_s, dact_s, ghn_s,
):
    dm = x_ref.shape[1]
    chans = y_ref.shape[1]
    half = chans // 2
    step = 256
    assemble(other_s, (p0, p1, p2, p3))
    wgo_o[...] = other_s[:, dm:]
    ggain_o[...] = jnp.zeros_like(ggain_o)

    @pl.loop(0, tiles)
    def _(i):
        start = pl.multiple_of(i * BLOCK, BLOCK)
        rows = pl.ds(start, BLOCK)
        nrows = normed[pl.ds(pl.multiple_of(start + HALO, HALO), BLOCK), :]
        squares = jnp.zeros((BLOCK, 128), F32)
        for lo in range(0, chans, step):
            if lo < half:
                heads = range(lo // HD, (lo + step) // HD)
                wg = jnp.concatenate([w_ref[h, 0:HD, :] for h in heads], axis=0)
            else:
                wg = other_s[lo - half : lo - half + step, dm:]
            gates = nt(nrows, wg)
            for at in range(0, step, 128):
                cols = slice(lo + at, lo + at + 128)
                act, dact = silu_parts(gates[:, at : at + 128])
                gated = y_ref[rows, cols].astype(F32) * act
                squares = squares + gated * gated
                gated_s[:, cols] = gated
                act_s[:, cols] = act
                dact_s[:, cols] = dact
        inv = lax.rsqrt(jnp.sum(squares, axis=1, keepdims=True) * (1.0 / chans) + EPS)
        inv = jnp.broadcast_to(inv, (BLOCK, 128))
        g = g_ref[rows, :]
        across = jnp.zeros((BLOCK, 128), F32)
        for lo in range(0, chans, step):
            wo = wout_a[lo : lo + step, :] if lo < half else other_s[lo - half : lo - half + step, 0:dm]
            ghns = nt(g, wo)
            for at in range(0, step, 128):
                cols = slice(lo + at, lo + at + 128)
                gainv = gain[0:1, cols]
                gated = gated_s[:, cols]
                nrm = gated * inv
                hn_s[rows, cols] = (nrm * gainv).astype(BF16)
                ghn = ghns[:, at : at + 128]
                ggain_o[0:1, cols] += jnp.sum(ghn * nrm, axis=0, keepdims=True)
                wgt = ghn * gainv
                ghn_s[:, cols] = wgt
                across = across + wgt * gated
        cross = jnp.sum(across, axis=1, keepdims=True) * (1.0 / chans)
        cross = jnp.broadcast_to(cross, (BLOCK, 128)) * (inv * inv * inv)
        hn = hn_s[rows, :]
        branch = mm(hn[:, 0:half], wout_a[...]) + mm(hn[:, half:], other_s[:, 0:dm])
        out_o[rows, :] = (x_ref[rows, :].astype(F32) + branch).astype(BF16)
        for lo in range(0, chans, 128):
            cols = slice(lo, lo + 128)
            ggated = inv * ghn_s[:, cols] - gated_s[:, cols] * cross
            gy_o[rows, cols] = (ggated * act_s[:, cols]).astype(BF16)
            ggate_o[rows, cols] = (ggated * y_ref[rows, cols].astype(F32) * dact_s[:, cols]).astype(BF16)

    length = g_ref.shape[0]
    gt = g_ref[...].T
    nt_ = normed[HALO : HALO + length, :].T
    for k in range(2):
        for p in range(half // 256):
            cols = slice(k * half + p * 256, k * half + (p + 1) * 256)
            dst = slice(p * 256, (p + 1) * 256)
            dst2 = slice(half + p * 256, half + (p + 1) * 256)
            by_core(mm(gt, hn_s[:, cols]), keep_o.at[k, :, dst], send_o.at[k, :, dst])
            by_core(mm(nt_, ggate_o[:, cols]), keep_o.at[k, :, dst2], send_o.at[k, :, dst2])


def gstate_kernel(length, first_pair, info, gy_ref, coltt, cet, dpt, *refs):
    nb = length // BLOCK
    gs_o, bnd_o = refs[-2:]
    j = pl.program_id(0) + first_pair
    lane = iota((BLOCK, 128), 1)
    top = iota((BLOCK, 128), 0) < 64
    loc = []
    for b in range(nb):
        blk = slice(b * BLOCK, (b + 1) * BLOCK)
        gy = gy_ref[blk, :]
        got = []
        for i in range(2):
            h = 2 * j + i
            e = jnp.where(top, jnp.exp(coltt[b, pl.ds(h, 1), :]), jnp.exp(coltt[b, pl.ds(64 + h, 1), :]))
            got.append((cet[b] * e).astype(BF16))
        got = mm(jnp.concatenate(got, axis=0), gy)
        loc.append(jnp.where(lane < 64, got[0:BLOCK, :], got[BLOCK:, :]))
    state = jnp.zeros((64, 128), F32)
    gs_o[0, nb, 0:64, :] = state.astype(BF16)
    for b in range(nb - 1, -1, -1):
        state = pair_rows(dpt, j, 0, b, 0) * state + loc[b][0:64, :]
        gs_o[0, b, 0:64, :] = state.astype(BF16)
    end_f = state
    state = jnp.zeros((64, 128), F32)
    gs_o[0, 0, 64:128, :] = state.astype(BF16)
    for b in range(nb):
        state = pair_rows(dpt, j, 0, b, 1) * state + loc[b][64:128, :]
        gs_o[0, b + 1, 64:128, :] = state.astype(BF16)
    bnd_o[0] = jnp.where(info[7] == 1, end_f, state).astype(BF16)


def gscan_kernel(
    length, first_pair, info, xc_ref, ds_ref, gy_ref, st_ref, gs_ref, gs0_ref, dpt, rowst, wt, coltt, tc, skip,
    *refs,
):
    nb = length // BLOCK
    gmix_o, ggt_o, gb_o, gct_o, k_o, r_o, phi_o, gskip_o, edge_o, gst_s = refs[-10:]
    step = pl.program_id(0)
    j = step + first_pair
    right = (info[7] == 1).astype(F32)
    s0 = gs0_ref[0].astype(F32)
    sub = iota((BLOCK, BLOCK), 0)
    lane = iota((BLOCK, 128), 1)
    first = lane < 64
    later = lane > sub
    top = sub < 64

    @pl.when(step == 0)
    def _():
        for k, acc in enumerate((ggt_o, gb_o, gct_o, k_o, r_o)):
            acc[...] = jnp.zeros_like(acc) if first_pair else refs[3 + k][...]

    base = row_base(4, [[(0, 128)], [(128, 256)], [(256, 320)], [(320, 384)]])

    phi_o[...] = jnp.zeros_like(phi_o)
    for i in range(nb + 1):
        f = gs_ref[0, i, 0:64, :].astype(F32) + pair_rows(dpt, j, 32, i, 0) * (s0 * (1.0 - right))
        r = gs_ref[0, i, 64:128, :].astype(F32) + pair_rows(dpt, j, 32, i, 1) * (s0 * right)
        f = f.astype(BF16)
        r = r.astype(BF16)
        gst_s[i, 0:64, :] = f
        gst_s[i, 64:128, :] = r
        if i > 0:
            phi_o[i - 1 : i, :] = jnp.sum(f.astype(F32) * st_ref[0, i, 0:64, :].astype(F32), axis=0, keepdims=True)
        if i < nb:
            phi_o[8 + i : 9 + i, :] = jnp.sum(
                r.astype(F32) * st_ref[0, i, 64:128, :].astype(F32), axis=0, keepdims=True
            )
    gskip = jnp.zeros((1, 128), F32)
    for b in range(nb):
        blk = slice(b * BLOCK, (b + 1) * BLOCK)
        xb = xc_ref[blk, :]
        gy = gy_ref[blk, :]
        gyf = gy.astype(F32)
        gskip = gskip + jnp.sum(gyf * xb.astype(F32), axis=0, keepdims=True)
        rhs = jnp.concatenate([gy, gst_s[b + 1, 0:64, :], gst_s[b, 64:128, :]], axis=0)
        left = jnp.concatenate([xb, st_ref[0, b, 0:64, :], st_ref[0, b + 1, 64:128, :]], axis=0)
        first2 = iota((2 * BLOCK, 128), 1) < 64
        none = jnp.zeros_like(left)
        big2 = nt(jnp.concatenate([jnp.where(first2, left, none), jnp.where(first2, none, left)], axis=0), rhs)
        got = []
        sum_ge, sum_gct, sum_gb, kparts = [], [], [], []
        for i in range(2):
            h = 2 * j + i
            terms = column_terms([v[b, pl.ds(at + h, 1), :] for v in (rowst, wt) for at in (0, 64)])
            expo = tn(terms, row_terms(4, base, coltt[b, pl.ds(h, 1), :], coltt[b, pl.ds(64 + h, 1), :]))
            diff = jnp.where(later, expo[:, 0:128], expo[:, 128:256])
            et_m = jnp.exp(jnp.minimum(diff, 60.0))
            mt = et_m * tc[0, b]
            w = jnp.exp(expo[:, 256:])
            bt = tc[1, b] * w
            big = big2[2 * BLOCK * i : 2 * BLOCK * (i + 1), :]
            gmt = big[0:BLOCK, 0:BLOCK]
            gbt = big[0:BLOCK, BLOCK:]
            gctt = big[BLOCK:, 0:BLOCK]
            ge = gmt * et_m
            sum_ge.append(ge)
            q = gmt * mt
            qf = jnp.where(later, q, 0.0)
            e = jnp.where(top, jnp.exp(coltt[b, pl.ds(h, 1), :]), jnp.exp(coltt[b, pl.ds(64 + h, 1), :]))
            gce = gctt * e
            sum_gct.append(gce)
            ct = gce * tc[2, b]
            rf = jnp.sum(qf, axis=0, keepdims=True)
            rall = jnp.sum(q, axis=0, keepdims=True)
            r_o[b, pl.ds(h, 1), :] = rf + jnp.sum(ct[0:64, :], axis=0, keepdims=True)
            r_o[b, pl.ds(64 + h, 1), :] = rall - rf + jnp.sum(ct[64:128, :], axis=0, keepdims=True)
            gbw = gbt * w
            sum_gb.append(gbw)
            u = gbw * tc[1, b]
            kf = jnp.sum(qf + jnp.where(first, u, 0.0), axis=1, keepdims=True)
            kb = jnp.sum(q + u, axis=1, keepdims=True) - kf
            kparts += [kf, kb]
            lhs = jnp.concatenate([mt.astype(BF16), bt.astype(BF16)], axis=1)
            got.append(lhs)
        ggt_o[b] += sum_ge[0] + sum_ge[1]
        gct_o[b] += sum_gct[0] + sum_gct[1]
        gb_o[b] += sum_gb[0] + sum_gb[1]
        two = jnp.where(lane % 64 == 0, jnp.where(first, kparts[0], kparts[1]), jnp.where(first, kparts[2], kparts[3]))
        k_o[blk, :] += pltpu.roll(jnp.where(lane % 64 < 2, two, 0.0), 2 * j, 1)
        got = mm(jnp.concatenate(got, axis=0), rhs)
        gx = jnp.where(first, got[0:BLOCK, :], got[BLOCK:, :]) + skip[0:1, :] * gyf
        gmix = (gx * ds_ref[blk, :].astype(F32)).astype(BF16)
        gmix_o[blk, :] = gmix
        if b == 0:
            edge_o[...] = gmix[0:HALO, :]
        if b == nb - 1:
            edge_o[...] = jnp.where(info[7] == 0, gmix[BLOCK - HALO :, :], edge_o[...])
    gskip_o[...] = jnp.broadcast_to(gskip, (8, 128))


def join_kernel(
    length, heads, info, ggt, gb, gct, k_ref, r_ref, phi, maps, dsl, sig,
    gmb_o, gv_o, small_o, edge_o, gc_s, gm_s,
):
    nb = length // BLOCK
    off = info[5]
    chans = phi.shape[1]
    sub = iota((BLOCK, BLOCK), 0)
    lane = iota((BLOCK, 128), 1)
    first = lane < 64
    low = sub > lane
    high = sub < lane
    upper_strict = high.astype(F32)
    upper = (sub <= lane).astype(F32)
    lower_strict = low.astype(F32)
    lower = (sub >= lane).astype(F32)
    owner = iota((chans, 128), 0) // 64
    to_f = (owner == iota((chans, 128), 1)).astype(F32)
    to_b = (owner + 64 == iota((chans, 128), 1)).astype(F32)
    phi_f = mm(phi[0:8, :], to_f, precision=HIGH)
    phi_b = mm(phi[8:16, :], to_b, precision=HIGH)
    gc_s[...] = jnp.zeros_like(gc_s)
    gm_s[...] = jnp.zeros_like(gm_s)
    sum_bias = jnp.zeros((1, 128), F32)
    sum_rate = jnp.zeros((1, 128), F32)
    for b in range(nb):
        blk = slice(b * BLOCK, (b + 1) * BLOCK)
        ext = slice(HALO + b * BLOCK, HALO + (b + 1) * BLOCK)
        first_pos = off + b * BLOCK
        sp = seg_at(info, sub + first_pos)
        st = seg_at(info, lane + first_pos)
        before = seg_at(info, sub * 0 + (first_pos - 1))
        begin = seg_at(info, sub * 0 + first_pos)
        last = seg_at(info, sub * 0 + (first_pos + BLOCK - 1))
        after = seg_at(info, sub * 0 + (first_pos + BLOCK))
        enter = jnp.where(first, (sp == before).astype(F32), (sp == after).astype(F32))
        keep = jnp.where(first, (sp == last).astype(F32), (sp == begin).astype(F32))
        same = sp == st
        gg = ggt[b]
        gf = jnp.where(same & high, gg, 0.0).astype(BF16)
        gr = jnp.where(same & low, gg, 0.0).astype(BF16)
        cm = maps[blk, 128:256]
        bm = maps[blk, 0:128]
        gm_s[ext, 0:128] = jnp.where(first, mm(gf, cm), mm(gr, cm)) + gb[b] * keep
        gc_s[ext, :] = jnp.where(first, tn(gf, bm), tn(gr, bm)) + gct[b].T * enter
        kb = k_ref[blk, :]
        rb = r_ref[b].T
        ga_f = mm(upper_strict, rb, precision=HIGH) - mm(upper, kb, precision=HIGH) + phi_f[b : b + 1, :]
        ga_b = mm(lower_strict, rb, precision=HIGH) - mm(lower, kb, precision=HIGH) + phi_b[b : b + 1, :]
        ga = jnp.where(first, ga_f, ga_b)
        gv = kb * sig[blk, 128:256] + ga * sig[blk, 0:128]
        gv_o[blk, :] = gv.astype(BF16)
        sum_bias = sum_bias + jnp.sum(gv, axis=0, keepdims=True)
        sum_rate = sum_rate + jnp.sum(ga * sig[blk, 256:384], axis=0, keepdims=True)
    small_o[...] = jnp.zeros_like(small_o)
    small_o[0:1, :] = sum_bias
    small_o[1:2, :] = sum_rate
    small_o[8:9, :] = pltpu.roll(sum_bias, 128 - heads // 2, 1)
    small_o[9:10, :] = pltpu.roll(sum_rate, 128 - heads // 2, 1)
    mid = length + HALO
    lo = HALO // 2
    pos = iota((mid, 128), 0) + (off - HALO + lo)
    seg0 = seg_at(info, pos)
    segn = seg_at(info, pos + 1)
    segp = seg_at(info, pos - 1)
    from_next = jnp.where(seg0 == segn, gc_s[lo + 1 : lo + 1 + mid, :], 0.0)
    from_prev = jnp.where(seg0 == segp, gc_s[lo - 1 : lo - 1 + mid, :], 0.0)
    gm_s[lo : lo + mid, 128:256] = jnp.where(iota((mid, 128), 1) < 64, from_next, from_prev)
    gmb_o[...] = gm_s[...] * dsl[...]
    lo = HALO // 2
    edge_o[...] = jnp.where(
        info[7] == 0, gmb_o[length + lo : length + lo + HALO, :], gmb_o[lo : lo + HALO, :]
    )


def back_conv(length, seg_s, live, grad, data, tap):
    own = slice(HALO, HALO + length)
    seg0 = seg_s[own, :]
    mine = grad[own, :]
    total = mine * tap[3:4, :]
    gtap = [None] * 7
    gtap[3] = jnp.sum(mine * data[own, :], axis=0, keepdims=True)
    for k in (0, 1, 2, 4, 5, 6):
        lo = HALO + 3 - k
        same = seg_s[lo : lo + length, :] == seg0
        total = total + jnp.where(same, grad[lo : lo + length, :], 0.0) * tap[k : k + 1, :]
        up = HALO + k - 3
        same = seg_s[up : up + length, :] == seg0
        gtap[k] = jnp.sum(jnp.where(same, data[up : up + length, :], 0.0) * mine, axis=0, keepdims=True)
    return jnp.where(live, total, 0.0), gtap


def back_kernel(
    length, steps, info, gmix, edge_a, edge_b, vm, normed, taps, ggain, gskip,
    gvals_o, keep_o, send_o, tiny_o, ext_s, vm_s, seg_s, turned_s,
):
    ext = length + 2 * HALO
    off, count = info[5], info[4]
    own = slice(HALO, HALO + length)
    seg_s[...] = seg_at(info, iota((ext, 128), 0) + (off - HALO))
    tiny_o[...] = jnp.zeros_like(tiny_o)
    turned_s[...] = normed[own, :].T
    live = iota((length, 128), 0) + off < count
    right = info[7] == 1
    per = steps // 2

    @pl.loop(0, steps)
    def _(j):
        near = j < per
        half = j // per
        at = (j % per) * 256
        both = []
        for p in range(2):
            here = pl.ds(pl.multiple_of(at + 128 * p, 128), 128)
            cols = pl.ds(pl.multiple_of(j * 256 + 128 * p, 128), 128)
            ext_s[own, :] = gmix[:, cols].astype(F32)
            halo = jnp.where(near, edge_a[:, here].astype(F32), edge_b[:, here].astype(F32))
            ext_s[0:HALO, :] = jnp.where(right, halo, 0.0)
            ext_s[HALO + length : ext, :] = jnp.where(right, 0.0, halo)
            vm_s[...] = vm[:, cols].astype(F32)
            gvals, gtap = back_conv(length, seg_s, live, ext_s, vm_s, taps[:, cols])
            both.append(gvals.astype(BF16))
            for t in range(7):
                tiny_o[half, t : t + 1, here] = gtap[t]
            tiny_o[half, 7:8, here] = ggain[0:1, cols]
            tiny_o[half, 8:9, here] = gskip[0:1, cols]
        both = jnp.concatenate(both, axis=1)
        gvals_o[:, pl.ds(pl.multiple_of(j * 256, 256), 256)] = both
        here = pl.ds(pl.multiple_of(at, 256), 256)
        by_core(mm(turned_s[...], both), keep_o.at[half, :, here], send_o.at[half, :, here])


def last_kernel(
    length, hl, info, gvals, ggate, w_ref, wv_b, wg_b, normed, gmb, edge, bcm, taps_bc, gv, wdt, wbc, x_ref, g_ref, rs, pre,
    small, tiny, keep_o, send_o, tiny_o, gin_o, ext_s, vm_s, seg_s,
):
    ext = length + 2 * HALO
    ch = hl * HD
    off, count = info[5], info[4]
    own = slice(HALO, HALO + length)
    seg_s[...] = seg_at(info, iota((ext, 128), 0) + (off - HALO))
    live = iota((length, 128), 0) + off < count
    tiny_o[...] = tiny[...]
    for half in range(2):
        tiny_o[half, 10:11, 0:128] = small[8 * half : 8 * half + 1, :]
        tiny_o[half, 10:11, 128:256] = small[8 * half + 1 : 8 * half + 2, :]
    both = []
    for k in range(2):
        cols = slice(k * 128, (k + 1) * 128)
        ext_s[...] = gmb[:, cols]
        lo = HALO // 2
        hi = length + lo
        got = edge[:, cols]
        ext_s[lo : lo + HALO, :] += jnp.where(info[7] == 1, got, 0.0)
        ext_s[hi : hi + HALO, :] += jnp.where(info[7] == 1, 0.0, got)
        vm_s[...] = bcm[:, cols]
        gbc, gtap = back_conv(length, seg_s, live, ext_s, vm_s, taps_bc[:, cols])
        for t in range(7):
            at = (t % 3) * 256 + k * 128
            for half in range(2):
                tiny_o[half, 11 + t // 3 : 12 + t // 3, at : at + 128] = gtap[t]
        both.append(gbc.astype(BF16))
    gbc = jnp.concatenate(both + [gv[...]], axis=1)
    gw = tn(normed[own, :], gbc)
    by_core(gw, keep_o.at[0], send_o.at[0])
    turned = pltpu.roll(gw[:, 256:], 128 - hl, 1)
    by_core(jnp.concatenate([gw[:, 0:256], turned], axis=1), keep_o.at[1], send_o.at[1])
    wv_a = jnp.concatenate([w_ref[h, HD : 2 * HD, :] for h in range(hl)], axis=0)
    wg_a = jnp.concatenate([w_ref[h, 0:HD, :] for h in range(hl)], axis=0)
    gn = mm(gvals[:, 0:ch], wv_a) + mm(gvals[:, ch:], wv_b[...])
    gn = gn + mm(ggate[:, 0:ch], wg_a) + mm(ggate[:, ch:], wg_b[...])
    gn = gn + nt(gbc[:, 0:256], wbc[...]) + mm(gv[...], wdt[...])
    x = x_ref[...].astype(F32)
    r = rs[...]
    wp = gn * pre[...]
    mean = jnp.mean(wp * x, axis=1, keepdims=True)
    gin_o[...] = g_ref[...].astype(F32) + r * wp - x * (r * r * r * mean)
    gpre = jnp.sum(gn * x * r, axis=0, keepdims=True)
    for half in range(2):
        tiny_o[half, 9:10, 0 : gpre.shape[1]] = gpre


def finish_kernel(hl, tiny, own_a, x_a, y_a, d_a, wb, heads_o, wout_o, bc_o, conv_o, convbc_o, pre_o, bias_o, rate_o, skip_o, gain_o):
    ch = tiny.shape[1]
    w = lax.axis_index("wide")
    share = pre_o.shape[1]
    lanes = gain_o.shape[0]
    dm = own_a.shape[1] - ch
    total = own_a[...].astype(F32) + x_a[...].astype(F32) + y_a[...].astype(F32) + d_a[...].astype(F32)
    for h in range(hl):
        cols = slice(h * HD, (h + 1) * HD)
        wout_o[h] = total[:, cols]
        heads_o[h, :, 0:HD] = total[:, dm + h * HD : dm + (h + 1) * HD]
        heads_o[h, :, HD : 2 * HD] = wb[:, cols]
        heads_o[h, :, 2 * HD : 2 * HD + 1] = wb[:, ch + 256 + h : ch + 257 + h]
        heads_o[h, :, 2 * HD + 1 :] = wb[:, ch + 320 + h : ch + 321 + h]
    bc_o[...] = pack_columns(wb[:, ch : ch + 256])
    rows = tiny[...]
    src = iota((ch, 128), 0)
    dst = iota((ch, 128), 1)
    for q in range(lanes):
        chosen = ((src == dst * HD + lanes * w + q) & (dst < hl)).astype(F32)
        got = mm(rows, chosen, precision=HIGH)
        for k in range(7):
            conv_o[k, q : q + 1, :] = got[k : k + 1, 0:hl]
        gain_o[q : q + 1, :] = got[7:8, 0:hl]
    chosen = ((src == share * w + dst) & (dst < share)).astype(F32)
    pre_o[...] = mm(rows[8:16, :], chosen, precision=HIGH)[1:2, 0:share]
    per = (src // HD == dst).astype(F32)
    skip_o[...] = mm(rows[8:16, :], per, precision=HIGH)[0:1, 0:hl]
    size = convbc_o.shape[1]
    group = (size * w) // 64
    start = ((group % 2) * 2 + group // 2) * 64 + (size * w) % 64
    src = iota((256, 128), 0)
    dst = iota((256, 128), 1)
    chosen = ((src == start + dst) & (dst < size)).astype(F32)
    for k in range(3):
        part = mm(rows[8:16, 256 * k : 256 * (k + 1)], chosen, precision=HIGH)
        for r in range(3):
            if 3 * r + k < 7:
                convbc_o[3 * r + k : 3 * r + k + 1, :] = part[3 + r : 4 + r, 0:size]
    both = rows[10:11, 0:128]
    bias_o[0:1, :] = both[:, 0:hl]
    bias_o[1:2, :] = pltpu.roll(both, 64, 1)[:, 0:hl]
    rate = rows[10:11, 128:256]
    rate_o[...] = (rate + pltpu.roll(rate, 64, 1))[:, 0:hl]


def collect_kernel(
    keep, got_v, keep_bc, send_bc, tiny, out_o, tiny_o,
    core_s, mine_s, piece_s, got_s, zsend_s, zgot_s, tcore_s, tsum_s, tgot_s, tz_s, tzgot_s,
    core_out, core_in, plane_out, plane_in, z_out, z_in,
):
    w = lax.axis_index("wide")
    n = lax.axis_index("narrow")
    c, xx, z = w % 2, (w // 2) % 2, w // 4
    share = out_o.shape[0]
    core = (w + 1 - 2 * c, n)
    over_x = (w + 2 - 4 * xx, n)
    over_y = (w, 1 - n)
    over_d = (w + 2 - 4 * xx, 1 - n)
    steps = (2, 1, 3)
    over_z = [(((z + d) % 4) * 4 + w % 4, n) for d in steps]
    mesh_ids = pl.DeviceIdType.MESH
    barrier = pltpu.get_barrier_semaphore()
    for other in [core, over_x, over_y, over_d] + over_z:
        pl.semaphore_signal(barrier, inc=1, device_id=other, device_id_type=mesh_ids)
    pl.semaphore_wait(barrier, 7)

    def copy(src, dst, out_sem, in_sem, other):
        got = pltpu.make_async_remote_copy(
            src_ref=src, dst_ref=dst, send_sem=out_sem, recv_sem=in_sem, device_id=other, device_id_type=mesh_ids
        )
        got.start()
        return got

    rows = [pl.ds(pl.multiple_of(((z + d) % 4) * (2 * share), 2 * share), 2 * share) for d in steps + (0,)]
    first = [copy(tiny, tcore_s, core_out.at[4], core_in.at[4], core)]
    for i in range(4):
        first.append(copy(send_bc.at[:, rows[i], :], core_s.at[i], core_out.at[i], core_in.at[i], core))
    ways = (over_x, over_y, over_d)
    first[0].wait()
    tsum_s[...] = tiny[...] + tcore_s[...]
    second = [[]]
    for k, other in enumerate(ways):
        half = 0 if k == 0 else 1
        second[0].append(copy(tsum_s.at[half], tgot_s.at[k], plane_out.at[4, k], plane_in.at[4, k], other))
    for i in range(4):
        first[i + 1].wait()
        chv = keep.shape[2]
        for cols, both in (
            (slice(0, chv), keep[:, rows[i], :].astype(F32) + got_v[:, rows[i], :].astype(F32)),
            (slice(chv, out_o.shape[1]), keep_bc[:, rows[i], :].astype(F32) + core_s[i].astype(F32)),
        ):
            low, high = both[:, 0:share, :], both[:, share:, :]
            near = jnp.where(xx == 0, low, high)
            far = jnp.where(xx == 0, high, low)
            mine_s[i, :, cols] = near[0]
            piece_s[i, 0, :, cols] = far[0].astype(BF16)
            piece_s[i, 1, :, cols] = near[1].astype(BF16)
            piece_s[i, 2, :, cols] = far[1].astype(BF16)
        second.append(
            [copy(piece_s.at[i, k], got_s.at[i, k], plane_out.at[i, k], plane_in.at[i, k], ways[k]) for k in range(3)]
        )
    for one in second[0]:
        one.wait()
    tsum = tsum_s[0] + tgot_s[0] + tgot_s[1] + tgot_s[2]
    tz_s[...] = tsum
    third = [copy(tz_s, tzgot_s.at[k], z_out.at[1, k], z_in.at[1, k], over_z[k]) for k in range(3)]
    total = None
    for i in range(4):
        for one in second[i + 1]:
            one.wait()
        total = mine_s[i] + got_s[i, 0].astype(F32) + got_s[i, 1].astype(F32) + got_s[i, 2].astype(F32)
        if i < 3:
            zsend_s[i] = total.astype(BF16)
            third.append(copy(zsend_s.at[i], zgot_s.at[i], z_out.at[0, i], z_in.at[0, i], over_z[i]))
    for one in third:
        one.wait()
    out_o[...] = total + zgot_s[0].astype(F32) + zgot_s[1].astype(F32) + zgot_s[2].astype(F32)
    tiny_o[...] = tsum + tzgot_s[0] + tzgot_s[1] + tzgot_s[2]


def whole(shape, grid):
    zeros = (0,) * len(shape)
    if grid:
        return pl.BlockSpec(shape, lambda j: zeros)
    return pl.BlockSpec(shape, lambda: zeros)


def columns(rows, first=0):
    return pl.BlockSpec((rows, 128), lambda j: (0, first + j))


SMEM = pl.BlockSpec(memory_space=pltpu.SMEM)
VMEM = pl.BlockSpec(memory_space=pltpu.VMEM)
ANY = pl.BlockSpec(memory_space=pl.ANY)


def sds(shape, dtype):
    return jax.ShapeDtypeStruct(shape, dtype)


def params(grid, mib):
    if grid:
        return pltpu.CompilerParams(vmem_limit_bytes=mib * 2**20, dimension_semantics=("arbitrary",))
    return pltpu.CompilerParams(vmem_limit_bytes=mib * 2**20)


def cost(us):
    return pl.CostEstimate(flops=int(us * 1.1e9), bytes_accessed=int(us * 1e6), transcendentals=0)


def pack_columns(v):
    n = v.shape[-1] // 4
    return jnp.concatenate([v[..., 0:n], v[..., 2 * n : 3 * n], v[..., n : 2 * n], v[..., 3 * n :]], axis=-1)


def small_kernel(hl, conv, gain, dtb, alog, skip, wdt, start_ref, end_ref, out_o):
    ch = out_o.shape[1]
    lane = iota((1, 128), 1)
    wide_lane = iota((1, ch), 1)
    bias = jnp.zeros((1, 128), F32)
    rate = jnp.zeros((1, 128), F32)
    diag = jnp.zeros((1, ch), F32)
    out_o[0:16, :] = jnp.zeros((16, ch), F32)
    for h in range(hl):
        cols = slice(h * HD, (h + 1) * HD)
        out_o[0:7, cols] = conv[h]
        out_o[7:8, cols] = gain[h : h + 1, :]
        bias = jnp.where(lane == h, dtb[0, h], jnp.where(lane == 64 + h, dtb[1, h], bias))
        rate = jnp.where((lane == h) | (lane == 64 + h), alog[h], rate)
        diag = jnp.where(wide_lane // HD == h, skip[h], diag)
        out_o[16 + 2 * h : 18 + 2 * h, :] = wdt[h].astype(F32)[0:2, :]
    out_o[8:9, :] = diag
    out_o[9:10, 0:128] = bias
    out_o[9:10, 128:256] = rate
    n = lax.axis_index("narrow")
    start, end = start_ref[...].astype(F32), end_ref[...].astype(F32)
    out_o[16 + 2 * hl :, :] = jnp.where(n == 0, end[8:16, :], start[0:8, :])


def swap(v):
    return lax.ppermute(v, "narrow", [(0, 1), (1, 0)])


def flip(v, bit, wide):
    return lax.ppermute(v, "wide", [(i, i ^ bit) for i in range(wide)])


def cross(v, bit, wide):
    pairs = [(i * 2 + k, (i ^ bit) * 2 + 1 - k) for i in range(wide) for k in range(2)]
    return lax.ppermute(v, ("wide", "narrow"), pairs)


def pick(v, dim, index):
    return lax.dynamic_index_in_dim(v, index, dim, keepdims=False)


def total(*parts):
    acc = parts[0].astype(F32)
    for v in parts[1:]:
        acc = acc + v.astype(F32)
    return acc


def split_positions(
    wide, layer_in, pre_gain, w_heads, w_bc, conv_x, conv_bc, dt_bias, a_log, skip_d, norm_gain, w_out, cotangent, starts, live
):
    n = lax.axis_index("narrow")
    w = lax.axis_index("wide")
    left = n == 0
    _, length, dm = layer_in.shape
    hl = w_heads.shape[1]
    heads = 2 * hl
    ch = hl * HD
    chans = 2 * ch
    pairs = heads // 2
    hp = pairs // 2
    nb = length // BLOCK
    ext = length + 2 * HALO
    share = dm // wide
    x = layer_in[0]
    g = cotangent[0]
    xbit = (w // 2) % 2
    zbits = w // 4

    w_turned = jnp.transpose(w_heads, (1, 2, 0))
    small_own = pl.pallas_call(
        functools.partial(small_kernel, hl),
        grid=(1,),
        out_shape=sds((24 + 2 * hl, ch), F32),
        in_specs=[
            whole((hl, 7, HD), 1), whole((hl, HD), 1), SMEM, SMEM, SMEM, pl.BlockSpec((hl, 16, dm), lambda j: (0, 8, 0)),
            pl.BlockSpec((HALO, dm), lambda j: (0, 0)), pl.BlockSpec((HALO, dm), lambda j: (length // HALO - 1, 0)),
        ],
        out_specs=whole((24 + 2 * hl, ch), 1),
        cost_estimate=cost(2),
        name="small",
    )(jnp.transpose(conv_x, (1, 0, 2)), norm_gain, dt_bias.T, a_log, skip_d, w_turned, x, x)
    small_other = swap(small_own)

    quarter = ch // 4
    q = w % 4

    def gather(own):
        p0 = swap(own)
        p1 = flip(p0, 2, wide)
        return p0, p1, flip(p0, 1, wide), flip(p1, 1, wide)

    def heads_rows(lo):
        return lax.dynamic_slice(w_turned, (q * (hl // 4), lo, 0), (hl // 4, HD, dm)).reshape(quarter, dm)

    wo = w_out.reshape(ch, dm)
    wv_pieces = gather(heads_rows(HD))
    wo_rows = lax.dynamic_slice(wo, (q * quarter, 0), (quarter, dm))
    wog_pieces = gather(jnp.concatenate([wo_rows, heads_rows(0)], axis=1))

    pos = (length, 128)
    sq = (nb, BLOCK, BLOCK)
    front_shapes = [
        ((8, chans), F32), ((8, chans), F32), ((8, chans), F32), ((128, dm), BF16), ((dm, 256), BF16), ((7, 256), F32),
        ((ext, dm), BF16), ((length, 1), F32), ((ext, 256), F32), ((ext, 256), F32), ((length, 256), BF16),
        ((2,) + sq, F32), ((4,) + sq, F32), ((3,) + sq, F32), ((128, 128), F32), ((length, 384), F32),
    ]
    (
        info, taps, gain, skip, wdt_all, wbc, taps_bc, normed, rs, bcm, dsl, maps, tab_a, tab_b, tab_c, dpt, sig,
    ) = pl.pallas_call(
        functools.partial(front_kernel, length, hl),
        out_shape=[sds((8,), jnp.int32)] + [sds(*v) for v in front_shapes],
        in_specs=[SMEM] + [VMEM] * 7,
        out_specs=[SMEM] + [VMEM] * len(front_shapes),
        scratch_shapes=[
            pltpu.VMEM((ext, 256), jnp.int32), pltpu.VMEM((ext, 256), F32), pltpu.VMEM((128, 128), F32),
            pltpu.VMEM((ext, dm), BF16),
        ],
        compiler_params=params(False, 10),
        cost_estimate=cost(8),
        name="front",
    )(starts, live, x, pre_gain.reshape(1, dm), w_bc, conv_bc, small_own, small_other)

    def states(first):
        return pl.BlockSpec((1, nb + 1, 128, 128), lambda j: (j + first, 0, 0, 0))

    bnd_spec = pl.BlockSpec((1, 64, 128), lambda j: (j, 0, 0))
    state_shape = sds((pairs, nb + 1, 128, 128), BF16)
    bnd_shape = sds((hp, 64, 128), BF16)
    act_shape = sds((length, chans), BF16)
    def twin(rows, first):
        return pl.BlockSpec((rows, 256), lambda j: (0, first + j))

    def vals(other, weights, before):
        steps = hp // 2
        first = steps if other else 0
        specs = [SMEM, whole((ext, dm), 1)]
        specs += [whole((quarter, dm), 1)] * 4 if other else [pl.BlockSpec((4, 2 * HD + 2, dm), lambda j: (j, 0, 0))]
        specs += [twin(8, first), whole((2,) + sq, 1), whole((128, 128), 1)] + [ANY] * len(before)
        return pl.pallas_call(
            functools.partial(vals_kernel, length, other),
            grid=(steps,),
            out_shape=[act_shape, sds((ext, chans), BF16), act_shape, state_shape, bnd_shape] + [sds((ch, dm), BF16)] * other,
            in_specs=specs,
            out_specs=[
                twin(length, first), twin(ext, first), twin(length, first),
                pl.BlockSpec((2, nb + 1, 128, 128), lambda j: (j + first, 0, 0, 0)),
                pl.BlockSpec((2, 64, 128), lambda j: (j, 0, 0)),
            ] + [whole((ch, dm), 1)] * other,
            scratch_shapes=[pltpu.VMEM((ext, 128), F32), pltpu.VMEM((ext, 128), F32), pltpu.VMEM((ext, 128), jnp.int32)],
            input_output_aliases={len(specs) - len(before) + i: i for i in range(len(before))},
            compiler_params=params(True, 16),
            cost_estimate=cost(9),
            name="vals_other" if other else "vals_own",
        )(info, normed, *weights, taps, tab_a, dpt, *before)

    *own_vals, bnd_own = vals(False, (w_turned,), ())
    xc, vm, ds, s_loc, bnd_other, wv_other = vals(True, wv_pieces, own_vals)

    def aliases(specs, before):
        return {len(specs) - len(before) + i: i for i in range(len(before))}

    def scan(first, s0, before):
        specs = [
            SMEM, columns(length, first), states(first), bnd_spec, whole((128, 128), 1), whole((4,) + sq, 1), columns(8, first),
        ] + [ANY] * len(before)
        return pl.pallas_call(
            functools.partial(scan_kernel, length, first),
            grid=(hp,),
            out_shape=[act_shape, state_shape],
            in_specs=specs,
            out_specs=[columns(length, first), states(first)],
            input_output_aliases=aliases(specs, before),
            compiler_params=params(True, 8),
            cost_estimate=cost(10),
            name="scan_other" if first else "scan_own",
        )(info, xc, s_loc, s0, dpt, tab_b, skip, *before)

    y, s_true = scan(0, swap(bnd_other), scan(hp, swap(bnd_own), ()))

    gw_shape = (2, dm // 2, dm + ch)
    out, gy, keep_a, send_a, ggate, ggain, wg_other = pl.pallas_call(
        functools.partial(gate_kernel, nb),
        out_shape=[
            sds((length, dm), BF16), act_shape, sds(gw_shape, BF16), sds(gw_shape, BF16), act_shape, sds((8, chans), F32),
            sds((ch, dm), BF16),
        ],
        in_specs=[VMEM] * 11,
        out_specs=[VMEM] * 7,
        scratch_shapes=[pltpu.VMEM((length, chans), BF16), pltpu.VMEM((ch, 2 * dm), BF16)]
        + [pltpu.VMEM((BLOCK, chans), F32)] * 4,
        compiler_params=params(False, 14),
        cost_estimate=cost(22),
        name="gated",
    )(x, g, normed, y, wo, w_turned, *wog_pieces, gain)

    def meet(keep, got):
        cols = keep.shape[-1]
        keep = keep.reshape(2, wide // 4, 2, share, cols)
        got = got.reshape(2, wide // 4, 2, share, cols)

        def piece(half, xx):
            return total(pick(keep[half], 1, xx), pick(got[half], 1, xx)).astype(BF16)

        return piece(0, xbit), piece(0, 1 - xbit), piece(1, xbit), piece(1, 1 - xbit)

    def plane(mine, to_x, to_y, to_d):
        return total(mine, flip(to_x, 2, wide), swap(to_y), cross(to_d, 2, wide)).astype(mine.dtype)

    def depth(v):
        return [pick(v, 0, zbits)] + [flip(pick(v, 0, zbits ^ k), 4 * k, wide) for k in (1, 2, 3)]

    a_pieces = meet(keep_a, flip(send_a, 1, wide))

    def table(k):
        return pl.BlockSpec((None,) + sq, lambda j: (k, 0, 0, 0))

    def gstate(first, before):
        specs = [SMEM, columns(length, first), table(0), table(2), whole((128, 128), 1)] + [ANY] * len(before)
        return pl.pallas_call(
            functools.partial(gstate_kernel, length, first),
            grid=(hp,),
            out_shape=[state_shape, bnd_shape],
            in_specs=specs,
            out_specs=[states(first), bnd_spec],
            input_output_aliases=aliases(specs, before),
            compiler_params=params(True, 6),
            cost_estimate=cost(5),
            name="gstate_other" if first else "gstate_own",
        )(info, gy, tab_b, tab_c, dpt, *before)

    gs_loc, gbnd_own = gstate(0, ())
    gs_loc, gbnd_other = gstate(hp, (gs_loc,))

    gs_loc, gbnd_other, *a_pieces = lax.optimization_barrier((gs_loc, gbnd_other, *a_pieces))
    a_plane = plane(*a_pieces)

    def gscan(first, gs0, before):
        sums = [whole(sq, 1), whole(sq, 1), whole(sq, 1), whole(pos, 1), whole(sq, 1)]
        specs = [
            SMEM, columns(length, first), columns(length, first), columns(length, first), states(first), states(first),
            bnd_spec, whole((128, 128), 1), table(1), table(0), table(0), whole((3,) + sq, 1), columns(8, first),
        ]
        at = len(specs)
        if before:
            specs += [ANY] * 3 + sums
        return pl.pallas_call(
            functools.partial(gscan_kernel, length, first),
            grid=(hp,),
            out_shape=[
                act_shape, sds(sq, F32), sds(sq, F32), sds(sq, F32), sds(pos, F32), sds(sq, F32), sds((16, chans), F32),
                sds((8, chans), F32), sds((HALO, ch), BF16),
            ],
            in_specs=specs,
            out_specs=[columns(length, first)] + sums + [columns(16, first), columns(8, first), columns(HALO)],
            scratch_shapes=[pltpu.VMEM((nb + 1, 128, 128), BF16)],
            input_output_aliases={at: 0, at + 1: 6, at + 2: 7} if before else {},
            compiler_params=params(True, 14),
            cost_estimate=cost(17),
            name="gscan_other" if first else "gscan_own",
        )(info, xc, ds, gy, s_true, gs_loc, gs0, dpt, tab_b, tab_a, tab_b, tab_c, skip, *before)

    gmix, ggt, gb, gct, ksum, rsum, phi, gskip, edge_other = gscan(hp, swap(gbnd_own), ())
    gmix, ggt, gb, gct, ksum, rsum, phi, gskip, edge_own = gscan(
        0, swap(gbnd_other), (gmix, phi, gskip, ggt, gb, gct, ksum, rsum)
    )

    gmix, ggt, a_plane = lax.optimization_barrier((gmix, ggt, a_plane))
    wa = depth(a_plane)

    gmb, gv, small, edge_bc = pl.pallas_call(
        functools.partial(join_kernel, length, heads),
        out_shape=[sds((ext, 256), F32), sds(pos, BF16), sds((16, 128), F32), sds((HALO, 256), F32)],
        in_specs=[SMEM] + [VMEM] * 9,
        out_specs=[VMEM] * 4,
        scratch_shapes=[pltpu.VMEM((ext, 128), F32), pltpu.VMEM((ext, 256), F32)],
        compiler_params=params(False, 8),
        cost_estimate=cost(6),
        name="join",
    )(info, ggt, gb, gct, ksum, rsum, phi, maps, dsl, sig)

    edge_a, edge_b = swap(edge_other), swap(edge_own)
    edge_bc = swap(edge_bc)
    sum_shape = (2, dm // 2, ch)
    gvals, keep_v, send_v, tiny = pl.pallas_call(
        functools.partial(back_kernel, length, pairs // 2),
        out_shape=[act_shape, sds(sum_shape, BF16), sds(sum_shape, BF16), sds((2, 16, ch), F32)],
        in_specs=[SMEM] + [VMEM] * 8,
        out_specs=[VMEM] * 4,
        scratch_shapes=[
            pltpu.VMEM((ext, 128), F32), pltpu.VMEM((ext, 128), F32), pltpu.VMEM((ext, 128), jnp.int32),
            pltpu.VMEM((dm, length), BF16),
        ],
        compiler_params=params(False, 12),
        cost_estimate=cost(12),
        name="back",
    )(info, gmix, edge_a, edge_b, vm, normed, taps, ggain, gskip)

    got_v = flip(send_v, 1, wide)
    keep_bc, send_bc, tiny, grad_in = pl.pallas_call(
        functools.partial(last_kernel, length, hl),
        out_shape=[
            sds((2, dm // 2, 384), BF16), sds((2, dm // 2, 384), BF16), sds((2, 16, ch), F32), sds((length, dm), F32),
        ],
        in_specs=[SMEM] + [VMEM] * 19,
        out_specs=[VMEM] * 4,
        scratch_shapes=[pltpu.VMEM((ext, 128), F32), pltpu.VMEM((ext, 128), F32), pltpu.VMEM((ext, 128), jnp.int32)],
        compiler_params=params(False, 20),
        cost_estimate=cost(8),
        name="last",
    )(
        info, gvals, ggate, w_turned, wv_other, wg_other, normed, gmb, edge_bc, bcm, taps_bc, gv, wdt_all, wbc, x, g, rs,
        pre_gain.reshape(1, dm), small, tiny,
    )
    keep_bc, got_v, *wa = lax.optimization_barrier((keep_bc, got_v, *wa))

    cols = ch + 384
    wb, tiny = pl.pallas_call(
        collect_kernel,
        out_shape=[sds((share, cols), F32), sds((16, ch), F32)],
        in_specs=[VMEM] * 5,
        out_specs=[VMEM] * 2,
        scratch_shapes=[
            pltpu.VMEM((4, 2, 2 * share, 384), BF16),
            pltpu.VMEM((4, share, cols), F32),
            pltpu.VMEM((4, 3, share, cols), BF16),
            pltpu.VMEM((4, 3, share, cols), BF16),
            pltpu.VMEM((3, share, cols), BF16),
            pltpu.VMEM((3, share, cols), BF16),
            pltpu.VMEM((2, 16, ch), F32),
            pltpu.VMEM((2, 16, ch), F32),
            pltpu.VMEM((3, 16, ch), F32),
            pltpu.VMEM((16, ch), F32),
            pltpu.VMEM((3, 16, ch), F32),
            pltpu.SemaphoreType.DMA((5,)),
            pltpu.SemaphoreType.DMA((5,)),
            pltpu.SemaphoreType.DMA((5, 3)),
            pltpu.SemaphoreType.DMA((5, 3)),
            pltpu.SemaphoreType.DMA((2, 3)),
            pltpu.SemaphoreType.DMA((2, 3)),
        ],
        compiler_params=pltpu.CompilerParams(collective_id=0, has_side_effects=True, vmem_limit_bytes=16 * 2**20),
        name="collect",
    )(keep_v, got_v, keep_bc, send_bc, tiny)

    g_w_heads, g_w_out, g_w_bc, g_conv_x, g_conv_bc, g_pre, g_bias, g_rate, g_skip, g_gain = pl.pallas_call(
        functools.partial(finish_kernel, hl),
        out_shape=[
            sds((hl, share, 2 * HD + 2), F32), sds((hl, share, HD), F32), sds((share, 256), F32), sds((7, HD // wide, hl), F32),
            sds((7, 256 // wide), F32), sds((1, share), F32), sds((2, hl), F32), sds((1, hl), F32), sds((1, hl), F32),
            sds((HD // wide, hl), F32),
        ],
        in_specs=[VMEM] * 6,
        out_specs=[VMEM] * 10,
        compiler_params=params(False, 8),
        name="finish",
    )(tiny, *wa, wb)
    return (
        out[None],
        grad_in[None],
        g_pre[0],
        jnp.transpose(g_w_heads, (1, 0, 2)),
        g_w_bc,
        jnp.transpose(g_conv_x, (0, 2, 1)),
        g_conv_bc,
        g_bias.T,
        g_rate[0],
        g_skip[0],
        g_gain.T,
        jnp.transpose(g_w_out, (0, 2, 1)),
    )


def solution(mesh):
    body = shards
    if mesh.shape["narrow"] == 2 and mesh.shape["wide"] == 16:
        body = functools.partial(split_positions, mesh.shape["wide"])
    return jax.shard_map(
        body,
        mesh=mesh,
        in_specs=(
            P("wide", "narrow", None),
            P(),
            P(None, "narrow", None),
            P(),
            P(None, "narrow", None),
            P(),
            P("narrow", None),
            P("narrow"),
            P("narrow"),
            P("narrow", None),
            P("narrow", None, None),
            P("wide", "narrow", None),
            P("wide", None),
            P("wide", None),
        ),
        out_specs=(
            P("wide", "narrow", None),
            P("wide", "narrow", None),
            P("wide"),
            P("wide", "narrow", None),
            P("wide", None),
            P(None, "narrow", "wide"),
            P(None, "wide"),
            P("narrow", None),
            P("narrow"),
            P("narrow"),
            P("narrow", "wide"),
            P("narrow", None, "wide"),
        ),
        check_vma=False,
    )
```

```python
import functools

import jax
import jax.numpy as jnp
from jax import lax
from jax.experimental import pallas as pl
from jax.experimental.pallas import tpu as pltpu
from jax.sharding import PartitionSpec as P

H = 24
HD = 64
BLOCK = 128
SEQ_LEN = 1280


EPS = 1e-05
HIGH = lax.Precision.HIGHEST


def rounded(value):
    return value + lax.stop_gradient(value.astype(jnp.bfloat16).astype(jnp.float32) - value)


def segment_ids(starts):
    where_at = jnp.arange(SEQ_LEN, dtype=jnp.int32)
    hits = (starts[:, :, None] <= where_at[None, None, :]).astype(jnp.int32)
    return jnp.sum(hits, axis=1) - 1


def conv_doc(values, taps, seg):
    half = (taps.shape[0] - 1) // 2
    length = values.shape[1]
    padded = jnp.pad(values, ((0, 0), (half, half), (0, 0)))
    seg_pad = jnp.pad(seg, ((0, 0), (half, half)), constant_values=-1)
    total = jnp.zeros_like(values)
    for offset in range(taps.shape[0]):
        same = (seg_pad[:, offset : offset + length] == seg).astype(values.dtype)
        total = total + taps[offset] * padded[:, offset : offset + length] * same[:, :, None]
    return total


def ssd_forward(xc, steps, decays, bmat, cmat, seg, prec):
    rows, length, heads, hdim = xc.shape
    blocks = length // BLOCK
    xb = xc.reshape(rows, blocks, BLOCK, heads, hdim)
    stepb = steps.reshape(rows, blocks, BLOCK, heads)
    cum = jnp.cumsum(decays.reshape(rows, blocks, BLOCK, heads), axis=2)
    bb = bmat.reshape(rows, blocks, BLOCK, -1)
    cb = cmat.reshape(rows, blocks, BLOCK, -1)
    sb = seg.reshape(rows, blocks, BLOCK)
    order = jnp.arange(BLOCK, dtype=jnp.int32)
    causal = order[:, None] >= order[None, :]
    same = ((sb[:, :, :, None] == sb[:, :, None, :]) & causal)[..., None]
    diff = cum[:, :, :, None, :] - cum[:, :, None, :, :]
    weights = jnp.where(same, jnp.exp(jnp.where(same, diff, 0.0)), 0.0)
    inner = jnp.einsum("rbtn,rbsn->rbts", cb, bb, precision=prec)
    mix = weights * inner[..., None] * stepb[:, :, None, :, :]
    intra = jnp.einsum("rbtsh,rbshp->rbthp", mix, xb, precision=prec)
    last = sb[:, :, -1]
    cum_end = cum[:, :, -1, :]
    to_end = (
        (sb == last[:, :, None]).astype(cum.dtype)[..., None]
        * jnp.exp(cum_end[:, :, None, :] - cum)
        * stepb
    )
    states = jnp.einsum("rbshp,rbsn->rbhpn", to_end[..., None] * xb, bb, precision=prec)
    decay_end = jnp.exp(cum_end)

    def carry_step(carry, item):
        state, seg_prev = carry
        block_state, block_last, block_decay = item
        keep = (block_last == seg_prev).astype(state.dtype)[:, None, None, None]
        fresh = keep * block_decay[:, :, None, None] * state + block_state
        return ((fresh, block_last), (state, seg_prev))

    init = (
        jnp.zeros((rows, heads, hdim, bb.shape[-1]), xc.dtype),
        jnp.full((rows,), -1, jnp.int32),
    )
    items = (jnp.moveaxis(states, 1, 0), jnp.moveaxis(last, 1, 0), jnp.moveaxis(decay_end, 1, 0))
    _, (before, seg_before) = lax.scan(carry_step, init, items)
    before = jnp.moveaxis(before, 0, 1)
    seg_before = jnp.moveaxis(seg_before, 0, 1)
    enter = (sb == seg_before[:, :, None]).astype(cum.dtype)[..., None] * jnp.exp(cum)
    inter = jnp.einsum("rbtn,rbhpn->rbthp", cb, before, precision=prec) * enter[..., None]
    return (intra + inter).reshape(rows, length, heads, hdim)


def mixer(proj, bcproj, conv_x, conv_bc, dt_bias, a_log, skip_d, seg, mask, rounder, prec):
    rows, length, heads, width = proj.shape
    hdim = (width - 2) // 2
    state = bcproj.shape[-1] // 4
    gate = proj[..., :hdim]
    values = proj[..., hdim : 2 * hdim] * mask[:, :, None, None]
    mixed_x = conv_doc(
        values.reshape(rows, length, heads * hdim),
        conv_x.reshape(conv_x.shape[0], heads * hdim),
        seg,
    )
    xc = rounder(jax.nn.silu(mixed_x)).reshape(rows, length, heads, hdim)
    maps = rounder(jax.nn.silu(conv_doc(bcproj * mask[:, :, None], conv_bc, seg)))
    b_fwd = maps[..., :state]
    c_fwd = maps[..., state : 2 * state]
    b_bwd = maps[..., 2 * state : 3 * state]
    c_bwd = maps[..., 3 * state :]
    rate = -jnp.exp(a_log)
    dt_fwd = jax.nn.softplus(proj[..., 2 * hdim] + dt_bias[:, 0]) * mask[:, :, None]
    dt_bwd = jax.nn.softplus(proj[..., 2 * hdim + 1] + dt_bias[:, 1]) * mask[:, :, None]
    out_fwd = ssd_forward(xc, dt_fwd, dt_fwd * rate, b_fwd, c_fwd, seg, prec)

    def flip(v):
        return jnp.flip(v, axis=1)

    out_bwd = flip(
        ssd_forward(
            flip(xc), flip(dt_bwd), flip(dt_bwd * rate), flip(b_bwd), flip(c_bwd), flip(seg), prec
        )
    )
    keep_prev = (seg[:, 1:] == seg[:, :-1]).astype(xc.dtype)[:, :, None, None]
    shifted_fwd = jnp.pad(out_fwd[:, :-1] * keep_prev, ((0, 0), (1, 0), (0, 0), (0, 0)))
    shifted_bwd = jnp.pad(out_bwd[:, 1:] * keep_prev, ((0, 0), (0, 1), (0, 0), (0, 0)))
    return (shifted_fwd + shifted_bwd + skip_d[:, None] * xc, gate)


def shards(
    layer_in,
    pre_gain,
    w_heads,
    w_bc,
    conv_x,
    conv_bc,
    dt_bias,
    a_log,
    skip_d,
    norm_gain,
    w_out,
    cotangent,
    starts,
    live,
):
    seg = segment_ids(starts)
    mask = live.astype(jnp.float32)
    x_here = layer_in.astype(jnp.float32)
    scale = lax.rsqrt(jnp.mean(x_here * x_here, axis=-1, keepdims=True) + EPS)
    normed_here = (x_here * scale * pre_gain).astype(jnp.bfloat16)
    normed = lax.all_gather(normed_here, "narrow", axis=1, tiled=True)
    proj = jnp.einsum("rld,dhc->rlhc", normed, w_heads, preferred_element_type=jnp.float32)
    bcproj = jnp.einsum("rld,dc->rlc", normed, w_bc, preferred_element_type=jnp.float32)

    def mix_local(proj_in, bc_in, taps_x, taps_bc, bias_in, log_rate, diag_in):
        return mixer(
            proj_in, bc_in, taps_x, taps_bc, bias_in, log_rate, diag_in, seg, mask, rounded, HIGH
        )

    (ymix, gate), pull_mix = jax.vjp(
        mix_local, proj, bcproj, conv_x, conv_bc, dt_bias, a_log, skip_d
    )
    rows, length, heads, hdim = ymix.shape
    sigma = jax.nn.sigmoid(gate)
    act = gate * sigma
    gated = (ymix * act).reshape(rows, length, heads * hdim)
    squares = lax.psum(jnp.sum(gated * gated, axis=-1), "narrow")
    inv = lax.rsqrt(squares / (H * HD) + EPS)[..., None]
    gain_flat = norm_gain.reshape(-1)
    normalized = gated * inv
    hn = (normalized * gain_flat).astype(jnp.bfloat16)
    w_flat = w_out.reshape(heads * hdim, -1)
    partial_value = jnp.einsum("rlc,cd->rld", hn, w_flat, preferred_element_type=jnp.float32)
    branch = lax.psum_scatter(partial_value, "narrow", scatter_dimension=1, tiled=True)
    out = (x_here + branch).astype(jnp.bfloat16)
    grad_out = lax.all_gather(cotangent, "narrow", axis=1, tiled=True)
    g_w_out = jnp.einsum("rlc,rld->cd", hn, grad_out, preferred_element_type=jnp.float32)
    g_hn = jnp.einsum("rld,cd->rlc", grad_out, w_flat, preferred_element_type=jnp.float32)
    g_gain = jnp.sum(g_hn * normalized, axis=(0, 1))
    weighted = g_hn * gain_flat
    cross = lax.psum(jnp.sum(weighted * gated, axis=-1), "narrow")
    g_gated = inv * weighted - gated * (inv * inv * inv) * (cross / (H * HD))[..., None]
    g_gated = g_gated.reshape(rows, length, heads, hdim)
    g_ymix = g_gated * act
    g_gate = g_gated * ymix * (sigma * (1.0 + gate * (1.0 - sigma)))
    g_proj, g_bcproj, g_conv_x, g_conv_bc, g_dt_bias, g_a_log, g_skip = pull_mix((g_ymix, g_gate))
    g_proj_low = g_proj.astype(jnp.bfloat16)
    g_w_heads = jnp.einsum("rld,rlhc->dhc", normed, g_proj_low, preferred_element_type=jnp.float32)
    g_w_bc = jnp.einsum(
        "rld,rlc->dc", normed, g_bcproj, precision=HIGH, preferred_element_type=jnp.float32
    )
    g_normed = jnp.einsum("rlhc,dhc->rld", g_proj_low, w_heads, preferred_element_type=jnp.float32)
    g_normed = g_normed + jnp.einsum(
        "rlc,dc->rld", g_bcproj, w_bc, precision=HIGH, preferred_element_type=jnp.float32
    )
    g_normed_here = lax.psum_scatter(g_normed, "narrow", scatter_dimension=1, tiled=True)
    weighted_in = g_normed_here * pre_gain
    g_pre = jnp.sum(g_normed_here * x_here * scale, axis=(0, 1))
    g_x = scale * weighted_in - x_here * (scale * scale * scale) * jnp.mean(
        weighted_in * x_here, axis=-1, keepdims=True
    )
    grad_input = cotangent.astype(jnp.float32) + g_x
    g_pre, g_w_bc, g_conv_bc = lax.psum((g_pre, g_w_bc, g_conv_bc), "narrow")
    reduced = (
        lax.psum_scatter(g_w_heads, "wide", scatter_dimension=0, tiled=True),
        lax.psum_scatter(g_w_out.reshape(heads, hdim, -1), "wide", scatter_dimension=2, tiled=True),
        lax.psum_scatter(g_conv_x, "wide", scatter_dimension=2, tiled=True),
        lax.psum_scatter(g_gain.reshape(heads, hdim), "wide", scatter_dimension=1, tiled=True),
        lax.psum_scatter(g_pre, "wide", scatter_dimension=0, tiled=True),
        lax.psum_scatter(g_w_bc, "wide", scatter_dimension=0, tiled=True),
        lax.psum_scatter(g_conv_bc, "wide", scatter_dimension=1, tiled=True),
    )
    share_pre, share_bc, share_conv = (reduced[4], reduced[5], reduced[6])
    head_bias, head_rate, head_diag = lax.psum((g_dt_bias, g_a_log, g_skip), "wide")
    return (
        out,
        grad_input,
        share_pre,
        reduced[0],
        share_bc,
        reduced[2],
        share_conv,
        head_bias,
        head_rate,
        head_diag,
        reduced[3],
        reduced[1],
    )


HALO = 16
F32 = jnp.float32
BF16 = jnp.bfloat16
LOGZERO = -1e30


def mm(a, b, dims=((1,), (0,)), precision=None):
    return lax.dot_general(a, b, (dims, ((), ())), precision=precision, preferred_element_type=F32)


def nt(a, b):
    return mm(a, b, ((1,), (1,)))


def tn(a, b):
    return mm(a, b, ((0,), (0,)))


def seg_at(info, pos):
    seg = jnp.full(pos.shape, -1, jnp.int32)
    for j in range(4):
        seg = seg + (pos >= info[j]).astype(jnp.int32)
    return jnp.where(pos >= info[6], 99, seg)


def iota(shape, dim):
    return lax.broadcasted_iota(jnp.int32, shape, dim)


def silu_parts(v):
    sg = 0.5 * jnp.tanh(0.5 * v) + 0.5
    act = v * sg
    return act, sg + act * (1.0 - sg)


def thirds(v):
    hi = v.astype(BF16).astype(F32)
    rest = v - hi
    mid = rest.astype(BF16).astype(F32)
    return hi, mid, rest - mid


def column_terms(values):
    sub = iota((16, 128), 0)
    v = jnp.ones((16, 128), F32)
    for k, value in enumerate(values):
        v = jnp.where((sub >= 3 * k) & (sub < 3 * k + 3), value, v)
    hi, mid, low = thirds(v)
    part = sub % 3
    out = jnp.where(part == 0, hi, jnp.where(part == 1, mid, low))
    return jnp.where(sub < 3 * len(values), out, 1.0).astype(BF16)


def row_base(count, places):
    sub = iota((16, 384), 0)
    lane = iota((16, 384), 1)
    out = jnp.zeros((16, 384), F32)
    for k, spans in enumerate(places):
        for lo, hi in spans:
            out = jnp.where((sub >= 3 * k) & (sub < 3 * k + 3) & (lane >= lo) & (lane < hi), 1.0, out)
    return out


def row_terms(count, base, one, two):
    sub = iota((16, 128), 0)
    part = sub - 3 * count
    made = []
    for k, value in enumerate((one, two)):
        hi, mid, low = thirds(jnp.broadcast_to(value, (16, 128)))
        here = base[:, 128 * k : 128 * (k + 1)]
        made.append(
            jnp.where(part == 0, hi, jnp.where(part == 1, mid, jnp.where(part == 2, low, here))).astype(BF16)
        )
    return jnp.concatenate(made + [base[:, 256:].astype(BF16)], axis=1)


def conv_taps(src, seg_src, taps, first, rows):
    seg0 = seg_src[first : first + rows, :]
    total = src[first : first + rows, :] * taps[3:4, :]
    for k in (0, 1, 2, 4, 5, 6):
        lo = first + k - 3
        same = seg_src[lo : lo + rows, :] == seg0
        total = total + jnp.where(same, src[lo : lo + rows, :], 0.0) * taps[k : k + 1, :]
    return total


def front_kernel(
    length, hl, starts, live_ref, x_in, gain, wbc_ref, taps_ref, small_a, small_b,
    info, taps_o, gain_o, skip_o, wdt, wbc, taps, normed_o, rs_o, bcm_h, dsl_h, maps_h, ta_o, tb_o, tc_h, dpt_o, sig_h, seg_s, maps_s, cum_s, x_s, bcm_o, dsl_o, maps_o, tc_o, sig_o, sems,
):
    late = []

    def send(src, dst):
        late.append(pltpu.make_async_copy(src, dst, sems.at[len(late)]))
        late[-1].start()

    nb = length // BLOCK
    ext = length + 2 * HALO
    dm = x_in.shape[1]
    n = lax.axis_index("narrow")
    for i in range(4):
        info[i] = starts[0, i]
    count = jnp.sum(live_ref[...].astype(F32)).astype(jnp.int32)
    off = n * length
    info[4] = count
    info[5] = off
    info[6] = live_ref.shape[1]
    info[7] = n
    ch = small_a.shape[1]
    for k, small in enumerate((small_a, small_b)):
        cols = slice(k * ch, (k + 1) * ch)
        taps_o[:, cols] = small[0:8, :]
        gain_o[:, cols] = jnp.broadcast_to(small[7:8, :], (8, ch))
        skip_o[:, cols] = jnp.broadcast_to(small[8:9, :], (8, ch))
    dst = iota((128, 2 * hl), 0)
    src = iota((128, 2 * hl), 1)
    place = (src % 2) * 64 + src // 2
    at_a = jnp.where(dst == place, 1.0, 0.0).astype(BF16)
    at_b = jnp.where(dst == place + hl, 1.0, 0.0).astype(BF16)
    own_steps = small_a[16 : 16 + 2 * hl, :].astype(BF16)
    far_steps = small_b[16 : 16 + 2 * hl, :].astype(BF16)
    wdt[...] = (mm(at_a, own_steps) + mm(at_b, far_steps)).astype(BF16)
    wbc[...] = pack_columns(wbc_ref[...])
    taps[...] = pack_columns(taps_ref[...])

    bias = small_a[9:10, 0:128] + pltpu.roll(small_b[9:10, 0:128], hl, 1)
    alog = small_a[9:10, 128:256] + pltpu.roll(small_b[9:10, 128:256], hl, 1)
    edge = small_b[16 + 2 * hl : 24 + 2 * hl, :]
    zero_edge = jnp.zeros((8, dm), F32)
    before = jnp.concatenate([zero_edge, jnp.where(n == 1, edge, 0.0)], axis=0)
    behind = jnp.concatenate([jnp.where(n == 1, 0.0, edge), zero_edge], axis=0)
    x_s[0:HALO, :] = before.astype(BF16)
    x_s[HALO : HALO + length, :] = x_in[...]
    x_s[HALO + length : ext, :] = behind.astype(BF16)
    x = x_s[...].astype(F32)
    rs = lax.rsqrt(jnp.mean(x * x, axis=1, keepdims=True) + EPS)
    normed = (x * rs * gain[...]).astype(BF16)
    normed_o[...] = normed
    rs_o[...] = rs[HALO : HALO + length, :]
    pos256 = iota((ext, 256), 0) + (off - HALO)
    seg_s[...] = seg_at(info, pos256)
    live = pos256 < count
    bcm_o[...] = jnp.where(live, mm(normed, wbc[...]), 0.0)
    send(bcm_o, bcm_h)
    crows = length + HALO
    cfirst = HALO // 2
    mix = conv_taps(bcm_o, seg_s, taps, cfirst, crows)
    maps, dsl = silu_parts(mix)
    dsl_o[...] = jnp.zeros_like(dsl_o)
    dsl_o[cfirst : cfirst + crows, :] = dsl
    send(dsl_o, dsl_h)
    maps_s[...] = jnp.zeros_like(maps_s)
    maps_s[cfirst : cfirst + crows, :] = maps.astype(BF16).astype(F32)
    own = slice(HALO, HALO + length)
    segx = seg_s[own, 0:128]
    lane = iota((length, 128), 1)
    fwd = lane < 64
    segp = seg_s[HALO - 1 : HALO - 1 + length, 0:128]
    segn = seg_s[HALO + 1 : HALO + 1 + length, 0:128]
    bmap = maps_s[own, 0:128]
    cprev = jnp.where(segp == segx, maps_s[HALO - 1 : HALO - 1 + length, 128:256], 0.0)
    cnext = jnp.where(segn == segx, maps_s[HALO + 1 : HALO + 1 + length, 128:256], 0.0)
    cmap = jnp.where(fwd, cprev, cnext)
    maps_o[:, 0:128] = bmap.astype(BF16)
    maps_o[:, 128:256] = cmap.astype(BF16)
    send(maps_o, maps_h)
    raw = nt(normed[own, :], wdt[...]) + bias
    softp = jnp.maximum(raw, 0.0) + jnp.log(1.0 + jnp.exp(-jnp.abs(raw)))
    softp = jnp.where(raw < -15.0, jnp.exp(jnp.minimum(raw, 0.0)), softp)
    pos128 = iota((length, 128), 0) + off
    m = pos128 < count
    dt = jnp.where(m, softp, 0.0)
    sg = jnp.where(m, 1.0 / (1.0 + jnp.exp(-raw)), 0.0)
    ratio = jnp.where(m, jnp.where(raw < -15.0, 1.0, sg / jnp.maximum(softp, 1e-30)), 0.0)
    rate = -jnp.exp(alog)
    a = dt * rate
    sig_o[:, 256:384] = a
    sig_o[:, 0:128] = sg * rate
    sig_o[:, 128:256] = ratio
    tri = (iota((BLOCK, BLOCK), 0) >= iota((BLOCK, BLOCK), 1)).astype(F32)
    logdt = jnp.maximum(jnp.log(dt), LOGZERO)
    sub = iota((BLOCK, BLOCK), 0)
    ln = iota((BLOCK, BLOCK), 1)
    fwdb = ln < 64
    cum_s[...] = jnp.zeros_like(cum_s)
    dvals, ends = [], []
    for b in range(nb):
        blk = slice(b * BLOCK, (b + 1) * BLOCK)
        ab = a[blk, :]
        cum = mm(tri, ab, precision=HIGH)
        cx = cum - ab
        end = cum[BLOCK - 1 : BLOCK, :]
        colt = jnp.where(fwdb, cx, end - cum)
        rows = jnp.where(fwdb, logdt[blk, :] - cum, cx + logdt[blk, :] - end)
        tb_o[0, b] = colt.T
        tb_o[1, b] = rows.T
        ta_o[0, b] = jnp.minimum(rows + end, 60.0).T
        first_pos = off + b * BLOCK
        sp = seg_at(info, sub + first_pos)
        st = seg_at(info, ln + first_pos)
        before = seg_at(info, sub * 0 + (first_pos - 1))
        begin = seg_at(info, sub * 0 + first_pos)
        last = seg_at(info, sub * 0 + (first_pos + BLOCK - 1))
        after = seg_at(info, sub * 0 + (first_pos + BLOCK))
        enter = jnp.where(fwdb, (sp == before).astype(F32), (sp == after).astype(F32))
        keep = jnp.where(fwdb, (sp == last).astype(F32), (sp == begin).astype(F32))
        ce = cmap[blk, :] * enter
        bk = bmap[blk, :] * keep
        tb_o[3, b] = ce
        tc_o[1, b] = bk
        tc_o[2, b] = ce.T
        ta_o[1, b] = bk.T
        chain = jnp.where(fwdb[0:1, :], (last == before).astype(F32)[0:1, :], (begin == after).astype(F32)[0:1, :])
        dvals.append(jnp.exp(end) * chain)
        ends.append(end)
        cb = cmap[blk, :].astype(BF16)
        bb = bmap[blk, :].astype(BF16)
        zero = jnp.zeros_like(bb)
        same = sp == st
        low = same & (sub > ln)
        high = same & (sub < ln)
        bf = jnp.where(fwdb, bb, zero)
        br = jnp.where(fwdb, zero, bb)
        tb_o[2, b] = jnp.where(low, nt(cb, bf), jnp.where(high, nt(cb, br), 0.0))
        tc_o[0, b] = jnp.where(high, nt(bf, cb), jnp.where(low, nt(br, cb), 0.0))
    ones = jnp.ones((1, 128), F32)
    prefix, suffix = [ones], [ones]
    for b in range(nb):
        prefix.append(prefix[-1] * dvals[b])
        suffix.append(suffix[-1] * dvals[nb - 1 - b])
    suffix = suffix[::-1]
    f1 = fwdb[0:1, :]
    for b in range(nb):
        cum_s[b : b + 1, :] = dvals[b]
        cum_s[48 + b : 49 + b, :] = ends[b]
    for i in range(nb + 1):
        cum_s[16 + i : 17 + i, :] = jnp.where(f1, prefix[i], suffix[i])
        cum_s[32 + i : 33 + i, :] = jnp.where(f1, suffix[i], prefix[i])
    dpt_o[...] = cum_s[...].T
    send(sig_o, sig_h)
    send(tc_o, tc_h)
    for one in late:
        one.wait()


def pair_rows(dpt, j, base, i, half):
    lane = iota((1, 128), 1)
    one = dpt[pl.ds(half * 64 + 2 * j, 1), :][:, base + i : base + i + 1]
    two = dpt[pl.ds(half * 64 + 2 * j + 1, 1), :][:, base + i : base + i + 1]
    return jnp.where(lane < 64, one, two)


def assemble(dst, pieces):
    quarter = dst.shape[0] // 4
    q = lax.axis_index("wide") % 4
    cbit = q % 2
    xbit = q // 2
    places = (q, (1 - xbit) * 2 + cbit, xbit * 2 + 1 - cbit, (1 - xbit) * 2 + 1 - cbit)
    for place, piece in zip(places, pieces):
        dst[pl.ds(pl.multiple_of(place * quarter, quarter), quarter), :] = piece[...]


def vals_kernel(length, other, info, normed, *refs):
    nb = length // BLOCK
    ext = length + 2 * HALO
    step = pl.program_id(0)
    first = step
    if other:
        p0, p1, p2, p3, taps, ta, dpt = refs[:7]
        xc_o, vm_o, ds_o, s_o, bnd_o, wvo_o, vm_a, vm_b, seg_s = refs[11:]
        first = step + pl.num_programs(0)

        @pl.when(step == 0)
        def _():
            assemble(wvo_o, (p0, p1, p2, p3))

        wv = wvo_o[pl.ds(pl.multiple_of(step * 256, 256), 256), :]
    else:
        w_ref, taps, ta, dpt, xc_o, vm_o, ds_o, s_o, bnd_o, vm_a, vm_b, seg_s = refs
        wv = jnp.concatenate([w_ref[h, HD : 2 * HD, :] for h in range(4)], axis=0)
    off, count = info[5], info[4]

    @pl.when(step == 0)
    def _():
        seg_s[...] = seg_at(info, iota((ext, 128), 0) + (off - HALO))

    live = iota((ext, 128), 0) + (off - HALO) < count
    both = nt(normed[...], wv)
    lane = iota((BLOCK, 128), 1)
    top = iota((BLOCK, 128), 0) < 64
    for p, vm_s in enumerate((vm_a, vm_b)):
        j = 2 * first + p
        here = slice(128 * p, 128 * (p + 1))
        vm = jnp.where(live, both[:, here], 0.0)
        vm_s[...] = vm
        vm_o[:, here] = vm.astype(BF16)
        act, ds = silu_parts(conv_taps(vm_s, seg_s, taps[:, here], HALO, length))
        xc = act.astype(BF16)
        xc_o[:, here] = xc
        ds_o[:, here] = ds.astype(BF16)
        loc = []
        for b in range(nb):
            blk = slice(b * BLOCK, (b + 1) * BLOCK)
            got = []
            for i in range(2):
                h = 2 * j + i
                w = jnp.where(top, jnp.exp(ta[0, b, pl.ds(h, 1), :]), jnp.exp(ta[0, b, pl.ds(64 + h, 1), :]))
                got.append((ta[1, b] * w).astype(BF16))
            got = mm(jnp.concatenate(got, axis=0), xc[blk, :])
            loc.append(jnp.where(lane < 64, got[0:BLOCK, :], got[BLOCK:, :]))
        state = jnp.zeros((64, 128), F32)
        s_o[p, 0, 0:64, :] = state.astype(BF16)
        for b in range(nb):
            state = pair_rows(dpt, j, 0, b, 0) * state + loc[b][0:64, :]
            s_o[p, b + 1, 0:64, :] = state.astype(BF16)
        end_f = state
        state = jnp.zeros((64, 128), F32)
        s_o[p, nb, 64:128, :] = state.astype(BF16)
        for b in range(nb - 1, -1, -1):
            state = pair_rows(dpt, j, 0, b, 1) * state + loc[b][64:128, :]
            s_o[p, b, 64:128, :] = state.astype(BF16)
        bnd_o[p] = jnp.where(info[7] == 0, end_f, state).astype(BF16)


def scan_kernel(length, first_pair, info, xc_ref, s_ref, s0_ref, dpt, tb, skip, *refs):
    nb = length // BLOCK
    y_o, st_o = refs[-2:]
    j = pl.program_id(0) + first_pair
    right = (info[7] == 1).astype(F32)
    s0 = s0_ref[0].astype(F32)
    lane = iota((BLOCK, 128), 1)
    first = lane < 64
    low = iota((BLOCK, BLOCK), 0) > lane
    base = row_base(2, [[(0, 128), (256, 320)], [(128, 256), (320, 384)]])
    for i in range(nb + 1):
        f = s_ref[0, i, 0:64, :].astype(F32) + pair_rows(dpt, j, 16, i, 0) * (s0 * right)
        r = s_ref[0, i, 64:128, :].astype(F32) + pair_rows(dpt, j, 16, i, 1) * (s0 * (1.0 - right))
        st_o[0, i, 0:64, :] = f.astype(BF16)
        st_o[0, i, 64:128, :] = r.astype(BF16)
    for b in range(nb):
        blk = slice(b * BLOCK, (b + 1) * BLOCK)
        xb = xc_ref[blk, :]
        rhs = jnp.concatenate([xb, st_o[0, b, 0:64, :], st_o[0, b + 1, 64:128, :]], axis=0)
        got = []
        for i in range(2):
            h = 2 * j + i
            terms = column_terms([tb[0, b, pl.ds(h, 1), :], tb[0, b, pl.ds(64 + h, 1), :]])
            expo = tn(terms, row_terms(2, base, tb[1, b, pl.ds(h, 1), :], tb[1, b, pl.ds(64 + h, 1), :]))
            diff = jnp.where(low, expo[:, 0:128], expo[:, 128:256])
            mix = jnp.exp(jnp.minimum(diff, 60.0)) * tb[2, b]
            ct = tb[3, b] * jnp.exp(expo[:, 256:])
            lhs = jnp.concatenate([mix.astype(BF16), ct.astype(BF16)], axis=1)
            got.append(lhs)
        got = mm(jnp.concatenate(got, axis=0), rhs)
        y = jnp.where(first, got[0:BLOCK, :], got[BLOCK:, :]) + skip[0:1, :] * xb.astype(F32)
        y_o[blk, :] = y.astype(BF16)


def by_core(v, keep, send):
    share = v.shape[0] // 16
    cbit = lax.axis_index("wide") % 2
    v = v.astype(BF16).reshape(8, 2, share, v.shape[1])
    keep[...] = jnp.where(cbit == 0, v[:, 0], v[:, 1]).reshape(8 * share, v.shape[3])
    send[...] = jnp.where(cbit == 0, v[:, 1], v[:, 0]).reshape(8 * share, v.shape[3])


def gate_kernel(
    tiles, x_ref, g_ref, normed, y_ref, wout_a, w_ref, p0, p1, p2, p3, gain,
    out_h, gy_o, keep_h, send_h, ggate_h, ggain_o, wgo_h, hn_s, other_s, gated_s, act_s, dact_s, ghn_s,
    out_o, keep_o, send_o, ggate_o, sems,
):
    late = []

    def send(src, dst):
        late.append(pltpu.make_async_copy(src, dst, sems.at[len(late)]))
        late[-1].start()

    dm = x_ref.shape[1]
    chans = y_ref.shape[1]
    half = chans // 2
    step = 256
    assemble(other_s, (p0, p1, p2, p3))
    send(other_s.at[:, dm:], wgo_h)
    ggain_o[...] = jnp.zeros_like(ggain_o)

    @pl.loop(0, tiles)
    def _(i):
        start = pl.multiple_of(i * BLOCK, BLOCK)
        rows = pl.ds(start, BLOCK)
        nrows = normed[pl.ds(pl.multiple_of(start + HALO, HALO), BLOCK), :]
        squares = jnp.zeros((BLOCK, 128), F32)
        for lo in range(0, chans, step):
            if lo < half:
                heads = range(lo // HD, (lo + step) // HD)
                wg = jnp.concatenate([w_ref[h, 0:HD, :] for h in heads], axis=0)
            else:
                wg = other_s[lo - half : lo - half + step, dm:]
            gates = nt(nrows, wg)
            for at in range(0, step, 128):
                cols = slice(lo + at, lo + at + 128)
                act, dact = silu_parts(gates[:, at : at + 128])
                gated = y_ref[rows, cols].astype(F32) * act
                squares = squares + gated * gated
                gated_s[:, cols] = gated
                act_s[:, cols] = act
                dact_s[:, cols] = dact
        inv = lax.rsqrt(jnp.sum(squares, axis=1, keepdims=True) * (1.0 / chans) + EPS)
        inv = jnp.broadcast_to(inv, (BLOCK, 128))
        g = g_ref[rows, :]
        across = jnp.zeros((BLOCK, 128), F32)
        for lo in range(0, chans, step):
            wo = wout_a[lo : lo + step, :] if lo < half else other_s[lo - half : lo - half + step, 0:dm]
            ghns = nt(g, wo)
            for at in range(0, step, 128):
                cols = slice(lo + at, lo + at + 128)
                gainv = gain[0:1, cols]
                gated = gated_s[:, cols]
                nrm = gated * inv
                hn_s[rows, cols] = (nrm * gainv).astype(BF16)
                ghn = ghns[:, at : at + 128]
                ggain_o[0:1, cols] += jnp.sum(ghn * nrm, axis=0, keepdims=True)
                wgt = ghn * gainv
                ghn_s[:, cols] = wgt
                across = across + wgt * gated
        cross = jnp.sum(across, axis=1, keepdims=True) * (1.0 / chans)
        cross = jnp.broadcast_to(cross, (BLOCK, 128)) * (inv * inv * inv)
        hn = hn_s[rows, :]
        branch = mm(hn[:, 0:half], wout_a[...]) + mm(hn[:, half:], other_s[:, 0:dm])
        out_o[rows, :] = (x_ref[rows, :].astype(F32) + branch).astype(BF16)
        for lo in range(0, chans, 128):
            cols = slice(lo, lo + 128)
            ggated = inv * ghn_s[:, cols] - gated_s[:, cols] * cross
            gy_o[rows, cols] = (ggated * act_s[:, cols]).astype(BF16)
            ggate_o[rows, cols] = (ggated * y_ref[rows, cols].astype(F32) * dact_s[:, cols]).astype(BF16)

    send(out_o, out_h)
    send(ggate_o, ggate_h)
    length = g_ref.shape[0]
    gt = g_ref[...].T
    nt_ = normed[HALO : HALO + length, :].T
    for k in range(2):
        for p in range(half // 256):
            cols = slice(k * half + p * 256, k * half + (p + 1) * 256)
            dst = slice(p * 256, (p + 1) * 256)
            dst2 = slice(half + p * 256, half + (p + 1) * 256)
            by_core(mm(gt, hn_s[:, cols]), keep_o.at[k, :, dst], send_o.at[k, :, dst])
            by_core(mm(nt_, ggate_o[:, cols]), keep_o.at[k, :, dst2], send_o.at[k, :, dst2])
        send(send_o.at[k], send_h.at[k])
        send(keep_o.at[k], keep_h.at[k])
    for one in late:
        one.wait()


def gstate_kernel(length, first_pair, info, gy_ref, coltt, cet, dpt, *refs):
    nb = length // BLOCK
    gs_o, bnd_o = refs[-2:]
    j = pl.program_id(0) + first_pair
    lane = iota((BLOCK, 128), 1)
    top = iota((BLOCK, 128), 0) < 64
    loc = []
    for b in range(nb):
        blk = slice(b * BLOCK, (b + 1) * BLOCK)
        gy = gy_ref[blk, :]
        got = []
        for i in range(2):
            h = 2 * j + i
            e = jnp.where(top, jnp.exp(coltt[b, pl.ds(h, 1), :]), jnp.exp(coltt[b, pl.ds(64 + h, 1), :]))
            got.append((cet[b] * e).astype(BF16))
        got = mm(jnp.concatenate(got, axis=0), gy)
        loc.append(jnp.where(lane < 64, got[0:BLOCK, :], got[BLOCK:, :]))
    state = jnp.zeros((64, 128), F32)
    gs_o[0, nb, 0:64, :] = state.astype(BF16)
    for b in range(nb - 1, -1, -1):
        state = pair_rows(dpt, j, 0, b, 0) * state + loc[b][0:64, :]
        gs_o[0, b, 0:64, :] = state.astype(BF16)
    end_f = state
    state = jnp.zeros((64, 128), F32)
    gs_o[0, 0, 64:128, :] = state.astype(BF16)
    for b in range(nb):
        state = pair_rows(dpt, j, 0, b, 1) * state + loc[b][64:128, :]
        gs_o[0, b + 1, 64:128, :] = state.astype(BF16)
    bnd_o[0] = jnp.where(info[7] == 1, end_f, state).astype(BF16)


def gscan_kernel(
    length, first_pair, info, xc_ref, ds_ref, gy_ref, st_ref, gs_ref, gs0_ref, dpt, rowst, wt, coltt, tc, skip,
    *refs,
):
    nb = length // BLOCK
    gmix_o, ggt_o, gb_o, gct_o, k_o, r_o, phi_o, gskip_o, edge_o, gst_s = refs[-10:]
    step = pl.program_id(0)
    j = step + first_pair
    right = (info[7] == 1).astype(F32)
    s0 = gs0_ref[0].astype(F32)
    sub = iota((BLOCK, BLOCK), 0)
    lane = iota((BLOCK, 128), 1)
    first = lane < 64
    later = lane > sub
    top = sub < 64

    @pl.when(step == 0)
    def _():
        for k, acc in enumerate((ggt_o, gb_o, gct_o, k_o, r_o)):
            acc[...] = jnp.zeros_like(acc) if first_pair else refs[3 + k][...]

    base = row_base(4, [[(0, 128)], [(128, 256)], [(256, 320)], [(320, 384)]])

    phi_o[...] = jnp.zeros_like(phi_o)
    for i in range(nb + 1):
        f = gs_ref[0, i, 0:64, :].astype(F32) + pair_rows(dpt, j, 32, i, 0) * (s0 * (1.0 - right))
        r = gs_ref[0, i, 64:128, :].astype(F32) + pair_rows(dpt, j, 32, i, 1) * (s0 * right)
        f = f.astype(BF16)
        r = r.astype(BF16)
        gst_s[i, 0:64, :] = f
        gst_s[i, 64:128, :] = r
        if i > 0:
            phi_o[i - 1 : i, :] = jnp.sum(f.astype(F32) * st_ref[0, i, 0:64, :].astype(F32), axis=0, keepdims=True)
        if i < nb:
            phi_o[8 + i : 9 + i, :] = jnp.sum(
                r.astype(F32) * st_ref[0, i, 64:128, :].astype(F32), axis=0, keepdims=True
            )
    gskip = jnp.zeros((1, 128), F32)
    for b in range(nb):
        blk = slice(b * BLOCK, (b + 1) * BLOCK)
        xb = xc_ref[blk, :]
        gy = gy_ref[blk, :]
        gyf = gy.astype(F32)
        gskip = gskip + jnp.sum(gyf * xb.astype(F32), axis=0, keepdims=True)
        rhs = jnp.concatenate([gy, gst_s[b + 1, 0:64, :], gst_s[b, 64:128, :]], axis=0)
        left = jnp.concatenate([xb, st_ref[0, b, 0:64, :], st_ref[0, b + 1, 64:128, :]], axis=0)
        first2 = iota((2 * BLOCK, 128), 1) < 64
        none = jnp.zeros_like(left)
        big2 = nt(jnp.concatenate([jnp.where(first2, left, none), jnp.where(first2, none, left)], axis=0), rhs)
        got = []
        sum_ge, sum_gct, sum_gb, kparts = [], [], [], []
        for i in range(2):
            h = 2 * j + i
            terms = column_terms([v[b, pl.ds(at + h, 1), :] for v in (rowst, wt) for at in (0, 64)])
            expo = tn(terms, row_terms(4, base, coltt[b, pl.ds(h, 1), :], coltt[b, pl.ds(64 + h, 1), :]))
            diff = jnp.where(later, expo[:, 0:128], expo[:, 128:256])
            et_m = jnp.exp(jnp.minimum(diff, 60.0))
            mt = et_m * tc[0, b]
            w = jnp.exp(expo[:, 256:])
            bt = tc[1, b] * w
            big = big2[2 * BLOCK * i : 2 * BLOCK * (i + 1), :]
            gmt = big[0:BLOCK, 0:BLOCK]
            gbt = big[0:BLOCK, BLOCK:]
            gctt = big[BLOCK:, 0:BLOCK]
            ge = gmt * et_m
            sum_ge.append(ge)
            q = gmt * mt
            qf = jnp.where(later, q, 0.0)
            e = jnp.where(top, jnp.exp(coltt[b, pl.ds(h, 1), :]), jnp.exp(coltt[b, pl.ds(64 + h, 1), :]))
            gce = gctt * e
            sum_gct.append(gce)
            ct = gce * tc[2, b]
            rf = jnp.sum(qf, axis=0, keepdims=True)
            rall = jnp.sum(q, axis=0, keepdims=True)
            r_o[b, pl.ds(h, 1), :] = rf + jnp.sum(ct[0:64, :], axis=0, keepdims=True)
            r_o[b, pl.ds(64 + h, 1), :] = rall - rf + jnp.sum(ct[64:128, :], axis=0, keepdims=True)
            gbw = gbt * w
            sum_gb.append(gbw)
            u = gbw * tc[1, b]
            kf = jnp.sum(qf + jnp.where(first, u, 0.0), axis=1, keepdims=True)
            kb = jnp.sum(q + u, axis=1, keepdims=True) - kf
            kparts += [kf, kb]
            lhs = jnp.concatenate([mt.astype(BF16), bt.astype(BF16)], axis=1)
            got.append(lhs)
        ggt_o[b] += sum_ge[0] + sum_ge[1]
        gct_o[b] += sum_gct[0] + sum_gct[1]
        gb_o[b] += sum_gb[0] + sum_gb[1]
        two = jnp.where(lane % 64 == 0, jnp.where(first, kparts[0], kparts[1]), jnp.where(first, kparts[2], kparts[3]))
        k_o[blk, :] += pltpu.roll(jnp.where(lane % 64 < 2, two, 0.0), 2 * j, 1)
        got = mm(jnp.concatenate(got, axis=0), rhs)
        gx = jnp.where(first, got[0:BLOCK, :], got[BLOCK:, :]) + skip[0:1, :] * gyf
        gmix = (gx * ds_ref[blk, :].astype(F32)).astype(BF16)
        gmix_o[blk, :] = gmix
        if b == 0:
            edge_o[...] = gmix[0:HALO, :]
        if b == nb - 1:
            edge_o[...] = jnp.where(info[7] == 0, gmix[BLOCK - HALO :, :], edge_o[...])
    gskip_o[...] = jnp.broadcast_to(gskip, (8, 128))


def join_kernel(
    length, heads, info, ggt, gb, gct, k_ref, r_ref, phi, maps, dsl, sig,
    gmb_o, gv_o, small_o, edge_o, gc_s, gm_s,
):
    nb = length // BLOCK
    off = info[5]
    chans = phi.shape[1]
    sub = iota((BLOCK, BLOCK), 0)
    lane = iota((BLOCK, 128), 1)
    first = lane < 64
    low = sub > lane
    high = sub < lane
    upper_strict = high.astype(F32)
    upper = (sub <= lane).astype(F32)
    lower_strict = low.astype(F32)
    lower = (sub >= lane).astype(F32)
    owner = iota((chans, 128), 0) // 64
    to_f = (owner == iota((chans, 128), 1)).astype(F32)
    to_b = (owner + 64 == iota((chans, 128), 1)).astype(F32)
    phi_f = mm(phi[0:8, :], to_f, precision=HIGH)
    phi_b = mm(phi[8:16, :], to_b, precision=HIGH)
    gc_s[...] = jnp.zeros_like(gc_s)
    gm_s[...] = jnp.zeros_like(gm_s)
    sum_bias = jnp.zeros((1, 128), F32)
    sum_rate = jnp.zeros((1, 128), F32)
    for b in range(nb):
        blk = slice(b * BLOCK, (b + 1) * BLOCK)
        ext = slice(HALO + b * BLOCK, HALO + (b + 1) * BLOCK)
        first_pos = off + b * BLOCK
        sp = seg_at(info, sub + first_pos)
        st = seg_at(info, lane + first_pos)
        before = seg_at(info, sub * 0 + (first_pos - 1))
        begin = seg_at(info, sub * 0 + first_pos)
        last = seg_at(info, sub * 0 + (first_pos + BLOCK - 1))
        after = seg_at(info, sub * 0 + (first_pos + BLOCK))
        enter = jnp.where(first, (sp == before).astype(F32), (sp == after).astype(F32))
        keep = jnp.where(first, (sp == last).astype(F32), (sp == begin).astype(F32))
        same = sp == st
        gg = ggt[b]
        gf = jnp.where(same & high, gg, 0.0).astype(BF16)
        gr = jnp.where(same & low, gg, 0.0).astype(BF16)
        cm = maps[blk, 128:256]
        bm = maps[blk, 0:128]
        gm_s[ext, 0:128] = jnp.where(first, mm(gf, cm), mm(gr, cm)) + gb[b] * keep
        gc_s[ext, :] = jnp.where(first, tn(gf, bm), tn(gr, bm)) + gct[b].T * enter
        kb = k_ref[blk, :]
        rb = r_ref[b].T
        ga_f = mm(upper_strict, rb, precision=HIGH) - mm(upper, kb, precision=HIGH) + phi_f[b : b + 1, :]
        ga_b = mm(lower_strict, rb, precision=HIGH) - mm(lower, kb, precision=HIGH) + phi_b[b : b + 1, :]
        ga = jnp.where(first, ga_f, ga_b)
        gv = kb * sig[blk, 128:256] + ga * sig[blk, 0:128]
        gv_o[blk, :] = gv.astype(BF16)
        sum_bias = sum_bias + jnp.sum(gv, axis=0, keepdims=True)
        sum_rate = sum_rate + jnp.sum(ga * sig[blk, 256:384], axis=0, keepdims=True)
    small_o[...] = jnp.zeros_like(small_o)
    small_o[0:1, :] = sum_bias
    small_o[1:2, :] = sum_rate
    small_o[8:9, :] = pltpu.roll(sum_bias, 128 - heads // 2, 1)
    small_o[9:10, :] = pltpu.roll(sum_rate, 128 - heads // 2, 1)
    mid = length + HALO
    lo = HALO // 2
    pos = iota((mid, 128), 0) + (off - HALO + lo)
    seg0 = seg_at(info, pos)
    segn = seg_at(info, pos + 1)
    segp = seg_at(info, pos - 1)
    from_next = jnp.where(seg0 == segn, gc_s[lo + 1 : lo + 1 + mid, :], 0.0)
    from_prev = jnp.where(seg0 == segp, gc_s[lo - 1 : lo - 1 + mid, :], 0.0)
    gm_s[lo : lo + mid, 128:256] = jnp.where(iota((mid, 128), 1) < 64, from_next, from_prev)
    gmb_o[...] = gm_s[...] * dsl[...]
    lo = HALO // 2
    edge_o[...] = jnp.where(
        info[7] == 0, gmb_o[length + lo : length + lo + HALO, :], gmb_o[lo : lo + HALO, :]
    )


def back_conv(length, seg_s, live, grad, data, tap):
    own = slice(HALO, HALO + length)
    seg0 = seg_s[own, :]
    mine = grad[own, :]
    total = mine * tap[3:4, :]
    gtap = [None] * 7
    gtap[3] = jnp.sum(mine * data[own, :], axis=0, keepdims=True)
    for k in (0, 1, 2, 4, 5, 6):
        lo = HALO + 3 - k
        same = seg_s[lo : lo + length, :] == seg0
        total = total + jnp.where(same, grad[lo : lo + length, :], 0.0) * tap[k : k + 1, :]
        up = HALO + k - 3
        same = seg_s[up : up + length, :] == seg0
        gtap[k] = jnp.sum(jnp.where(same, data[up : up + length, :], 0.0) * mine, axis=0, keepdims=True)
    return jnp.where(live, total, 0.0), gtap


def back_kernel(
    length, steps, info, gmix, edge_a, edge_b, vm, normed, taps, ggain, gskip,
    gvals_o, keep_o, send_o, tiny_o, ext_s, vm_s, seg_s, turned_s,
):
    ext = length + 2 * HALO
    off, count = info[5], info[4]
    own = slice(HALO, HALO + length)
    seg_s[...] = seg_at(info, iota((ext, 128), 0) + (off - HALO))
    tiny_o[...] = jnp.zeros_like(tiny_o)
    turned_s[...] = normed[own, :].T
    live = iota((length, 128), 0) + off < count
    right = info[7] == 1
    per = steps // 2

    @pl.loop(0, steps)
    def _(j):
        near = j < per
        half = j // per
        at = (j % per) * 256
        both = []
        for p in range(2):
            here = pl.ds(pl.multiple_of(at + 128 * p, 128), 128)
            cols = pl.ds(pl.multiple_of(j * 256 + 128 * p, 128), 128)
            ext_s[own, :] = gmix[:, cols].astype(F32)
            halo = jnp.where(near, edge_a[:, here].astype(F32), edge_b[:, here].astype(F32))
            ext_s[0:HALO, :] = jnp.where(right, halo, 0.0)
            ext_s[HALO + length : ext, :] = jnp.where(right, 0.0, halo)
            vm_s[...] = vm[:, cols].astype(F32)
            gvals, gtap = back_conv(length, seg_s, live, ext_s, vm_s, taps[:, cols])
            both.append(gvals.astype(BF16))
            for t in range(7):
                tiny_o[half, t : t + 1, here] = gtap[t]
            tiny_o[half, 7:8, here] = ggain[0:1, cols]
            tiny_o[half, 8:9, here] = gskip[0:1, cols]
        both = jnp.concatenate(both, axis=1)
        gvals_o[:, pl.ds(pl.multiple_of(j * 256, 256), 256)] = both
        here = pl.ds(pl.multiple_of(at, 256), 256)
        by_core(mm(turned_s[...], both), keep_o.at[half, :, here], send_o.at[half, :, here])


def last_kernel(
    length, hl, info, gvals, ggate, w_ref, wv_b, wg_b, normed, gmb, edge, bcm, taps_bc, gv, wdt, wbc, x_ref, g_ref, rs, pre,
    small, tiny, keep_o, send_o, tiny_o, gin_o, ext_s, vm_s, seg_s,
):
    ext = length + 2 * HALO
    ch = hl * HD
    off, count = info[5], info[4]
    own = slice(HALO, HALO + length)
    seg_s[...] = seg_at(info, iota((ext, 128), 0) + (off - HALO))
    live = iota((length, 128), 0) + off < count
    tiny_o[...] = tiny[...]
    for half in range(2):
        tiny_o[half, 10:11, 0:128] = small[8 * half : 8 * half + 1, :]
        tiny_o[half, 10:11, 128:256] = small[8 * half + 1 : 8 * half + 2, :]
    both = []
    for k in range(2):
        cols = slice(k * 128, (k + 1) * 128)
        ext_s[...] = gmb[:, cols]
        lo = HALO // 2
        hi = length + lo
        got = edge[:, cols]
        ext_s[lo : lo + HALO, :] += jnp.where(info[7] == 1, got, 0.0)
        ext_s[hi : hi + HALO, :] += jnp.where(info[7] == 1, 0.0, got)
        vm_s[...] = bcm[:, cols]
        gbc, gtap = back_conv(length, seg_s, live, ext_s, vm_s, taps_bc[:, cols])
        for t in range(7):
            at = (t % 3) * 256 + k * 128
            for half in range(2):
                tiny_o[half, 11 + t // 3 : 12 + t // 3, at : at + 128] = gtap[t]
        both.append(gbc.astype(BF16))
    gbc = jnp.concatenate(both + [gv[...]], axis=1)
    gw = tn(normed[own, :], gbc)
    by_core(gw, keep_o.at[0], send_o.at[0])
    turned = pltpu.roll(gw[:, 256:], 128 - hl, 1)
    by_core(jnp.concatenate([gw[:, 0:256], turned], axis=1), keep_o.at[1], send_o.at[1])
    wv_a = jnp.concatenate([w_ref[h, HD : 2 * HD, :] for h in range(hl)], axis=0)
    wg_a = jnp.concatenate([w_ref[h, 0:HD, :] for h in range(hl)], axis=0)
    gn = mm(gvals[:, 0:ch], wv_a) + mm(gvals[:, ch:], wv_b[...])
    gn = gn + mm(ggate[:, 0:ch], wg_a) + mm(ggate[:, ch:], wg_b[...])
    gn = gn + nt(gbc[:, 0:256], wbc[...]) + mm(gv[...], wdt[...])
    x = x_ref[...].astype(F32)
    r = rs[...]
    wp = gn * pre[...]
    mean = jnp.mean(wp * x, axis=1, keepdims=True)
    gin_o[...] = g_ref[...].astype(F32) + r * wp - x * (r * r * r * mean)
    gpre = jnp.sum(gn * x * r, axis=0, keepdims=True)
    for half in range(2):
        tiny_o[half, 9:10, 0 : gpre.shape[1]] = gpre


def finish_kernel(hl, tiny, total, wb, heads_o, wout_o, bc_o, conv_o, convbc_o, pre_o, bias_o, rate_o, skip_o, gain_o):
    ch = tiny.shape[1]
    w = lax.axis_index("wide")
    share = pre_o.shape[1]
    lanes = gain_o.shape[0]
    dm = total.shape[1] - ch
    for h in range(hl):
        cols = slice(h * HD, (h + 1) * HD)
        wout_o[h] = total[:, cols]
        heads_o[h, :, 0:HD] = total[:, dm + h * HD : dm + (h + 1) * HD]
        heads_o[h, :, HD : 2 * HD] = wb[:, cols]
        heads_o[h, :, 2 * HD : 2 * HD + 1] = wb[:, ch + 256 + h : ch + 257 + h]
        heads_o[h, :, 2 * HD + 1 :] = wb[:, ch + 320 + h : ch + 321 + h]
    bc_o[...] = pack_columns(wb[:, ch : ch + 256])
    rows = tiny[...]
    src = iota((ch, 128), 0)
    dst = iota((ch, 128), 1)
    for q in range(lanes):
        chosen = ((src == dst * HD + lanes * w + q) & (dst < hl)).astype(F32)
        got = mm(rows, chosen, precision=HIGH)
        for k in range(7):
            conv_o[k, q : q + 1, :] = got[k : k + 1, 0:hl]
        gain_o[q : q + 1, :] = got[7:8, 0:hl]
    chosen = ((src == share * w + dst) & (dst < share)).astype(F32)
    pre_o[...] = mm(rows[8:16, :], chosen, precision=HIGH)[1:2, 0:share]
    per = (src // HD == dst).astype(F32)
    skip_o[...] = mm(rows[8:16, :], per, precision=HIGH)[0:1, 0:hl]
    size = convbc_o.shape[1]
    group = (size * w) // 64
    start = ((group % 2) * 2 + group // 2) * 64 + (size * w) % 64
    src = iota((256, 128), 0)
    dst = iota((256, 128), 1)
    chosen = ((src == start + dst) & (dst < size)).astype(F32)
    for k in range(3):
        part = mm(rows[8:16, 256 * k : 256 * (k + 1)], chosen, precision=HIGH)
        for r in range(3):
            if 3 * r + k < 7:
                convbc_o[3 * r + k : 3 * r + k + 1, :] = part[3 + r : 4 + r, 0:size]
    both = rows[10:11, 0:128]
    bias_o[0:1, :] = both[:, 0:hl]
    bias_o[1:2, :] = pltpu.roll(both, 64, 1)[:, 0:hl]
    rate = rows[10:11, 128:256]
    rate_o[...] = (rate + pltpu.roll(rate, 64, 1))[:, 0:hl]


def collect_kernel(
    keep, got_v, keep_bc, send_bc, tiny, plane_a, out_o, tiny_o, a_o,
    core_s, left_s, right_s, left_out, left_in, right_out, right_in, left2_out, left2_in, right2_out, right2_in,
    zsend_s, zgot_s, tcore_s, tsum_s, tgot_s, tz_s, tzgot_s, agot_s,
    core_sem, one_sem, two_sem, tiny_sem, z_sem, core_rem, one_rem, two_rem, tiny_rem, z_rem,
):
    w = lax.axis_index("wide")
    n = lax.axis_index("narrow")
    c, xx, z = w % 2, (w // 2) % 2, w // 4
    share, cols = out_o.shape
    chv = keep.shape[2]
    cut = left_s.shape[3]
    core = (w + 1 - 2 * c, n)
    over_x = (w + 2 - 4 * xx, n)
    over_y = (w, 1 - n)
    over_d = (w + 2 - 4 * xx, 1 - n)
    steps = (2, 1, 3)
    over_z = [(((z + d) % 4) * 4 + w % 4, n) for d in steps]
    mesh_ids = pl.DeviceIdType.MESH
    barrier = pltpu.get_barrier_semaphore()
    for other in [core, over_x, over_y, over_d] + over_z:
        pl.semaphore_signal(barrier, inc=1, device_id=other, device_id_type=mesh_ids)
    pl.semaphore_wait(barrier, 7)

    def copy(src, dst, out_sem, in_sem, other):
        got = pltpu.make_async_remote_copy(
            src_ref=src, dst_ref=dst, send_sem=out_sem, recv_sem=in_sem, device_id=other, device_id_type=mesh_ids
        )
        got.start()
        return got

    rows = [pl.ds(pl.multiple_of(((z + d) % 4) * (2 * share), 2 * share), 2 * share) for d in steps + (0,)]
    first = [copy(tiny, tcore_s, core_sem.at[4], core_rem.at[4], core)]
    for i in range(4):
        first.append(copy(send_bc.at[:, rows[i], :], core_s.at[i], core_sem.at[i], core_rem.at[i], core))
    a_copies = [
        copy(plane_a.at[(z + steps[k]) % 4], agot_s.at[k], z_sem.at[2, k], z_rem.at[2, k], over_z[k]) for k in range(3)
    ]
    first[0].wait()
    tsum_s[...] = tiny[...] + tcore_s[...]
    small = []
    for k, other in enumerate((over_x, over_y, over_d)):
        half = 0 if k == 0 else 1
        small.append(copy(tsum_s.at[half], tgot_s.at[k], tiny_sem.at[k], tiny_rem.at[k], other))
    second = []
    for i in range(4):
        first[i + 1].wait()
        both = jnp.concatenate(
            [
                keep[:, rows[i], :].astype(F32) + got_v[:, rows[i], :].astype(F32),
                keep_bc[:, rows[i], :].astype(F32) + core_s[i].astype(F32),
            ],
            axis=2,
        )
        low, high = both[:, 0:share, :], both[:, share:, :]
        near = jnp.where(xx == 0, low, high)
        far = jnp.where(xx == 0, high, low)
        left_s[i] = near[:, :, 0:cut]
        right_s[i, 0] = near[0, :, cut:]
        right_s[i, 1] = far[0, :, cut:]
        left_out[i] = far[:, :, 0:cut].astype(BF16)
        right_out[i, 0] = near[1, :, cut:].astype(BF16)
        right_out[i, 1] = far[1, :, cut:].astype(BF16)
        second.append(
            (
                copy(left_out.at[i], left_in.at[i], one_sem.at[i, 0], one_rem.at[i, 0], over_x),
                copy(right_out.at[i], right_in.at[i], one_sem.at[i, 1], one_rem.at[i, 1], over_y),
            )
        )
    for one in small:
        one.wait()
    tsum = tsum_s[0] + tgot_s[0] + tgot_s[1] + tgot_s[2]
    tz_s[...] = tsum
    last = [copy(tz_s, tzgot_s.at[k], z_sem.at[1, k], z_rem.at[1, k], over_z[k]) for k in range(3)]
    third = []
    for i in range(4):
        second[i][0].wait()
        left_s[i] = left_s[i] + left_in[i].astype(F32)
        left2_out[i] = left_s[i, 1].astype(BF16)
        go_left = copy(left2_out.at[i], left2_in.at[i], two_sem.at[i, 0], two_rem.at[i, 0], over_y)
        second[i][1].wait()
        right_s[i] = right_s[i] + right_in[i].astype(F32)
        right2_out[i] = right_s[i, 1].astype(BF16)
        go_right = copy(right2_out.at[i], right2_in.at[i], two_sem.at[i, 1], two_rem.at[i, 1], over_x)
        third.append((go_left, go_right))
    for i in range(4):
        third[i][0].wait()
        third[i][1].wait()
        left = left_s[i, 0] + left2_in[i].astype(F32)
        right = right_s[i, 0] + right2_in[i].astype(F32)
        if i < 3:
            zsend_s[i, :, 0:cut] = left.astype(BF16)
            zsend_s[i, :, cut:] = right.astype(BF16)
            last.append(copy(zsend_s.at[i], zgot_s.at[i], z_sem.at[0, i], z_rem.at[0, i], over_z[i]))
        else:
            out_o[:, 0:cut] = left
            out_o[:, cut:] = right
    for one in a_copies:
        one.wait()
    a_o[...] = plane_a[z].astype(F32) + agot_s[0].astype(F32) + agot_s[1].astype(F32) + agot_s[2].astype(F32)
    for one in last:
        one.wait()
    out_o[...] = out_o[...] + zgot_s[0].astype(F32) + zgot_s[1].astype(F32) + zgot_s[2].astype(F32)
    tiny_o[...] = tsum + tzgot_s[0] + tzgot_s[1] + tzgot_s[2]


def whole(shape, grid):
    zeros = (0,) * len(shape)
    if grid:
        return pl.BlockSpec(shape, lambda j: zeros)
    return pl.BlockSpec(shape, lambda: zeros)


def columns(rows, first=0):
    return pl.BlockSpec((rows, 128), lambda j: (0, first + j))


SMEM = pl.BlockSpec(memory_space=pltpu.SMEM)
VMEM = pl.BlockSpec(memory_space=pltpu.VMEM)
ANY = pl.BlockSpec(memory_space=pl.ANY)
HBM = pl.BlockSpec(memory_space=pltpu.HBM)


def sds(shape, dtype):
    return jax.ShapeDtypeStruct(shape, dtype)


def params(grid, mib):
    if grid:
        return pltpu.CompilerParams(vmem_limit_bytes=mib * 2**20, dimension_semantics=("arbitrary",))
    return pltpu.CompilerParams(vmem_limit_bytes=mib * 2**20)


def cost(us):
    return pl.CostEstimate(flops=int(us * 1.1e9), bytes_accessed=int(us * 1e6), transcendentals=0)


def pack_columns(v):
    n = v.shape[-1] // 4
    return jnp.concatenate([v[..., 0:n], v[..., 2 * n : 3 * n], v[..., n : 2 * n], v[..., 3 * n :]], axis=-1)


def small_kernel(hl, conv, gain, dtb, alog, skip, wdt, start_ref, end_ref, out_o):
    ch = out_o.shape[1]
    lane = iota((1, 128), 1)
    wide_lane = iota((1, ch), 1)
    bias = jnp.zeros((1, 128), F32)
    rate = jnp.zeros((1, 128), F32)
    diag = jnp.zeros((1, ch), F32)
    out_o[0:16, :] = jnp.zeros((16, ch), F32)
    for h in range(hl):
        cols = slice(h * HD, (h + 1) * HD)
        out_o[0:7, cols] = conv[h]
        out_o[7:8, cols] = gain[h : h + 1, :]
        bias = jnp.where(lane == h, dtb[0, h], jnp.where(lane == 64 + h, dtb[1, h], bias))
        rate = jnp.where((lane == h) | (lane == 64 + h), alog[h], rate)
        diag = jnp.where(wide_lane // HD == h, skip[h], diag)
        out_o[16 + 2 * h : 18 + 2 * h, :] = wdt[h].astype(F32)[0:2, :]
    out_o[8:9, :] = diag
    out_o[9:10, 0:128] = bias
    out_o[9:10, 128:256] = rate
    n = lax.axis_index("narrow")
    start, end = start_ref[...].astype(F32), end_ref[...].astype(F32)
    out_o[16 + 2 * hl :, :] = jnp.where(n == 0, end[8:16, :], start[0:8, :])


def swap(v):
    return lax.ppermute(v, "narrow", [(0, 1), (1, 0)])


def flip(v, bit, wide):
    return lax.ppermute(v, "wide", [(i, i ^ bit) for i in range(wide)])


def cross(v, bit, wide):
    pairs = [(i * 2 + k, (i ^ bit) * 2 + 1 - k) for i in range(wide) for k in range(2)]
    return lax.ppermute(v, ("wide", "narrow"), pairs)


def total(*parts):
    acc = parts[0].astype(F32)
    for v in parts[1:]:
        acc = acc + v.astype(F32)
    return acc


def split_positions(
    wide, layer_in, pre_gain, w_heads, w_bc, conv_x, conv_bc, dt_bias, a_log, skip_d, norm_gain, w_out, cotangent, starts, live
):
    n = lax.axis_index("narrow")
    w = lax.axis_index("wide")
    left = n == 0
    _, length, dm = layer_in.shape
    hl = w_heads.shape[1]
    heads = 2 * hl
    ch = hl * HD
    chans = 2 * ch
    pairs = heads // 2
    hp = pairs // 2
    nb = length // BLOCK
    ext = length + 2 * HALO
    share = dm // wide
    x = layer_in[0]
    g = cotangent[0]
    xbit = (w // 2) % 2

    w_turned = jnp.transpose(w_heads, (1, 2, 0))
    small_own = pl.pallas_call(
        functools.partial(small_kernel, hl),
        grid=(1,),
        out_shape=sds((24 + 2 * hl, ch), F32),
        in_specs=[
            whole((hl, 7, HD), 1), whole((hl, HD), 1), SMEM, SMEM, SMEM, pl.BlockSpec((hl, 16, dm), lambda j: (0, 8, 0)),
            pl.BlockSpec((HALO, dm), lambda j: (0, 0)), pl.BlockSpec((HALO, dm), lambda j: (length // HALO - 1, 0)),
        ],
        out_specs=whole((24 + 2 * hl, ch), 1),
        cost_estimate=cost(2),
        name="small",
    )(jnp.transpose(conv_x, (1, 0, 2)), norm_gain, dt_bias.T, a_log, skip_d, w_turned, x, x)
    small_other = swap(small_own)

    quarter = ch // 4
    q = w % 4

    def gather(p0):
        p1 = flip(p0, 2, wide)
        return p0, p1, flip(p0, 1, wide), flip(p1, 1, wide)

    def heads_rows(lo):
        return lax.dynamic_slice(w_turned, (q * (hl // 4), lo, 0), (hl // 4, HD, dm)).reshape(quarter, dm)

    wo = w_out.reshape(ch, dm)
    wv_first = swap(heads_rows(HD))
    wo_rows = lax.dynamic_slice(wo, (q * quarter, 0), (quarter, dm))
    wog_pieces = gather(swap(jnp.concatenate([wo_rows, heads_rows(0)], axis=1)))

    pos = (length, 128)
    sq = (nb, BLOCK, BLOCK)
    front_shapes = [
        ((8, chans), F32), ((8, chans), F32), ((8, chans), F32), ((128, dm), BF16), ((dm, 256), BF16), ((7, 256), F32),
        ((ext, dm), BF16), ((length, 1), F32), ((ext, 256), F32), ((ext, 256), F32), ((length, 256), BF16),
        ((2,) + sq, F32), ((4,) + sq, F32), ((3,) + sq, F32), ((128, 128), F32), ((length, 384), F32),
    ]
    late_front = (8, 9, 10, 13, 15)
    (
        info, taps, gain, skip, wdt_all, wbc, taps_bc, normed, rs, bcm, dsl, maps, tab_a, tab_b, tab_c, dpt, sig,
    ) = pl.pallas_call(
        functools.partial(front_kernel, length, hl),
        out_shape=[sds((8,), jnp.int32)]
        + [pltpu.HBM(*v) if k in late_front else sds(*v) for k, v in enumerate(front_shapes)],
        in_specs=[SMEM] + [VMEM] * 7,
        out_specs=[SMEM] + [HBM if k in late_front else VMEM for k in range(len(front_shapes))],
        scratch_shapes=[
            pltpu.VMEM((ext, 256), jnp.int32), pltpu.VMEM((ext, 256), F32), pltpu.VMEM((128, 128), F32),
            pltpu.VMEM((ext, dm), BF16),
        ]
        + [pltpu.VMEM(*front_shapes[k]) for k in late_front]
        + [pltpu.SemaphoreType.DMA((len(late_front),))],
        compiler_params=params(False, 14),
        cost_estimate=cost(6),
        name="front",
    )(starts, live, x, pre_gain.reshape(1, dm), w_bc, conv_bc, small_own, small_other)

    wv_first, normed = lax.optimization_barrier((wv_first, normed))
    wv_over_x = flip(wv_first, 2, wide)

    def states(first):
        return pl.BlockSpec((1, nb + 1, 128, 128), lambda j: (j + first, 0, 0, 0))

    bnd_spec = pl.BlockSpec((1, 64, 128), lambda j: (j, 0, 0))
    state_shape = sds((pairs, nb + 1, 128, 128), BF16)
    bnd_shape = sds((hp, 64, 128), BF16)
    act_shape = sds((length, chans), BF16)
    def twin(rows, first):
        return pl.BlockSpec((rows, 256), lambda j: (0, first + j))

    def vals(other, weights, before):
        steps = hp // 2
        first = steps if other else 0
        specs = [SMEM, whole((ext, dm), 1)]
        specs += [whole((quarter, dm), 1)] * 4 if other else [pl.BlockSpec((4, 2 * HD + 2, dm), lambda j: (j, 0, 0))]
        specs += [twin(8, first), whole((2,) + sq, 1), whole((128, 128), 1)] + [ANY] * len(before)
        return pl.pallas_call(
            functools.partial(vals_kernel, length, other),
            grid=(steps,),
            out_shape=[act_shape, sds((ext, chans), BF16), act_shape, state_shape, bnd_shape] + [sds((ch, dm), BF16)] * other,
            in_specs=specs,
            out_specs=[
                twin(length, first), twin(ext, first), twin(length, first),
                pl.BlockSpec((2, nb + 1, 128, 128), lambda j: (j + first, 0, 0, 0)),
                pl.BlockSpec((2, 64, 128), lambda j: (j, 0, 0)),
            ] + [whole((ch, dm), 1)] * other,
            scratch_shapes=[pltpu.VMEM((ext, 128), F32), pltpu.VMEM((ext, 128), F32), pltpu.VMEM((ext, 128), jnp.int32)],
            input_output_aliases={len(specs) - len(before) + i: i for i in range(len(before))},
            compiler_params=params(True, 10),
            cost_estimate=cost(9),
            name="vals_other" if other else "vals_own",
        )(info, normed, *weights, taps, tab_a, dpt, *before)

    *own_vals, bnd_own = vals(False, (w_turned,), ())
    bnd_own, wv_over_x = lax.optimization_barrier((bnd_own, wv_over_x))
    wv_pieces = wv_first, wv_over_x, flip(wv_first, 1, wide), flip(wv_over_x, 1, wide)
    xc, vm, ds, s_loc, bnd_other, wv_other = vals(True, wv_pieces, own_vals)

    def aliases(specs, before):
        return {len(specs) - len(before) + i: i for i in range(len(before))}

    def scan(first, s0, before):
        specs = [
            SMEM, columns(length, first), states(first), bnd_spec, whole((128, 128), 1), whole((4,) + sq, 1), columns(8, first),
        ] + [ANY] * len(before)
        return pl.pallas_call(
            functools.partial(scan_kernel, length, first),
            grid=(hp,),
            out_shape=[act_shape, state_shape],
            in_specs=specs,
            out_specs=[columns(length, first), states(first)],
            input_output_aliases=aliases(specs, before),
            compiler_params=params(True, 5),
            cost_estimate=cost(10),
            name="scan_other" if first else "scan_own",
        )(info, xc, s_loc, s0, dpt, tab_b, skip, *before)

    y, s_true = scan(0, swap(bnd_other), scan(hp, swap(bnd_own), ()))

    gw_shape = (2, dm // 2, dm + ch)
    out, gy, keep_a, send_a, ggate, ggain, wg_other = pl.pallas_call(
        functools.partial(gate_kernel, nb),
        out_shape=[
            pltpu.HBM((length, dm), BF16), act_shape, pltpu.HBM(gw_shape, BF16), pltpu.HBM(gw_shape, BF16),
            pltpu.HBM((length, chans), BF16), sds((8, chans), F32), pltpu.HBM((ch, dm), BF16),
        ],
        in_specs=[VMEM] * 11,
        out_specs=[HBM, VMEM, HBM, HBM, HBM, VMEM, HBM],
        scratch_shapes=[pltpu.VMEM((length, chans), BF16), pltpu.VMEM((ch, 2 * dm), BF16)]
        + [pltpu.VMEM((BLOCK, chans), F32)] * 4
        + [pltpu.VMEM((length, dm), BF16), pltpu.VMEM(gw_shape, BF16), pltpu.VMEM(gw_shape, BF16)]
        + [pltpu.VMEM((length, chans), BF16), pltpu.SemaphoreType.DMA((7,))],
        compiler_params=params(False, 22),
        cost_estimate=cost(17),
        name="gated",
    )(x, g, normed, y, wo, w_turned, *wog_pieces, gain)

    def meet(keep, got):
        cols = keep.shape[-1]
        keep = keep.reshape(2, wide // 4, 2, share, cols)
        got = got.reshape(2, wide // 4, 2, share, cols)

        def piece(half, xx):
            def cut(v):
                return lax.dynamic_slice(v, (half, 0, xx, 0, 0), (1, wide // 4, 1, share, cols)).reshape(-1, share, cols)

            return total(cut(keep), cut(got)).astype(BF16)

        return piece(0, xbit), piece(0, 1 - xbit), piece(1, xbit), piece(1, 1 - xbit)

    def plane(mine, to_x, to_y, to_d):
        return total(mine, flip(to_x, 2, wide), swap(to_y), cross(to_d, 2, wide)).astype(mine.dtype)

    a_pieces = meet(keep_a, flip(send_a, 1, wide))

    def table(k):
        return pl.BlockSpec((None,) + sq, lambda j: (k, 0, 0, 0))

    def gstate(first, before):
        specs = [SMEM, columns(length, first), table(0), table(2), whole((128, 128), 1)] + [ANY] * len(before)
        return pl.pallas_call(
            functools.partial(gstate_kernel, length, first),
            grid=(hp,),
            out_shape=[state_shape, bnd_shape],
            in_specs=specs,
            out_specs=[states(first), bnd_spec],
            input_output_aliases=aliases(specs, before),
            compiler_params=params(True, 4),
            cost_estimate=cost(5),
            name="gstate_other" if first else "gstate_own",
        )(info, gy, tab_b, tab_c, dpt, *before)

    gs_loc, gbnd_own = gstate(0, ())
    gs_loc, gbnd_other = gstate(hp, (gs_loc,))

    gs_loc, gbnd_other, *a_pieces = lax.optimization_barrier((gs_loc, gbnd_other, *a_pieces))
    a_plane = plane(*a_pieces)

    def gscan(first, gs0, before):
        sums = [whole(sq, 1), whole(sq, 1), whole(sq, 1), whole(pos, 1), whole(sq, 1)]
        specs = [
            SMEM, columns(length, first), columns(length, first), columns(length, first), states(first), states(first),
            bnd_spec, whole((128, 128), 1), table(1), table(0), table(0), whole((3,) + sq, 1), columns(8, first),
        ]
        at = len(specs)
        if before:
            specs += [ANY] * 3 + sums
        return pl.pallas_call(
            functools.partial(gscan_kernel, length, first),
            grid=(hp,),
            out_shape=[
                act_shape, sds(sq, F32), sds(sq, F32), sds(sq, F32), sds(pos, F32), sds(sq, F32), sds((16, chans), F32),
                sds((8, chans), F32), sds((HALO, ch), BF16),
            ],
            in_specs=specs,
            out_specs=[columns(length, first)] + sums + [columns(16, first), columns(8, first), columns(HALO)],
            scratch_shapes=[pltpu.VMEM((nb + 1, 128, 128), BF16)],
            input_output_aliases={at: 0, at + 1: 6, at + 2: 7} if before else {},
            compiler_params=params(True, 7),
            cost_estimate=cost(17),
            name="gscan_other" if first else "gscan_own",
        )(info, xc, ds, gy, s_true, gs_loc, gs0, dpt, tab_b, tab_a, tab_b, tab_c, skip, *before)

    gmix, ggt, gb, gct, ksum, rsum, phi, gskip, edge_other = gscan(hp, swap(gbnd_own), ())
    gmix, ggt, gb, gct, ksum, rsum, phi, gskip, edge_own = gscan(
        0, swap(gbnd_other), (gmix, phi, gskip, ggt, gb, gct, ksum, rsum)
    )

    gmix, ggt, a_plane = lax.optimization_barrier((gmix, ggt, a_plane))

    gmb, gv, small, edge_bc = pl.pallas_call(
        functools.partial(join_kernel, length, heads),
        out_shape=[sds((ext, 256), F32), sds(pos, BF16), sds((16, 128), F32), sds((HALO, 256), F32)],
        in_specs=[SMEM] + [VMEM] * 9,
        out_specs=[VMEM] * 4,
        scratch_shapes=[pltpu.VMEM((ext, 128), F32), pltpu.VMEM((ext, 256), F32)],
        compiler_params=params(False, 6),
        cost_estimate=cost(6),
        name="join",
    )(info, ggt, gb, gct, ksum, rsum, phi, maps, dsl, sig)

    edge_a, edge_b = swap(edge_other), swap(edge_own)
    edge_bc = swap(edge_bc)
    sum_shape = (2, dm // 2, ch)
    gvals, keep_v, send_v, tiny = pl.pallas_call(
        functools.partial(back_kernel, length, pairs // 2),
        out_shape=[act_shape, sds(sum_shape, BF16), sds(sum_shape, BF16), sds((2, 16, ch), F32)],
        in_specs=[SMEM] + [VMEM] * 8,
        out_specs=[VMEM] * 4,
        scratch_shapes=[
            pltpu.VMEM((ext, 128), F32), pltpu.VMEM((ext, 128), F32), pltpu.VMEM((ext, 128), jnp.int32),
            pltpu.VMEM((dm, length), BF16),
        ],
        compiler_params=params(False, 10),
        cost_estimate=cost(12),
        name="back",
    )(info, gmix, edge_a, edge_b, vm, normed, taps, ggain, gskip)

    got_v = flip(send_v, 1, wide)
    keep_bc, send_bc, tiny, grad_in = pl.pallas_call(
        functools.partial(last_kernel, length, hl),
        out_shape=[
            sds((2, dm // 2, 384), BF16), sds((2, dm // 2, 384), BF16), sds((2, 16, ch), F32), sds((length, dm), F32),
        ],
        in_specs=[SMEM] + [VMEM] * 19,
        out_specs=[VMEM] * 4,
        scratch_shapes=[pltpu.VMEM((ext, 128), F32), pltpu.VMEM((ext, 128), F32), pltpu.VMEM((ext, 128), jnp.int32)],
        compiler_params=params(False, 12),
        cost_estimate=cost(8),
        name="last",
    )(
        info, gvals, ggate, w_turned, wv_other, wg_other, normed, gmb, edge_bc, bcm, taps_bc, gv, wdt_all, wbc, x, g, rs,
        pre_gain.reshape(1, dm), small, tiny,
    )

    cols = ch + 384
    cut = 5 * cols // 9
    rest = cols - cut
    wb, tiny, wa = pl.pallas_call(
        collect_kernel,
        out_shape=[sds((share, cols), F32), sds((16, ch), F32), sds((share, dm + ch), F32)],
        in_specs=[VMEM] * 6,
        out_specs=[VMEM] * 3,
        scratch_shapes=[
            pltpu.VMEM((4, 2, 2 * share, 384), BF16),
            pltpu.VMEM((4, 2, share, cut), F32),
            pltpu.VMEM((4, 2, share, rest), F32),
        ]
        + [pltpu.VMEM((4, 2, share, cut), BF16)] * 2
        + [pltpu.VMEM((4, 2, share, rest), BF16)] * 2
        + [pltpu.VMEM((4, share, cut), BF16)] * 2
        + [pltpu.VMEM((4, share, rest), BF16)] * 2
        + [
            pltpu.VMEM((3, share, cols), BF16),
            pltpu.VMEM((3, share, cols), BF16),
            pltpu.VMEM((2, 16, ch), F32),
            pltpu.VMEM((2, 16, ch), F32),
            pltpu.VMEM((3, 16, ch), F32),
            pltpu.VMEM((16, ch), F32),
            pltpu.VMEM((3, 16, ch), F32),
            pltpu.VMEM((3, share, dm + ch), BF16),
        ]
        + [pltpu.SemaphoreType.DMA(v) for v in ((5,), (4, 2), (4, 2), (3,), (3, 3)) * 2],
        compiler_params=pltpu.CompilerParams(collective_id=0, has_side_effects=True, vmem_limit_bytes=14 * 2**20),
        name="collect",
    )(keep_v, got_v, keep_bc, send_bc, tiny, a_plane)

    g_w_heads, g_w_out, g_w_bc, g_conv_x, g_conv_bc, g_pre, g_bias, g_rate, g_skip, g_gain = pl.pallas_call(
        functools.partial(finish_kernel, hl),
        out_shape=[
            sds((hl, share, 2 * HD + 2), F32), sds((hl, share, HD), F32), sds((share, 256), F32), sds((7, HD // wide, hl), F32),
            sds((7, 256 // wide), F32), sds((1, share), F32), sds((2, hl), F32), sds((1, hl), F32), sds((1, hl), F32),
            sds((HD // wide, hl), F32),
        ],
        in_specs=[VMEM] * 3,
        out_specs=[VMEM] * 10,
        compiler_params=params(False, 8),
        name="finish",
    )(tiny, wa, wb)
    return (
        out[None],
        grad_in[None],
        g_pre[0],
        jnp.transpose(g_w_heads, (1, 0, 2)),
        g_w_bc,
        jnp.transpose(g_conv_x, (0, 2, 1)),
        g_conv_bc,
        g_bias.T,
        g_rate[0],
        g_skip[0],
        g_gain.T,
        jnp.transpose(g_w_out, (0, 2, 1)),
    )


def solution(mesh):
    body = shards
    if mesh.shape["narrow"] == 2 and mesh.shape["wide"] == 16:
        body = functools.partial(split_positions, mesh.shape["wide"])
    return jax.shard_map(
        body,
        mesh=mesh,
        in_specs=(
            P("wide", "narrow", None),
            P(),
            P(None, "narrow", None),
            P(),
            P(None, "narrow", None),
            P(),
            P("narrow", None),
            P("narrow"),
            P("narrow"),
            P("narrow", None),
            P("narrow", None, None),
            P("wide", "narrow", None),
            P("wide", None),
            P("wide", None),
        ),
        out_specs=(
            P("wide", "narrow", None),
            P("wide", "narrow", None),
            P("wide"),
            P("wide", "narrow", None),
            P("wide", None),
            P(None, "narrow", "wide"),
            P(None, "wide"),
            P("narrow", None),
            P("narrow"),
            P("narrow"),
            P("narrow", "wide"),
            P("narrow", None, "wide"),
        ),
        check_vma=False,
    )
```

```python
import functools

import jax
import jax.numpy as jnp
from jax import lax
from jax.experimental import pallas as pl
from jax.experimental.pallas import tpu as pltpu
from jax.sharding import PartitionSpec as P

H = 24
HD = 64
BLOCK = 128
SEQ_LEN = 1280


EPS = 1e-05
HIGH = lax.Precision.HIGHEST


def rounded(value):
    return value + lax.stop_gradient(value.astype(jnp.bfloat16).astype(jnp.float32) - value)


def segment_ids(starts):
    where_at = jnp.arange(SEQ_LEN, dtype=jnp.int32)
    hits = (starts[:, :, None] <= where_at[None, None, :]).astype(jnp.int32)
    return jnp.sum(hits, axis=1) - 1


def conv_doc(values, taps, seg):
    half = (taps.shape[0] - 1) // 2
    length = values.shape[1]
    padded = jnp.pad(values, ((0, 0), (half, half), (0, 0)))
    seg_pad = jnp.pad(seg, ((0, 0), (half, half)), constant_values=-1)
    total = jnp.zeros_like(values)
    for offset in range(taps.shape[0]):
        same = (seg_pad[:, offset : offset + length] == seg).astype(values.dtype)
        total = total + taps[offset] * padded[:, offset : offset + length] * same[:, :, None]
    return total


def ssd_forward(xc, steps, decays, bmat, cmat, seg, prec):
    rows, length, heads, hdim = xc.shape
    blocks = length // BLOCK
    xb = xc.reshape(rows, blocks, BLOCK, heads, hdim)
    stepb = steps.reshape(rows, blocks, BLOCK, heads)
    cum = jnp.cumsum(decays.reshape(rows, blocks, BLOCK, heads), axis=2)
    bb = bmat.reshape(rows, blocks, BLOCK, -1)
    cb = cmat.reshape(rows, blocks, BLOCK, -1)
    sb = seg.reshape(rows, blocks, BLOCK)
    order = jnp.arange(BLOCK, dtype=jnp.int32)
    causal = order[:, None] >= order[None, :]
    same = ((sb[:, :, :, None] == sb[:, :, None, :]) & causal)[..., None]
    diff = cum[:, :, :, None, :] - cum[:, :, None, :, :]
    weights = jnp.where(same, jnp.exp(jnp.where(same, diff, 0.0)), 0.0)
    inner = jnp.einsum("rbtn,rbsn->rbts", cb, bb, precision=prec)
    mix = weights * inner[..., None] * stepb[:, :, None, :, :]
    intra = jnp.einsum("rbtsh,rbshp->rbthp", mix, xb, precision=prec)
    last = sb[:, :, -1]
    cum_end = cum[:, :, -1, :]
    to_end = (
        (sb == last[:, :, None]).astype(cum.dtype)[..., None]
        * jnp.exp(cum_end[:, :, None, :] - cum)
        * stepb
    )
    states = jnp.einsum("rbshp,rbsn->rbhpn", to_end[..., None] * xb, bb, precision=prec)
    decay_end = jnp.exp(cum_end)

    def carry_step(carry, item):
        state, seg_prev = carry
        block_state, block_last, block_decay = item
        keep = (block_last == seg_prev).astype(state.dtype)[:, None, None, None]
        fresh = keep * block_decay[:, :, None, None] * state + block_state
        return ((fresh, block_last), (state, seg_prev))

    init = (
        jnp.zeros((rows, heads, hdim, bb.shape[-1]), xc.dtype),
        jnp.full((rows,), -1, jnp.int32),
    )
    items = (jnp.moveaxis(states, 1, 0), jnp.moveaxis(last, 1, 0), jnp.moveaxis(decay_end, 1, 0))
    _, (before, seg_before) = lax.scan(carry_step, init, items)
    before = jnp.moveaxis(before, 0, 1)
    seg_before = jnp.moveaxis(seg_before, 0, 1)
    enter = (sb == seg_before[:, :, None]).astype(cum.dtype)[..., None] * jnp.exp(cum)
    inter = jnp.einsum("rbtn,rbhpn->rbthp", cb, before, precision=prec) * enter[..., None]
    return (intra + inter).reshape(rows, length, heads, hdim)


def mixer(proj, bcproj, conv_x, conv_bc, dt_bias, a_log, skip_d, seg, mask, rounder, prec):
    rows, length, heads, width = proj.shape
    hdim = (width - 2) // 2
    state = bcproj.shape[-1] // 4
    gate = proj[..., :hdim]
    values = proj[..., hdim : 2 * hdim] * mask[:, :, None, None]
    mixed_x = conv_doc(
        values.reshape(rows, length, heads * hdim),
        conv_x.reshape(conv_x.shape[0], heads * hdim),
        seg,
    )
    xc = rounder(jax.nn.silu(mixed_x)).reshape(rows, length, heads, hdim)
    maps = rounder(jax.nn.silu(conv_doc(bcproj * mask[:, :, None], conv_bc, seg)))
    b_fwd = maps[..., :state]
    c_fwd = maps[..., state : 2 * state]
    b_bwd = maps[..., 2 * state : 3 * state]
    c_bwd = maps[..., 3 * state :]
    rate = -jnp.exp(a_log)
    dt_fwd = jax.nn.softplus(proj[..., 2 * hdim] + dt_bias[:, 0]) * mask[:, :, None]
    dt_bwd = jax.nn.softplus(proj[..., 2 * hdim + 1] + dt_bias[:, 1]) * mask[:, :, None]
    out_fwd = ssd_forward(xc, dt_fwd, dt_fwd * rate, b_fwd, c_fwd, seg, prec)

    def flip(v):
        return jnp.flip(v, axis=1)

    out_bwd = flip(
        ssd_forward(
            flip(xc), flip(dt_bwd), flip(dt_bwd * rate), flip(b_bwd), flip(c_bwd), flip(seg), prec
        )
    )
    keep_prev = (seg[:, 1:] == seg[:, :-1]).astype(xc.dtype)[:, :, None, None]
    shifted_fwd = jnp.pad(out_fwd[:, :-1] * keep_prev, ((0, 0), (1, 0), (0, 0), (0, 0)))
    shifted_bwd = jnp.pad(out_bwd[:, 1:] * keep_prev, ((0, 0), (0, 1), (0, 0), (0, 0)))
    return (shifted_fwd + shifted_bwd + skip_d[:, None] * xc, gate)


def shards(
    layer_in,
    pre_gain,
    w_heads,
    w_bc,
    conv_x,
    conv_bc,
    dt_bias,
    a_log,
    skip_d,
    norm_gain,
    w_out,
    cotangent,
    starts,
    live,
):
    seg = segment_ids(starts)
    mask = live.astype(jnp.float32)
    x_here = layer_in.astype(jnp.float32)
    scale = lax.rsqrt(jnp.mean(x_here * x_here, axis=-1, keepdims=True) + EPS)
    normed_here = (x_here * scale * pre_gain).astype(jnp.bfloat16)
    normed = lax.all_gather(normed_here, "narrow", axis=1, tiled=True)
    proj = jnp.einsum("rld,dhc->rlhc", normed, w_heads, preferred_element_type=jnp.float32)
    bcproj = jnp.einsum("rld,dc->rlc", normed, w_bc, preferred_element_type=jnp.float32)

    def mix_local(proj_in, bc_in, taps_x, taps_bc, bias_in, log_rate, diag_in):
        return mixer(
            proj_in, bc_in, taps_x, taps_bc, bias_in, log_rate, diag_in, seg, mask, rounded, HIGH
        )

    (ymix, gate), pull_mix = jax.vjp(
        mix_local, proj, bcproj, conv_x, conv_bc, dt_bias, a_log, skip_d
    )
    rows, length, heads, hdim = ymix.shape
    sigma = jax.nn.sigmoid(gate)
    act = gate * sigma
    gated = (ymix * act).reshape(rows, length, heads * hdim)
    squares = lax.psum(jnp.sum(gated * gated, axis=-1), "narrow")
    inv = lax.rsqrt(squares / (H * HD) + EPS)[..., None]
    gain_flat = norm_gain.reshape(-1)
    normalized = gated * inv
    hn = (normalized * gain_flat).astype(jnp.bfloat16)
    w_flat = w_out.reshape(heads * hdim, -1)
    partial_value = jnp.einsum("rlc,cd->rld", hn, w_flat, preferred_element_type=jnp.float32)
    branch = lax.psum_scatter(partial_value, "narrow", scatter_dimension=1, tiled=True)
    out = (x_here + branch).astype(jnp.bfloat16)
    grad_out = lax.all_gather(cotangent, "narrow", axis=1, tiled=True)
    g_w_out = jnp.einsum("rlc,rld->cd", hn, grad_out, preferred_element_type=jnp.float32)
    g_hn = jnp.einsum("rld,cd->rlc", grad_out, w_flat, preferred_element_type=jnp.float32)
    g_gain = jnp.sum(g_hn * normalized, axis=(0, 1))
    weighted = g_hn * gain_flat
    cross = lax.psum(jnp.sum(weighted * gated, axis=-1), "narrow")
    g_gated = inv * weighted - gated * (inv * inv * inv) * (cross / (H * HD))[..., None]
    g_gated = g_gated.reshape(rows, length, heads, hdim)
    g_ymix = g_gated * act
    g_gate = g_gated * ymix * (sigma * (1.0 + gate * (1.0 - sigma)))
    g_proj, g_bcproj, g_conv_x, g_conv_bc, g_dt_bias, g_a_log, g_skip = pull_mix((g_ymix, g_gate))
    g_proj_low = g_proj.astype(jnp.bfloat16)
    g_w_heads = jnp.einsum("rld,rlhc->dhc", normed, g_proj_low, preferred_element_type=jnp.float32)
    g_w_bc = jnp.einsum(
        "rld,rlc->dc", normed, g_bcproj, precision=HIGH, preferred_element_type=jnp.float32
    )
    g_normed = jnp.einsum("rlhc,dhc->rld", g_proj_low, w_heads, preferred_element_type=jnp.float32)
    g_normed = g_normed + jnp.einsum(
        "rlc,dc->rld", g_bcproj, w_bc, precision=HIGH, preferred_element_type=jnp.float32
    )
    g_normed_here = lax.psum_scatter(g_normed, "narrow", scatter_dimension=1, tiled=True)
    weighted_in = g_normed_here * pre_gain
    g_pre = jnp.sum(g_normed_here * x_here * scale, axis=(0, 1))
    g_x = scale * weighted_in - x_here * (scale * scale * scale) * jnp.mean(
        weighted_in * x_here, axis=-1, keepdims=True
    )
    grad_input = cotangent.astype(jnp.float32) + g_x
    g_pre, g_w_bc, g_conv_bc = lax.psum((g_pre, g_w_bc, g_conv_bc), "narrow")
    reduced = (
        lax.psum_scatter(g_w_heads, "wide", scatter_dimension=0, tiled=True),
        lax.psum_scatter(g_w_out.reshape(heads, hdim, -1), "wide", scatter_dimension=2, tiled=True),
        lax.psum_scatter(g_conv_x, "wide", scatter_dimension=2, tiled=True),
        lax.psum_scatter(g_gain.reshape(heads, hdim), "wide", scatter_dimension=1, tiled=True),
        lax.psum_scatter(g_pre, "wide", scatter_dimension=0, tiled=True),
        lax.psum_scatter(g_w_bc, "wide", scatter_dimension=0, tiled=True),
        lax.psum_scatter(g_conv_bc, "wide", scatter_dimension=1, tiled=True),
    )
    share_pre, share_bc, share_conv = (reduced[4], reduced[5], reduced[6])
    head_bias, head_rate, head_diag = lax.psum((g_dt_bias, g_a_log, g_skip), "wide")
    return (
        out,
        grad_input,
        share_pre,
        reduced[0],
        share_bc,
        reduced[2],
        share_conv,
        head_bias,
        head_rate,
        head_diag,
        reduced[3],
        reduced[1],
    )


HALO = 16
F32 = jnp.float32
BF16 = jnp.bfloat16
LOGZERO = -1e30


def mm(a, b, dims=((1,), (0,)), precision=None):
    return lax.dot_general(a, b, (dims, ((), ())), precision=precision, preferred_element_type=F32)


def nt(a, b):
    return mm(a, b, ((1,), (1,)))


def tn(a, b):
    return mm(a, b, ((0,), (0,)))


def seg_at(info, pos):
    seg = jnp.full(pos.shape, -1, jnp.int32)
    for j in range(4):
        seg = seg + (pos >= info[j]).astype(jnp.int32)
    return jnp.where(pos >= info[6], 99, seg)


def iota(shape, dim):
    return lax.broadcasted_iota(jnp.int32, shape, dim)


def silu_parts(v):
    sg = 0.5 * jnp.tanh(0.5 * v) + 0.5
    act = v * sg
    return act, sg + act * (1.0 - sg)


def thirds(v):
    hi = v.astype(BF16).astype(F32)
    rest = v - hi
    mid = rest.astype(BF16).astype(F32)
    return hi, mid, rest - mid


def column_terms(values):
    sub = iota((16, 128), 0)
    v = jnp.ones((16, 128), F32)
    for k, value in enumerate(values):
        v = jnp.where((sub >= 3 * k) & (sub < 3 * k + 3), value, v)
    hi, mid, low = thirds(v)
    part = sub % 3
    out = jnp.where(part == 0, hi, jnp.where(part == 1, mid, low))
    return jnp.where(sub < 3 * len(values), out, 1.0).astype(BF16)


def row_base(count, places):
    sub = iota((16, 384), 0)
    lane = iota((16, 384), 1)
    out = jnp.zeros((16, 384), F32)
    for k, spans in enumerate(places):
        for lo, hi in spans:
            out = jnp.where((sub >= 3 * k) & (sub < 3 * k + 3) & (lane >= lo) & (lane < hi), 1.0, out)
    return out


def row_terms(count, base, one, two):
    sub = iota((16, 128), 0)
    part = sub - 3 * count
    made = []
    for k, value in enumerate((one, two)):
        hi, mid, low = thirds(jnp.broadcast_to(value, (16, 128)))
        here = base[:, 128 * k : 128 * (k + 1)]
        made.append(
            jnp.where(part == 0, hi, jnp.where(part == 1, mid, jnp.where(part == 2, low, here))).astype(BF16)
        )
    return jnp.concatenate(made + [base[:, 256:].astype(BF16)], axis=1)


def conv_taps(src, seg_src, taps, first, rows):
    seg0 = seg_src[first : first + rows, :]
    total = src[first : first + rows, :] * taps[3:4, :]
    for k in (0, 1, 2, 4, 5, 6):
        lo = first + k - 3
        same = seg_src[lo : lo + rows, :] == seg0
        total = total + jnp.where(same, src[lo : lo + rows, :], 0.0) * taps[k : k + 1, :]
    return total


def front_kernel(
    length, hl, starts, live_ref, x_in, gain, wbc_ref, taps_ref, small_a, small_b,
    info, taps_o, gain_o, skip_o, wdt, wbc, taps, normed_o, rs_o, bcm_h, dsl_h, maps_h, ta_o, tb_o, tc_h, dpt_o, sig_h, seg_s, maps_s, cum_s, x_s, bcm_o, dsl_o, maps_o, tc_o, sig_o, sems,
):
    late = []

    def send(src, dst):
        late.append(pltpu.make_async_copy(src, dst, sems.at[len(late)]))
        late[-1].start()

    nb = length // BLOCK
    ext = length + 2 * HALO
    dm = x_in.shape[1]
    n = lax.axis_index("narrow")
    for i in range(4):
        info[i] = starts[0, i]
    count = jnp.sum(live_ref[...].astype(F32)).astype(jnp.int32)
    off = n * length
    info[4] = count
    info[5] = off
    info[6] = live_ref.shape[1]
    info[7] = n
    ch = small_a.shape[1]
    for k, small in enumerate((small_a, small_b)):
        cols = slice(k * ch, (k + 1) * ch)
        taps_o[:, cols] = small[0:8, :]
        gain_o[:, cols] = jnp.broadcast_to(small[7:8, :], (8, ch))
        skip_o[:, cols] = jnp.broadcast_to(small[8:9, :], (8, ch))
    dst = iota((128, 2 * hl), 0)
    src = iota((128, 2 * hl), 1)
    place = (src % 2) * 64 + src // 2
    at_a = jnp.where(dst == place, 1.0, 0.0).astype(BF16)
    at_b = jnp.where(dst == place + hl, 1.0, 0.0).astype(BF16)
    own_steps = small_a[16 : 16 + 2 * hl, :].astype(BF16)
    far_steps = small_b[16 : 16 + 2 * hl, :].astype(BF16)
    wdt[...] = (mm(at_a, own_steps) + mm(at_b, far_steps)).astype(BF16)
    wbc[...] = pack_columns(wbc_ref[...])
    taps[...] = pack_columns(taps_ref[...])

    bias = small_a[9:10, 0:128] + pltpu.roll(small_b[9:10, 0:128], hl, 1)
    alog = small_a[9:10, 128:256] + pltpu.roll(small_b[9:10, 128:256], hl, 1)
    edge = small_b[16 + 2 * hl : 24 + 2 * hl, :]
    zero_edge = jnp.zeros((8, dm), F32)
    before = jnp.concatenate([zero_edge, jnp.where(n == 1, edge, 0.0)], axis=0)
    behind = jnp.concatenate([jnp.where(n == 1, 0.0, edge), zero_edge], axis=0)
    x_s[0:HALO, :] = before.astype(BF16)
    x_s[HALO : HALO + length, :] = x_in[...]
    x_s[HALO + length : ext, :] = behind.astype(BF16)
    x = x_s[...].astype(F32)
    rs = lax.rsqrt(jnp.mean(x * x, axis=1, keepdims=True) + EPS)
    normed = (x * rs * gain[...]).astype(BF16)
    normed_o[...] = normed
    rs_o[...] = rs[HALO : HALO + length, :]
    pos256 = iota((ext, 256), 0) + (off - HALO)
    seg_s[...] = seg_at(info, pos256)
    live = pos256 < count
    bcm_o[...] = jnp.where(live, mm(normed, wbc[...]), 0.0)
    send(bcm_o, bcm_h)
    crows = length + HALO
    cfirst = HALO // 2
    mix = conv_taps(bcm_o, seg_s, taps, cfirst, crows)
    maps, dsl = silu_parts(mix)
    dsl_o[...] = jnp.zeros_like(dsl_o)
    dsl_o[cfirst : cfirst + crows, :] = dsl
    send(dsl_o, dsl_h)
    maps_s[...] = jnp.zeros_like(maps_s)
    maps_s[cfirst : cfirst + crows, :] = maps.astype(BF16).astype(F32)
    own = slice(HALO, HALO + length)
    segx = seg_s[own, 0:128]
    lane = iota((length, 128), 1)
    fwd = lane < 64
    segp = seg_s[HALO - 1 : HALO - 1 + length, 0:128]
    segn = seg_s[HALO + 1 : HALO + 1 + length, 0:128]
    bmap = maps_s[own, 0:128]
    cprev = jnp.where(segp == segx, maps_s[HALO - 1 : HALO - 1 + length, 128:256], 0.0)
    cnext = jnp.where(segn == segx, maps_s[HALO + 1 : HALO + 1 + length, 128:256], 0.0)
    cmap = jnp.where(fwd, cprev, cnext)
    maps_o[:, 0:128] = bmap.astype(BF16)
    maps_o[:, 128:256] = cmap.astype(BF16)
    send(maps_o, maps_h)
    raw = nt(normed[own, :], wdt[...]) + bias
    softp = jnp.maximum(raw, 0.0) + jnp.log(1.0 + jnp.exp(-jnp.abs(raw)))
    softp = jnp.where(raw < -15.0, jnp.exp(jnp.minimum(raw, 0.0)), softp)
    pos128 = iota((length, 128), 0) + off
    m = pos128 < count
    dt = jnp.where(m, softp, 0.0)
    sg = jnp.where(m, 1.0 / (1.0 + jnp.exp(-raw)), 0.0)
    ratio = jnp.where(m, jnp.where(raw < -15.0, 1.0, sg / jnp.maximum(softp, 1e-30)), 0.0)
    rate = -jnp.exp(alog)
    a = dt * rate
    sig_o[:, 256:384] = a
    sig_o[:, 0:128] = sg * rate
    sig_o[:, 128:256] = ratio
    tri = (iota((BLOCK, BLOCK), 0) >= iota((BLOCK, BLOCK), 1)).astype(F32)
    logdt = jnp.maximum(jnp.log(dt), LOGZERO)
    sub = iota((BLOCK, BLOCK), 0)
    ln = iota((BLOCK, BLOCK), 1)
    fwdb = ln < 64
    cum_s[...] = jnp.zeros_like(cum_s)
    dvals, ends = [], []
    for b in range(nb):
        blk = slice(b * BLOCK, (b + 1) * BLOCK)
        ab = a[blk, :]
        cum = mm(tri, ab, precision=HIGH)
        cx = cum - ab
        end = cum[BLOCK - 1 : BLOCK, :]
        colt = jnp.where(fwdb, cx, end - cum)
        rows = jnp.where(fwdb, logdt[blk, :] - cum, cx + logdt[blk, :] - end)
        tb_o[0, b] = colt.T
        tb_o[1, b] = rows.T
        ta_o[0, b] = jnp.minimum(rows + end, 60.0).T
        first_pos = off + b * BLOCK
        sp = seg_at(info, sub + first_pos)
        st = seg_at(info, ln + first_pos)
        before = seg_at(info, sub * 0 + (first_pos - 1))
        begin = seg_at(info, sub * 0 + first_pos)
        last = seg_at(info, sub * 0 + (first_pos + BLOCK - 1))
        after = seg_at(info, sub * 0 + (first_pos + BLOCK))
        enter = jnp.where(fwdb, (sp == before).astype(F32), (sp == after).astype(F32))
        keep = jnp.where(fwdb, (sp == last).astype(F32), (sp == begin).astype(F32))
        ce = cmap[blk, :] * enter
        bk = bmap[blk, :] * keep
        tb_o[3, b] = ce
        tc_o[1, b] = bk
        tc_o[2, b] = ce.T
        ta_o[1, b] = bk.T
        chain = jnp.where(fwdb[0:1, :], (last == before).astype(F32)[0:1, :], (begin == after).astype(F32)[0:1, :])
        dvals.append(jnp.exp(end) * chain)
        ends.append(end)
        cb = cmap[blk, :].astype(BF16)
        bb = bmap[blk, :].astype(BF16)
        zero = jnp.zeros_like(bb)
        same = sp == st
        low = same & (sub > ln)
        high = same & (sub < ln)
        bf = jnp.where(fwdb, bb, zero)
        br = jnp.where(fwdb, zero, bb)
        tb_o[2, b] = jnp.where(low, nt(cb, bf), jnp.where(high, nt(cb, br), 0.0))
        tc_o[0, b] = jnp.where(high, nt(bf, cb), jnp.where(low, nt(br, cb), 0.0))
    ones = jnp.ones((1, 128), F32)
    prefix, suffix = [ones], [ones]
    for b in range(nb):
        prefix.append(prefix[-1] * dvals[b])
        suffix.append(suffix[-1] * dvals[nb - 1 - b])
    suffix = suffix[::-1]
    f1 = fwdb[0:1, :]
    for b in range(nb):
        cum_s[b : b + 1, :] = dvals[b]
        cum_s[48 + b : 49 + b, :] = ends[b]
    for i in range(nb + 1):
        cum_s[16 + i : 17 + i, :] = jnp.where(f1, prefix[i], suffix[i])
        cum_s[32 + i : 33 + i, :] = jnp.where(f1, suffix[i], prefix[i])
    dpt_o[...] = cum_s[...].T
    send(sig_o, sig_h)
    send(tc_o, tc_h)
    for one in late:
        one.wait()


def pair_rows(dpt, j, base, i, half):
    lane = iota((1, 128), 1)
    one = dpt[pl.ds(half * 64 + 2 * j, 1), :][:, base + i : base + i + 1]
    two = dpt[pl.ds(half * 64 + 2 * j + 1, 1), :][:, base + i : base + i + 1]
    return jnp.where(lane < 64, one, two)


def assemble(dst, pieces):
    quarter = dst.shape[0] // 4
    q = lax.axis_index("wide") % 4
    cbit = q % 2
    xbit = q // 2
    places = (q, (1 - xbit) * 2 + cbit, xbit * 2 + 1 - cbit, (1 - xbit) * 2 + 1 - cbit)
    for place, piece in zip(places, pieces):
        dst[pl.ds(pl.multiple_of(place * quarter, quarter), quarter), :] = piece[...]


def vals_kernel(length, other, info, normed, *refs):
    nb = length // BLOCK
    ext = length + 2 * HALO
    step = pl.program_id(0)
    first = step
    if other:
        p0, p1, p2, p3, taps, ta, dpt = refs[:7]
        xc_o, vm_o, ds_o, s_o, bnd_o, wvo_o, vm_a, vm_b, seg_s = refs[11:]
        first = step + pl.num_programs(0)

        @pl.when(step == 0)
        def _():
            assemble(wvo_o, (p0, p1, p2, p3))

        wv = wvo_o[pl.ds(pl.multiple_of(step * 256, 256), 256), :]
    else:
        w_ref, taps, ta, dpt, xc_o, vm_o, ds_o, s_o, bnd_o, vm_a, vm_b, seg_s = refs
        wv = jnp.concatenate([w_ref[h, HD : 2 * HD, :] for h in range(4)], axis=0)
    off, count = info[5], info[4]

    @pl.when(step == 0)
    def _():
        seg_s[...] = seg_at(info, iota((ext, 128), 0) + (off - HALO))

    live = iota((ext, 128), 0) + (off - HALO) < count
    both = nt(normed[...], wv)
    lane = iota((BLOCK, 128), 1)
    top = iota((BLOCK, 128), 0) < 64
    for p, vm_s in enumerate((vm_a, vm_b)):
        j = 2 * first + p
        here = slice(128 * p, 128 * (p + 1))
        vm = jnp.where(live, both[:, here], 0.0)
        vm_s[...] = vm
        vm_o[:, here] = vm.astype(BF16)
        act, ds = silu_parts(conv_taps(vm_s, seg_s, taps[:, here], HALO, length))
        xc = act.astype(BF16)
        xc_o[:, here] = xc
        ds_o[:, here] = ds.astype(BF16)
        loc = []
        for b in range(nb):
            blk = slice(b * BLOCK, (b + 1) * BLOCK)
            got = []
            for i in range(2):
                h = 2 * j + i
                w = jnp.where(top, jnp.exp(ta[0, b, pl.ds(h, 1), :]), jnp.exp(ta[0, b, pl.ds(64 + h, 1), :]))
                got.append((ta[1, b] * w).astype(BF16))
            got = mm(jnp.concatenate(got, axis=0), xc[blk, :])
            loc.append(jnp.where(lane < 64, got[0:BLOCK, :], got[BLOCK:, :]))
        state = jnp.zeros((64, 128), F32)
        s_o[p, 0, 0:64, :] = state.astype(BF16)
        for b in range(nb):
            state = pair_rows(dpt, j, 0, b, 0) * state + loc[b][0:64, :]
            s_o[p, b + 1, 0:64, :] = state.astype(BF16)
        end_f = state
        state = jnp.zeros((64, 128), F32)
        s_o[p, nb, 64:128, :] = state.astype(BF16)
        for b in range(nb - 1, -1, -1):
            state = pair_rows(dpt, j, 0, b, 1) * state + loc[b][64:128, :]
            s_o[p, b, 64:128, :] = state.astype(BF16)
        bnd_o[p] = jnp.where(info[7] == 0, end_f, state).astype(BF16)


def scan_kernel(length, first_pair, info, xc_ref, s_ref, s0_ref, dpt, tb, skip, *refs):
    nb = length // BLOCK
    y_o, st_o = refs[-2:]
    j = pl.program_id(0) + first_pair
    right = (info[7] == 1).astype(F32)
    s0 = s0_ref[0].astype(F32)
    lane = iota((BLOCK, 128), 1)
    first = lane < 64
    low = iota((BLOCK, BLOCK), 0) > lane
    base = row_base(2, [[(0, 128), (256, 320)], [(128, 256), (320, 384)]])
    for i in range(nb + 1):
        f = s_ref[0, i, 0:64, :].astype(F32) + pair_rows(dpt, j, 16, i, 0) * (s0 * right)
        r = s_ref[0, i, 64:128, :].astype(F32) + pair_rows(dpt, j, 16, i, 1) * (s0 * (1.0 - right))
        st_o[0, i, 0:64, :] = f.astype(BF16)
        st_o[0, i, 64:128, :] = r.astype(BF16)
    for b in range(nb):
        blk = slice(b * BLOCK, (b + 1) * BLOCK)
        xb = xc_ref[blk, :]
        rhs = jnp.concatenate([xb, st_o[0, b, 0:64, :], st_o[0, b + 1, 64:128, :]], axis=0)
        got = []
        for i in range(2):
            h = 2 * j + i
            terms = column_terms([tb[0, b, pl.ds(h, 1), :], tb[0, b, pl.ds(64 + h, 1), :]])
            expo = tn(terms, row_terms(2, base, tb[1, b, pl.ds(h, 1), :], tb[1, b, pl.ds(64 + h, 1), :]))
            diff = jnp.where(low, expo[:, 0:128], expo[:, 128:256])
            mix = jnp.exp(jnp.minimum(diff, 60.0)) * tb[2, b]
            ct = tb[3, b] * jnp.exp(expo[:, 256:])
            lhs = jnp.concatenate([mix.astype(BF16), ct.astype(BF16)], axis=1)
            got.append(lhs)
        got = mm(jnp.concatenate(got, axis=0), rhs)
        y = jnp.where(first, got[0:BLOCK, :], got[BLOCK:, :]) + skip[0:1, :] * xb.astype(F32)
        y_o[blk, :] = y.astype(BF16)


def by_core(v, keep, send):
    share = v.shape[0] // 16
    cbit = lax.axis_index("wide") % 2
    v = v.astype(BF16).reshape(8, 2, share, v.shape[1])
    keep[...] = jnp.where(cbit == 0, v[:, 0], v[:, 1]).reshape(8 * share, v.shape[3])
    send[...] = jnp.where(cbit == 0, v[:, 1], v[:, 0]).reshape(8 * share, v.shape[3])


def gate_kernel(
    tiles, info, x_ref, g_ref, normed, y_ref, wout_a, w_ref, p0, p1, p2, p3, gain, tb, tc, dpt,
    out_h, gy_o, ggate_o, hn_s, ggain_o, wgo_h, gs_o, bnd_o, other_s, gated_s, act_s, dact_s, ghn_s, loc_s, out_o, sems,
):
    late = []

    def send(src, dst):
        late.append(pltpu.make_async_copy(src, dst, sems.at[len(late)]))
        late[-1].start()

    dm = x_ref.shape[1]
    chans = y_ref.shape[1]
    half = chans // 2
    step = 256
    assemble(other_s, (p0, p1, p2, p3))
    send(other_s.at[:, dm:], wgo_h)
    ggain_o[...] = jnp.zeros_like(ggain_o)
    first = iota((BLOCK, 128), 1) < 64
    top = iota((BLOCK, 128), 0) < 64

    @pl.loop(0, tiles)
    def _(i):
        start = pl.multiple_of(i * BLOCK, BLOCK)
        rows = pl.ds(start, BLOCK)
        nrows = normed[pl.ds(pl.multiple_of(start + HALO, HALO), BLOCK), :]
        squares = jnp.zeros((BLOCK, 128), F32)
        for lo in range(0, chans, step):
            if lo < half:
                heads = range(lo // HD, (lo + step) // HD)
                wg = jnp.concatenate([w_ref[h, 0:HD, :] for h in heads], axis=0)
            else:
                wg = other_s[lo - half : lo - half + step, dm:]
            gates = nt(nrows, wg)
            for at in range(0, step, 128):
                cols = slice(lo + at, lo + at + 128)
                act, dact = silu_parts(gates[:, at : at + 128])
                gated = y_ref[rows, cols].astype(F32) * act
                squares = squares + gated * gated
                gated_s[:, cols] = gated
                act_s[:, cols] = act
                dact_s[:, cols] = dact
        inv = lax.rsqrt(jnp.sum(squares, axis=1, keepdims=True) * (1.0 / chans) + EPS)
        inv = jnp.broadcast_to(inv, (BLOCK, 128))
        g = g_ref[rows, :]
        across = jnp.zeros((BLOCK, 128), F32)
        for lo in range(0, chans, step):
            wo = wout_a[lo : lo + step, :] if lo < half else other_s[lo - half : lo - half + step, 0:dm]
            ghns = nt(g, wo)
            for at in range(0, step, 128):
                cols = slice(lo + at, lo + at + 128)
                gainv = gain[0:1, cols]
                gated = gated_s[:, cols]
                nrm = gated * inv
                hn_s[rows, cols] = (nrm * gainv).astype(BF16)
                ghn = ghns[:, at : at + 128]
                ggain_o[0:1, cols] += jnp.sum(ghn * nrm, axis=0, keepdims=True)
                wgt = ghn * gainv
                ghn_s[:, cols] = wgt
                across = across + wgt * gated
        cross = jnp.sum(across, axis=1, keepdims=True) * (1.0 / chans)
        cross = jnp.broadcast_to(cross, (BLOCK, 128)) * (inv * inv * inv)
        hn = hn_s[rows, :]
        branch = mm(hn[:, 0:half], wout_a[...]) + mm(hn[:, half:], other_s[:, 0:dm])
        out_o[rows, :] = (x_ref[rows, :].astype(F32) + branch).astype(BF16)
        for lo in range(0, chans, 128):
            cols = slice(lo, lo + 128)
            ggated = inv * ghn_s[:, cols] - gated_s[:, cols] * cross
            gy = (ggated * act_s[:, cols]).astype(BF16)
            gy_o[rows, cols] = gy
            ggate_o[rows, cols] = (ggated * y_ref[rows, cols].astype(F32) * dact_s[:, cols]).astype(BF16)
            got = []
            for h in range(lo // HD, lo // HD + 2):
                e = jnp.where(top, jnp.exp(tb[0, i, h : h + 1, :]), jnp.exp(tb[0, i, 64 + h : 65 + h, :]))
                got.append((tc[2, i] * e).astype(BF16))
            got = mm(jnp.concatenate(got, axis=0), gy)
            loc_s[i, :, cols] = jnp.where(first, got[0:BLOCK, :], got[BLOCK:, :])

    send(out_o, out_h)

    @pl.loop(0, chans // 128)
    def _(j):
        cols = pl.ds(pl.multiple_of(j * 128, 128), 128)
        state = jnp.zeros((64, 128), F32)
        gs_o[j, tiles, 0:64, :] = state.astype(BF16)
        for b in range(tiles - 1, -1, -1):
            state = pair_rows(dpt, j, 0, b, 0) * state + loc_s[b, 0:64, cols]
            gs_o[j, b, 0:64, :] = state.astype(BF16)
        end_f = state
        state = jnp.zeros((64, 128), F32)
        gs_o[j, 0, 64:128, :] = state.astype(BF16)
        for b in range(tiles):
            state = pair_rows(dpt, j, 0, b, 1) * state + loc_s[b, 64:128, cols]
            gs_o[j, b + 1, 64:128, :] = state.astype(BF16)
        bnd_o[j] = jnp.where(info[7] == 1, end_f, state).astype(BF16)

    for one in late:
        one.wait()


def wsum_kernel(g_ref, normed, hn, ggate, keep_h, send_h, keep_o, send_o, sems):
    length, dm = g_ref.shape
    half = hn.shape[1] // 2
    late = []

    def send(src, dst):
        late.append(pltpu.make_async_copy(src, dst, sems.at[len(late)]))
        late[-1].start()

    gt = g_ref[...].T
    nt_ = normed[HALO : HALO + length, :].T
    for k in range(2):
        for p in range(half // 256):
            cols = slice(k * half + p * 256, k * half + (p + 1) * 256)
            dst = slice(p * 256, (p + 1) * 256)
            dst2 = slice(half + p * 256, half + (p + 1) * 256)
            by_core(mm(gt, hn[:, cols]), keep_o.at[k, :, dst], send_o.at[k, :, dst])
            by_core(mm(nt_, ggate[:, cols]), keep_o.at[k, :, dst2], send_o.at[k, :, dst2])
        send(send_o.at[k], send_h.at[k])
        send(keep_o.at[k], keep_h.at[k])
    for one in late:
        one.wait()


def gscan_kernel(
    length, info, xc_ref, ds_ref, gy_ref, st_ref, gs_ref, gs0_ref, dpt, rowst, wt, coltt, tc, skip,
    gmix_o, ggt_o, gb_o, gct_o, k_o, r_o, phi_o, gskip_o, edge_o, gst_s,
):
    nb = length // BLOCK
    j = pl.program_id(0)
    right = (info[7] == 1).astype(F32)
    s0 = gs0_ref[0].astype(F32)
    sub = iota((BLOCK, BLOCK), 0)
    lane = iota((BLOCK, 128), 1)
    first = lane < 64
    later = lane > sub
    top = sub < 64

    @pl.when(j == 0)
    def _():
        for acc in (ggt_o, gb_o, gct_o, k_o, r_o):
            acc[...] = jnp.zeros_like(acc)

    base = row_base(4, [[(0, 128)], [(128, 256)], [(256, 320)], [(320, 384)]])

    phi_o[...] = jnp.zeros_like(phi_o)
    for i in range(nb + 1):
        f = gs_ref[0, i, 0:64, :].astype(F32) + pair_rows(dpt, j, 32, i, 0) * (s0 * (1.0 - right))
        r = gs_ref[0, i, 64:128, :].astype(F32) + pair_rows(dpt, j, 32, i, 1) * (s0 * right)
        f = f.astype(BF16)
        r = r.astype(BF16)
        gst_s[i, 0:64, :] = f
        gst_s[i, 64:128, :] = r
        if i > 0:
            phi_o[i - 1 : i, :] = jnp.sum(f.astype(F32) * st_ref[0, i, 0:64, :].astype(F32), axis=0, keepdims=True)
        if i < nb:
            phi_o[8 + i : 9 + i, :] = jnp.sum(
                r.astype(F32) * st_ref[0, i, 64:128, :].astype(F32), axis=0, keepdims=True
            )
    gskip = jnp.zeros((1, 128), F32)
    for b in range(nb):
        blk = slice(b * BLOCK, (b + 1) * BLOCK)
        xb = xc_ref[blk, :]
        gy = gy_ref[blk, :]
        gyf = gy.astype(F32)
        gskip = gskip + jnp.sum(gyf * xb.astype(F32), axis=0, keepdims=True)
        rhs = jnp.concatenate([gy, gst_s[b + 1, 0:64, :], gst_s[b, 64:128, :]], axis=0)
        left = jnp.concatenate([xb, st_ref[0, b, 0:64, :], st_ref[0, b + 1, 64:128, :]], axis=0)
        first2 = iota((2 * BLOCK, 128), 1) < 64
        none = jnp.zeros_like(left)
        big2 = nt(jnp.concatenate([jnp.where(first2, left, none), jnp.where(first2, none, left)], axis=0), rhs)
        got = []
        sum_ge, sum_gct, sum_gb, kparts = [], [], [], []
        for i in range(2):
            h = 2 * j + i
            terms = column_terms([v[b, pl.ds(at + h, 1), :] for v in (rowst, wt) for at in (0, 64)])
            expo = tn(terms, row_terms(4, base, coltt[b, pl.ds(h, 1), :], coltt[b, pl.ds(64 + h, 1), :]))
            diff = jnp.where(later, expo[:, 0:128], expo[:, 128:256])
            et_m = jnp.exp(jnp.minimum(diff, 60.0))
            mt = et_m * tc[0, b]
            w = jnp.exp(expo[:, 256:])
            bt = tc[1, b] * w
            big = big2[2 * BLOCK * i : 2 * BLOCK * (i + 1), :]
            gmt = big[0:BLOCK, 0:BLOCK]
            gbt = big[0:BLOCK, BLOCK:]
            gctt = big[BLOCK:, 0:BLOCK]
            ge = gmt * et_m
            sum_ge.append(ge)
            q = gmt * mt
            qf = jnp.where(later, q, 0.0)
            e = jnp.where(top, jnp.exp(coltt[b, pl.ds(h, 1), :]), jnp.exp(coltt[b, pl.ds(64 + h, 1), :]))
            gce = gctt * e
            sum_gct.append(gce)
            ct = gce * tc[2, b]
            rf = jnp.sum(qf, axis=0, keepdims=True)
            rall = jnp.sum(q, axis=0, keepdims=True)
            r_o[b, pl.ds(h, 1), :] = rf + jnp.sum(ct[0:64, :], axis=0, keepdims=True)
            r_o[b, pl.ds(64 + h, 1), :] = rall - rf + jnp.sum(ct[64:128, :], axis=0, keepdims=True)
            gbw = gbt * w
            sum_gb.append(gbw)
            u = gbw * tc[1, b]
            kf = jnp.sum(qf + jnp.where(first, u, 0.0), axis=1, keepdims=True)
            kb = jnp.sum(q + u, axis=1, keepdims=True) - kf
            kparts += [kf, kb]
            lhs = jnp.concatenate([mt.astype(BF16), bt.astype(BF16)], axis=1)
            got.append(lhs)
        ggt_o[b] += sum_ge[0] + sum_ge[1]
        gct_o[b] += sum_gct[0] + sum_gct[1]
        gb_o[b] += sum_gb[0] + sum_gb[1]
        two = jnp.where(lane % 64 == 0, jnp.where(first, kparts[0], kparts[1]), jnp.where(first, kparts[2], kparts[3]))
        k_o[blk, :] += pltpu.roll(jnp.where(lane % 64 < 2, two, 0.0), 2 * j, 1)
        got = mm(jnp.concatenate(got, axis=0), rhs)
        gx = jnp.where(first, got[0:BLOCK, :], got[BLOCK:, :]) + skip[0:1, :] * gyf
        gmix = (gx * ds_ref[blk, :].astype(F32)).astype(BF16)
        gmix_o[blk, :] = gmix
        if b == 0:
            edge_o[...] = gmix[0:HALO, :]
        if b == nb - 1:
            edge_o[...] = jnp.where(info[7] == 0, gmix[BLOCK - HALO :, :], edge_o[...])
    gskip_o[...] = jnp.broadcast_to(gskip, (8, 128))


def join_kernel(
    length, heads, info, ggt, gb, gct, k_ref, r_ref, phi, maps, dsl, sig,
    gmb_o, gv_o, small_o, edge_o, gc_s, gm_s,
):
    nb = length // BLOCK
    off = info[5]
    chans = phi.shape[1]
    sub = iota((BLOCK, BLOCK), 0)
    lane = iota((BLOCK, 128), 1)
    first = lane < 64
    low = sub > lane
    high = sub < lane
    upper_strict = high.astype(F32)
    upper = (sub <= lane).astype(F32)
    lower_strict = low.astype(F32)
    lower = (sub >= lane).astype(F32)
    owner = iota((chans, 128), 0) // 64
    to_f = (owner == iota((chans, 128), 1)).astype(F32)
    to_b = (owner + 64 == iota((chans, 128), 1)).astype(F32)
    phi_f = mm(phi[0:8, :], to_f, precision=HIGH)
    phi_b = mm(phi[8:16, :], to_b, precision=HIGH)
    gc_s[...] = jnp.zeros_like(gc_s)
    gm_s[...] = jnp.zeros_like(gm_s)
    sum_bias = jnp.zeros((1, 128), F32)
    sum_rate = jnp.zeros((1, 128), F32)
    for b in range(nb):
        blk = slice(b * BLOCK, (b + 1) * BLOCK)
        ext = slice(HALO + b * BLOCK, HALO + (b + 1) * BLOCK)
        first_pos = off + b * BLOCK
        sp = seg_at(info, sub + first_pos)
        st = seg_at(info, lane + first_pos)
        before = seg_at(info, sub * 0 + (first_pos - 1))
        begin = seg_at(info, sub * 0 + first_pos)
        last = seg_at(info, sub * 0 + (first_pos + BLOCK - 1))
        after = seg_at(info, sub * 0 + (first_pos + BLOCK))
        enter = jnp.where(first, (sp == before).astype(F32), (sp == after).astype(F32))
        keep = jnp.where(first, (sp == last).astype(F32), (sp == begin).astype(F32))
        same = sp == st
        gg = ggt[b]
        gf = jnp.where(same & high, gg, 0.0).astype(BF16)
        gr = jnp.where(same & low, gg, 0.0).astype(BF16)
        cm = maps[blk, 128:256]
        bm = maps[blk, 0:128]
        gm_s[ext, 0:128] = jnp.where(first, mm(gf, cm), mm(gr, cm)) + gb[b] * keep
        gc_s[ext, :] = jnp.where(first, tn(gf, bm), tn(gr, bm)) + gct[b].T * enter
        kb = k_ref[blk, :]
        rb = r_ref[b].T
        ga_f = mm(upper_strict, rb, precision=HIGH) - mm(upper, kb, precision=HIGH) + phi_f[b : b + 1, :]
        ga_b = mm(lower_strict, rb, precision=HIGH) - mm(lower, kb, precision=HIGH) + phi_b[b : b + 1, :]
        ga = jnp.where(first, ga_f, ga_b)
        gv = kb * sig[blk, 128:256] + ga * sig[blk, 0:128]
        gv_o[blk, :] = gv.astype(BF16)
        sum_bias = sum_bias + jnp.sum(gv, axis=0, keepdims=True)
        sum_rate = sum_rate + jnp.sum(ga * sig[blk, 256:384], axis=0, keepdims=True)
    small_o[...] = jnp.zeros_like(small_o)
    small_o[0:1, :] = sum_bias
    small_o[1:2, :] = sum_rate
    small_o[8:9, :] = pltpu.roll(sum_bias, 128 - heads // 2, 1)
    small_o[9:10, :] = pltpu.roll(sum_rate, 128 - heads // 2, 1)
    mid = length + HALO
    lo = HALO // 2
    pos = iota((mid, 128), 0) + (off - HALO + lo)
    seg0 = seg_at(info, pos)
    segn = seg_at(info, pos + 1)
    segp = seg_at(info, pos - 1)
    from_next = jnp.where(seg0 == segn, gc_s[lo + 1 : lo + 1 + mid, :], 0.0)
    from_prev = jnp.where(seg0 == segp, gc_s[lo - 1 : lo - 1 + mid, :], 0.0)
    gm_s[lo : lo + mid, 128:256] = jnp.where(iota((mid, 128), 1) < 64, from_next, from_prev)
    gmb_o[...] = gm_s[...] * dsl[...]
    lo = HALO // 2
    edge_o[...] = jnp.where(
        info[7] == 0, gmb_o[length + lo : length + lo + HALO, :], gmb_o[lo : lo + HALO, :]
    )


def back_conv(length, seg_s, live, grad, data, tap):
    own = slice(HALO, HALO + length)
    seg0 = seg_s[own, :]
    mine = grad[own, :]
    total = mine * tap[3:4, :]
    gtap = [None] * 7
    gtap[3] = jnp.sum(mine * data[own, :], axis=0, keepdims=True)
    for k in (0, 1, 2, 4, 5, 6):
        lo = HALO + 3 - k
        same = seg_s[lo : lo + length, :] == seg0
        total = total + jnp.where(same, grad[lo : lo + length, :], 0.0) * tap[k : k + 1, :]
        up = HALO + k - 3
        same = seg_s[up : up + length, :] == seg0
        gtap[k] = jnp.sum(jnp.where(same, data[up : up + length, :], 0.0) * mine, axis=0, keepdims=True)
    return jnp.where(live, total, 0.0), gtap


def back_kernel(
    length, steps, info, gmix, edge, vm, normed, taps, ggain, gskip,
    gvals_o, keep_o, send_o, tiny_o, ext_s, vm_s, seg_s, turned_s,
):
    ext = length + 2 * HALO
    off, count = info[5], info[4]
    own = slice(HALO, HALO + length)
    seg_s[...] = seg_at(info, iota((ext, 128), 0) + (off - HALO))
    tiny_o[...] = jnp.zeros_like(tiny_o)
    turned_s[...] = normed[own, :].T
    live = iota((length, 128), 0) + off < count
    right = info[7] == 1
    per = steps // 2

    @pl.loop(0, steps)
    def _(j):
        half = j // per
        at = (j % per) * 256
        both = []
        for p in range(2):
            here = pl.ds(pl.multiple_of(at + 128 * p, 128), 128)
            cols = pl.ds(pl.multiple_of(j * 256 + 128 * p, 128), 128)
            ext_s[own, :] = gmix[:, cols].astype(F32)
            far = pl.ds(pl.multiple_of(((j + per) % steps) * 256 + 128 * p, 128), 128)
            halo = edge[:, far].astype(F32)
            ext_s[0:HALO, :] = jnp.where(right, halo, 0.0)
            ext_s[HALO + length : ext, :] = jnp.where(right, 0.0, halo)
            vm_s[...] = vm[:, cols].astype(F32)
            gvals, gtap = back_conv(length, seg_s, live, ext_s, vm_s, taps[:, cols])
            both.append(gvals.astype(BF16))
            for t in range(7):
                tiny_o[half, t : t + 1, here] = gtap[t]
            tiny_o[half, 7:8, here] = ggain[0:1, cols]
            tiny_o[half, 8:9, here] = gskip[0:1, cols]
        both = jnp.concatenate(both, axis=1)
        gvals_o[:, pl.ds(pl.multiple_of(j * 256, 256), 256)] = both
        here = pl.ds(pl.multiple_of(at, 256), 256)
        by_core(mm(turned_s[...], both), keep_o.at[half, :, here], send_o.at[half, :, here])


def last_kernel(
    length, hl, info, gvals, ggate, w_ref, wv_b, wg_b, normed, gmb, edge, bcm, taps_bc, gv, wdt, wbc, x_ref, g_ref, rs, pre,
    small, tiny, keep_o, send_o, tiny_o, gin_o, ext_s, vm_s, seg_s,
):
    ext = length + 2 * HALO
    ch = hl * HD
    off, count = info[5], info[4]
    own = slice(HALO, HALO + length)
    seg_s[...] = seg_at(info, iota((ext, 128), 0) + (off - HALO))
    live = iota((length, 128), 0) + off < count
    tiny_o[...] = tiny[...]
    for half in range(2):
        tiny_o[half, 10:11, 0:128] = small[8 * half : 8 * half + 1, :]
        tiny_o[half, 10:11, 128:256] = small[8 * half + 1 : 8 * half + 2, :]
    both = []
    for k in range(2):
        cols = slice(k * 128, (k + 1) * 128)
        ext_s[...] = gmb[:, cols]
        lo = HALO // 2
        hi = length + lo
        got = edge[:, cols]
        ext_s[lo : lo + HALO, :] += jnp.where(info[7] == 1, got, 0.0)
        ext_s[hi : hi + HALO, :] += jnp.where(info[7] == 1, 0.0, got)
        vm_s[...] = bcm[:, cols]
        gbc, gtap = back_conv(length, seg_s, live, ext_s, vm_s, taps_bc[:, cols])
        for t in range(7):
            at = (t % 3) * 256 + k * 128
            for half in range(2):
                tiny_o[half, 11 + t // 3 : 12 + t // 3, at : at + 128] = gtap[t]
        both.append(gbc.astype(BF16))
    gbc = jnp.concatenate(both + [gv[...]], axis=1)
    gw = tn(normed[own, :], gbc)
    by_core(gw, keep_o.at[0], send_o.at[0])
    turned = pltpu.roll(gw[:, 256:], 128 - hl, 1)
    by_core(jnp.concatenate([gw[:, 0:256], turned], axis=1), keep_o.at[1], send_o.at[1])
    wv_a = jnp.concatenate([w_ref[h, HD : 2 * HD, :] for h in range(hl)], axis=0)
    wg_a = jnp.concatenate([w_ref[h, 0:HD, :] for h in range(hl)], axis=0)
    gn = mm(gvals[:, 0:ch], wv_a) + mm(gvals[:, ch:], wv_b[...])
    gn = gn + mm(ggate[:, 0:ch], wg_a) + mm(ggate[:, ch:], wg_b[...])
    gn = gn + nt(gbc[:, 0:256], wbc[...]) + mm(gv[...], wdt[...])
    x = x_ref[...].astype(F32)
    r = rs[...]
    wp = gn * pre[...]
    mean = jnp.mean(wp * x, axis=1, keepdims=True)
    gin_o[...] = g_ref[...].astype(F32) + r * wp - x * (r * r * r * mean)
    gpre = jnp.sum(gn * x * r, axis=0, keepdims=True)
    for half in range(2):
        tiny_o[half, 9:10, 0 : gpre.shape[1]] = gpre


def finish_kernel(hl, tiny, total, wb, heads_o, wout_o, bc_o, conv_o, convbc_o, pre_o, bias_o, rate_o, skip_o, gain_o):
    ch = tiny.shape[1]
    w = lax.axis_index("wide")
    share = pre_o.shape[1]
    lanes = gain_o.shape[0]
    dm = total.shape[1] - ch
    for h in range(hl):
        cols = slice(h * HD, (h + 1) * HD)
        wout_o[h] = total[:, cols]
        heads_o[h, :, 0:HD] = total[:, dm + h * HD : dm + (h + 1) * HD]
        heads_o[h, :, HD : 2 * HD] = wb[:, cols]
        heads_o[h, :, 2 * HD : 2 * HD + 1] = wb[:, ch + 256 + h : ch + 257 + h]
        heads_o[h, :, 2 * HD + 1 :] = wb[:, ch + 320 + h : ch + 321 + h]
    bc_o[...] = pack_columns(wb[:, ch : ch + 256])
    rows = tiny[...]
    src = iota((ch, 128), 0)
    dst = iota((ch, 128), 1)
    for q in range(lanes):
        chosen = ((src == dst * HD + lanes * w + q) & (dst < hl)).astype(F32)
        got = mm(rows, chosen, precision=HIGH)
        for k in range(7):
            conv_o[k, q : q + 1, :] = got[k : k + 1, 0:hl]
        gain_o[q : q + 1, :] = got[7:8, 0:hl]
    chosen = ((src == share * w + dst) & (dst < share)).astype(F32)
    pre_o[...] = mm(rows[8:16, :], chosen, precision=HIGH)[1:2, 0:share]
    per = (src // HD == dst).astype(F32)
    skip_o[...] = mm(rows[8:16, :], per, precision=HIGH)[0:1, 0:hl]
    size = convbc_o.shape[1]
    group = (size * w) // 64
    start = ((group % 2) * 2 + group // 2) * 64 + (size * w) % 64
    src = iota((256, 128), 0)
    dst = iota((256, 128), 1)
    chosen = ((src == start + dst) & (dst < size)).astype(F32)
    for k in range(3):
        part = mm(rows[8:16, 256 * k : 256 * (k + 1)], chosen, precision=HIGH)
        for r in range(3):
            if 3 * r + k < 7:
                convbc_o[3 * r + k : 3 * r + k + 1, :] = part[3 + r : 4 + r, 0:size]
    both = rows[10:11, 0:128]
    bias_o[0:1, :] = both[:, 0:hl]
    bias_o[1:2, :] = pltpu.roll(both, 64, 1)[:, 0:hl]
    rate = rows[10:11, 128:256]
    rate_o[...] = (rate + pltpu.roll(rate, 64, 1))[:, 0:hl]


def collect_kernel(
    keep, got_v, keep_bc, send_bc, tiny, plane_a, out_o, tiny_o, a_o,
    core_s, left_s, right_s, left_out, left_in, right_out, right_in, left2_out, left2_in, right2_out, right2_in,
    zsend_s, zgot_s, tcore_s, tsum_s, tgot_s, tz_s, tzgot_s, agot_s,
    core_sem, one_sem, two_sem, tiny_sem, z_sem, core_rem, one_rem, two_rem, tiny_rem, z_rem,
):
    w = lax.axis_index("wide")
    n = lax.axis_index("narrow")
    c, xx, z = w % 2, (w // 2) % 2, w // 4
    share, cols = out_o.shape
    chv = keep.shape[2]
    cut = left_s.shape[3]
    core = (w + 1 - 2 * c, n)
    over_x = (w + 2 - 4 * xx, n)
    over_y = (w, 1 - n)
    over_d = (w + 2 - 4 * xx, 1 - n)
    steps = (2, 1, 3)
    over_z = [(((z + d) % 4) * 4 + w % 4, n) for d in steps]
    mesh_ids = pl.DeviceIdType.MESH
    barrier = pltpu.get_barrier_semaphore()
    for other in [core, over_x, over_y, over_d] + over_z:
        pl.semaphore_signal(barrier, inc=1, device_id=other, device_id_type=mesh_ids)
    pl.semaphore_wait(barrier, 7)

    def copy(src, dst, out_sem, in_sem, other):
        got = pltpu.make_async_remote_copy(
            src_ref=src, dst_ref=dst, send_sem=out_sem, recv_sem=in_sem, device_id=other, device_id_type=mesh_ids
        )
        got.start()
        return got

    rows = [pl.ds(pl.multiple_of(((z + d) % 4) * (2 * share), 2 * share), 2 * share) for d in steps + (0,)]
    first = [copy(tiny, tcore_s, core_sem.at[4], core_rem.at[4], core)]
    for i in range(4):
        first.append(copy(send_bc.at[:, rows[i], :], core_s.at[i], core_sem.at[i], core_rem.at[i], core))
    a_copies = [
        copy(plane_a.at[(z + steps[k]) % 4], agot_s.at[k], z_sem.at[2, k], z_rem.at[2, k], over_z[k]) for k in range(3)
    ]
    first[0].wait()
    tsum_s[...] = tiny[...] + tcore_s[...]
    small = []
    for k, other in enumerate((over_x, over_y, over_d)):
        half = 0 if k == 0 else 1
        small.append(copy(tsum_s.at[half], tgot_s.at[k], tiny_sem.at[k], tiny_rem.at[k], other))
    second = []
    for i in range(4):
        first[i + 1].wait()
        both = jnp.concatenate(
            [
                keep[:, rows[i], :].astype(F32) + got_v[:, rows[i], :].astype(F32),
                keep_bc[:, rows[i], :].astype(F32) + core_s[i].astype(F32),
            ],
            axis=2,
        )
        low, high = both[:, 0:share, :], both[:, share:, :]
        near = jnp.where(xx == 0, low, high)
        far = jnp.where(xx == 0, high, low)
        left_s[i] = near[:, :, 0:cut]
        right_s[i, 0] = near[0, :, cut:]
        right_s[i, 1] = far[0, :, cut:]
        left_out[i] = far[:, :, 0:cut].astype(BF16)
        right_out[i, 0] = near[1, :, cut:].astype(BF16)
        right_out[i, 1] = far[1, :, cut:].astype(BF16)
        second.append(
            (
                copy(left_out.at[i], left_in.at[i], one_sem.at[i, 0], one_rem.at[i, 0], over_x),
                copy(right_out.at[i], right_in.at[i], one_sem.at[i, 1], one_rem.at[i, 1], over_y),
            )
        )
    for one in small:
        one.wait()
    tsum = tsum_s[0] + tgot_s[0] + tgot_s[1] + tgot_s[2]
    tz_s[...] = tsum
    last = [copy(tz_s, tzgot_s.at[k], z_sem.at[1, k], z_rem.at[1, k], over_z[k]) for k in range(3)]
    third = []
    for i in range(4):
        second[i][0].wait()
        left_s[i] = left_s[i] + left_in[i].astype(F32)
        left2_out[i] = left_s[i, 1].astype(BF16)
        go_left = copy(left2_out.at[i], left2_in.at[i], two_sem.at[i, 0], two_rem.at[i, 0], over_y)
        second[i][1].wait()
        right_s[i] = right_s[i] + right_in[i].astype(F32)
        right2_out[i] = right_s[i, 1].astype(BF16)
        go_right = copy(right2_out.at[i], right2_in.at[i], two_sem.at[i, 1], two_rem.at[i, 1], over_x)
        third.append((go_left, go_right))
    for i in range(4):
        third[i][0].wait()
        third[i][1].wait()
        left = left_s[i, 0] + left2_in[i].astype(F32)
        right = right_s[i, 0] + right2_in[i].astype(F32)
        if i < 3:
            zsend_s[i, :, 0:cut] = left.astype(BF16)
            zsend_s[i, :, cut:] = right.astype(BF16)
            last.append(copy(zsend_s.at[i], zgot_s.at[i], z_sem.at[0, i], z_rem.at[0, i], over_z[i]))
        else:
            out_o[:, 0:cut] = left
            out_o[:, cut:] = right
    for one in a_copies:
        one.wait()
    a_o[...] = plane_a[z].astype(F32) + agot_s[0].astype(F32) + agot_s[1].astype(F32) + agot_s[2].astype(F32)
    for one in last:
        one.wait()
    out_o[...] = out_o[...] + zgot_s[0].astype(F32) + zgot_s[1].astype(F32) + zgot_s[2].astype(F32)
    tiny_o[...] = tsum + tzgot_s[0] + tzgot_s[1] + tzgot_s[2]


def whole(shape, grid):
    zeros = (0,) * len(shape)
    if grid:
        return pl.BlockSpec(shape, lambda j: zeros)
    return pl.BlockSpec(shape, lambda: zeros)


def columns(rows, first=0):
    return pl.BlockSpec((rows, 128), lambda j: (0, first + j))


SMEM = pl.BlockSpec(memory_space=pltpu.SMEM)
VMEM = pl.BlockSpec(memory_space=pltpu.VMEM)
ANY = pl.BlockSpec(memory_space=pl.ANY)
HBM = pl.BlockSpec(memory_space=pltpu.HBM)


def sds(shape, dtype):
    return jax.ShapeDtypeStruct(shape, dtype)


def params(grid, mib):
    if grid:
        return pltpu.CompilerParams(vmem_limit_bytes=mib * 2**20, dimension_semantics=("arbitrary",))
    return pltpu.CompilerParams(vmem_limit_bytes=mib * 2**20)


def cost(us):
    return pl.CostEstimate(flops=int(us * 1.1e9), bytes_accessed=int(us * 1e6), transcendentals=0)


def pack_columns(v):
    n = v.shape[-1] // 4
    return jnp.concatenate([v[..., 0:n], v[..., 2 * n : 3 * n], v[..., n : 2 * n], v[..., 3 * n :]], axis=-1)


def small_kernel(hl, conv, gain, dtb, alog, skip, wdt, start_ref, end_ref, out_o):
    ch = out_o.shape[1]
    lane = iota((1, 128), 1)
    wide_lane = iota((1, ch), 1)
    bias = jnp.zeros((1, 128), F32)
    rate = jnp.zeros((1, 128), F32)
    diag = jnp.zeros((1, ch), F32)
    out_o[0:16, :] = jnp.zeros((16, ch), F32)
    for h in range(hl):
        cols = slice(h * HD, (h + 1) * HD)
        out_o[0:7, cols] = conv[h]
        out_o[7:8, cols] = gain[h : h + 1, :]
        bias = jnp.where(lane == h, dtb[0, h], jnp.where(lane == 64 + h, dtb[1, h], bias))
        rate = jnp.where((lane == h) | (lane == 64 + h), alog[h], rate)
        diag = jnp.where(wide_lane // HD == h, skip[h], diag)
        out_o[16 + 2 * h : 18 + 2 * h, :] = wdt[h].astype(F32)[0:2, :]
    out_o[8:9, :] = diag
    out_o[9:10, 0:128] = bias
    out_o[9:10, 128:256] = rate
    n = lax.axis_index("narrow")
    start, end = start_ref[...].astype(F32), end_ref[...].astype(F32)
    out_o[16 + 2 * hl :, :] = jnp.where(n == 0, end[8:16, :], start[0:8, :])


def swap(v):
    return lax.ppermute(v, "narrow", [(0, 1), (1, 0)])


def flip(v, bit, wide):
    return lax.ppermute(v, "wide", [(i, i ^ bit) for i in range(wide)])


def cross(v, bit, wide):
    pairs = [(i * 2 + k, (i ^ bit) * 2 + 1 - k) for i in range(wide) for k in range(2)]
    return lax.ppermute(v, ("wide", "narrow"), pairs)


def total(*parts):
    acc = parts[0].astype(F32)
    for v in parts[1:]:
        acc = acc + v.astype(F32)
    return acc


def split_positions(
    wide, layer_in, pre_gain, w_heads, w_bc, conv_x, conv_bc, dt_bias, a_log, skip_d, norm_gain, w_out, cotangent, starts, live
):
    n = lax.axis_index("narrow")
    w = lax.axis_index("wide")
    left = n == 0
    _, length, dm = layer_in.shape
    hl = w_heads.shape[1]
    heads = 2 * hl
    ch = hl * HD
    chans = 2 * ch
    pairs = heads // 2
    hp = pairs // 2
    nb = length // BLOCK
    ext = length + 2 * HALO
    share = dm // wide
    x = layer_in[0]
    g = cotangent[0]
    xbit = (w // 2) % 2

    w_turned = jnp.transpose(w_heads, (1, 2, 0))
    small_own = pl.pallas_call(
        functools.partial(small_kernel, hl),
        grid=(1,),
        out_shape=sds((24 + 2 * hl, ch), F32),
        in_specs=[
            whole((hl, 7, HD), 1), whole((hl, HD), 1), SMEM, SMEM, SMEM, pl.BlockSpec((hl, 16, dm), lambda j: (0, 8, 0)),
            pl.BlockSpec((HALO, dm), lambda j: (0, 0)), pl.BlockSpec((HALO, dm), lambda j: (length // HALO - 1, 0)),
        ],
        out_specs=whole((24 + 2 * hl, ch), 1),
        cost_estimate=cost(2),
        name="small",
    )(jnp.transpose(conv_x, (1, 0, 2)), norm_gain, dt_bias.T, a_log, skip_d, w_turned, x, x)
    small_other = swap(small_own)

    quarter = ch // 4
    q = w % 4

    def gather(p0):
        p1 = flip(p0, 2, wide)
        return p0, p1, flip(p0, 1, wide), flip(p1, 1, wide)

    def heads_rows(lo):
        return lax.dynamic_slice(w_turned, (q * (hl // 4), lo, 0), (hl // 4, HD, dm)).reshape(quarter, dm)

    wo = w_out.reshape(ch, dm)
    wv_first = swap(heads_rows(HD))
    wo_rows = lax.dynamic_slice(wo, (q * quarter, 0), (quarter, dm))
    wog_pieces = gather(swap(jnp.concatenate([wo_rows, heads_rows(0)], axis=1)))

    pos = (length, 128)
    sq = (nb, BLOCK, BLOCK)
    front_shapes = [
        ((8, chans), F32), ((8, chans), F32), ((8, chans), F32), ((128, dm), BF16), ((dm, 256), BF16), ((7, 256), F32),
        ((ext, dm), BF16), ((length, 1), F32), ((ext, 256), F32), ((ext, 256), F32), ((length, 256), BF16),
        ((2,) + sq, F32), ((4,) + sq, F32), ((3,) + sq, F32), ((128, 128), F32), ((length, 384), F32),
    ]
    late_front = (8, 9, 10, 13, 15)
    (
        info, taps, gain, skip, wdt_all, wbc, taps_bc, normed, rs, bcm, dsl, maps, tab_a, tab_b, tab_c, dpt, sig,
    ) = pl.pallas_call(
        functools.partial(front_kernel, length, hl),
        out_shape=[sds((8,), jnp.int32)]
        + [pltpu.HBM(*v) if k in late_front else sds(*v) for k, v in enumerate(front_shapes)],
        in_specs=[SMEM] + [VMEM] * 7,
        out_specs=[SMEM] + [HBM if k in late_front else VMEM for k in range(len(front_shapes))],
        scratch_shapes=[
            pltpu.VMEM((ext, 256), jnp.int32), pltpu.VMEM((ext, 256), F32), pltpu.VMEM((128, 128), F32),
            pltpu.VMEM((ext, dm), BF16),
        ]
        + [pltpu.VMEM(*front_shapes[k]) for k in late_front]
        + [pltpu.SemaphoreType.DMA((len(late_front),))],
        compiler_params=params(False, 14),
        cost_estimate=cost(6),
        name="front",
    )(starts, live, x, pre_gain.reshape(1, dm), w_bc, conv_bc, small_own, small_other)

    wv_over_x = flip(wv_first, 2, wide)

    def states(first):
        return pl.BlockSpec((1, nb + 1, 128, 128), lambda j: (j + first, 0, 0, 0))

    bnd_spec = pl.BlockSpec((1, 64, 128), lambda j: (j, 0, 0))
    state_shape = sds((pairs, nb + 1, 128, 128), BF16)
    bnd_shape = sds((hp, 64, 128), BF16)
    act_shape = sds((length, chans), BF16)
    def twin(rows, first):
        return pl.BlockSpec((rows, 256), lambda j: (0, first + j))

    def vals(other, weights, before):
        steps = hp // 2
        first = steps if other else 0
        specs = [SMEM, whole((ext, dm), 1)]
        specs += [whole((quarter, dm), 1)] * 4 if other else [pl.BlockSpec((4, 2 * HD + 2, dm), lambda j: (j, 0, 0))]
        specs += [twin(8, first), whole((2,) + sq, 1), whole((128, 128), 1)] + [ANY] * len(before)
        return pl.pallas_call(
            functools.partial(vals_kernel, length, other),
            grid=(steps,),
            out_shape=[act_shape, sds((ext, chans), BF16), act_shape, state_shape, bnd_shape] + [sds((ch, dm), BF16)] * other,
            in_specs=specs,
            out_specs=[
                twin(length, first), twin(ext, first), twin(length, first),
                pl.BlockSpec((2, nb + 1, 128, 128), lambda j: (j + first, 0, 0, 0)),
                pl.BlockSpec((2, 64, 128), lambda j: (j, 0, 0)),
            ] + [whole((ch, dm), 1)] * other,
            scratch_shapes=[pltpu.VMEM((ext, 128), F32), pltpu.VMEM((ext, 128), F32), pltpu.VMEM((ext, 128), jnp.int32)],
            input_output_aliases={len(specs) - len(before) + i: i for i in range(len(before))},
            compiler_params=params(True, 10),
            cost_estimate=cost(9),
            name="vals_other" if other else "vals_own",
        )(info, normed, *weights, taps, tab_a, dpt, *before)

    *own_vals, bnd_own = vals(False, (w_turned,), ())
    wv_pieces = wv_first, wv_over_x, flip(wv_first, 1, wide), flip(wv_over_x, 1, wide)
    xc, vm, ds, s_loc, bnd_other, wv_other = vals(True, wv_pieces, own_vals)

    def aliases(specs, before):
        return {len(specs) - len(before) + i: i for i in range(len(before))}

    def scan(first, s0, before):
        specs = [
            SMEM, columns(length, first), states(first), bnd_spec, whole((128, 128), 1), whole((4,) + sq, 1), columns(8, first),
        ] + [ANY] * len(before)
        return pl.pallas_call(
            functools.partial(scan_kernel, length, first),
            grid=(hp,),
            out_shape=[act_shape, state_shape],
            in_specs=specs,
            out_specs=[columns(length, first), states(first)],
            input_output_aliases=aliases(specs, before),
            compiler_params=params(True, 5),
            cost_estimate=cost(10),
            name="scan_other" if first else "scan_own",
        )(info, xc, s_loc, s0, dpt, tab_b, skip, *before)

    y, s_true = scan(0, swap(bnd_other), scan(hp, swap(bnd_own), ()))

    out, gy, ggate, hn, ggain, wg_other, gs_loc, gbnd = pl.pallas_call(
        functools.partial(gate_kernel, nb),
        out_shape=[
            pltpu.HBM((length, dm), BF16), act_shape, act_shape, act_shape, sds((8, chans), F32), pltpu.HBM((ch, dm), BF16),
            state_shape, sds((pairs, 64, 128), BF16),
        ],
        in_specs=[SMEM] + [VMEM] * 14,
        out_specs=[HBM, VMEM, VMEM, VMEM, VMEM, HBM, VMEM, VMEM],
        scratch_shapes=[pltpu.VMEM((ch, 2 * dm), BF16)]
        + [pltpu.VMEM((BLOCK, chans), F32)] * 4
        + [pltpu.VMEM((nb, BLOCK, chans), F32), pltpu.VMEM((length, dm), BF16), pltpu.SemaphoreType.DMA((2,))],
        compiler_params=params(False, 18),
        cost_estimate=cost(16),
        name="gated",
    )(info, x, g, normed, y, wo, w_turned, *wog_pieces, gain, tab_b, tab_c, dpt)

    gw_shape = (2, dm // 2, dm + ch)
    keep_a, send_a = pl.pallas_call(
        wsum_kernel,
        out_shape=[pltpu.HBM(gw_shape, BF16)] * 2,
        in_specs=[VMEM] * 4,
        out_specs=[HBM] * 2,
        scratch_shapes=[pltpu.VMEM(gw_shape, BF16)] * 2 + [pltpu.SemaphoreType.DMA((4,))],
        compiler_params=params(False, 10),
        cost_estimate=cost(5),
        name="wsum",
    )(g, normed, hn, ggate)

    def meet(keep, got):
        cols = keep.shape[-1]
        keep = keep.reshape(2, wide // 4, 2, share, cols)
        got = got.reshape(2, wide // 4, 2, share, cols)

        def piece(half, xx):
            def cut(v):
                return lax.dynamic_slice(v, (half, 0, xx, 0, 0), (1, wide // 4, 1, share, cols)).reshape(-1, share, cols)

            return total(cut(keep), cut(got)).astype(BF16)

        return piece(0, xbit), piece(0, 1 - xbit), piece(1, xbit), piece(1, 1 - xbit)

    def plane(mine, to_x, to_y, to_d):
        return total(mine, flip(to_x, 2, wide), swap(to_y), cross(to_d, 2, wide)).astype(mine.dtype)

    a_pieces = meet(keep_a, flip(send_a, 1, wide))

    def table(k):
        return pl.BlockSpec((None,) + sq, lambda j: (k, 0, 0, 0))

    sums = [whole(sq, 1), whole(sq, 1), whole(sq, 1), whole(pos, 1), whole(sq, 1)]
    gmix, ggt, gb, gct, ksum, rsum, phi, gskip, edge = pl.pallas_call(
        functools.partial(gscan_kernel, length),
        grid=(pairs,),
        out_shape=[
            act_shape, sds(sq, F32), sds(sq, F32), sds(sq, F32), sds(pos, F32), sds(sq, F32), sds((16, chans), F32),
            sds((8, chans), F32), sds((HALO, chans), BF16),
        ],
        in_specs=[
            SMEM, columns(length), columns(length), columns(length), states(0), states(0),
            pl.BlockSpec((1, 64, 128), lambda j: ((j + hp) % pairs, 0, 0)), whole((128, 128), 1), table(1), table(0), table(0),
            whole((3,) + sq, 1), columns(8),
        ],
        out_specs=[columns(length)] + sums + [columns(16), columns(8), columns(HALO)],
        scratch_shapes=[pltpu.VMEM((nb + 1, 128, 128), BF16)],
        compiler_params=params(True, 8),
        cost_estimate=cost(22),
        name="gscan",
    )(info, xc, ds, gy, s_true, gs_loc, swap(gbnd), dpt, tab_b, tab_a, tab_b, tab_c, skip)
    edge = swap(edge)

    gmix, *a_pieces = lax.optimization_barrier((gmix, *a_pieces))
    a_plane = plane(*a_pieces)

    gmb, gv, small, edge_bc = pl.pallas_call(
        functools.partial(join_kernel, length, heads),
        out_shape=[sds((ext, 256), F32), sds(pos, BF16), sds((16, 128), F32), sds((HALO, 256), F32)],
        in_specs=[SMEM] + [VMEM] * 9,
        out_specs=[VMEM] * 4,
        scratch_shapes=[pltpu.VMEM((ext, 128), F32), pltpu.VMEM((ext, 256), F32)],
        compiler_params=params(False, 6),
        cost_estimate=cost(6),
        name="join",
    )(info, ggt, gb, gct, ksum, rsum, phi, maps, dsl, sig)

    edge_bc = swap(edge_bc)
    sum_shape = (2, dm // 2, ch)
    gvals, keep_v, send_v, tiny = pl.pallas_call(
        functools.partial(back_kernel, length, pairs // 2),
        out_shape=[act_shape, sds(sum_shape, BF16), sds(sum_shape, BF16), sds((2, 16, ch), F32)],
        in_specs=[SMEM] + [VMEM] * 7,
        out_specs=[VMEM] * 4,
        scratch_shapes=[
            pltpu.VMEM((ext, 128), F32), pltpu.VMEM((ext, 128), F32), pltpu.VMEM((ext, 128), jnp.int32),
            pltpu.VMEM((dm, length), BF16),
        ],
        compiler_params=params(False, 10),
        cost_estimate=cost(12),
        name="back",
    )(info, gmix, edge, vm, normed, taps, ggain, gskip)

    got_v = flip(send_v, 1, wide)
    keep_bc, send_bc, tiny, grad_in = pl.pallas_call(
        functools.partial(last_kernel, length, hl),
        out_shape=[
            sds((2, dm // 2, 384), BF16), sds((2, dm // 2, 384), BF16), sds((2, 16, ch), F32), sds((length, dm), F32),
        ],
        in_specs=[SMEM] + [VMEM] * 19,
        out_specs=[VMEM] * 4,
        scratch_shapes=[pltpu.VMEM((ext, 128), F32), pltpu.VMEM((ext, 128), F32), pltpu.VMEM((ext, 128), jnp.int32)],
        compiler_params=params(False, 12),
        cost_estimate=cost(8),
        name="last",
    )(
        info, gvals, ggate, w_turned, wv_other, wg_other, normed, gmb, edge_bc, bcm, taps_bc, gv, wdt_all, wbc, x, g, rs,
        pre_gain.reshape(1, dm), small, tiny,
    )

    cols = ch + 384
    cut = 5 * cols // 9
    rest = cols - cut
    wb, tiny, wa = pl.pallas_call(
        collect_kernel,
        out_shape=[sds((share, cols), F32), sds((16, ch), F32), sds((share, dm + ch), F32)],
        in_specs=[VMEM] * 6,
        out_specs=[VMEM] * 3,
        scratch_shapes=[
            pltpu.VMEM((4, 2, 2 * share, 384), BF16),
            pltpu.VMEM((4, 2, share, cut), F32),
            pltpu.VMEM((4, 2, share, rest), F32),
        ]
        + [pltpu.VMEM((4, 2, share, cut), BF16)] * 2
        + [pltpu.VMEM((4, 2, share, rest), BF16)] * 2
        + [pltpu.VMEM((4, share, cut), BF16)] * 2
        + [pltpu.VMEM((4, share, rest), BF16)] * 2
        + [
            pltpu.VMEM((3, share, cols), BF16),
            pltpu.VMEM((3, share, cols), BF16),
            pltpu.VMEM((2, 16, ch), F32),
            pltpu.VMEM((2, 16, ch), F32),
            pltpu.VMEM((3, 16, ch), F32),
            pltpu.VMEM((16, ch), F32),
            pltpu.VMEM((3, 16, ch), F32),
            pltpu.VMEM((3, share, dm + ch), BF16),
        ]
        + [pltpu.SemaphoreType.DMA(v) for v in ((5,), (4, 2), (4, 2), (3,), (3, 3)) * 2],
        compiler_params=pltpu.CompilerParams(collective_id=0, has_side_effects=True, vmem_limit_bytes=14 * 2**20),
        name="collect",
    )(keep_v, got_v, keep_bc, send_bc, tiny, a_plane)

    g_w_heads, g_w_out, g_w_bc, g_conv_x, g_conv_bc, g_pre, g_bias, g_rate, g_skip, g_gain = pl.pallas_call(
        functools.partial(finish_kernel, hl),
        out_shape=[
            sds((hl, share, 2 * HD + 2), F32), sds((hl, share, HD), F32), sds((share, 256), F32), sds((7, HD // wide, hl), F32),
            sds((7, 256 // wide), F32), sds((1, share), F32), sds((2, hl), F32), sds((1, hl), F32), sds((1, hl), F32),
            sds((HD // wide, hl), F32),
        ],
        in_specs=[VMEM] * 3,
        out_specs=[VMEM] * 10,
        compiler_params=params(False, 8),
        name="finish",
    )(tiny, wa, wb)
    return (
        out[None],
        grad_in[None],
        g_pre[0],
        jnp.transpose(g_w_heads, (1, 0, 2)),
        g_w_bc,
        jnp.transpose(g_conv_x, (0, 2, 1)),
        g_conv_bc,
        g_bias.T,
        g_rate[0],
        g_skip[0],
        g_gain.T,
        jnp.transpose(g_w_out, (0, 2, 1)),
    )


def solution(mesh):
    body = shards
    if mesh.shape["narrow"] == 2 and mesh.shape["wide"] == 16:
        body = functools.partial(split_positions, mesh.shape["wide"])
    return jax.shard_map(
        body,
        mesh=mesh,
        in_specs=(
            P("wide", "narrow", None),
            P(),
            P(None, "narrow", None),
            P(),
            P(None, "narrow", None),
            P(),
            P("narrow", None),
            P("narrow"),
            P("narrow"),
            P("narrow", None),
            P("narrow", None, None),
            P("wide", "narrow", None),
            P("wide", None),
            P("wide", None),
        ),
        out_specs=(
            P("wide", "narrow", None),
            P("wide", "narrow", None),
            P("wide"),
            P("wide", "narrow", None),
            P("wide", None),
            P(None, "narrow", "wide"),
            P(None, "wide"),
            P("narrow", None),
            P("narrow"),
            P("narrow"),
            P("narrow", "wide"),
            P("narrow", None, "wide"),
        ),
        check_vma=False,
    )
```

```python
import functools

import jax
import jax.numpy as jnp
from jax import lax
from jax.experimental import pallas as pl
from jax.experimental.pallas import tpu as pltpu
from jax.sharding import PartitionSpec as P

H = 24
HD = 64
BLOCK = 128
SEQ_LEN = 1280


EPS = 1e-05
HIGH = lax.Precision.HIGHEST


def rounded(value):
    return value + lax.stop_gradient(value.astype(jnp.bfloat16).astype(jnp.float32) - value)


def segment_ids(starts):
    where_at = jnp.arange(SEQ_LEN, dtype=jnp.int32)
    hits = (starts[:, :, None] <= where_at[None, None, :]).astype(jnp.int32)
    return jnp.sum(hits, axis=1) - 1


def conv_doc(values, taps, seg):
    half = (taps.shape[0] - 1) // 2
    length = values.shape[1]
    padded = jnp.pad(values, ((0, 0), (half, half), (0, 0)))
    seg_pad = jnp.pad(seg, ((0, 0), (half, half)), constant_values=-1)
    total = jnp.zeros_like(values)
    for offset in range(taps.shape[0]):
        same = (seg_pad[:, offset : offset + length] == seg).astype(values.dtype)
        total = total + taps[offset] * padded[:, offset : offset + length] * same[:, :, None]
    return total


def ssd_forward(xc, steps, decays, bmat, cmat, seg, prec):
    rows, length, heads, hdim = xc.shape
    blocks = length // BLOCK
    xb = xc.reshape(rows, blocks, BLOCK, heads, hdim)
    stepb = steps.reshape(rows, blocks, BLOCK, heads)
    cum = jnp.cumsum(decays.reshape(rows, blocks, BLOCK, heads), axis=2)
    bb = bmat.reshape(rows, blocks, BLOCK, -1)
    cb = cmat.reshape(rows, blocks, BLOCK, -1)
    sb = seg.reshape(rows, blocks, BLOCK)
    order = jnp.arange(BLOCK, dtype=jnp.int32)
    causal = order[:, None] >= order[None, :]
    same = ((sb[:, :, :, None] == sb[:, :, None, :]) & causal)[..., None]
    diff = cum[:, :, :, None, :] - cum[:, :, None, :, :]
    weights = jnp.where(same, jnp.exp(jnp.where(same, diff, 0.0)), 0.0)
    inner = jnp.einsum("rbtn,rbsn->rbts", cb, bb, precision=prec)
    mix = weights * inner[..., None] * stepb[:, :, None, :, :]
    intra = jnp.einsum("rbtsh,rbshp->rbthp", mix, xb, precision=prec)
    last = sb[:, :, -1]
    cum_end = cum[:, :, -1, :]
    to_end = (
        (sb == last[:, :, None]).astype(cum.dtype)[..., None]
        * jnp.exp(cum_end[:, :, None, :] - cum)
        * stepb
    )
    states = jnp.einsum("rbshp,rbsn->rbhpn", to_end[..., None] * xb, bb, precision=prec)
    decay_end = jnp.exp(cum_end)

    def carry_step(carry, item):
        state, seg_prev = carry
        block_state, block_last, block_decay = item
        keep = (block_last == seg_prev).astype(state.dtype)[:, None, None, None]
        fresh = keep * block_decay[:, :, None, None] * state + block_state
        return ((fresh, block_last), (state, seg_prev))

    init = (
        jnp.zeros((rows, heads, hdim, bb.shape[-1]), xc.dtype),
        jnp.full((rows,), -1, jnp.int32),
    )
    items = (jnp.moveaxis(states, 1, 0), jnp.moveaxis(last, 1, 0), jnp.moveaxis(decay_end, 1, 0))
    _, (before, seg_before) = lax.scan(carry_step, init, items)
    before = jnp.moveaxis(before, 0, 1)
    seg_before = jnp.moveaxis(seg_before, 0, 1)
    enter = (sb == seg_before[:, :, None]).astype(cum.dtype)[..., None] * jnp.exp(cum)
    inter = jnp.einsum("rbtn,rbhpn->rbthp", cb, before, precision=prec) * enter[..., None]
    return (intra + inter).reshape(rows, length, heads, hdim)


def mixer(proj, bcproj, conv_x, conv_bc, dt_bias, a_log, skip_d, seg, mask, rounder, prec):
    rows, length, heads, width = proj.shape
    hdim = (width - 2) // 2
    state = bcproj.shape[-1] // 4
    gate = proj[..., :hdim]
    values = proj[..., hdim : 2 * hdim] * mask[:, :, None, None]
    mixed_x = conv_doc(
        values.reshape(rows, length, heads * hdim),
        conv_x.reshape(conv_x.shape[0], heads * hdim),
        seg,
    )
    xc = rounder(jax.nn.silu(mixed_x)).reshape(rows, length, heads, hdim)
    maps = rounder(jax.nn.silu(conv_doc(bcproj * mask[:, :, None], conv_bc, seg)))
    b_fwd = maps[..., :state]
    c_fwd = maps[..., state : 2 * state]
    b_bwd = maps[..., 2 * state : 3 * state]
    c_bwd = maps[..., 3 * state :]
    rate = -jnp.exp(a_log)
    dt_fwd = jax.nn.softplus(proj[..., 2 * hdim] + dt_bias[:, 0]) * mask[:, :, None]
    dt_bwd = jax.nn.softplus(proj[..., 2 * hdim + 1] + dt_bias[:, 1]) * mask[:, :, None]
    out_fwd = ssd_forward(xc, dt_fwd, dt_fwd * rate, b_fwd, c_fwd, seg, prec)

    def flip(v):
        return jnp.flip(v, axis=1)

    out_bwd = flip(
        ssd_forward(
            flip(xc), flip(dt_bwd), flip(dt_bwd * rate), flip(b_bwd), flip(c_bwd), flip(seg), prec
        )
    )
    keep_prev = (seg[:, 1:] == seg[:, :-1]).astype(xc.dtype)[:, :, None, None]
    shifted_fwd = jnp.pad(out_fwd[:, :-1] * keep_prev, ((0, 0), (1, 0), (0, 0), (0, 0)))
    shifted_bwd = jnp.pad(out_bwd[:, 1:] * keep_prev, ((0, 0), (0, 1), (0, 0), (0, 0)))
    return (shifted_fwd + shifted_bwd + skip_d[:, None] * xc, gate)


def shards(
    layer_in,
    pre_gain,
    w_heads,
    w_bc,
    conv_x,
    conv_bc,
    dt_bias,
    a_log,
    skip_d,
    norm_gain,
    w_out,
    cotangent,
    starts,
    live,
):
    seg = segment_ids(starts)
    mask = live.astype(jnp.float32)
    x_here = layer_in.astype(jnp.float32)
    scale = lax.rsqrt(jnp.mean(x_here * x_here, axis=-1, keepdims=True) + EPS)
    normed_here = (x_here * scale * pre_gain).astype(jnp.bfloat16)
    normed = lax.all_gather(normed_here, "narrow", axis=1, tiled=True)
    proj = jnp.einsum("rld,dhc->rlhc", normed, w_heads, preferred_element_type=jnp.float32)
    bcproj = jnp.einsum("rld,dc->rlc", normed, w_bc, preferred_element_type=jnp.float32)

    def mix_local(proj_in, bc_in, taps_x, taps_bc, bias_in, log_rate, diag_in):
        return mixer(
            proj_in, bc_in, taps_x, taps_bc, bias_in, log_rate, diag_in, seg, mask, rounded, HIGH
        )

    (ymix, gate), pull_mix = jax.vjp(
        mix_local, proj, bcproj, conv_x, conv_bc, dt_bias, a_log, skip_d
    )
    rows, length, heads, hdim = ymix.shape
    sigma = jax.nn.sigmoid(gate)
    act = gate * sigma
    gated = (ymix * act).reshape(rows, length, heads * hdim)
    squares = lax.psum(jnp.sum(gated * gated, axis=-1), "narrow")
    inv = lax.rsqrt(squares / (H * HD) + EPS)[..., None]
    gain_flat = norm_gain.reshape(-1)
    normalized = gated * inv
    hn = (normalized * gain_flat).astype(jnp.bfloat16)
    w_flat = w_out.reshape(heads * hdim, -1)
    partial_value = jnp.einsum("rlc,cd->rld", hn, w_flat, preferred_element_type=jnp.float32)
    branch = lax.psum_scatter(partial_value, "narrow", scatter_dimension=1, tiled=True)
    out = (x_here + branch).astype(jnp.bfloat16)
    grad_out = lax.all_gather(cotangent, "narrow", axis=1, tiled=True)
    g_w_out = jnp.einsum("rlc,rld->cd", hn, grad_out, preferred_element_type=jnp.float32)
    g_hn = jnp.einsum("rld,cd->rlc", grad_out, w_flat, preferred_element_type=jnp.float32)
    g_gain = jnp.sum(g_hn * normalized, axis=(0, 1))
    weighted = g_hn * gain_flat
    cross = lax.psum(jnp.sum(weighted * gated, axis=-1), "narrow")
    g_gated = inv * weighted - gated * (inv * inv * inv) * (cross / (H * HD))[..., None]
    g_gated = g_gated.reshape(rows, length, heads, hdim)
    g_ymix = g_gated * act
    g_gate = g_gated * ymix * (sigma * (1.0 + gate * (1.0 - sigma)))
    g_proj, g_bcproj, g_conv_x, g_conv_bc, g_dt_bias, g_a_log, g_skip = pull_mix((g_ymix, g_gate))
    g_proj_low = g_proj.astype(jnp.bfloat16)
    g_w_heads = jnp.einsum("rld,rlhc->dhc", normed, g_proj_low, preferred_element_type=jnp.float32)
    g_w_bc = jnp.einsum(
        "rld,rlc->dc", normed, g_bcproj, precision=HIGH, preferred_element_type=jnp.float32
    )
    g_normed = jnp.einsum("rlhc,dhc->rld", g_proj_low, w_heads, preferred_element_type=jnp.float32)
    g_normed = g_normed + jnp.einsum(
        "rlc,dc->rld", g_bcproj, w_bc, precision=HIGH, preferred_element_type=jnp.float32
    )
    g_normed_here = lax.psum_scatter(g_normed, "narrow", scatter_dimension=1, tiled=True)
    weighted_in = g_normed_here * pre_gain
    g_pre = jnp.sum(g_normed_here * x_here * scale, axis=(0, 1))
    g_x = scale * weighted_in - x_here * (scale * scale * scale) * jnp.mean(
        weighted_in * x_here, axis=-1, keepdims=True
    )
    grad_input = cotangent.astype(jnp.float32) + g_x
    g_pre, g_w_bc, g_conv_bc = lax.psum((g_pre, g_w_bc, g_conv_bc), "narrow")
    reduced = (
        lax.psum_scatter(g_w_heads, "wide", scatter_dimension=0, tiled=True),
        lax.psum_scatter(g_w_out.reshape(heads, hdim, -1), "wide", scatter_dimension=2, tiled=True),
        lax.psum_scatter(g_conv_x, "wide", scatter_dimension=2, tiled=True),
        lax.psum_scatter(g_gain.reshape(heads, hdim), "wide", scatter_dimension=1, tiled=True),
        lax.psum_scatter(g_pre, "wide", scatter_dimension=0, tiled=True),
        lax.psum_scatter(g_w_bc, "wide", scatter_dimension=0, tiled=True),
        lax.psum_scatter(g_conv_bc, "wide", scatter_dimension=1, tiled=True),
    )
    share_pre, share_bc, share_conv = (reduced[4], reduced[5], reduced[6])
    head_bias, head_rate, head_diag = lax.psum((g_dt_bias, g_a_log, g_skip), "wide")
    return (
        out,
        grad_input,
        share_pre,
        reduced[0],
        share_bc,
        reduced[2],
        share_conv,
        head_bias,
        head_rate,
        head_diag,
        reduced[3],
        reduced[1],
    )


HALO = 16
F32 = jnp.float32
BF16 = jnp.bfloat16
LOGZERO = -1e30


def mm(a, b, dims=((1,), (0,)), precision=None):
    return lax.dot_general(a, b, (dims, ((), ())), precision=precision, preferred_element_type=F32)


def nt(a, b):
    return mm(a, b, ((1,), (1,)))


def tn(a, b):
    return mm(a, b, ((0,), (0,)))


def seg_at(info, pos):
    seg = jnp.full(pos.shape, -1, jnp.int32)
    for j in range(4):
        seg = seg + (pos >= info[j]).astype(jnp.int32)
    return jnp.where(pos >= info[6], 99, seg)


def iota(shape, dim):
    return lax.broadcasted_iota(jnp.int32, shape, dim)


def silu_parts(v):
    sg = 0.5 * jnp.tanh(0.5 * v) + 0.5
    act = v * sg
    return act, sg + act * (1.0 - sg)


def thirds(v):
    hi = v.astype(BF16).astype(F32)
    rest = v - hi
    mid = rest.astype(BF16).astype(F32)
    return hi, mid, rest - mid


def column_terms(values):
    sub = iota((16, 128), 0)
    v = jnp.ones((16, 128), F32)
    for k, value in enumerate(values):
        v = jnp.where((sub >= 3 * k) & (sub < 3 * k + 3), value, v)
    hi, mid, low = thirds(v)
    part = sub % 3
    out = jnp.where(part == 0, hi, jnp.where(part == 1, mid, low))
    return jnp.where(sub < 3 * len(values), out, 1.0).astype(BF16)


def row_base(count, places):
    sub = iota((16, 384), 0)
    lane = iota((16, 384), 1)
    out = jnp.zeros((16, 384), F32)
    for k, spans in enumerate(places):
        for lo, hi in spans:
            out = jnp.where((sub >= 3 * k) & (sub < 3 * k + 3) & (lane >= lo) & (lane < hi), 1.0, out)
    return out


def row_terms(count, base, one, two):
    sub = iota((16, 128), 0)
    part = sub - 3 * count
    made = []
    for k, value in enumerate((one, two)):
        hi, mid, low = thirds(jnp.broadcast_to(value, (16, 128)))
        here = base[:, 128 * k : 128 * (k + 1)]
        made.append(
            jnp.where(part == 0, hi, jnp.where(part == 1, mid, jnp.where(part == 2, low, here))).astype(BF16)
        )
    return jnp.concatenate(made + [base[:, 256:].astype(BF16)], axis=1)


def conv_taps(src, seg_src, taps, first, rows):
    seg0 = seg_src[first : first + rows, :]
    total = src[first : first + rows, :] * taps[3:4, :]
    for k in (0, 1, 2, 4, 5, 6):
        lo = first + k - 3
        same = seg_src[lo : lo + rows, :] == seg0
        total = total + jnp.where(same, src[lo : lo + rows, :], 0.0) * taps[k : k + 1, :]
    return total


def front_kernel(
    length, hl, starts, live_ref, x_in, gain, wbc_ref, taps_ref, small_a, small_b,
    info, taps_o, gain_o, skip_o, wdt, wbc, taps, normed_o, rs_o, bcm_h, dsl_h, maps_h, ta_o, tb_o, tc_h, dpt_o, sig_h, seg_s, maps_s, cum_s, x_s, bcm_o, dsl_o, maps_o, tc_o, sig_o, sems,
):
    late = []

    def send(src, dst):
        late.append(pltpu.make_async_copy(src, dst, sems.at[len(late)]))
        late[-1].start()

    nb = length // BLOCK
    ext = length + 2 * HALO
    dm = x_in.shape[1]
    n = lax.axis_index("narrow")
    for i in range(4):
        info[i] = starts[0, i]
    count = jnp.sum(live_ref[...].astype(F32)).astype(jnp.int32)
    off = n * length
    info[4] = count
    info[5] = off
    info[6] = live_ref.shape[1]
    info[7] = n
    ch = small_a.shape[1]
    for k, small in enumerate((small_a, small_b)):
        cols = slice(k * ch, (k + 1) * ch)
        taps_o[:, cols] = small[0:8, :]
        gain_o[:, cols] = jnp.broadcast_to(small[7:8, :], (8, ch))
        skip_o[:, cols] = jnp.broadcast_to(small[8:9, :], (8, ch))
    dst = iota((128, 2 * hl), 0)
    src = iota((128, 2 * hl), 1)
    place = (src % 2) * 64 + src // 2
    at_a = jnp.where(dst == place, 1.0, 0.0).astype(BF16)
    at_b = jnp.where(dst == place + hl, 1.0, 0.0).astype(BF16)
    own_steps = small_a[16 : 16 + 2 * hl, :].astype(BF16)
    far_steps = small_b[16 : 16 + 2 * hl, :].astype(BF16)
    wdt[...] = (mm(at_a, own_steps) + mm(at_b, far_steps)).astype(BF16)
    wbc[...] = pack_columns(wbc_ref[...])
    taps[...] = pack_columns(taps_ref[...])

    bias = small_a[9:10, 0:128] + pltpu.roll(small_b[9:10, 0:128], hl, 1)
    alog = small_a[9:10, 128:256] + pltpu.roll(small_b[9:10, 128:256], hl, 1)
    edge = small_b[16 + 2 * hl : 24 + 2 * hl, :]
    zero_edge = jnp.zeros((8, dm), F32)
    before = jnp.concatenate([zero_edge, jnp.where(n == 1, edge, 0.0)], axis=0)
    behind = jnp.concatenate([jnp.where(n == 1, 0.0, edge), zero_edge], axis=0)
    x_s[0:HALO, :] = before.astype(BF16)
    x_s[HALO : HALO + length, :] = x_in[...]
    x_s[HALO + length : ext, :] = behind.astype(BF16)
    x = x_s[...].astype(F32)
    rs = lax.rsqrt(jnp.mean(x * x, axis=1, keepdims=True) + EPS)
    normed = (x * rs * gain[...]).astype(BF16)
    normed_o[...] = normed
    rs_o[...] = rs[HALO : HALO + length, :]
    pos256 = iota((ext, 256), 0) + (off - HALO)
    seg_s[...] = seg_at(info, pos256)
    live = pos256 < count
    bcm_o[...] = jnp.where(live, mm(normed, wbc[...]), 0.0)
    send(bcm_o, bcm_h)
    crows = length + HALO
    cfirst = HALO // 2
    mix = conv_taps(bcm_o, seg_s, taps, cfirst, crows)
    maps, dsl = silu_parts(mix)
    dsl_o[...] = jnp.zeros_like(dsl_o)
    dsl_o[cfirst : cfirst + crows, :] = dsl
    send(dsl_o, dsl_h)
    maps_s[...] = jnp.zeros_like(maps_s)
    maps_s[cfirst : cfirst + crows, :] = maps.astype(BF16).astype(F32)
    own = slice(HALO, HALO + length)
    segx = seg_s[own, 0:128]
    lane = iota((length, 128), 1)
    fwd = lane < 64
    segp = seg_s[HALO - 1 : HALO - 1 + length, 0:128]
    segn = seg_s[HALO + 1 : HALO + 1 + length, 0:128]
    bmap = maps_s[own, 0:128]
    cprev = jnp.where(segp == segx, maps_s[HALO - 1 : HALO - 1 + length, 128:256], 0.0)
    cnext = jnp.where(segn == segx, maps_s[HALO + 1 : HALO + 1 + length, 128:256], 0.0)
    cmap = jnp.where(fwd, cprev, cnext)
    maps_o[:, 0:128] = bmap.astype(BF16)
    maps_o[:, 128:256] = cmap.astype(BF16)
    send(maps_o, maps_h)
    raw = nt(normed[own, :], wdt[...]) + bias
    softp = jnp.maximum(raw, 0.0) + jnp.log(1.0 + jnp.exp(-jnp.abs(raw)))
    softp = jnp.where(raw < -15.0, jnp.exp(jnp.minimum(raw, 0.0)), softp)
    pos128 = iota((length, 128), 0) + off
    m = pos128 < count
    dt = jnp.where(m, softp, 0.0)
    sg = jnp.where(m, 1.0 / (1.0 + jnp.exp(-raw)), 0.0)
    ratio = jnp.where(m, jnp.where(raw < -15.0, 1.0, sg / jnp.maximum(softp, 1e-30)), 0.0)
    rate = -jnp.exp(alog)
    a = dt * rate
    sig_o[:, 256:384] = a
    sig_o[:, 0:128] = sg * rate
    sig_o[:, 128:256] = ratio
    tri = (iota((BLOCK, BLOCK), 0) >= iota((BLOCK, BLOCK), 1)).astype(F32)
    logdt = jnp.maximum(jnp.log(dt), LOGZERO)
    sub = iota((BLOCK, BLOCK), 0)
    ln = iota((BLOCK, BLOCK), 1)
    fwdb = ln < 64
    cum_s[...] = jnp.zeros_like(cum_s)
    dvals, ends = [], []
    for b in range(nb):
        blk = slice(b * BLOCK, (b + 1) * BLOCK)
        ab = a[blk, :]
        cum = mm(tri, ab, precision=HIGH)
        cx = cum - ab
        end = cum[BLOCK - 1 : BLOCK, :]
        colt = jnp.where(fwdb, cx, end - cum)
        rows = jnp.where(fwdb, logdt[blk, :] - cum, cx + logdt[blk, :] - end)
        tb_o[0, b] = colt.T
        tb_o[1, b] = rows.T
        ta_o[0, b] = jnp.minimum(rows + end, 60.0).T
        first_pos = off + b * BLOCK
        sp = seg_at(info, sub + first_pos)
        st = seg_at(info, ln + first_pos)
        before = seg_at(info, sub * 0 + (first_pos - 1))
        begin = seg_at(info, sub * 0 + first_pos)
        last = seg_at(info, sub * 0 + (first_pos + BLOCK - 1))
        after = seg_at(info, sub * 0 + (first_pos + BLOCK))
        enter = jnp.where(fwdb, (sp == before).astype(F32), (sp == after).astype(F32))
        keep = jnp.where(fwdb, (sp == last).astype(F32), (sp == begin).astype(F32))
        ce = cmap[blk, :] * enter
        bk = bmap[blk, :] * keep
        tb_o[3, b] = ce
        tc_o[1, b] = bk
        tc_o[2, b] = ce.T
        ta_o[1, b] = bk.T
        chain = jnp.where(fwdb[0:1, :], (last == before).astype(F32)[0:1, :], (begin == after).astype(F32)[0:1, :])
        dvals.append(jnp.exp(end) * chain)
        ends.append(end)
        cb = cmap[blk, :].astype(BF16)
        bb = bmap[blk, :].astype(BF16)
        zero = jnp.zeros_like(bb)
        same = sp == st
        low = same & (sub > ln)
        high = same & (sub < ln)
        bf = jnp.where(fwdb, bb, zero)
        br = jnp.where(fwdb, zero, bb)
        tb_o[2, b] = jnp.where(low, nt(cb, bf), jnp.where(high, nt(cb, br), 0.0))
        tc_o[0, b] = jnp.where(high, nt(bf, cb), jnp.where(low, nt(br, cb), 0.0))
    ones = jnp.ones((1, 128), F32)
    prefix, suffix = [ones], [ones]
    for b in range(nb):
        prefix.append(prefix[-1] * dvals[b])
        suffix.append(suffix[-1] * dvals[nb - 1 - b])
    suffix = suffix[::-1]
    f1 = fwdb[0:1, :]
    for b in range(nb):
        cum_s[b : b + 1, :] = dvals[b]
        cum_s[48 + b : 49 + b, :] = ends[b]
    for i in range(nb + 1):
        cum_s[16 + i : 17 + i, :] = jnp.where(f1, prefix[i], suffix[i])
        cum_s[32 + i : 33 + i, :] = jnp.where(f1, suffix[i], prefix[i])
    dpt_o[...] = cum_s[...].T
    send(sig_o, sig_h)
    send(tc_o, tc_h)
    for one in late:
        one.wait()


def pair_rows(dpt, j, base, i, half):
    lane = iota((1, 128), 1)
    one = dpt[pl.ds(half * 64 + 2 * j, 1), :][:, base + i : base + i + 1]
    two = dpt[pl.ds(half * 64 + 2 * j + 1, 1), :][:, base + i : base + i + 1]
    return jnp.where(lane < 64, one, two)


def assemble(dst, pieces):
    quarter = dst.shape[0] // 4
    q = lax.axis_index("wide") % 4
    cbit = q % 2
    xbit = q // 2
    places = (q, (1 - xbit) * 2 + cbit, xbit * 2 + 1 - cbit, (1 - xbit) * 2 + 1 - cbit)
    for place, piece in zip(places, pieces):
        dst[pl.ds(pl.multiple_of(place * quarter, quarter), quarter), :] = piece[...]


def vals_kernel(length, other, info, normed, *refs):
    nb = length // BLOCK
    ext = length + 2 * HALO
    step = pl.program_id(0)
    first = step
    if other:
        p0, p1, p2, p3, taps, ta, dpt = refs[:7]
        xc_o, vm_o, ds_o, s_o, bnd_o, wvo_o, vm_a, vm_b, seg_s = refs[11:]
        first = step + pl.num_programs(0)

        @pl.when(step == 0)
        def _():
            assemble(wvo_o, (p0, p1, p2, p3))

        wv = wvo_o[pl.ds(pl.multiple_of(step * 256, 256), 256), :]
    else:
        w_ref, taps, ta, dpt, xc_o, vm_o, ds_o, s_o, bnd_o, vm_a, vm_b, seg_s = refs
        wv = jnp.concatenate([w_ref[h, HD : 2 * HD, :] for h in range(4)], axis=0)
    off, count = info[5], info[4]

    @pl.when(step == 0)
    def _():
        seg_s[...] = seg_at(info, iota((ext, 128), 0) + (off - HALO))

    live = iota((ext, 128), 0) + (off - HALO) < count
    both = nt(normed[...], wv)
    lane = iota((BLOCK, 128), 1)
    top = iota((BLOCK, 128), 0) < 64
    for p, vm_s in enumerate((vm_a, vm_b)):
        j = 2 * first + p
        here = slice(128 * p, 128 * (p + 1))
        vm = jnp.where(live, both[:, here], 0.0)
        vm_s[...] = vm
        vm_o[:, here] = vm.astype(BF16)
        act, ds = silu_parts(conv_taps(vm_s, seg_s, taps[:, here], HALO, length))
        xc = act.astype(BF16)
        xc_o[:, here] = xc
        ds_o[:, here] = ds.astype(BF16)
        loc = []
        for b in range(nb):
            blk = slice(b * BLOCK, (b + 1) * BLOCK)
            got = []
            for i in range(2):
                h = 2 * j + i
                w = jnp.where(top, jnp.exp(ta[0, b, pl.ds(h, 1), :]), jnp.exp(ta[0, b, pl.ds(64 + h, 1), :]))
                got.append((ta[1, b] * w).astype(BF16))
            got = mm(jnp.concatenate(got, axis=0), xc[blk, :])
            loc.append(jnp.where(lane < 64, got[0:BLOCK, :], got[BLOCK:, :]))
        state = jnp.zeros((64, 128), F32)
        s_o[p, 0, 0:64, :] = state.astype(BF16)
        for b in range(nb):
            state = pair_rows(dpt, j, 0, b, 0) * state + loc[b][0:64, :]
            s_o[p, b + 1, 0:64, :] = state.astype(BF16)
        end_f = state
        state = jnp.zeros((64, 128), F32)
        s_o[p, nb, 64:128, :] = state.astype(BF16)
        for b in range(nb - 1, -1, -1):
            state = pair_rows(dpt, j, 0, b, 1) * state + loc[b][64:128, :]
            s_o[p, b, 64:128, :] = state.astype(BF16)
        bnd_o[p] = jnp.where(info[7] == 0, end_f, state).astype(BF16)


def scan_kernel(length, first_pair, info, xc_ref, s_ref, s0_ref, dpt, tb, skip, *refs):
    nb = length // BLOCK
    y_o, st_o = refs[-2:]
    j = pl.program_id(0) + first_pair
    right = (info[7] == 1).astype(F32)
    s0 = s0_ref[0].astype(F32)
    lane = iota((BLOCK, 128), 1)
    first = lane < 64
    low = iota((BLOCK, BLOCK), 0) > lane
    base = row_base(2, [[(0, 128), (256, 320)], [(128, 256), (320, 384)]])
    for i in range(nb + 1):
        f = s_ref[0, i, 0:64, :].astype(F32) + pair_rows(dpt, j, 16, i, 0) * (s0 * right)
        r = s_ref[0, i, 64:128, :].astype(F32) + pair_rows(dpt, j, 16, i, 1) * (s0 * (1.0 - right))
        st_o[0, i, 0:64, :] = f.astype(BF16)
        st_o[0, i, 64:128, :] = r.astype(BF16)
    for b in range(nb):
        blk = slice(b * BLOCK, (b + 1) * BLOCK)
        xb = xc_ref[blk, :]
        rhs = jnp.concatenate([xb, st_o[0, b, 0:64, :], st_o[0, b + 1, 64:128, :]], axis=0)
        got = []
        for i in range(2):
            h = 2 * j + i
            terms = column_terms([tb[0, b, pl.ds(h, 1), :], tb[0, b, pl.ds(64 + h, 1), :]])
            expo = tn(terms, row_terms(2, base, tb[1, b, pl.ds(h, 1), :], tb[1, b, pl.ds(64 + h, 1), :]))
            diff = jnp.where(low, expo[:, 0:128], expo[:, 128:256])
            mix = jnp.exp(jnp.minimum(diff, 60.0)) * tb[2, b]
            ct = tb[3, b] * jnp.exp(expo[:, 256:])
            lhs = jnp.concatenate([mix.astype(BF16), ct.astype(BF16)], axis=1)
            got.append(lhs)
        got = mm(jnp.concatenate(got, axis=0), rhs)
        y = jnp.where(first, got[0:BLOCK, :], got[BLOCK:, :]) + skip[0:1, :] * xb.astype(F32)
        y_o[blk, :] = y.astype(BF16)


def by_core(v, keep, send):
    share = v.shape[0] // 16
    cbit = lax.axis_index("wide") % 2
    v = v.astype(BF16).reshape(8, 2, share, v.shape[1])
    keep[...] = jnp.where(cbit == 0, v[:, 0], v[:, 1]).reshape(8 * share, v.shape[3])
    send[...] = jnp.where(cbit == 0, v[:, 1], v[:, 0]).reshape(8 * share, v.shape[3])


def gate_kernel(
    tiles, info, x_ref, g_ref, normed, y_ref, wout_a, w_ref, p0, p1, p2, p3, gain, tb, tc, dpt,
    out_h, gy_o, ggate_o, hn_s, ggain_o, wgo_h, gs_o, bnd_o, other_s, gated_s, act_s, dact_s, ghn_s, loc_s, out_o, sems,
):
    late = []

    def send(src, dst):
        late.append(pltpu.make_async_copy(src, dst, sems.at[len(late)]))
        late[-1].start()

    dm = x_ref.shape[1]
    chans = y_ref.shape[1]
    half = chans // 2
    step = 256
    assemble(other_s, (p0, p1, p2, p3))
    send(other_s.at[:, dm:], wgo_h)
    ggain_o[...] = jnp.zeros_like(ggain_o)
    first = iota((BLOCK, 128), 1) < 64
    top = iota((BLOCK, 128), 0) < 64

    @pl.loop(0, tiles)
    def _(i):
        start = pl.multiple_of(i * BLOCK, BLOCK)
        rows = pl.ds(start, BLOCK)
        nrows = normed[pl.ds(pl.multiple_of(start + HALO, HALO), BLOCK), :]
        squares = jnp.zeros((BLOCK, 128), F32)
        for lo in range(0, chans, step):
            if lo < half:
                heads = range(lo // HD, (lo + step) // HD)
                wg = jnp.concatenate([w_ref[h, 0:HD, :] for h in heads], axis=0)
            else:
                wg = other_s[lo - half : lo - half + step, dm:]
            gates = nt(nrows, wg)
            for at in range(0, step, 128):
                cols = slice(lo + at, lo + at + 128)
                act, dact = silu_parts(gates[:, at : at + 128])
                gated = y_ref[rows, cols].astype(F32) * act
                squares = squares + gated * gated
                gated_s[:, cols] = gated
                act_s[:, cols] = act
                dact_s[:, cols] = dact
        inv = lax.rsqrt(jnp.sum(squares, axis=1, keepdims=True) * (1.0 / chans) + EPS)
        inv = jnp.broadcast_to(inv, (BLOCK, 128))
        g = g_ref[rows, :]
        across = jnp.zeros((BLOCK, 128), F32)
        for lo in range(0, chans, step):
            wo = wout_a[lo : lo + step, :] if lo < half else other_s[lo - half : lo - half + step, 0:dm]
            ghns = nt(g, wo)
            for at in range(0, step, 128):
                cols = slice(lo + at, lo + at + 128)
                gainv = gain[0:1, cols]
                gated = gated_s[:, cols]
                nrm = gated * inv
                hn_s[rows, cols] = (nrm * gainv).astype(BF16)
                ghn = ghns[:, at : at + 128]
                ggain_o[0:1, cols] += jnp.sum(ghn * nrm, axis=0, keepdims=True)
                wgt = ghn * gainv
                ghn_s[:, cols] = wgt
                across = across + wgt * gated
        cross = jnp.sum(across, axis=1, keepdims=True) * (1.0 / chans)
        cross = jnp.broadcast_to(cross, (BLOCK, 128)) * (inv * inv * inv)
        hn = hn_s[rows, :]
        branch = mm(hn[:, 0:half], wout_a[...]) + mm(hn[:, half:], other_s[:, 0:dm])
        out_o[rows, :] = (x_ref[rows, :].astype(F32) + branch).astype(BF16)
        for lo in range(0, chans, 128):
            cols = slice(lo, lo + 128)
            ggated = inv * ghn_s[:, cols] - gated_s[:, cols] * cross
            gy = (ggated * act_s[:, cols]).astype(BF16)
            gy_o[rows, cols] = gy
            ggate_o[rows, cols] = (ggated * y_ref[rows, cols].astype(F32) * dact_s[:, cols]).astype(BF16)
            got = []
            for h in range(lo // HD, lo // HD + 2):
                e = jnp.where(top, jnp.exp(tb[0, i, h : h + 1, :]), jnp.exp(tb[0, i, 64 + h : 65 + h, :]))
                got.append((tc[2, i] * e).astype(BF16))
            got = mm(jnp.concatenate(got, axis=0), gy)
            loc_s[i, :, cols] = jnp.where(first, got[0:BLOCK, :], got[BLOCK:, :])

    send(out_o, out_h)

    @pl.loop(0, chans // 128)
    def _(j):
        cols = pl.ds(pl.multiple_of(j * 128, 128), 128)
        state = jnp.zeros((64, 128), F32)
        gs_o[j, tiles, 0:64, :] = state.astype(BF16)
        for b in range(tiles - 1, -1, -1):
            state = pair_rows(dpt, j, 0, b, 0) * state + loc_s[b, 0:64, cols]
            gs_o[j, b, 0:64, :] = state.astype(BF16)
        end_f = state
        state = jnp.zeros((64, 128), F32)
        gs_o[j, 0, 64:128, :] = state.astype(BF16)
        for b in range(tiles):
            state = pair_rows(dpt, j, 0, b, 1) * state + loc_s[b, 64:128, cols]
            gs_o[j, b + 1, 64:128, :] = state.astype(BF16)
        bnd_o[j] = jnp.where(info[7] == 1, end_f, state).astype(BF16)

    for one in late:
        one.wait()


def wsum_kernel(g_ref, normed, hn, ggate, mine_o, x_o, y_o, d_o, keep_s, send_s, got_s, out_sem, in_sem):
    length, dm = g_ref.shape
    half = hn.shape[1] // 2
    share = mine_o.shape[1]
    w = lax.axis_index("wide")
    core = (w + 1 - 2 * (w % 2), lax.axis_index("narrow"))
    xx = (w // 2) % 2
    mesh_ids = pl.DeviceIdType.MESH
    barrier = pltpu.get_barrier_semaphore()
    pl.semaphore_signal(barrier, inc=1, device_id=core, device_id_type=mesh_ids)
    turned = (g_ref[...].T, normed[HALO : HALO + length, :].T)
    going = []
    for k in range(2):
        for part, source in enumerate((hn, ggate)):
            for p in range(half // 256):
                cols = slice(k * half + p * 256, k * half + (p + 1) * 256)
                dst = slice(part * half + p * 256, part * half + (p + 1) * 256)
                by_core(mm(turned[part], source[:, cols]), keep_s.at[k, :, dst], send_s.at[k, :, dst])
            if not going:
                pl.semaphore_wait(barrier, 1)
            cols = slice(part * half, (part + 1) * half)
            one = pltpu.make_async_remote_copy(
                src_ref=send_s.at[k, :, cols], dst_ref=got_s.at[k, :, cols], send_sem=out_sem.at[k, part],
                recv_sem=in_sem.at[k, part], device_id=core, device_id_type=mesh_ids,
            )
            one.start()
            going.append((k, cols, one))
    for k, cols, one in going:
        one.wait()
        near_o, far_o = ((mine_o, x_o), (y_o, d_o))[k]
        for q in range(4):
            rows = slice(q * 2 * share, (q + 1) * 2 * share)
            both = (keep_s[k, rows, cols].astype(F32) + got_s[k, rows, cols].astype(F32)).astype(BF16)
            low, high = both[0:share, :], both[share:, :]
            near_o[q, :, cols] = jnp.where(xx == 0, low, high)
            far_o[q, :, cols] = jnp.where(xx == 0, high, low)


def gscan_kernel(
    length, info, xc_ref, ds_ref, gy_ref, st_ref, gs_ref, gs0_ref, dpt, rowst, wt, coltt, tc, skip,
    gmix_o, ggt_o, gb_o, gct_o, k_o, r_o, phi_o, gskip_o, edge_o, gst_s,
):
    nb = length // BLOCK
    j = pl.program_id(0)
    right = (info[7] == 1).astype(F32)
    s0 = gs0_ref[0].astype(F32)
    sub = iota((BLOCK, BLOCK), 0)
    lane = iota((BLOCK, 128), 1)
    first = lane < 64
    later = lane > sub
    top = sub < 64

    @pl.when(j == 0)
    def _():
        for acc in (ggt_o, gb_o, gct_o, k_o, r_o):
            acc[...] = jnp.zeros_like(acc)

    base = row_base(4, [[(0, 128)], [(128, 256)], [(256, 320)], [(320, 384)]])

    phi_o[...] = jnp.zeros_like(phi_o)
    for i in range(nb + 1):
        f = gs_ref[0, i, 0:64, :].astype(F32) + pair_rows(dpt, j, 32, i, 0) * (s0 * (1.0 - right))
        r = gs_ref[0, i, 64:128, :].astype(F32) + pair_rows(dpt, j, 32, i, 1) * (s0 * right)
        f = f.astype(BF16)
        r = r.astype(BF16)
        gst_s[i, 0:64, :] = f
        gst_s[i, 64:128, :] = r
        if i > 0:
            phi_o[i - 1 : i, :] = jnp.sum(f.astype(F32) * st_ref[0, i, 0:64, :].astype(F32), axis=0, keepdims=True)
        if i < nb:
            phi_o[8 + i : 9 + i, :] = jnp.sum(
                r.astype(F32) * st_ref[0, i, 64:128, :].astype(F32), axis=0, keepdims=True
            )
    gskip = jnp.zeros((1, 128), F32)
    for b in range(nb):
        blk = slice(b * BLOCK, (b + 1) * BLOCK)
        xb = xc_ref[blk, :]
        gy = gy_ref[blk, :]
        gyf = gy.astype(F32)
        gskip = gskip + jnp.sum(gyf * xb.astype(F32), axis=0, keepdims=True)
        rhs = jnp.concatenate([gy, gst_s[b + 1, 0:64, :], gst_s[b, 64:128, :]], axis=0)
        left = jnp.concatenate([xb, st_ref[0, b, 0:64, :], st_ref[0, b + 1, 64:128, :]], axis=0)
        first2 = iota((2 * BLOCK, 128), 1) < 64
        none = jnp.zeros_like(left)
        big2 = nt(jnp.concatenate([jnp.where(first2, left, none), jnp.where(first2, none, left)], axis=0), rhs)
        got = []
        sum_ge, sum_gct, sum_gb, kparts = [], [], [], []
        for i in range(2):
            h = 2 * j + i
            terms = column_terms([v[b, pl.ds(at + h, 1), :] for v in (rowst, wt) for at in (0, 64)])
            expo = tn(terms, row_terms(4, base, coltt[b, pl.ds(h, 1), :], coltt[b, pl.ds(64 + h, 1), :]))
            diff = jnp.where(later, expo[:, 0:128], expo[:, 128:256])
            et_m = jnp.exp(jnp.minimum(diff, 60.0))
            mt = et_m * tc[0, b]
            w = jnp.exp(expo[:, 256:])
            bt = tc[1, b] * w
            big = big2[2 * BLOCK * i : 2 * BLOCK * (i + 1), :]
            gmt = big[0:BLOCK, 0:BLOCK]
            gbt = big[0:BLOCK, BLOCK:]
            gctt = big[BLOCK:, 0:BLOCK]
            ge = gmt * et_m
            sum_ge.append(ge)
            q = gmt * mt
            qf = jnp.where(later, q, 0.0)
            e = jnp.where(top, jnp.exp(coltt[b, pl.ds(h, 1), :]), jnp.exp(coltt[b, pl.ds(64 + h, 1), :]))
            gce = gctt * e
            sum_gct.append(gce)
            ct = gce * tc[2, b]
            rf = jnp.sum(qf, axis=0, keepdims=True)
            rall = jnp.sum(q, axis=0, keepdims=True)
            r_o[b, pl.ds(h, 1), :] = rf + jnp.sum(ct[0:64, :], axis=0, keepdims=True)
            r_o[b, pl.ds(64 + h, 1), :] = rall - rf + jnp.sum(ct[64:128, :], axis=0, keepdims=True)
            gbw = gbt * w
            sum_gb.append(gbw)
            u = gbw * tc[1, b]
            kf = jnp.sum(qf + jnp.where(first, u, 0.0), axis=1, keepdims=True)
            kb = jnp.sum(q + u, axis=1, keepdims=True) - kf
            kparts += [kf, kb]
            lhs = jnp.concatenate([mt.astype(BF16), bt.astype(BF16)], axis=1)
            got.append(lhs)
        ggt_o[b] += sum_ge[0] + sum_ge[1]
        gct_o[b] += sum_gct[0] + sum_gct[1]
        gb_o[b] += sum_gb[0] + sum_gb[1]
        two = jnp.where(lane % 64 == 0, jnp.where(first, kparts[0], kparts[1]), jnp.where(first, kparts[2], kparts[3]))
        k_o[blk, :] += pltpu.roll(jnp.where(lane % 64 < 2, two, 0.0), 2 * j, 1)
        got = mm(jnp.concatenate(got, axis=0), rhs)
        gx = jnp.where(first, got[0:BLOCK, :], got[BLOCK:, :]) + skip[0:1, :] * gyf
        gmix = (gx * ds_ref[blk, :].astype(F32)).astype(BF16)
        gmix_o[blk, :] = gmix
        if b == 0:
            edge_o[...] = gmix[0:HALO, :]
        if b == nb - 1:
            edge_o[...] = jnp.where(info[7] == 0, gmix[BLOCK - HALO :, :], edge_o[...])
    gskip_o[...] = jnp.broadcast_to(gskip, (8, 128))


def join_kernel(
    length, heads, info, ggt, gb, gct, k_ref, r_ref, phi, maps, dsl, sig,
    gmb_o, gv_o, small_o, edge_o, gc_s, gm_s,
):
    nb = length // BLOCK
    off = info[5]
    chans = phi.shape[1]
    sub = iota((BLOCK, BLOCK), 0)
    lane = iota((BLOCK, 128), 1)
    first = lane < 64
    low = sub > lane
    high = sub < lane
    upper_strict = high.astype(F32)
    upper = (sub <= lane).astype(F32)
    lower_strict = low.astype(F32)
    lower = (sub >= lane).astype(F32)
    owner = iota((chans, 128), 0) // 64
    to_f = (owner == iota((chans, 128), 1)).astype(F32)
    to_b = (owner + 64 == iota((chans, 128), 1)).astype(F32)
    phi_f = mm(phi[0:8, :], to_f, precision=HIGH)
    phi_b = mm(phi[8:16, :], to_b, precision=HIGH)
    gc_s[...] = jnp.zeros_like(gc_s)
    gm_s[...] = jnp.zeros_like(gm_s)
    sum_bias = jnp.zeros((1, 128), F32)
    sum_rate = jnp.zeros((1, 128), F32)
    for b in range(nb):
        blk = slice(b * BLOCK, (b + 1) * BLOCK)
        ext = slice(HALO + b * BLOCK, HALO + (b + 1) * BLOCK)
        first_pos = off + b * BLOCK
        sp = seg_at(info, sub + first_pos)
        st = seg_at(info, lane + first_pos)
        before = seg_at(info, sub * 0 + (first_pos - 1))
        begin = seg_at(info, sub * 0 + first_pos)
        last = seg_at(info, sub * 0 + (first_pos + BLOCK - 1))
        after = seg_at(info, sub * 0 + (first_pos + BLOCK))
        enter = jnp.where(first, (sp == before).astype(F32), (sp == after).astype(F32))
        keep = jnp.where(first, (sp == last).astype(F32), (sp == begin).astype(F32))
        same = sp == st
        gg = ggt[b]
        gf = jnp.where(same & high, gg, 0.0).astype(BF16)
        gr = jnp.where(same & low, gg, 0.0).astype(BF16)
        cm = maps[blk, 128:256]
        bm = maps[blk, 0:128]
        gm_s[ext, 0:128] = jnp.where(first, mm(gf, cm), mm(gr, cm)) + gb[b] * keep
        gc_s[ext, :] = jnp.where(first, tn(gf, bm), tn(gr, bm)) + gct[b].T * enter
        kb = k_ref[blk, :]
        rb = r_ref[b].T
        ga_f = mm(upper_strict, rb, precision=HIGH) - mm(upper, kb, precision=HIGH) + phi_f[b : b + 1, :]
        ga_b = mm(lower_strict, rb, precision=HIGH) - mm(lower, kb, precision=HIGH) + phi_b[b : b + 1, :]
        ga = jnp.where(first, ga_f, ga_b)
        gv = kb * sig[blk, 128:256] + ga * sig[blk, 0:128]
        gv_o[blk, :] = gv.astype(BF16)
        sum_bias = sum_bias + jnp.sum(gv, axis=0, keepdims=True)
        sum_rate = sum_rate + jnp.sum(ga * sig[blk, 256:384], axis=0, keepdims=True)
    small_o[...] = jnp.zeros_like(small_o)
    small_o[0:1, :] = sum_bias
    small_o[1:2, :] = sum_rate
    small_o[8:9, :] = pltpu.roll(sum_bias, 128 - heads // 2, 1)
    small_o[9:10, :] = pltpu.roll(sum_rate, 128 - heads // 2, 1)
    mid = length + HALO
    lo = HALO // 2
    pos = iota((mid, 128), 0) + (off - HALO + lo)
    seg0 = seg_at(info, pos)
    segn = seg_at(info, pos + 1)
    segp = seg_at(info, pos - 1)
    from_next = jnp.where(seg0 == segn, gc_s[lo + 1 : lo + 1 + mid, :], 0.0)
    from_prev = jnp.where(seg0 == segp, gc_s[lo - 1 : lo - 1 + mid, :], 0.0)
    gm_s[lo : lo + mid, 128:256] = jnp.where(iota((mid, 128), 1) < 64, from_next, from_prev)
    gmb_o[...] = gm_s[...] * dsl[...]
    lo = HALO // 2
    edge_o[...] = jnp.where(
        info[7] == 0, gmb_o[length + lo : length + lo + HALO, :], gmb_o[lo : lo + HALO, :]
    )


def back_conv(length, seg_s, live, grad, data, tap):
    own = slice(HALO, HALO + length)
    seg0 = seg_s[own, :]
    mine = grad[own, :]
    here = data[own, :].astype(F32)
    total = mine * tap[3:4, :]
    gtap = [None] * 7
    gtap[3] = jnp.sum(mine * here, axis=0, keepdims=True)
    for k in (0, 1, 2, 4, 5, 6):
        lo = HALO + 3 - k
        same = seg_s[lo : lo + length, :] == seg0
        moved = jnp.where(same, grad[lo : lo + length, :], 0.0)
        total = total + moved * tap[k : k + 1, :]
        gtap[k] = jnp.sum(moved * here, axis=0, keepdims=True)
    return jnp.where(live, total, 0.0), gtap


def back_kernel(
    length, steps, info, gmix, edge, vm, normed, taps, ggain, gskip,
    gvals_o, keep_o, send_o, tiny_o, ext_s, seg_s, turned_s,
):
    ext = length + 2 * HALO
    off, count = info[5], info[4]
    own = slice(HALO, HALO + length)
    seg_s[...] = seg_at(info, iota((ext, 128), 0) + (off - HALO))
    tiny_o[...] = jnp.zeros_like(tiny_o)
    turned_s[...] = normed[own, :].T
    live = iota((length, 128), 0) + off < count
    right = info[7] == 1
    per = steps // 2

    @pl.loop(0, steps)
    def _(j):
        half = j // per
        at = (j % per) * 256
        both = []
        for p in range(2):
            here = pl.ds(pl.multiple_of(at + 128 * p, 128), 128)
            cols = pl.ds(pl.multiple_of(j * 256 + 128 * p, 128), 128)
            ext_s[own, :] = gmix[:, cols].astype(F32)
            far = pl.ds(pl.multiple_of(((j + per) % steps) * 256 + 128 * p, 128), 128)
            halo = edge[:, far].astype(F32)
            ext_s[0:HALO, :] = jnp.where(right, halo, 0.0)
            ext_s[HALO + length : ext, :] = jnp.where(right, 0.0, halo)
            gvals, gtap = back_conv(length, seg_s, live, ext_s, vm[:, cols], taps[:, cols])
            both.append(gvals.astype(BF16))
            for t in range(7):
                tiny_o[half, t : t + 1, here] = gtap[t]
            tiny_o[half, 7:8, here] = ggain[0:1, cols]
            tiny_o[half, 8:9, here] = gskip[0:1, cols]
        both = jnp.concatenate(both, axis=1)
        gvals_o[:, pl.ds(pl.multiple_of(j * 256, 256), 256)] = both
        here = pl.ds(pl.multiple_of(at, 256), 256)
        by_core(mm(turned_s[...], both), keep_o.at[half, :, here], send_o.at[half, :, here])


def finish_kernel(hl, tiny, total, wb, heads_o, wout_o, bc_o, conv_o, convbc_o, pre_o, bias_o, rate_o, skip_o, gain_o):
    ch = tiny.shape[1]
    w = lax.axis_index("wide")
    share = pre_o.shape[1]
    lanes = gain_o.shape[0]
    dm = total.shape[1] - ch
    for h in range(hl):
        cols = slice(h * HD, (h + 1) * HD)
        wout_o[h] = total[:, cols]
        heads_o[h, :, 0:HD] = total[:, dm + h * HD : dm + (h + 1) * HD]
        heads_o[h, :, HD : 2 * HD] = wb[:, cols]
        heads_o[h, :, 2 * HD : 2 * HD + 1] = wb[:, ch + 256 + h : ch + 257 + h]
        heads_o[h, :, 2 * HD + 1 :] = wb[:, ch + 320 + h : ch + 321 + h]
    bc_o[...] = pack_columns(wb[:, ch : ch + 256])
    rows = tiny[...]
    src = iota((ch, 128), 0)
    dst = iota((ch, 128), 1)
    for q in range(lanes):
        chosen = ((src == dst * HD + lanes * w + q) & (dst < hl)).astype(F32)
        got = mm(rows, chosen, precision=HIGH)
        for k in range(7):
            conv_o[k, q : q + 1, :] = got[k : k + 1, 0:hl]
        gain_o[q : q + 1, :] = got[7:8, 0:hl]
    chosen = ((src == share * w + dst) & (dst < share)).astype(F32)
    pre_o[...] = mm(rows[8:16, :], chosen, precision=HIGH)[1:2, 0:share]
    per = (src // HD == dst).astype(F32)
    skip_o[...] = mm(rows[8:16, :], per, precision=HIGH)[0:1, 0:hl]
    size = convbc_o.shape[1]
    group = (size * w) // 64
    start = ((group % 2) * 2 + group // 2) * 64 + (size * w) % 64
    src = iota((256, 128), 0)
    dst = iota((256, 128), 1)
    chosen = ((src == start + dst) & (dst < size)).astype(F32)
    for k in range(3):
        part = mm(rows[8:16, 256 * k : 256 * (k + 1)], chosen, precision=HIGH)
        for r in range(3):
            if 3 * r + k < 7:
                convbc_o[3 * r + k : 3 * r + k + 1, :] = part[3 + r : 4 + r, 0:size]
    both = rows[10:11, 0:128]
    bias_o[0:1, :] = both[:, 0:hl]
    bias_o[1:2, :] = pltpu.roll(both, 64, 1)[:, 0:hl]
    rate = rows[10:11, 128:256]
    rate_o[...] = (rate + pltpu.roll(rate, 64, 1))[:, 0:hl]


def collect_kernel(
    length, hl, info, gvals, ggate, w_ref, wv_b, wg_b, normed, gmb, edge, bcm, taps_bc, gv, wdt, wbc, x_ref, g_ref, rs, pre,
    small, tiny, keep, send, plane_a, out_o, tiny_o, a_o, gin_o, ext_s, seg_s, keepbc_s, sendbc_s, tinyin_s, acc_s, *refs,
):
    value, maps = refs[0:13], refs[13:26]
    tcore_s, tsum_s, tgot_s, tz_s, tzgot_s, agot_s = refs[26:32]
    sems = (refs[32:37], refs[37:42])
    w = lax.axis_index("wide")
    n = lax.axis_index("narrow")
    c, xx, z = w % 2, (w // 2) % 2, w // 4
    share = out_o.shape[0]
    ch = keep.shape[2]
    core = (w + 1 - 2 * c, n)
    over_x = (w + 2 - 4 * xx, n)
    over_y = (w, 1 - n)
    over_d = (w + 2 - 4 * xx, 1 - n)
    steps = (2, 1, 3)
    over_z = [(((z + d) % 4) * 4 + w % 4, n) for d in steps]
    mesh_ids = pl.DeviceIdType.MESH
    barrier = pltpu.get_barrier_semaphore()
    for other in [core, over_x, over_y, over_d] + over_z:
        pl.semaphore_signal(barrier, inc=1, device_id=other, device_id_type=mesh_ids)
    pl.semaphore_wait(barrier, 7)

    def copy(src, dst, group, at, other):
        got = pltpu.make_async_remote_copy(
            src_ref=src, dst_ref=dst, send_sem=sems[0][group].at[at], recv_sem=sems[1][group].at[at], device_id=other,
            device_id_type=mesh_ids,
        )
        got.start()
        return got

    rows = [pl.ds(pl.multiple_of(((z + d) % 4) * (2 * share), 2 * share), 2 * share) for d in steps + (0,)]

    def split(kind, i, kept, bufs):
        core_s, left_s, right_s, left_out, left_in, right_out, right_in = bufs[:7]
        cut = left_s.shape[3]
        both = kept[:, rows[i], :].astype(F32) + core_s[i].astype(F32)
        low, high = both[:, 0:share, :], both[:, share:, :]
        near = jnp.where(xx == 0, low, high)
        far = jnp.where(xx == 0, high, low)
        left_s[i] = near[:, :, 0:cut]
        right_s[i, 0] = near[0, :, cut:]
        right_s[i, 1] = far[0, :, cut:]
        left_out[i] = far[:, :, 0:cut].astype(BF16)
        right_out[i, 0] = near[1, :, cut:].astype(BF16)
        right_out[i, 1] = far[1, :, cut:].astype(BF16)
        return (
            copy(left_out.at[i], left_in.at[i], 1, (kind, i, 0), over_x),
            copy(right_out.at[i], right_in.at[i], 1, (kind, i, 1), over_y),
        )

    def cross_over(kind, i, going, bufs):
        left_s, right_s, _, left_in, _, right_in, left2_out, left2_in, right2_out, right2_in = bufs[1:11]
        going[0].wait()
        left_s[i] = left_s[i] + left_in[i].astype(F32)
        left2_out[i] = left_s[i, 1].astype(BF16)
        go_left = copy(left2_out.at[i], left2_in.at[i], 2, (kind, i, 0), over_y)
        going[1].wait()
        right_s[i] = right_s[i] + right_in[i].astype(F32)
        right2_out[i] = right_s[i, 1].astype(BF16)
        return go_left, copy(right2_out.at[i], right2_in.at[i], 2, (kind, i, 1), over_x)

    def deepen(kind, i, going, bufs, first):
        left_s, right_s = bufs[1:3]
        left2_in, right2_in = bufs[8], bufs[10]
        z_out, z_in = bufs[11:13]
        cut, cols = left_s.shape[3], z_out.shape[2]
        going[0].wait()
        going[1].wait()
        left = left_s[i, 0] + left2_in[i].astype(F32)
        right = right_s[i, 0] + right2_in[i].astype(F32)
        if i == 3:
            out_o[:, first : first + cut] = left
            out_o[:, first + cut : first + cols] = right
            return []
        z_out[i, :, 0:cut] = left.astype(BF16)
        z_out[i, :, cut:] = right.astype(BF16)
        return [copy(z_out.at[i], z_in.at[i], 4, (kind, i), over_z[i])]

    v_core = [copy(send.at[:, rows[i], :], value[0].at[i], 0, i, core) for i in range(4)]
    a_copies = [copy(plane_a.at[(z + steps[k]) % 4], agot_s.at[k], 4, (3, k), over_z[k]) for k in range(3)]

    ext = length + 2 * HALO
    off, count = info[5], info[4]
    own = slice(HALO, HALO + length)
    seg_s[...] = seg_at(info, iota((ext, 128), 0) + (off - HALO))
    live = iota((length, 128), 0) + off < count
    tinyin_s[...] = tiny[...]
    for half in range(2):
        tinyin_s[half, 10:11, 0:128] = small[8 * half : 8 * half + 1, :]
        tinyin_s[half, 10:11, 128:256] = small[8 * half + 1 : 8 * half + 2, :]
    both = []
    v_first, v_second, m_first, m_second, last = {}, {}, {}, {}, []

    def v_split(i):
        v_core[i].wait()
        v_first[i] = split(0, i, keep, value)

    def v_cross(i):
        v_second[i] = cross_over(0, i, v_first[i], value)

    def v_deepen(i):
        last.extend(deepen(0, i, v_second[i], value, 0))

    def m_split(i):
        m_core[i].wait()
        m_first[i] = split(1, i, keepbc_s, maps)

    def m_cross(i):
        m_second[i] = cross_over(1, i, m_first[i], maps)

    def m_deepen(i):
        last.extend(deepen(1, i, m_second[i], maps, ch))

    for k in range(2):
        cols = slice(k * 128, (k + 1) * 128)
        ext_s[...] = gmb[:, cols]
        lo = HALO // 2
        hi = length + lo
        got = edge[:, cols]
        ext_s[lo : lo + HALO, :] += jnp.where(info[7] == 1, got, 0.0)
        ext_s[hi : hi + HALO, :] += jnp.where(info[7] == 1, 0.0, got)
        gbc, gtap = back_conv(length, seg_s, live, ext_s, bcm[:, cols], taps_bc[:, cols])
        for t in range(7):
            at = (t % 3) * 256 + k * 128
            for half in range(2):
                tinyin_s[half, 11 + t // 3 : 12 + t // 3, at : at + 128] = gtap[t]
        both.append(gbc.astype(BF16))
        if k == 0:
            v_split(0)
            v_split(1)
    gbc = jnp.concatenate(both + [gv[...]], axis=1)
    gw = tn(normed[own, :], gbc)
    by_core(gw, keepbc_s.at[0], sendbc_s.at[0])
    turned = pltpu.roll(gw[:, 256:], 128 - hl, 1)
    by_core(jnp.concatenate([gw[:, 0:256], turned], axis=1), keepbc_s.at[1], sendbc_s.at[1])
    m_core = [copy(sendbc_s.at[:, rows[i], :], maps[0].at[i], 0, 4 + i, core) for i in range(4)]
    wv_a = jnp.concatenate([w_ref[h, HD : 2 * HD, :] for h in range(hl)], axis=0)
    wg_a = jnp.concatenate([w_ref[h, 0:HD, :] for h in range(hl)], axis=0)
    v_cross(0)
    v_split(2)
    acc_s[...] = mm(gvals[:, 0:ch], wv_a) + mm(gvals[:, ch:], wv_b[...])
    v_cross(1)
    v_deepen(0)
    v_split(3)
    m_split(0)
    m_split(1)
    gn = acc_s[...] + mm(ggate[:, 0:ch], wg_a) + mm(ggate[:, ch:], wg_b[...])
    gn = gn + nt(gbc[:, 0:256], wbc[...]) + mm(gv[...], wdt[...])
    acc_s[...] = gn
    r = rs[...]
    gpre = jnp.sum(gn * x_ref[...].astype(F32) * r, axis=0, keepdims=True)
    for half in range(2):
        tinyin_s[half, 9:10, 0 : gpre.shape[1]] = gpre
    t_core = copy(tinyin_s, tcore_s, 0, 8, core)
    v_cross(2)
    v_deepen(1)
    m_split(2)
    m_cross(0)
    v_cross(3)
    v_deepen(2)
    m_split(3)
    m_cross(1)
    m_deepen(0)
    t_core.wait()
    tsum_s[...] = tinyin_s[...] + tcore_s[...]
    t_plane = [copy(tsum_s.at[min(k, 1)], tgot_s.at[k], 3, k, other) for k, other in enumerate((over_x, over_y, over_d))]
    m_cross(2)
    m_deepen(1)
    m_cross(3)
    m_deepen(2)
    for one in t_plane:
        one.wait()
    tsum = tsum_s[0] + tgot_s[0] + tgot_s[1] + tgot_s[2]
    tz_s[...] = tsum
    last += [copy(tz_s, tzgot_s.at[k], 4, (2, k), over_z[k]) for k in range(3)]
    v_deepen(3)
    m_deepen(3)
    x = x_ref[...].astype(F32)
    gn = acc_s[...]
    wp = gn * pre[...]
    mean = jnp.mean(wp * x, axis=1, keepdims=True)
    gin_o[...] = g_ref[...].astype(F32) + r * wp - x * (r * r * r * mean)
    for one in a_copies:
        one.wait()
    a_o[...] = plane_a[z].astype(F32) + agot_s[0].astype(F32) + agot_s[1].astype(F32) + agot_s[2].astype(F32)
    for one in last:
        one.wait()
    for bufs, cols in ((value, slice(0, ch)), (maps, slice(ch, out_o.shape[1]))):
        z_in = bufs[12]
        out_o[:, cols] = out_o[:, cols] + z_in[0].astype(F32) + z_in[1].astype(F32) + z_in[2].astype(F32)
    tiny_o[...] = tsum + tzgot_s[0] + tzgot_s[1] + tzgot_s[2]


def whole(shape, grid):
    zeros = (0,) * len(shape)
    if grid:
        return pl.BlockSpec(shape, lambda j: zeros)
    return pl.BlockSpec(shape, lambda: zeros)


def columns(rows, first=0):
    return pl.BlockSpec((rows, 128), lambda j: (0, first + j))


SMEM = pl.BlockSpec(memory_space=pltpu.SMEM)
VMEM = pl.BlockSpec(memory_space=pltpu.VMEM)
ANY = pl.BlockSpec(memory_space=pl.ANY)
HBM = pl.BlockSpec(memory_space=pltpu.HBM)


def sds(shape, dtype):
    return jax.ShapeDtypeStruct(shape, dtype)


def params(grid, mib):
    if grid:
        return pltpu.CompilerParams(vmem_limit_bytes=mib * 2**20, dimension_semantics=("arbitrary",))
    return pltpu.CompilerParams(vmem_limit_bytes=mib * 2**20)


def cost(us):
    return pl.CostEstimate(flops=int(us * 1.1e9), bytes_accessed=int(us * 1e6), transcendentals=0)


def pack_columns(v):
    n = v.shape[-1] // 4
    return jnp.concatenate([v[..., 0:n], v[..., 2 * n : 3 * n], v[..., n : 2 * n], v[..., 3 * n :]], axis=-1)


def small_kernel(hl, conv, gain, dtb, alog, skip, wdt, start_ref, end_ref, out_o):
    ch = out_o.shape[1]
    lane = iota((1, 128), 1)
    wide_lane = iota((1, ch), 1)
    bias = jnp.zeros((1, 128), F32)
    rate = jnp.zeros((1, 128), F32)
    diag = jnp.zeros((1, ch), F32)
    out_o[0:16, :] = jnp.zeros((16, ch), F32)
    for h in range(hl):
        cols = slice(h * HD, (h + 1) * HD)
        out_o[0:7, cols] = conv[h]
        out_o[7:8, cols] = gain[h : h + 1, :]
        bias = jnp.where(lane == h, dtb[0, h], jnp.where(lane == 64 + h, dtb[1, h], bias))
        rate = jnp.where((lane == h) | (lane == 64 + h), alog[h], rate)
        diag = jnp.where(wide_lane // HD == h, skip[h], diag)
        out_o[16 + 2 * h : 18 + 2 * h, :] = wdt[h].astype(F32)[0:2, :]
    out_o[8:9, :] = diag
    out_o[9:10, 0:128] = bias
    out_o[9:10, 128:256] = rate
    n = lax.axis_index("narrow")
    start, end = start_ref[...].astype(F32), end_ref[...].astype(F32)
    out_o[16 + 2 * hl :, :] = jnp.where(n == 0, end[8:16, :], start[0:8, :])


def swap(v):
    return lax.ppermute(v, "narrow", [(0, 1), (1, 0)])


def flip(v, bit, wide):
    return lax.ppermute(v, "wide", [(i, i ^ bit) for i in range(wide)])


def cross(v, bit, wide):
    pairs = [(i * 2 + k, (i ^ bit) * 2 + 1 - k) for i in range(wide) for k in range(2)]
    return lax.ppermute(v, ("wide", "narrow"), pairs)


def total(*parts):
    acc = parts[0].astype(F32)
    for v in parts[1:]:
        acc = acc + v.astype(F32)
    return acc


def split_positions(
    wide, layer_in, pre_gain, w_heads, w_bc, conv_x, conv_bc, dt_bias, a_log, skip_d, norm_gain, w_out, cotangent, starts, live
):
    n = lax.axis_index("narrow")
    w = lax.axis_index("wide")
    left = n == 0
    _, length, dm = layer_in.shape
    hl = w_heads.shape[1]
    heads = 2 * hl
    ch = hl * HD
    chans = 2 * ch
    pairs = heads // 2
    hp = pairs // 2
    nb = length // BLOCK
    ext = length + 2 * HALO
    share = dm // wide
    x = layer_in[0]
    g = cotangent[0]

    w_turned = jnp.transpose(w_heads, (1, 2, 0))
    small_own = pl.pallas_call(
        functools.partial(small_kernel, hl),
        grid=(1,),
        out_shape=sds((24 + 2 * hl, ch), F32),
        in_specs=[
            whole((hl, 7, HD), 1), whole((hl, HD), 1), SMEM, SMEM, SMEM, pl.BlockSpec((hl, 16, dm), lambda j: (0, 8, 0)),
            pl.BlockSpec((HALO, dm), lambda j: (0, 0)), pl.BlockSpec((HALO, dm), lambda j: (length // HALO - 1, 0)),
        ],
        out_specs=whole((24 + 2 * hl, ch), 1),
        cost_estimate=cost(2),
        name="small",
    )(jnp.transpose(conv_x, (1, 0, 2)), norm_gain, dt_bias.T, a_log, skip_d, w_turned, x, x)
    small_other = swap(small_own)

    quarter = ch // 4
    q = w % 4

    def gather(p0):
        p1 = flip(p0, 2, wide)
        return p0, p1, flip(p0, 1, wide), flip(p1, 1, wide)

    def heads_rows(lo):
        return lax.dynamic_slice(w_turned, (q * (hl // 4), lo, 0), (hl // 4, HD, dm)).reshape(quarter, dm)

    wo = w_out.reshape(ch, dm)
    wv_first = swap(heads_rows(HD))
    wo_rows = lax.dynamic_slice(wo, (q * quarter, 0), (quarter, dm))
    wog_pieces = gather(swap(jnp.concatenate([wo_rows, heads_rows(0)], axis=1)))

    pos = (length, 128)
    sq = (nb, BLOCK, BLOCK)
    front_shapes = [
        ((8, chans), F32), ((8, chans), F32), ((8, chans), F32), ((128, dm), BF16), ((dm, 256), BF16), ((7, 256), F32),
        ((ext, dm), BF16), ((length, 1), F32), ((ext, 256), F32), ((ext, 256), F32), ((length, 256), BF16),
        ((2,) + sq, F32), ((4,) + sq, F32), ((3,) + sq, F32), ((128, 128), F32), ((length, 384), F32),
    ]
    late_front = (8, 9, 10, 13, 15)
    (
        info, taps, gain, skip, wdt_all, wbc, taps_bc, normed, rs, bcm, dsl, maps, tab_a, tab_b, tab_c, dpt, sig,
    ) = pl.pallas_call(
        functools.partial(front_kernel, length, hl),
        out_shape=[sds((8,), jnp.int32)]
        + [pltpu.HBM(*v) if k in late_front else sds(*v) for k, v in enumerate(front_shapes)],
        in_specs=[SMEM] + [VMEM] * 7,
        out_specs=[SMEM] + [HBM if k in late_front else VMEM for k in range(len(front_shapes))],
        scratch_shapes=[
            pltpu.VMEM((ext, 256), jnp.int32), pltpu.VMEM((ext, 256), F32), pltpu.VMEM((128, 128), F32),
            pltpu.VMEM((ext, dm), BF16),
        ]
        + [pltpu.VMEM(*front_shapes[k]) for k in late_front]
        + [pltpu.SemaphoreType.DMA((len(late_front),))],
        compiler_params=params(False, 14),
        cost_estimate=cost(6),
        name="front",
    )(starts, live, x, pre_gain.reshape(1, dm), w_bc, conv_bc, small_own, small_other)

    wv_over_x = flip(wv_first, 2, wide)

    def states(first):
        return pl.BlockSpec((1, nb + 1, 128, 128), lambda j: (j + first, 0, 0, 0))

    bnd_spec = pl.BlockSpec((1, 64, 128), lambda j: (j, 0, 0))
    state_shape = sds((pairs, nb + 1, 128, 128), BF16)
    bnd_shape = sds((hp, 64, 128), BF16)
    act_shape = sds((length, chans), BF16)
    def twin(rows, first):
        return pl.BlockSpec((rows, 256), lambda j: (0, first + j))

    def vals(other, weights, before):
        steps = hp // 2
        first = steps if other else 0
        specs = [SMEM, whole((ext, dm), 1)]
        specs += [whole((quarter, dm), 1)] * 4 if other else [pl.BlockSpec((4, 2 * HD + 2, dm), lambda j: (j, 0, 0))]
        specs += [twin(8, first), whole((2,) + sq, 1), whole((128, 128), 1)] + [ANY] * len(before)
        return pl.pallas_call(
            functools.partial(vals_kernel, length, other),
            grid=(steps,),
            out_shape=[act_shape, sds((ext, chans), BF16), act_shape, state_shape, bnd_shape] + [sds((ch, dm), BF16)] * other,
            in_specs=specs,
            out_specs=[
                twin(length, first), twin(ext, first), twin(length, first),
                pl.BlockSpec((2, nb + 1, 128, 128), lambda j: (j + first, 0, 0, 0)),
                pl.BlockSpec((2, 64, 128), lambda j: (j, 0, 0)),
            ] + [whole((ch, dm), 1)] * other,
            scratch_shapes=[pltpu.VMEM((ext, 128), F32), pltpu.VMEM((ext, 128), F32), pltpu.VMEM((ext, 128), jnp.int32)],
            input_output_aliases={len(specs) - len(before) + i: i for i in range(len(before))},
            compiler_params=params(True, 10),
            cost_estimate=cost(9),
            name="vals_other" if other else "vals_own",
        )(info, normed, *weights, taps, tab_a, dpt, *before)

    *own_vals, bnd_own = vals(False, (w_turned,), ())
    wv_pieces = wv_first, wv_over_x, flip(wv_first, 1, wide), flip(wv_over_x, 1, wide)
    xc, vm, ds, s_loc, bnd_other, wv_other = vals(True, wv_pieces, own_vals)

    def aliases(specs, before):
        return {len(specs) - len(before) + i: i for i in range(len(before))}

    def scan(first, s0, before):
        specs = [
            SMEM, columns(length, first), states(first), bnd_spec, whole((128, 128), 1), whole((4,) + sq, 1), columns(8, first),
        ] + [ANY] * len(before)
        return pl.pallas_call(
            functools.partial(scan_kernel, length, first),
            grid=(hp,),
            out_shape=[act_shape, state_shape],
            in_specs=specs,
            out_specs=[columns(length, first), states(first)],
            input_output_aliases=aliases(specs, before),
            compiler_params=params(True, 5),
            cost_estimate=cost(10),
            name="scan_other" if first else "scan_own",
        )(info, xc, s_loc, s0, dpt, tab_b, skip, *before)

    y, s_true = scan(0, swap(bnd_other), scan(hp, swap(bnd_own), ()))

    out, gy, ggate, hn, ggain, wg_other, gs_loc, gbnd = pl.pallas_call(
        functools.partial(gate_kernel, nb),
        out_shape=[
            pltpu.HBM((length, dm), BF16), act_shape, act_shape, act_shape, sds((8, chans), F32), pltpu.HBM((ch, dm), BF16),
            state_shape, sds((pairs, 64, 128), BF16),
        ],
        in_specs=[SMEM] + [VMEM] * 14,
        out_specs=[HBM, VMEM, VMEM, VMEM, VMEM, HBM, VMEM, VMEM],
        scratch_shapes=[pltpu.VMEM((ch, 2 * dm), BF16)]
        + [pltpu.VMEM((BLOCK, chans), F32)] * 4
        + [pltpu.VMEM((nb, BLOCK, chans), F32), pltpu.VMEM((length, dm), BF16), pltpu.SemaphoreType.DMA((2,))],
        compiler_params=params(False, 18),
        cost_estimate=cost(16),
        name="gated",
    )(info, x, g, normed, y, wo, w_turned, *wog_pieces, gain, tab_b, tab_c, dpt)

    gw_shape = (2, dm // 2, dm + ch)
    piece = sds((4, share, dm + ch), BF16)
    a_pieces = pl.pallas_call(
        wsum_kernel,
        out_shape=[piece] * 4,
        in_specs=[VMEM] * 4,
        out_specs=[VMEM] * 4,
        scratch_shapes=[pltpu.VMEM(gw_shape, BF16)] * 3 + [pltpu.SemaphoreType.DMA((2, 2))] * 2,
        compiler_params=pltpu.CompilerParams(collective_id=1, has_side_effects=True, vmem_limit_bytes=16 * 2**20),
        cost_estimate=cost(7),
        name="wsum",
    )(g, normed, hn, ggate)

    def plane(mine, to_x, to_y, to_d):
        return total(mine, flip(to_x, 2, wide), swap(to_y), cross(to_d, 2, wide)).astype(mine.dtype)

    a_plane = plane(*a_pieces)

    def table(k):
        return pl.BlockSpec((None,) + sq, lambda j: (k, 0, 0, 0))

    sums = [whole(sq, 1), whole(sq, 1), whole(sq, 1), whole(pos, 1), whole(sq, 1)]
    gmix, ggt, gb, gct, ksum, rsum, phi, gskip, edge = pl.pallas_call(
        functools.partial(gscan_kernel, length),
        grid=(pairs,),
        out_shape=[
            act_shape, sds(sq, F32), sds(sq, F32), sds(sq, F32), sds(pos, F32), sds(sq, F32), sds((16, chans), F32),
            sds((8, chans), F32), sds((HALO, chans), BF16),
        ],
        in_specs=[
            SMEM, columns(length), columns(length), columns(length), states(0), states(0),
            pl.BlockSpec((1, 64, 128), lambda j: ((j + hp) % pairs, 0, 0)), whole((128, 128), 1), table(1), table(0), table(0),
            whole((3,) + sq, 1), columns(8),
        ],
        out_specs=[columns(length)] + sums + [columns(16), columns(8), columns(HALO)],
        scratch_shapes=[pltpu.VMEM((nb + 1, 128, 128), BF16)],
        compiler_params=params(True, 8),
        cost_estimate=cost(22),
        name="gscan",
    )(info, xc, ds, gy, s_true, gs_loc, swap(gbnd), dpt, tab_b, tab_a, tab_b, tab_c, skip)
    edge = swap(edge)

    gmix, a_plane = lax.optimization_barrier((gmix, a_plane))

    gmb, gv, small, edge_bc = pl.pallas_call(
        functools.partial(join_kernel, length, heads),
        out_shape=[sds((ext, 256), F32), sds(pos, BF16), sds((16, 128), F32), sds((HALO, 256), F32)],
        in_specs=[SMEM] + [VMEM] * 9,
        out_specs=[VMEM] * 4,
        scratch_shapes=[pltpu.VMEM((ext, 128), F32), pltpu.VMEM((ext, 256), F32)],
        compiler_params=params(False, 6),
        cost_estimate=cost(6),
        name="join",
    )(info, ggt, gb, gct, ksum, rsum, phi, maps, dsl, sig)

    edge_bc = swap(edge_bc)
    sum_shape = (2, dm // 2, ch)
    gvals, keep_v, send_v, tiny = pl.pallas_call(
        functools.partial(back_kernel, length, pairs // 2),
        out_shape=[act_shape, sds(sum_shape, BF16), sds(sum_shape, BF16), sds((2, 16, ch), F32)],
        in_specs=[SMEM] + [VMEM] * 7,
        out_specs=[VMEM] * 4,
        scratch_shapes=[
            pltpu.VMEM((ext, 128), F32), pltpu.VMEM((ext, 128), jnp.int32), pltpu.VMEM((dm, length), BF16),
        ],
        compiler_params=params(False, 10),
        cost_estimate=cost(12),
        name="back",
    )(info, gmix, edge, vm, normed, taps, ggain, gskip)

    def buffers(cols, cut):
        rest = cols - cut
        return (
            [pltpu.VMEM((4, 2, 2 * share, cols), BF16), pltpu.VMEM((4, 2, share, cut), F32), pltpu.VMEM((4, 2, share, rest), F32)]
            + [pltpu.VMEM((4, 2, share, cut), BF16)] * 2
            + [pltpu.VMEM((4, 2, share, rest), BF16)] * 2
            + [pltpu.VMEM((4, share, cut), BF16)] * 2
            + [pltpu.VMEM((4, share, rest), BF16)] * 2
            + [pltpu.VMEM((3, share, cols), BF16)] * 2
        )

    cols = ch + 384
    wb, tiny, wa, grad_in = pl.pallas_call(
        functools.partial(collect_kernel, length, hl),
        out_shape=[sds((share, cols), F32), sds((16, ch), F32), sds((share, dm + ch), F32), sds((length, dm), F32)],
        in_specs=[SMEM] + [VMEM] * 22,
        out_specs=[VMEM] * 4,
        scratch_shapes=[
            pltpu.VMEM((ext, 128), F32), pltpu.VMEM((ext, 128), jnp.int32),
            pltpu.VMEM((2, dm // 2, 384), BF16), pltpu.VMEM((2, dm // 2, 384), BF16), pltpu.VMEM((2, 16, ch), F32),
            pltpu.VMEM((length, dm), F32),
        ]
        + buffers(ch, ch // 2)
        + buffers(384, 256)
        + [
            pltpu.VMEM((2, 16, ch), F32),
            pltpu.VMEM((2, 16, ch), F32),
            pltpu.VMEM((3, 16, ch), F32),
            pltpu.VMEM((16, ch), F32),
            pltpu.VMEM((3, 16, ch), F32),
            pltpu.VMEM((3, share, dm + ch), BF16),
        ]
        + [pltpu.SemaphoreType.DMA(v) for v in ((9,), (2, 4, 2), (2, 4, 2), (3,), (4, 3)) * 2],
        compiler_params=pltpu.CompilerParams(collective_id=0, has_side_effects=True, vmem_limit_bytes=24 * 2**20),
        name="collect",
    )(
        info, gvals, ggate, w_turned, wv_other, wg_other, normed, gmb, edge_bc, bcm, taps_bc, gv, wdt_all, wbc, x, g, rs,
        pre_gain.reshape(1, dm), small, tiny, keep_v, send_v, a_plane,
    )

    g_w_heads, g_w_out, g_w_bc, g_conv_x, g_conv_bc, g_pre, g_bias, g_rate, g_skip, g_gain = pl.pallas_call(
        functools.partial(finish_kernel, hl),
        out_shape=[
            sds((hl, share, 2 * HD + 2), F32), sds((hl, share, HD), F32), sds((share, 256), F32), sds((7, HD // wide, hl), F32),
            sds((7, 256 // wide), F32), sds((1, share), F32), sds((2, hl), F32), sds((1, hl), F32), sds((1, hl), F32),
            sds((HD // wide, hl), F32),
        ],
        in_specs=[VMEM] * 3,
        out_specs=[VMEM] * 10,
        compiler_params=params(False, 8),
        name="finish",
    )(tiny, wa, wb)
    return (
        out[None],
        grad_in[None],
        g_pre[0],
        jnp.transpose(g_w_heads, (1, 0, 2)),
        g_w_bc,
        jnp.transpose(g_conv_x, (0, 2, 1)),
        g_conv_bc,
        g_bias.T,
        g_rate[0],
        g_skip[0],
        g_gain.T,
        jnp.transpose(g_w_out, (0, 2, 1)),
    )


def solution(mesh):
    body = shards
    if mesh.shape["narrow"] == 2 and mesh.shape["wide"] == 16:
        body = functools.partial(split_positions, mesh.shape["wide"])
    return jax.shard_map(
        body,
        mesh=mesh,
        in_specs=(
            P("wide", "narrow", None),
            P(),
            P(None, "narrow", None),
            P(),
            P(None, "narrow", None),
            P(),
            P("narrow", None),
            P("narrow"),
            P("narrow"),
            P("narrow", None),
            P("narrow", None, None),
            P("wide", "narrow", None),
            P("wide", None),
            P("wide", None),
        ),
        out_specs=(
            P("wide", "narrow", None),
            P("wide", "narrow", None),
            P("wide"),
            P("wide", "narrow", None),
            P("wide", None),
            P(None, "narrow", "wide"),
            P(None, "wide"),
            P("narrow", None),
            P("narrow"),
            P("narrow"),
            P("narrow", "wide"),
            P("narrow", None, "wide"),
        ),
        check_vma=False,
    )
```

```python
import functools

import jax
import jax.numpy as jnp
from jax import lax
from jax.experimental import pallas as pl
from jax.experimental.pallas import tpu as pltpu
from jax.sharding import PartitionSpec as P

H = 24
HD = 64
BLOCK = 128
SEQ_LEN = 1280


EPS = 1e-05
HIGH = lax.Precision.HIGHEST


def rounded(value):
    return value + lax.stop_gradient(value.astype(jnp.bfloat16).astype(jnp.float32) - value)


def segment_ids(starts):
    where_at = jnp.arange(SEQ_LEN, dtype=jnp.int32)
    hits = (starts[:, :, None] <= where_at[None, None, :]).astype(jnp.int32)
    return jnp.sum(hits, axis=1) - 1


def conv_doc(values, taps, seg):
    half = (taps.shape[0] - 1) // 2
    length = values.shape[1]
    padded = jnp.pad(values, ((0, 0), (half, half), (0, 0)))
    seg_pad = jnp.pad(seg, ((0, 0), (half, half)), constant_values=-1)
    total = jnp.zeros_like(values)
    for offset in range(taps.shape[0]):
        same = (seg_pad[:, offset : offset + length] == seg).astype(values.dtype)
        total = total + taps[offset] * padded[:, offset : offset + length] * same[:, :, None]
    return total


def ssd_forward(xc, steps, decays, bmat, cmat, seg, prec):
    rows, length, heads, hdim = xc.shape
    blocks = length // BLOCK
    xb = xc.reshape(rows, blocks, BLOCK, heads, hdim)
    stepb = steps.reshape(rows, blocks, BLOCK, heads)
    cum = jnp.cumsum(decays.reshape(rows, blocks, BLOCK, heads), axis=2)
    bb = bmat.reshape(rows, blocks, BLOCK, -1)
    cb = cmat.reshape(rows, blocks, BLOCK, -1)
    sb = seg.reshape(rows, blocks, BLOCK)
    order = jnp.arange(BLOCK, dtype=jnp.int32)
    causal = order[:, None] >= order[None, :]
    same = ((sb[:, :, :, None] == sb[:, :, None, :]) & causal)[..., None]
    diff = cum[:, :, :, None, :] - cum[:, :, None, :, :]
    weights = jnp.where(same, jnp.exp(jnp.where(same, diff, 0.0)), 0.0)
    inner = jnp.einsum("rbtn,rbsn->rbts", cb, bb, precision=prec)
    mix = weights * inner[..., None] * stepb[:, :, None, :, :]
    intra = jnp.einsum("rbtsh,rbshp->rbthp", mix, xb, precision=prec)
    last = sb[:, :, -1]
    cum_end = cum[:, :, -1, :]
    to_end = (
        (sb == last[:, :, None]).astype(cum.dtype)[..., None]
        * jnp.exp(cum_end[:, :, None, :] - cum)
        * stepb
    )
    states = jnp.einsum("rbshp,rbsn->rbhpn", to_end[..., None] * xb, bb, precision=prec)
    decay_end = jnp.exp(cum_end)

    def carry_step(carry, item):
        state, seg_prev = carry
        block_state, block_last, block_decay = item
        keep = (block_last == seg_prev).astype(state.dtype)[:, None, None, None]
        fresh = keep * block_decay[:, :, None, None] * state + block_state
        return ((fresh, block_last), (state, seg_prev))

    init = (
        jnp.zeros((rows, heads, hdim, bb.shape[-1]), xc.dtype),
        jnp.full((rows,), -1, jnp.int32),
    )
    items = (jnp.moveaxis(states, 1, 0), jnp.moveaxis(last, 1, 0), jnp.moveaxis(decay_end, 1, 0))
    _, (before, seg_before) = lax.scan(carry_step, init, items)
    before = jnp.moveaxis(before, 0, 1)
    seg_before = jnp.moveaxis(seg_before, 0, 1)
    enter = (sb == seg_before[:, :, None]).astype(cum.dtype)[..., None] * jnp.exp(cum)
    inter = jnp.einsum("rbtn,rbhpn->rbthp", cb, before, precision=prec) * enter[..., None]
    return (intra + inter).reshape(rows, length, heads, hdim)


def mixer(proj, bcproj, conv_x, conv_bc, dt_bias, a_log, skip_d, seg, mask, rounder, prec):
    rows, length, heads, width = proj.shape
    hdim = (width - 2) // 2
    state = bcproj.shape[-1] // 4
    gate = proj[..., :hdim]
    values = proj[..., hdim : 2 * hdim] * mask[:, :, None, None]
    mixed_x = conv_doc(
        values.reshape(rows, length, heads * hdim),
        conv_x.reshape(conv_x.shape[0], heads * hdim),
        seg,
    )
    xc = rounder(jax.nn.silu(mixed_x)).reshape(rows, length, heads, hdim)
    maps = rounder(jax.nn.silu(conv_doc(bcproj * mask[:, :, None], conv_bc, seg)))
    b_fwd = maps[..., :state]
    c_fwd = maps[..., state : 2 * state]
    b_bwd = maps[..., 2 * state : 3 * state]
    c_bwd = maps[..., 3 * state :]
    rate = -jnp.exp(a_log)
    dt_fwd = jax.nn.softplus(proj[..., 2 * hdim] + dt_bias[:, 0]) * mask[:, :, None]
    dt_bwd = jax.nn.softplus(proj[..., 2 * hdim + 1] + dt_bias[:, 1]) * mask[:, :, None]
    out_fwd = ssd_forward(xc, dt_fwd, dt_fwd * rate, b_fwd, c_fwd, seg, prec)

    def flip(v):
        return jnp.flip(v, axis=1)

    out_bwd = flip(
        ssd_forward(
            flip(xc), flip(dt_bwd), flip(dt_bwd * rate), flip(b_bwd), flip(c_bwd), flip(seg), prec
        )
    )
    keep_prev = (seg[:, 1:] == seg[:, :-1]).astype(xc.dtype)[:, :, None, None]
    shifted_fwd = jnp.pad(out_fwd[:, :-1] * keep_prev, ((0, 0), (1, 0), (0, 0), (0, 0)))
    shifted_bwd = jnp.pad(out_bwd[:, 1:] * keep_prev, ((0, 0), (0, 1), (0, 0), (0, 0)))
    return (shifted_fwd + shifted_bwd + skip_d[:, None] * xc, gate)


def shards(
    layer_in,
    pre_gain,
    w_heads,
    w_bc,
    conv_x,
    conv_bc,
    dt_bias,
    a_log,
    skip_d,
    norm_gain,
    w_out,
    cotangent,
    starts,
    live,
):
    seg = segment_ids(starts)
    mask = live.astype(jnp.float32)
    x_here = layer_in.astype(jnp.float32)
    scale = lax.rsqrt(jnp.mean(x_here * x_here, axis=-1, keepdims=True) + EPS)
    normed_here = (x_here * scale * pre_gain).astype(jnp.bfloat16)
    normed = lax.all_gather(normed_here, "narrow", axis=1, tiled=True)
    proj = jnp.einsum("rld,dhc->rlhc", normed, w_heads, preferred_element_type=jnp.float32)
    bcproj = jnp.einsum("rld,dc->rlc", normed, w_bc, preferred_element_type=jnp.float32)

    def mix_local(proj_in, bc_in, taps_x, taps_bc, bias_in, log_rate, diag_in):
        return mixer(
            proj_in, bc_in, taps_x, taps_bc, bias_in, log_rate, diag_in, seg, mask, rounded, HIGH
        )

    (ymix, gate), pull_mix = jax.vjp(
        mix_local, proj, bcproj, conv_x, conv_bc, dt_bias, a_log, skip_d
    )
    rows, length, heads, hdim = ymix.shape
    sigma = jax.nn.sigmoid(gate)
    act = gate * sigma
    gated = (ymix * act).reshape(rows, length, heads * hdim)
    squares = lax.psum(jnp.sum(gated * gated, axis=-1), "narrow")
    inv = lax.rsqrt(squares / (H * HD) + EPS)[..., None]
    gain_flat = norm_gain.reshape(-1)
    normalized = gated * inv
    hn = (normalized * gain_flat).astype(jnp.bfloat16)
    w_flat = w_out.reshape(heads * hdim, -1)
    partial_value = jnp.einsum("rlc,cd->rld", hn, w_flat, preferred_element_type=jnp.float32)
    branch = lax.psum_scatter(partial_value, "narrow", scatter_dimension=1, tiled=True)
    out = (x_here + branch).astype(jnp.bfloat16)
    grad_out = lax.all_gather(cotangent, "narrow", axis=1, tiled=True)
    g_w_out = jnp.einsum("rlc,rld->cd", hn, grad_out, preferred_element_type=jnp.float32)
    g_hn = jnp.einsum("rld,cd->rlc", grad_out, w_flat, preferred_element_type=jnp.float32)
    g_gain = jnp.sum(g_hn * normalized, axis=(0, 1))
    weighted = g_hn * gain_flat
    cross = lax.psum(jnp.sum(weighted * gated, axis=-1), "narrow")
    g_gated = inv * weighted - gated * (inv * inv * inv) * (cross / (H * HD))[..., None]
    g_gated = g_gated.reshape(rows, length, heads, hdim)
    g_ymix = g_gated * act
    g_gate = g_gated * ymix * (sigma * (1.0 + gate * (1.0 - sigma)))
    g_proj, g_bcproj, g_conv_x, g_conv_bc, g_dt_bias, g_a_log, g_skip = pull_mix((g_ymix, g_gate))
    g_proj_low = g_proj.astype(jnp.bfloat16)
    g_w_heads = jnp.einsum("rld,rlhc->dhc", normed, g_proj_low, preferred_element_type=jnp.float32)
    g_w_bc = jnp.einsum(
        "rld,rlc->dc", normed, g_bcproj, precision=HIGH, preferred_element_type=jnp.float32
    )
    g_normed = jnp.einsum("rlhc,dhc->rld", g_proj_low, w_heads, preferred_element_type=jnp.float32)
    g_normed = g_normed + jnp.einsum(
        "rlc,dc->rld", g_bcproj, w_bc, precision=HIGH, preferred_element_type=jnp.float32
    )
    g_normed_here = lax.psum_scatter(g_normed, "narrow", scatter_dimension=1, tiled=True)
    weighted_in = g_normed_here * pre_gain
    g_pre = jnp.sum(g_normed_here * x_here * scale, axis=(0, 1))
    g_x = scale * weighted_in - x_here * (scale * scale * scale) * jnp.mean(
        weighted_in * x_here, axis=-1, keepdims=True
    )
    grad_input = cotangent.astype(jnp.float32) + g_x
    g_pre, g_w_bc, g_conv_bc = lax.psum((g_pre, g_w_bc, g_conv_bc), "narrow")
    reduced = (
        lax.psum_scatter(g_w_heads, "wide", scatter_dimension=0, tiled=True),
        lax.psum_scatter(g_w_out.reshape(heads, hdim, -1), "wide", scatter_dimension=2, tiled=True),
        lax.psum_scatter(g_conv_x, "wide", scatter_dimension=2, tiled=True),
        lax.psum_scatter(g_gain.reshape(heads, hdim), "wide", scatter_dimension=1, tiled=True),
        lax.psum_scatter(g_pre, "wide", scatter_dimension=0, tiled=True),
        lax.psum_scatter(g_w_bc, "wide", scatter_dimension=0, tiled=True),
        lax.psum_scatter(g_conv_bc, "wide", scatter_dimension=1, tiled=True),
    )
    share_pre, share_bc, share_conv = (reduced[4], reduced[5], reduced[6])
    head_bias, head_rate, head_diag = lax.psum((g_dt_bias, g_a_log, g_skip), "wide")
    return (
        out,
        grad_input,
        share_pre,
        reduced[0],
        share_bc,
        reduced[2],
        share_conv,
        head_bias,
        head_rate,
        head_diag,
        reduced[3],
        reduced[1],
    )


HALO = 16
F32 = jnp.float32
BF16 = jnp.bfloat16
LOGZERO = -1e30


def mm(a, b, dims=((1,), (0,)), precision=None):
    return lax.dot_general(a, b, (dims, ((), ())), precision=precision, preferred_element_type=F32)


def nt(a, b):
    return mm(a, b, ((1,), (1,)))


def tn(a, b):
    return mm(a, b, ((0,), (0,)))


def seg_at(info, pos):
    seg = jnp.full(pos.shape, -1, jnp.int32)
    for j in range(4):
        seg = seg + (pos >= info[j]).astype(jnp.int32)
    return jnp.where(pos >= info[6], 99, seg)


def iota(shape, dim):
    return lax.broadcasted_iota(jnp.int32, shape, dim)


def silu_parts(v):
    sg = 0.5 * jnp.tanh(0.5 * v) + 0.5
    act = v * sg
    return act, sg + act * (1.0 - sg)


def thirds(v):
    hi = v.astype(BF16).astype(F32)
    rest = v - hi
    mid = rest.astype(BF16).astype(F32)
    return hi, mid, rest - mid


def column_terms(values):
    sub = iota((16, 128), 0)
    v = jnp.ones((16, 128), F32)
    for k, value in enumerate(values):
        v = jnp.where((sub >= 3 * k) & (sub < 3 * k + 3), value, v)
    hi, mid, low = thirds(v)
    part = sub % 3
    out = jnp.where(part == 0, hi, jnp.where(part == 1, mid, low))
    return jnp.where(sub < 3 * len(values), out, 1.0).astype(BF16)


def row_base(count, places):
    sub = iota((16, 384), 0)
    lane = iota((16, 384), 1)
    out = jnp.zeros((16, 384), F32)
    for k, spans in enumerate(places):
        for lo, hi in spans:
            out = jnp.where((sub >= 3 * k) & (sub < 3 * k + 3) & (lane >= lo) & (lane < hi), 1.0, out)
    return out


def row_terms(count, base, one, two):
    sub = iota((16, 128), 0)
    part = sub - 3 * count
    made = []
    for k, value in enumerate((one, two)):
        hi, mid, low = thirds(jnp.broadcast_to(value, (16, 128)))
        here = base[:, 128 * k : 128 * (k + 1)]
        made.append(
            jnp.where(part == 0, hi, jnp.where(part == 1, mid, jnp.where(part == 2, low, here))).astype(BF16)
        )
    return jnp.concatenate(made + [base[:, 256:].astype(BF16)], axis=1)


def conv_taps(src, seg_src, taps, first, rows):
    seg0 = seg_src[first : first + rows, :]
    total = src[first : first + rows, :] * taps[3:4, :]
    for k in (0, 1, 2, 4, 5, 6):
        lo = first + k - 3
        same = seg_src[lo : lo + rows, :] == seg0
        total = total + jnp.where(same, src[lo : lo + rows, :], 0.0) * taps[k : k + 1, :]
    return total


def front_kernel(
    length, hl, starts, live_ref, x_in, gain, wbc_ref, taps_ref, small_a, small_b,
    info, taps_o, gain_o, skip_o, wdt, wbc, taps, normed_o, rs_o, bcm_h, dsl_h, maps_h, ta_o, tb_o, tc_h, dpt_o, sig_h, seg_s, maps_s, cum_s, x_s, bcm_o, dsl_o, maps_o, tc_o, sig_o, sems,
):
    late = []

    def send(src, dst):
        late.append(pltpu.make_async_copy(src, dst, sems.at[len(late)]))
        late[-1].start()

    nb = length // BLOCK
    ext = length + 2 * HALO
    dm = x_in.shape[1]
    n = lax.axis_index("narrow")
    for i in range(4):
        info[i] = starts[0, i]
    count = jnp.sum(live_ref[...].astype(F32)).astype(jnp.int32)
    off = n * length
    info[4] = count
    info[5] = off
    info[6] = live_ref.shape[1]
    info[7] = n
    ch = small_a.shape[1]
    for k, small in enumerate((small_a, small_b)):
        cols = slice(k * ch, (k + 1) * ch)
        taps_o[:, cols] = small[0:8, :]
        gain_o[:, cols] = jnp.broadcast_to(small[7:8, :], (8, ch))
        skip_o[:, cols] = jnp.broadcast_to(small[8:9, :], (8, ch))
    dst = iota((128, 2 * hl), 0)
    src = iota((128, 2 * hl), 1)
    place = (src % 2) * 64 + src // 2
    at_a = jnp.where(dst == place, 1.0, 0.0).astype(BF16)
    at_b = jnp.where(dst == place + hl, 1.0, 0.0).astype(BF16)
    own_steps = small_a[16 : 16 + 2 * hl, :].astype(BF16)
    far_steps = small_b[16 : 16 + 2 * hl, :].astype(BF16)
    wdt[...] = (mm(at_a, own_steps) + mm(at_b, far_steps)).astype(BF16)
    wbc[...] = pack_columns(wbc_ref[...])
    taps[...] = pack_columns(taps_ref[...])

    bias = small_a[9:10, 0:128] + pltpu.roll(small_b[9:10, 0:128], hl, 1)
    alog = small_a[9:10, 128:256] + pltpu.roll(small_b[9:10, 128:256], hl, 1)
    edge = small_b[16 + 2 * hl : 24 + 2 * hl, :]
    zero_edge = jnp.zeros((8, dm), F32)
    before = jnp.concatenate([zero_edge, jnp.where(n == 1, edge, 0.0)], axis=0)
    behind = jnp.concatenate([jnp.where(n == 1, 0.0, edge), zero_edge], axis=0)
    x_s[0:HALO, :] = before.astype(BF16)
    x_s[HALO : HALO + length, :] = x_in[...]
    x_s[HALO + length : ext, :] = behind.astype(BF16)
    x = x_s[...].astype(F32)
    rs = lax.rsqrt(jnp.mean(x * x, axis=1, keepdims=True) + EPS)
    normed = (x * rs * gain[...]).astype(BF16)
    normed_o[...] = normed
    rs_o[...] = rs[HALO : HALO + length, :]
    pos256 = iota((ext, 256), 0) + (off - HALO)
    seg_s[...] = seg_at(info, pos256)
    live = pos256 < count
    bcm_o[...] = jnp.where(live, mm(normed, wbc[...]), 0.0)
    send(bcm_o, bcm_h)
    crows = length + HALO
    cfirst = HALO // 2
    mix = conv_taps(bcm_o, seg_s, taps, cfirst, crows)
    maps, dsl = silu_parts(mix)
    dsl_o[...] = jnp.zeros_like(dsl_o)
    dsl_o[cfirst : cfirst + crows, :] = dsl
    send(dsl_o, dsl_h)
    maps_s[...] = jnp.zeros_like(maps_s)
    maps_s[cfirst : cfirst + crows, :] = maps.astype(BF16).astype(F32)
    own = slice(HALO, HALO + length)
    segx = seg_s[own, 0:128]
    lane = iota((length, 128), 1)
    fwd = lane < 64
    segp = seg_s[HALO - 1 : HALO - 1 + length, 0:128]
    segn = seg_s[HALO + 1 : HALO + 1 + length, 0:128]
    bmap = maps_s[own, 0:128]
    cprev = jnp.where(segp == segx, maps_s[HALO - 1 : HALO - 1 + length, 128:256], 0.0)
    cnext = jnp.where(segn == segx, maps_s[HALO + 1 : HALO + 1 + length, 128:256], 0.0)
    cmap = jnp.where(fwd, cprev, cnext)
    maps_o[:, 0:128] = bmap.astype(BF16)
    maps_o[:, 128:256] = cmap.astype(BF16)
    send(maps_o, maps_h)
    raw = nt(normed[own, :], wdt[...]) + bias
    softp = jnp.maximum(raw, 0.0) + jnp.log(1.0 + jnp.exp(-jnp.abs(raw)))
    softp = jnp.where(raw < -15.0, jnp.exp(jnp.minimum(raw, 0.0)), softp)
    pos128 = iota((length, 128), 0) + off
    m = pos128 < count
    dt = jnp.where(m, softp, 0.0)
    sg = jnp.where(m, 1.0 / (1.0 + jnp.exp(-raw)), 0.0)
    ratio = jnp.where(m, jnp.where(raw < -15.0, 1.0, sg / jnp.maximum(softp, 1e-30)), 0.0)
    rate = -jnp.exp(alog)
    a = dt * rate
    sig_o[:, 256:384] = a
    sig_o[:, 0:128] = sg * rate
    sig_o[:, 128:256] = ratio
    tri = (iota((BLOCK, BLOCK), 0) >= iota((BLOCK, BLOCK), 1)).astype(F32)
    logdt = jnp.maximum(jnp.log(dt), LOGZERO)
    sub = iota((BLOCK, BLOCK), 0)
    ln = iota((BLOCK, BLOCK), 1)
    fwdb = ln < 64
    cum_s[...] = jnp.zeros_like(cum_s)
    dvals, ends = [], []
    for b in range(nb):
        blk = slice(b * BLOCK, (b + 1) * BLOCK)
        ab = a[blk, :]
        cum = mm(tri, ab, precision=HIGH)
        cx = cum - ab
        end = cum[BLOCK - 1 : BLOCK, :]
        colt = jnp.where(fwdb, cx, end - cum)
        rows = jnp.where(fwdb, logdt[blk, :] - cum, cx + logdt[blk, :] - end)
        tb_o[0, b] = colt.T
        tb_o[1, b] = rows.T
        ta_o[0, b] = jnp.minimum(rows + end, 60.0).T
        first_pos = off + b * BLOCK
        sp = seg_at(info, sub + first_pos)
        st = seg_at(info, ln + first_pos)
        before = seg_at(info, sub * 0 + (first_pos - 1))
        begin = seg_at(info, sub * 0 + first_pos)
        last = seg_at(info, sub * 0 + (first_pos + BLOCK - 1))
        after = seg_at(info, sub * 0 + (first_pos + BLOCK))
        enter = jnp.where(fwdb, (sp == before).astype(F32), (sp == after).astype(F32))
        keep = jnp.where(fwdb, (sp == last).astype(F32), (sp == begin).astype(F32))
        ce = cmap[blk, :] * enter
        bk = bmap[blk, :] * keep
        tb_o[3, b] = ce
        tc_o[1, b] = bk
        tc_o[2, b] = ce.T
        ta_o[1, b] = bk.T
        chain = jnp.where(fwdb[0:1, :], (last == before).astype(F32)[0:1, :], (begin == after).astype(F32)[0:1, :])
        dvals.append(jnp.exp(end) * chain)
        ends.append(end)
        cb = cmap[blk, :].astype(BF16)
        bb = bmap[blk, :].astype(BF16)
        zero = jnp.zeros_like(bb)
        same = sp == st
        low = same & (sub > ln)
        high = same & (sub < ln)
        bf = jnp.where(fwdb, bb, zero)
        br = jnp.where(fwdb, zero, bb)
        tb_o[2, b] = jnp.where(low, nt(cb, bf), jnp.where(high, nt(cb, br), 0.0))
        tc_o[0, b] = jnp.where(high, nt(bf, cb), jnp.where(low, nt(br, cb), 0.0))
    ones = jnp.ones((1, 128), F32)
    prefix, suffix = [ones], [ones]
    for b in range(nb):
        prefix.append(prefix[-1] * dvals[b])
        suffix.append(suffix[-1] * dvals[nb - 1 - b])
    suffix = suffix[::-1]
    f1 = fwdb[0:1, :]
    for b in range(nb):
        cum_s[b : b + 1, :] = dvals[b]
        cum_s[48 + b : 49 + b, :] = ends[b]
    for i in range(nb + 1):
        cum_s[16 + i : 17 + i, :] = jnp.where(f1, prefix[i], suffix[i])
        cum_s[32 + i : 33 + i, :] = jnp.where(f1, suffix[i], prefix[i])
    dpt_o[...] = cum_s[...].T
    send(sig_o, sig_h)
    send(tc_o, tc_h)
    for one in late:
        one.wait()


def pair_rows(dpt, j, base, i, half):
    lane = iota((1, 128), 1)
    one = dpt[pl.ds(half * 64 + 2 * j, 1), :][:, base + i : base + i + 1]
    two = dpt[pl.ds(half * 64 + 2 * j + 1, 1), :][:, base + i : base + i + 1]
    return jnp.where(lane < 64, one, two)


def assemble(dst, pieces):
    quarter = dst.shape[0] // 4
    q = lax.axis_index("wide") % 4
    cbit = q % 2
    xbit = q // 2
    places = (q, (1 - xbit) * 2 + cbit, xbit * 2 + 1 - cbit, (1 - xbit) * 2 + 1 - cbit)
    for place, piece in zip(places, pieces):
        dst[pl.ds(pl.multiple_of(place * quarter, quarter), quarter), :] = piece[...]


def vals_kernel(length, other, info, normed, *refs):
    nb = length // BLOCK
    ext = length + 2 * HALO
    step = pl.program_id(0)
    first = step
    if other:
        p0, p1, p2, p3, taps, ta, dpt = refs[:7]
        xc_o, vm_o, ds_o, s_o, bnd_o, wvo_o, vm_a, vm_b, seg_s = refs[11:]
        first = step + pl.num_programs(0)

        @pl.when(step == 0)
        def _():
            assemble(wvo_o, (p0, p1, p2, p3))

        wv = wvo_o[pl.ds(pl.multiple_of(step * 256, 256), 256), :]
    else:
        w_ref, taps, ta, dpt, xc_o, vm_o, ds_o, s_o, bnd_o, vm_a, vm_b, seg_s = refs
        wv = jnp.concatenate([w_ref[h, HD : 2 * HD, :] for h in range(4)], axis=0)
    off, count = info[5], info[4]

    @pl.when(step == 0)
    def _():
        seg_s[...] = seg_at(info, iota((ext, 128), 0) + (off - HALO))

    live = iota((ext, 128), 0) + (off - HALO) < count
    both = nt(normed[...], wv)
    lane = iota((BLOCK, 128), 1)
    top = iota((BLOCK, 128), 0) < 64
    for p, vm_s in enumerate((vm_a, vm_b)):
        j = 2 * first + p
        here = slice(128 * p, 128 * (p + 1))
        vm = jnp.where(live, both[:, here], 0.0)
        vm_s[...] = vm
        vm_o[:, here] = vm.astype(BF16)
        act, ds = silu_parts(conv_taps(vm_s, seg_s, taps[:, here], HALO, length))
        xc = act.astype(BF16)
        xc_o[:, here] = xc
        ds_o[:, here] = ds.astype(BF16)
        loc = []
        for b in range(nb):
            blk = slice(b * BLOCK, (b + 1) * BLOCK)
            got = []
            for i in range(2):
                h = 2 * j + i
                w = jnp.where(top, jnp.exp(ta[0, b, pl.ds(h, 1), :]), jnp.exp(ta[0, b, pl.ds(64 + h, 1), :]))
                got.append((ta[1, b] * w).astype(BF16))
            got = mm(jnp.concatenate(got, axis=0), xc[blk, :])
            loc.append(jnp.where(lane < 64, got[0:BLOCK, :], got[BLOCK:, :]))
        state = jnp.zeros((64, 128), F32)
        s_o[p, 0, 0:64, :] = state.astype(BF16)
        for b in range(nb):
            state = pair_rows(dpt, j, 0, b, 0) * state + loc[b][0:64, :]
            s_o[p, b + 1, 0:64, :] = state.astype(BF16)
        end_f = state
        state = jnp.zeros((64, 128), F32)
        s_o[p, nb, 64:128, :] = state.astype(BF16)
        for b in range(nb - 1, -1, -1):
            state = pair_rows(dpt, j, 0, b, 1) * state + loc[b][64:128, :]
            s_o[p, b, 64:128, :] = state.astype(BF16)
        bnd_o[p] = jnp.where(info[7] == 0, end_f, state).astype(BF16)


def scan_kernel(length, first_pair, info, xc_ref, s_ref, s0_ref, dpt, tb, skip, *refs):
    nb = length // BLOCK
    y_o, st_o = refs[-2:]
    j = pl.program_id(0) + first_pair
    right = (info[7] == 1).astype(F32)
    s0 = s0_ref[0].astype(F32)
    lane = iota((BLOCK, 128), 1)
    first = lane < 64
    low = iota((BLOCK, BLOCK), 0) > lane
    base = row_base(2, [[(0, 128), (256, 320)], [(128, 256), (320, 384)]])
    for i in range(nb + 1):
        f = s_ref[0, i, 0:64, :].astype(F32) + pair_rows(dpt, j, 16, i, 0) * (s0 * right)
        r = s_ref[0, i, 64:128, :].astype(F32) + pair_rows(dpt, j, 16, i, 1) * (s0 * (1.0 - right))
        st_o[0, i, 0:64, :] = f.astype(BF16)
        st_o[0, i, 64:128, :] = r.astype(BF16)
    for b in range(nb):
        blk = slice(b * BLOCK, (b + 1) * BLOCK)
        xb = xc_ref[blk, :]
        rhs = jnp.concatenate([xb, st_o[0, b, 0:64, :], st_o[0, b + 1, 64:128, :]], axis=0)
        got = []
        for i in range(2):
            h = 2 * j + i
            terms = column_terms([tb[0, b, pl.ds(h, 1), :], tb[0, b, pl.ds(64 + h, 1), :]])
            expo = tn(terms, row_terms(2, base, tb[1, b, pl.ds(h, 1), :], tb[1, b, pl.ds(64 + h, 1), :]))
            diff = jnp.where(low, expo[:, 0:128], expo[:, 128:256])
            mix = jnp.exp(jnp.minimum(diff, 60.0)) * tb[2, b]
            ct = tb[3, b] * jnp.exp(expo[:, 256:])
            lhs = jnp.concatenate([mix.astype(BF16), ct.astype(BF16)], axis=1)
            got.append(lhs)
        got = mm(jnp.concatenate(got, axis=0), rhs)
        y = jnp.where(first, got[0:BLOCK, :], got[BLOCK:, :]) + skip[0:1, :] * xb.astype(F32)
        y_o[blk, :] = y.astype(BF16)


def by_core(v, keep, send):
    share = v.shape[0] // 16
    cbit = lax.axis_index("wide") % 2
    v = v.astype(BF16).reshape(8, 2, share, v.shape[1])
    keep[...] = jnp.where(cbit == 0, v[:, 0], v[:, 1]).reshape(8 * share, v.shape[3])
    send[...] = jnp.where(cbit == 0, v[:, 1], v[:, 0]).reshape(8 * share, v.shape[3])


def gate_kernel(
    tiles, info, x_ref, g_ref, normed, y_ref, wout_a, w_ref, p0, p1, p2, p3, gain, tb, tc, dpt,
    out_h, gy_o, ggate_o, hn_s, ggain_o, wgo_h, gs_o, bnd_o, other_s, gated_s, act_s, dact_s, ghn_s, loc_s, out_o, sems,
):
    late = []

    def send(src, dst):
        late.append(pltpu.make_async_copy(src, dst, sems.at[len(late)]))
        late[-1].start()

    dm = x_ref.shape[1]
    chans = y_ref.shape[1]
    half = chans // 2
    step = 256
    assemble(other_s, (p0, p1, p2, p3))
    send(other_s.at[:, dm:], wgo_h)
    ggain_o[...] = jnp.zeros_like(ggain_o)
    first = iota((BLOCK, 128), 1) < 64
    top = iota((BLOCK, 128), 0) < 64

    @pl.loop(0, tiles)
    def _(i):
        start = pl.multiple_of(i * BLOCK, BLOCK)
        rows = pl.ds(start, BLOCK)
        nrows = normed[pl.ds(pl.multiple_of(start + HALO, HALO), BLOCK), :]
        squares = jnp.zeros((BLOCK, 128), F32)
        for lo in range(0, chans, step):
            if lo < half:
                heads = range(lo // HD, (lo + step) // HD)
                wg = jnp.concatenate([w_ref[h, 0:HD, :] for h in heads], axis=0)
            else:
                wg = other_s[lo - half : lo - half + step, dm:]
            gates = nt(nrows, wg)
            for at in range(0, step, 128):
                cols = slice(lo + at, lo + at + 128)
                act, dact = silu_parts(gates[:, at : at + 128])
                gated = y_ref[rows, cols].astype(F32) * act
                squares = squares + gated * gated
                gated_s[:, cols] = gated
                act_s[:, cols] = act
                dact_s[:, cols] = dact
        inv = lax.rsqrt(jnp.sum(squares, axis=1, keepdims=True) * (1.0 / chans) + EPS)
        inv = jnp.broadcast_to(inv, (BLOCK, 128))
        g = g_ref[rows, :]
        across = jnp.zeros((BLOCK, 128), F32)
        for lo in range(0, chans, step):
            wo = wout_a[lo : lo + step, :] if lo < half else other_s[lo - half : lo - half + step, 0:dm]
            ghns = nt(g, wo)
            for at in range(0, step, 128):
                cols = slice(lo + at, lo + at + 128)
                gainv = gain[0:1, cols]
                gated = gated_s[:, cols]
                nrm = gated * inv
                hn_s[rows, cols] = (nrm * gainv).astype(BF16)
                ghn = ghns[:, at : at + 128]
                ggain_o[0:1, cols] += jnp.sum(ghn * nrm, axis=0, keepdims=True)
                wgt = ghn * gainv
                ghn_s[:, cols] = wgt
                across = across + wgt * gated
        cross = jnp.sum(across, axis=1, keepdims=True) * (1.0 / chans)
        cross = jnp.broadcast_to(cross, (BLOCK, 128)) * (inv * inv * inv)
        hn = hn_s[rows, :]
        branch = mm(hn[:, 0:half], wout_a[...]) + mm(hn[:, half:], other_s[:, 0:dm])
        out_o[rows, :] = (x_ref[rows, :].astype(F32) + branch).astype(BF16)
        for lo in range(0, chans, 128):
            cols = slice(lo, lo + 128)
            ggated = inv * ghn_s[:, cols] - gated_s[:, cols] * cross
            gy = (ggated * act_s[:, cols]).astype(BF16)
            gy_o[rows, cols] = gy
            ggate_o[rows, cols] = (ggated * y_ref[rows, cols].astype(F32) * dact_s[:, cols]).astype(BF16)
            got = []
            for h in range(lo // HD, lo // HD + 2):
                e = jnp.where(top, jnp.exp(tb[0, i, h : h + 1, :]), jnp.exp(tb[0, i, 64 + h : 65 + h, :]))
                got.append((tc[2, i] * e).astype(BF16))
            got = mm(jnp.concatenate(got, axis=0), gy)
            loc_s[i, :, cols] = jnp.where(first, got[0:BLOCK, :], got[BLOCK:, :])

    send(out_o, out_h)

    @pl.loop(0, chans // 128)
    def _(j):
        cols = pl.ds(pl.multiple_of(j * 128, 128), 128)
        state = jnp.zeros((64, 128), F32)
        gs_o[j, tiles, 0:64, :] = state.astype(BF16)
        for b in range(tiles - 1, -1, -1):
            state = pair_rows(dpt, j, 0, b, 0) * state + loc_s[b, 0:64, cols]
            gs_o[j, b, 0:64, :] = state.astype(BF16)
        end_f = state
        state = jnp.zeros((64, 128), F32)
        gs_o[j, 0, 64:128, :] = state.astype(BF16)
        for b in range(tiles):
            state = pair_rows(dpt, j, 0, b, 1) * state + loc_s[b, 64:128, cols]
            gs_o[j, b + 1, 64:128, :] = state.astype(BF16)
        bnd_o[j] = jnp.where(info[7] == 1, end_f, state).astype(BF16)

    for one in late:
        one.wait()


def wsum_kernel(g_ref, normed, hn, ggate, mine_o, x_o, y_o, d_o, keep_s, send_s, got_s, out_sem, in_sem):
    length, dm = g_ref.shape
    half = hn.shape[1] // 2
    share = mine_o.shape[1]
    w = lax.axis_index("wide")
    core = (w + 1 - 2 * (w % 2), lax.axis_index("narrow"))
    xx = (w // 2) % 2
    mesh_ids = pl.DeviceIdType.MESH
    barrier = pltpu.get_barrier_semaphore()
    pl.semaphore_signal(barrier, inc=1, device_id=core, device_id_type=mesh_ids)
    turned = (g_ref[...].T, normed[HALO : HALO + length, :].T)
    going = []
    for k in range(2):
        for part, source in enumerate((hn, ggate)):
            for p in range(half // 256):
                cols = slice(k * half + p * 256, k * half + (p + 1) * 256)
                dst = slice(part * half + p * 256, part * half + (p + 1) * 256)
                by_core(mm(turned[part], source[:, cols]), keep_s.at[k, :, dst], send_s.at[k, :, dst])
            if not going:
                pl.semaphore_wait(barrier, 1)
            cols = slice(part * half, (part + 1) * half)
            one = pltpu.make_async_remote_copy(
                src_ref=send_s.at[k, :, cols], dst_ref=got_s.at[k, :, cols], send_sem=out_sem.at[k, part],
                recv_sem=in_sem.at[k, part], device_id=core, device_id_type=mesh_ids,
            )
            one.start()
            going.append((k, cols, one))
    for k, cols, one in going:
        one.wait()
        near_o, far_o = ((mine_o, x_o), (y_o, d_o))[k]
        for q in range(4):
            rows = slice(q * 2 * share, (q + 1) * 2 * share)
            both = (keep_s[k, rows, cols].astype(F32) + got_s[k, rows, cols].astype(F32)).astype(BF16)
            low, high = both[0:share, :], both[share:, :]
            near_o[q, :, cols] = jnp.where(xx == 0, low, high)
            far_o[q, :, cols] = jnp.where(xx == 0, high, low)


def gscan_kernel(
    length, info, xc_ref, ds_ref, gy_ref, st_ref, gs_ref, gs0_ref, dpt, rowst, wt, coltt, tc, skip,
    gmix_o, ggt_o, gb_o, gct_o, k_o, r_o, phi_o, gskip_o, edge_o, gst_s,
):
    nb = length // BLOCK
    j = pl.program_id(0)
    right = (info[7] == 1).astype(F32)
    s0 = gs0_ref[0].astype(F32)
    sub = iota((BLOCK, BLOCK), 0)
    lane = iota((BLOCK, 128), 1)
    first = lane < 64
    later = lane > sub
    top = sub < 64

    @pl.when(j == 0)
    def _():
        for acc in (ggt_o, gb_o, gct_o, k_o, r_o):
            acc[...] = jnp.zeros_like(acc)

    base = row_base(4, [[(0, 128)], [(128, 256)], [(256, 320)], [(320, 384)]])

    phi_o[...] = jnp.zeros_like(phi_o)
    for i in range(nb + 1):
        f = gs_ref[0, i, 0:64, :].astype(F32) + pair_rows(dpt, j, 32, i, 0) * (s0 * (1.0 - right))
        r = gs_ref[0, i, 64:128, :].astype(F32) + pair_rows(dpt, j, 32, i, 1) * (s0 * right)
        f = f.astype(BF16)
        r = r.astype(BF16)
        gst_s[i, 0:64, :] = f
        gst_s[i, 64:128, :] = r
        if i > 0:
            phi_o[i - 1 : i, :] = jnp.sum(f.astype(F32) * st_ref[0, i, 0:64, :].astype(F32), axis=0, keepdims=True)
        if i < nb:
            phi_o[8 + i : 9 + i, :] = jnp.sum(
                r.astype(F32) * st_ref[0, i, 64:128, :].astype(F32), axis=0, keepdims=True
            )
    gskip = jnp.zeros((1, 128), F32)
    for b in range(nb):
        blk = slice(b * BLOCK, (b + 1) * BLOCK)
        xb = xc_ref[blk, :]
        gy = gy_ref[blk, :]
        gyf = gy.astype(F32)
        gskip = gskip + jnp.sum(gyf * xb.astype(F32), axis=0, keepdims=True)
        rhs = jnp.concatenate([gy, gst_s[b + 1, 0:64, :], gst_s[b, 64:128, :]], axis=0)
        left = jnp.concatenate([xb, st_ref[0, b, 0:64, :], st_ref[0, b + 1, 64:128, :]], axis=0)
        first2 = iota((2 * BLOCK, 128), 1) < 64
        none = jnp.zeros_like(left)
        big2 = nt(jnp.concatenate([jnp.where(first2, left, none), jnp.where(first2, none, left)], axis=0), rhs)
        got = []
        sum_ge, sum_gct, sum_gb, kparts = [], [], [], []
        for i in range(2):
            h = 2 * j + i
            terms = column_terms([v[b, pl.ds(at + h, 1), :] for v in (rowst, wt) for at in (0, 64)])
            expo = tn(terms, row_terms(4, base, coltt[b, pl.ds(h, 1), :], coltt[b, pl.ds(64 + h, 1), :]))
            diff = jnp.where(later, expo[:, 0:128], expo[:, 128:256])
            et_m = jnp.exp(jnp.minimum(diff, 60.0))
            mt = et_m * tc[0, b]
            w = jnp.exp(expo[:, 256:])
            bt = tc[1, b] * w
            big = big2[2 * BLOCK * i : 2 * BLOCK * (i + 1), :]
            gmt = big[0:BLOCK, 0:BLOCK]
            gbt = big[0:BLOCK, BLOCK:]
            gctt = big[BLOCK:, 0:BLOCK]
            ge = gmt * et_m
            sum_ge.append(ge)
            q = gmt * mt
            qf = jnp.where(later, q, 0.0)
            e = jnp.where(top, jnp.exp(coltt[b, pl.ds(h, 1), :]), jnp.exp(coltt[b, pl.ds(64 + h, 1), :]))
            gce = gctt * e
            sum_gct.append(gce)
            ct = gce * tc[2, b]
            rf = jnp.sum(qf, axis=0, keepdims=True)
            rall = jnp.sum(q, axis=0, keepdims=True)
            r_o[b, pl.ds(h, 1), :] = rf + jnp.sum(ct[0:64, :], axis=0, keepdims=True)
            r_o[b, pl.ds(64 + h, 1), :] = rall - rf + jnp.sum(ct[64:128, :], axis=0, keepdims=True)
            gbw = gbt * w
            sum_gb.append(gbw)
            u = gbw * tc[1, b]
            kf = jnp.sum(qf + jnp.where(first, u, 0.0), axis=1, keepdims=True)
            kb = jnp.sum(q + u, axis=1, keepdims=True) - kf
            kparts += [kf, kb]
            lhs = jnp.concatenate([mt.astype(BF16), bt.astype(BF16)], axis=1)
            got.append(lhs)
        ggt_o[b] += sum_ge[0] + sum_ge[1]
        gct_o[b] += sum_gct[0] + sum_gct[1]
        gb_o[b] += sum_gb[0] + sum_gb[1]
        two = jnp.where(lane % 64 == 0, jnp.where(first, kparts[0], kparts[1]), jnp.where(first, kparts[2], kparts[3]))
        k_o[blk, :] += pltpu.roll(jnp.where(lane % 64 < 2, two, 0.0), 2 * j, 1)
        got = mm(jnp.concatenate(got, axis=0), rhs)
        gx = jnp.where(first, got[0:BLOCK, :], got[BLOCK:, :]) + skip[0:1, :] * gyf
        gmix = (gx * ds_ref[blk, :].astype(F32)).astype(BF16)
        gmix_o[blk, :] = gmix
        if b == 0:
            edge_o[...] = gmix[0:HALO, :]
        if b == nb - 1:
            edge_o[...] = jnp.where(info[7] == 0, gmix[BLOCK - HALO :, :], edge_o[...])
    gskip_o[...] = jnp.broadcast_to(gskip, (8, 128))


def join_kernel(
    length, heads, info, ggt, gb, gct, k_ref, r_ref, phi, maps, dsl, sig,
    gmb_o, gv_o, small_o, edge_o, gc_s, gm_s,
):
    nb = length // BLOCK
    off = info[5]
    chans = phi.shape[1]
    sub = iota((BLOCK, BLOCK), 0)
    lane = iota((BLOCK, 128), 1)
    first = lane < 64
    low = sub > lane
    high = sub < lane
    upper_strict = high.astype(F32)
    upper = (sub <= lane).astype(F32)
    lower_strict = low.astype(F32)
    lower = (sub >= lane).astype(F32)
    owner = iota((chans, 128), 0) // 64
    to_f = (owner == iota((chans, 128), 1)).astype(F32)
    to_b = (owner + 64 == iota((chans, 128), 1)).astype(F32)
    phi_f = mm(phi[0:8, :], to_f, precision=HIGH)
    phi_b = mm(phi[8:16, :], to_b, precision=HIGH)
    gc_s[...] = jnp.zeros_like(gc_s)
    gm_s[...] = jnp.zeros_like(gm_s)
    sum_bias = jnp.zeros((1, 128), F32)
    sum_rate = jnp.zeros((1, 128), F32)
    for b in range(nb):
        blk = slice(b * BLOCK, (b + 1) * BLOCK)
        ext = slice(HALO + b * BLOCK, HALO + (b + 1) * BLOCK)
        first_pos = off + b * BLOCK
        sp = seg_at(info, sub + first_pos)
        st = seg_at(info, lane + first_pos)
        before = seg_at(info, sub * 0 + (first_pos - 1))
        begin = seg_at(info, sub * 0 + first_pos)
        last = seg_at(info, sub * 0 + (first_pos + BLOCK - 1))
        after = seg_at(info, sub * 0 + (first_pos + BLOCK))
        enter = jnp.where(first, (sp == before).astype(F32), (sp == after).astype(F32))
        keep = jnp.where(first, (sp == last).astype(F32), (sp == begin).astype(F32))
        same = sp == st
        gg = ggt[b]
        gf = jnp.where(same & high, gg, 0.0).astype(BF16)
        gr = jnp.where(same & low, gg, 0.0).astype(BF16)
        cm = maps[blk, 128:256]
        bm = maps[blk, 0:128]
        gm_s[ext, 0:128] = jnp.where(first, mm(gf, cm), mm(gr, cm)) + gb[b] * keep
        gc_s[ext, :] = jnp.where(first, tn(gf, bm), tn(gr, bm)) + gct[b].T * enter
        kb = k_ref[blk, :]
        rb = r_ref[b].T
        ga_f = mm(upper_strict, rb, precision=HIGH) - mm(upper, kb, precision=HIGH) + phi_f[b : b + 1, :]
        ga_b = mm(lower_strict, rb, precision=HIGH) - mm(lower, kb, precision=HIGH) + phi_b[b : b + 1, :]
        ga = jnp.where(first, ga_f, ga_b)
        gv = kb * sig[blk, 128:256] + ga * sig[blk, 0:128]
        gv_o[blk, :] = gv.astype(BF16)
        sum_bias = sum_bias + jnp.sum(gv, axis=0, keepdims=True)
        sum_rate = sum_rate + jnp.sum(ga * sig[blk, 256:384], axis=0, keepdims=True)
    small_o[...] = jnp.zeros_like(small_o)
    small_o[0:1, :] = sum_bias
    small_o[1:2, :] = sum_rate
    small_o[8:9, :] = pltpu.roll(sum_bias, 128 - heads // 2, 1)
    small_o[9:10, :] = pltpu.roll(sum_rate, 128 - heads // 2, 1)
    mid = length + HALO
    lo = HALO // 2
    pos = iota((mid, 128), 0) + (off - HALO + lo)
    seg0 = seg_at(info, pos)
    segn = seg_at(info, pos + 1)
    segp = seg_at(info, pos - 1)
    from_next = jnp.where(seg0 == segn, gc_s[lo + 1 : lo + 1 + mid, :], 0.0)
    from_prev = jnp.where(seg0 == segp, gc_s[lo - 1 : lo - 1 + mid, :], 0.0)
    gm_s[lo : lo + mid, 128:256] = jnp.where(iota((mid, 128), 1) < 64, from_next, from_prev)
    gmb_o[...] = gm_s[...] * dsl[...]
    lo = HALO // 2
    edge_o[...] = jnp.where(
        info[7] == 0, gmb_o[length + lo : length + lo + HALO, :], gmb_o[lo : lo + HALO, :]
    )


def back_conv(length, seg_s, live, grad, data, tap):
    own = slice(HALO, HALO + length)
    seg0 = seg_s[own, :]
    mine = grad[own, :]
    here = data[own, :].astype(F32)
    total = mine * tap[3:4, :]
    gtap = [None] * 7
    gtap[3] = jnp.sum(mine * here, axis=0, keepdims=True)
    for k in (0, 1, 2, 4, 5, 6):
        lo = HALO + 3 - k
        same = seg_s[lo : lo + length, :] == seg0
        moved = jnp.where(same, grad[lo : lo + length, :], 0.0)
        total = total + moved * tap[k : k + 1, :]
        gtap[k] = jnp.sum(moved * here, axis=0, keepdims=True)
    return jnp.where(live, total, 0.0), gtap


def back_kernel(
    length, steps, info, gmix, edge, vm, normed, taps, ggain, gskip,
    gvals_o, keep_o, send_o, tiny_o, ext_s, seg_s, turned_s,
):
    ext = length + 2 * HALO
    off, count = info[5], info[4]
    own = slice(HALO, HALO + length)
    seg_s[...] = seg_at(info, iota((ext, 128), 0) + (off - HALO))
    tiny_o[...] = jnp.zeros_like(tiny_o)
    turned_s[...] = normed[own, :].T
    live = iota((length, 128), 0) + off < count
    right = info[7] == 1
    per = steps // 2

    @pl.loop(0, steps)
    def _(j):
        half = j // per
        at = (j % per) * 256
        both = []
        for p in range(2):
            here = pl.ds(pl.multiple_of(at + 128 * p, 128), 128)
            cols = pl.ds(pl.multiple_of(j * 256 + 128 * p, 128), 128)
            ext_s[own, :] = gmix[:, cols].astype(F32)
            far = pl.ds(pl.multiple_of(((j + per) % steps) * 256 + 128 * p, 128), 128)
            halo = edge[:, far].astype(F32)
            ext_s[0:HALO, :] = jnp.where(right, halo, 0.0)
            ext_s[HALO + length : ext, :] = jnp.where(right, 0.0, halo)
            gvals, gtap = back_conv(length, seg_s, live, ext_s, vm[:, cols], taps[:, cols])
            both.append(gvals.astype(BF16))
            for t in range(7):
                tiny_o[half, t : t + 1, here] = gtap[t]
            tiny_o[half, 7:8, here] = ggain[0:1, cols]
            tiny_o[half, 8:9, here] = gskip[0:1, cols]
        both = jnp.concatenate(both, axis=1)
        gvals_o[:, pl.ds(pl.multiple_of(j * 256, 256), 256)] = both
        here = pl.ds(pl.multiple_of(at, 256), 256)
        by_core(mm(turned_s[...], both), keep_o.at[half, :, here], send_o.at[half, :, here])


def finish_kernel(hl, tiny, total, wb, heads_o, wout_o, bc_o, conv_o, convbc_o, pre_o, bias_o, rate_o, skip_o, gain_o):
    ch = tiny.shape[1]
    w = lax.axis_index("wide")
    share = pre_o.shape[1]
    lanes = gain_o.shape[0]
    dm = total.shape[1] - ch
    for h in range(hl):
        cols = slice(h * HD, (h + 1) * HD)
        wout_o[h] = total[:, cols]
        heads_o[h, :, 0:HD] = total[:, dm + h * HD : dm + (h + 1) * HD]
        heads_o[h, :, HD : 2 * HD] = wb[:, cols]
        heads_o[h, :, 2 * HD : 2 * HD + 1] = wb[:, ch + 256 + h : ch + 257 + h]
        heads_o[h, :, 2 * HD + 1 :] = wb[:, ch + 320 + h : ch + 321 + h]
    bc_o[...] = pack_columns(wb[:, ch : ch + 256])
    rows = tiny[...]
    parts = jnp.concatenate(thirds(rows), axis=0).astype(BF16)

    def chosen_sums(first, last, chosen):
        got = mm(parts[:, first:last], chosen.astype(F32).astype(BF16))
        return got[0:16, :] + got[16:32, :] + got[32:48, :]

    src = iota((ch, 128), 0)
    dst = iota((ch, 128), 1)
    for q in range(lanes):
        got = chosen_sums(0, ch, (src == dst * HD + lanes * w + q) & (dst < hl))
        for k in range(7):
            conv_o[k, q : q + 1, :] = got[k : k + 1, 0:hl]
        gain_o[q : q + 1, :] = got[7:8, 0:hl]
    pre_o[...] = chosen_sums(0, ch, (src == share * w + dst) & (dst < share))[9:10, 0:share]
    skip_o[...] = chosen_sums(0, ch, src // HD == dst)[8:9, 0:hl]
    size = convbc_o.shape[1]
    group = (size * w) // 64
    start = ((group % 2) * 2 + group // 2) * 64 + (size * w) % 64
    src = iota((256, 128), 0)
    dst = iota((256, 128), 1)
    chosen = (src == start + dst) & (dst < size)
    for k in range(3):
        part = chosen_sums(256 * k, 256 * (k + 1), chosen)
        for r in range(3):
            if 3 * r + k < 7:
                convbc_o[3 * r + k : 3 * r + k + 1, :] = part[11 + r : 12 + r, 0:size]
    both = rows[10:11, 0:128]
    bias_o[0:1, :] = both[:, 0:hl]
    bias_o[1:2, :] = pltpu.roll(both, 64, 1)[:, 0:hl]
    rate = rows[10:11, 128:256]
    rate_o[...] = (rate + pltpu.roll(rate, 64, 1))[:, 0:hl]


def collect_kernel(
    length, hl, info, gvals, ggate, w_ref, wv_b, wg_b, normed, gmb, edge, bcm, taps_bc, gv, wdt, wbc, x_ref, g_ref, rs, pre,
    small, tiny, keep, send, plane_a, out_o, tiny_o, a_o, gin_o, ext_s, seg_s, keepbc_s, sendbc_s, tinyin_s, acc_s, *refs,
):
    value, maps = refs[0:13], refs[13:26]
    tcore_s, tsum_s, tgot_s, tz_s, tzgot_s, agot_s = refs[26:32]
    sems = (refs[32:37], refs[37:42])
    w = lax.axis_index("wide")
    n = lax.axis_index("narrow")
    c, xx, z = w % 2, (w // 2) % 2, w // 4
    share = out_o.shape[0]
    ch = keep.shape[2]
    core = (w + 1 - 2 * c, n)
    over_x = (w + 2 - 4 * xx, n)
    over_y = (w, 1 - n)
    over_d = (w + 2 - 4 * xx, 1 - n)
    steps = (2, 1, 3)
    over_z = [(((z + d) % 4) * 4 + w % 4, n) for d in steps]
    mesh_ids = pl.DeviceIdType.MESH
    barrier = pltpu.get_barrier_semaphore()
    for other in [core, over_x, over_y, over_d] + over_z:
        pl.semaphore_signal(barrier, inc=1, device_id=other, device_id_type=mesh_ids)
    pl.semaphore_wait(barrier, 7)

    def copy(src, dst, group, at, other):
        got = pltpu.make_async_remote_copy(
            src_ref=src, dst_ref=dst, send_sem=sems[0][group].at[at], recv_sem=sems[1][group].at[at], device_id=other,
            device_id_type=mesh_ids,
        )
        got.start()
        return got

    rows = [pl.ds(pl.multiple_of(((z + d) % 4) * (2 * share), 2 * share), 2 * share) for d in steps + (0,)]

    def split(kind, i, kept, bufs):
        core_s, left_s, right_s, left_out, left_in, right_out, right_in = bufs[:7]
        cut = left_s.shape[3]
        both = kept[:, rows[i], :].astype(F32) + core_s[i].astype(F32)
        low, high = both[:, 0:share, :], both[:, share:, :]
        near = jnp.where(xx == 0, low, high)
        far = jnp.where(xx == 0, high, low)
        left_s[i] = near[:, :, 0:cut]
        right_s[i, 0] = near[0, :, cut:]
        right_s[i, 1] = far[0, :, cut:]
        left_out[i] = far[:, :, 0:cut].astype(BF16)
        right_out[i, 0] = near[1, :, cut:].astype(BF16)
        right_out[i, 1] = far[1, :, cut:].astype(BF16)
        return (
            copy(left_out.at[i], left_in.at[i], 1, (kind, i, 0), over_x),
            copy(right_out.at[i], right_in.at[i], 1, (kind, i, 1), over_y),
        )

    def cross_over(kind, i, going, bufs):
        left_s, right_s, _, left_in, _, right_in, left2_out, left2_in, right2_out, right2_in = bufs[1:11]
        going[0].wait()
        left_s[i] = left_s[i] + left_in[i].astype(F32)
        left2_out[i] = left_s[i, 1].astype(BF16)
        go_left = copy(left2_out.at[i], left2_in.at[i], 2, (kind, i, 0), over_y)
        going[1].wait()
        right_s[i] = right_s[i] + right_in[i].astype(F32)
        right2_out[i] = right_s[i, 1].astype(BF16)
        return go_left, copy(right2_out.at[i], right2_in.at[i], 2, (kind, i, 1), over_x)

    def deepen(kind, i, going, bufs, first):
        left_s, right_s = bufs[1:3]
        left2_in, right2_in = bufs[8], bufs[10]
        z_out, z_in = bufs[11:13]
        cut, cols = left_s.shape[3], z_out.shape[2]
        going[0].wait()
        going[1].wait()
        left = left_s[i, 0] + left2_in[i].astype(F32)
        right = right_s[i, 0] + right2_in[i].astype(F32)
        if i == 3:
            out_o[:, first : first + cut] = left
            out_o[:, first + cut : first + cols] = right
            return []
        z_out[i, :, 0:cut] = left.astype(BF16)
        z_out[i, :, cut:] = right.astype(BF16)
        return [copy(z_out.at[i], z_in.at[i], 4, (kind, i), over_z[i])]

    v_core = [copy(send.at[:, rows[i], :], value[0].at[i], 0, i, core) for i in range(4)]
    a_copies = [copy(plane_a.at[(z + steps[k]) % 4], agot_s.at[k], 4, (3, k), over_z[k]) for k in range(3)]

    ext = length + 2 * HALO
    off, count = info[5], info[4]
    own = slice(HALO, HALO + length)
    seg_s[...] = seg_at(info, iota((ext, 128), 0) + (off - HALO))
    live = iota((length, 128), 0) + off < count
    tinyin_s[...] = tiny[...]
    for half in range(2):
        tinyin_s[half, 10:11, 0:128] = small[8 * half : 8 * half + 1, :]
        tinyin_s[half, 10:11, 128:256] = small[8 * half + 1 : 8 * half + 2, :]
    both = []
    v_first, v_second, m_first, m_second, last = {}, {}, {}, {}, []

    def v_split(i):
        v_core[i].wait()
        v_first[i] = split(0, i, keep, value)

    def v_cross(i):
        v_second[i] = cross_over(0, i, v_first[i], value)

    def v_deepen(i):
        last.extend(deepen(0, i, v_second[i], value, 0))

    def m_split(i):
        m_core[i].wait()
        m_first[i] = split(1, i, keepbc_s, maps)

    def m_cross(i):
        m_second[i] = cross_over(1, i, m_first[i], maps)

    def m_deepen(i):
        last.extend(deepen(1, i, m_second[i], maps, ch))

    for k in range(2):
        cols = slice(k * 128, (k + 1) * 128)
        ext_s[...] = gmb[:, cols]
        lo = HALO // 2
        hi = length + lo
        got = edge[:, cols]
        ext_s[lo : lo + HALO, :] += jnp.where(info[7] == 1, got, 0.0)
        ext_s[hi : hi + HALO, :] += jnp.where(info[7] == 1, 0.0, got)
        gbc, gtap = back_conv(length, seg_s, live, ext_s, bcm[:, cols], taps_bc[:, cols])
        for t in range(7):
            at = (t % 3) * 256 + k * 128
            for half in range(2):
                tinyin_s[half, 11 + t // 3 : 12 + t // 3, at : at + 128] = gtap[t]
        both.append(gbc.astype(BF16))
        if k == 0:
            v_split(0)
            v_split(1)
    gbc = jnp.concatenate(both + [gv[...]], axis=1)
    gw = tn(normed[own, :], gbc)
    by_core(gw, keepbc_s.at[0], sendbc_s.at[0])
    turned = pltpu.roll(gw[:, 256:], 128 - hl, 1)
    by_core(jnp.concatenate([gw[:, 0:256], turned], axis=1), keepbc_s.at[1], sendbc_s.at[1])
    m_core = [copy(sendbc_s.at[:, rows[i], :], maps[0].at[i], 0, 4 + i, core) for i in range(4)]
    wv_a = jnp.concatenate([w_ref[h, HD : 2 * HD, :] for h in range(hl)], axis=0)
    wg_a = jnp.concatenate([w_ref[h, 0:HD, :] for h in range(hl)], axis=0)
    v_cross(0)
    v_split(2)
    acc_s[...] = mm(gvals[:, 0:ch], wv_a) + mm(gvals[:, ch:], wv_b[...])
    v_cross(1)
    v_deepen(0)
    v_split(3)
    m_split(0)
    m_split(1)
    gn = acc_s[...] + mm(ggate[:, 0:ch], wg_a) + mm(ggate[:, ch:], wg_b[...])
    gn = gn + nt(gbc[:, 0:256], wbc[...]) + mm(gv[...], wdt[...])
    acc_s[...] = gn
    r = rs[...]
    gpre = jnp.sum(gn * x_ref[...].astype(F32) * r, axis=0, keepdims=True)
    for half in range(2):
        tinyin_s[half, 9:10, 0 : gpre.shape[1]] = gpre
    t_core = copy(tinyin_s, tcore_s, 0, 8, core)
    v_cross(2)
    v_deepen(1)
    m_split(2)
    m_cross(0)
    v_cross(3)
    v_deepen(2)
    m_split(3)
    m_cross(1)
    m_deepen(0)
    t_core.wait()
    tsum_s[...] = tinyin_s[...] + tcore_s[...]
    t_plane = [copy(tsum_s.at[min(k, 1)], tgot_s.at[k], 3, k, other) for k, other in enumerate((over_x, over_y, over_d))]
    m_cross(2)
    m_deepen(1)
    m_cross(3)
    m_deepen(2)
    for one in t_plane:
        one.wait()
    tsum = tsum_s[0] + tgot_s[0] + tgot_s[1] + tgot_s[2]
    tz_s[...] = tsum
    last += [copy(tz_s, tzgot_s.at[k], 4, (2, k), over_z[k]) for k in range(3)]
    v_deepen(3)
    m_deepen(3)
    x = x_ref[...].astype(F32)
    gn = acc_s[...]
    wp = gn * pre[...]
    mean = jnp.mean(wp * x, axis=1, keepdims=True)
    gin_o[...] = g_ref[...].astype(F32) + r * wp - x * (r * r * r * mean)
    for one in a_copies:
        one.wait()
    a_o[...] = plane_a[z].astype(F32) + agot_s[0].astype(F32) + agot_s[1].astype(F32) + agot_s[2].astype(F32)
    for one in last:
        one.wait()
    for bufs, cols in ((value, slice(0, ch)), (maps, slice(ch, out_o.shape[1]))):
        z_in = bufs[12]
        out_o[:, cols] = out_o[:, cols] + z_in[0].astype(F32) + z_in[1].astype(F32) + z_in[2].astype(F32)
    tiny_o[...] = tsum + tzgot_s[0] + tzgot_s[1] + tzgot_s[2]


def whole(shape, grid):
    zeros = (0,) * len(shape)
    if grid:
        return pl.BlockSpec(shape, lambda j: zeros)
    return pl.BlockSpec(shape, lambda: zeros)


def columns(rows, first=0):
    return pl.BlockSpec((rows, 128), lambda j: (0, first + j))


SMEM = pl.BlockSpec(memory_space=pltpu.SMEM)
VMEM = pl.BlockSpec(memory_space=pltpu.VMEM)
ANY = pl.BlockSpec(memory_space=pl.ANY)
HBM = pl.BlockSpec(memory_space=pltpu.HBM)


def sds(shape, dtype):
    return jax.ShapeDtypeStruct(shape, dtype)


def params(grid, mib):
    if grid:
        return pltpu.CompilerParams(vmem_limit_bytes=mib * 2**20, dimension_semantics=("arbitrary",))
    return pltpu.CompilerParams(vmem_limit_bytes=mib * 2**20)


def cost(us):
    return pl.CostEstimate(flops=int(us * 1.1e9), bytes_accessed=int(us * 1e6), transcendentals=0)


def pack_columns(v):
    n = v.shape[-1] // 4
    return jnp.concatenate([v[..., 0:n], v[..., 2 * n : 3 * n], v[..., n : 2 * n], v[..., 3 * n :]], axis=-1)


def small_kernel(hl, conv, gain, dtb, alog, skip, wdt, start_ref, end_ref, out_o):
    ch = out_o.shape[1]
    lane = iota((1, 128), 1)
    wide_lane = iota((1, ch), 1)
    bias = jnp.zeros((1, 128), F32)
    rate = jnp.zeros((1, 128), F32)
    diag = jnp.zeros((1, ch), F32)
    out_o[0:16, :] = jnp.zeros((16, ch), F32)
    for h in range(hl):
        cols = slice(h * HD, (h + 1) * HD)
        out_o[0:7, cols] = conv[h]
        out_o[7:8, cols] = gain[h : h + 1, :]
        bias = jnp.where(lane == h, dtb[0, h], jnp.where(lane == 64 + h, dtb[1, h], bias))
        rate = jnp.where((lane == h) | (lane == 64 + h), alog[h], rate)
        diag = jnp.where(wide_lane // HD == h, skip[h], diag)
        out_o[16 + 2 * h : 18 + 2 * h, :] = wdt[h].astype(F32)[0:2, :]
    out_o[8:9, :] = diag
    out_o[9:10, 0:128] = bias
    out_o[9:10, 128:256] = rate
    n = lax.axis_index("narrow")
    start, end = start_ref[...].astype(F32), end_ref[...].astype(F32)
    out_o[16 + 2 * hl :, :] = jnp.where(n == 0, end[8:16, :], start[0:8, :])


def swap(v):
    return lax.ppermute(v, "narrow", [(0, 1), (1, 0)])


def flip(v, bit, wide):
    return lax.ppermute(v, "wide", [(i, i ^ bit) for i in range(wide)])


def cross(v, bit, wide):
    pairs = [(i * 2 + k, (i ^ bit) * 2 + 1 - k) for i in range(wide) for k in range(2)]
    return lax.ppermute(v, ("wide", "narrow"), pairs)


def total(*parts):
    acc = parts[0].astype(F32)
    for v in parts[1:]:
        acc = acc + v.astype(F32)
    return acc


def split_positions(
    wide, layer_in, pre_gain, w_heads, w_bc, conv_x, conv_bc, dt_bias, a_log, skip_d, norm_gain, w_out, cotangent, starts, live
):
    n = lax.axis_index("narrow")
    w = lax.axis_index("wide")
    left = n == 0
    _, length, dm = layer_in.shape
    hl = w_heads.shape[1]
    heads = 2 * hl
    ch = hl * HD
    chans = 2 * ch
    pairs = heads // 2
    hp = pairs // 2
    nb = length // BLOCK
    ext = length + 2 * HALO
    share = dm // wide
    x = layer_in[0]
    g = cotangent[0]

    w_turned = jnp.transpose(w_heads, (1, 2, 0))
    small_own = pl.pallas_call(
        functools.partial(small_kernel, hl),
        grid=(1,),
        out_shape=sds((24 + 2 * hl, ch), F32),
        in_specs=[
            whole((hl, 7, HD), 1), whole((hl, HD), 1), SMEM, SMEM, SMEM, pl.BlockSpec((hl, 16, dm), lambda j: (0, 8, 0)),
            pl.BlockSpec((HALO, dm), lambda j: (0, 0)), pl.BlockSpec((HALO, dm), lambda j: (length // HALO - 1, 0)),
        ],
        out_specs=whole((24 + 2 * hl, ch), 1),
        cost_estimate=cost(2),
        name="small",
    )(jnp.transpose(conv_x, (1, 0, 2)), norm_gain, dt_bias.T, a_log, skip_d, w_turned, x, x)
    small_other = swap(small_own)

    quarter = ch // 4
    q = w % 4

    def gather(p0):
        p1 = flip(p0, 2, wide)
        return p0, p1, flip(p0, 1, wide), flip(p1, 1, wide)

    def heads_rows(lo):
        return lax.dynamic_slice(w_turned, (q * (hl // 4), lo, 0), (hl // 4, HD, dm)).reshape(quarter, dm)

    wo = w_out.reshape(ch, dm)
    wv_first = swap(heads_rows(HD))
    wo_rows = lax.dynamic_slice(wo, (q * quarter, 0), (quarter, dm))
    wog_pieces = gather(swap(jnp.concatenate([wo_rows, heads_rows(0)], axis=1)))

    pos = (length, 128)
    sq = (nb, BLOCK, BLOCK)
    front_shapes = [
        ((8, chans), F32), ((8, chans), F32), ((8, chans), F32), ((128, dm), BF16), ((dm, 256), BF16), ((7, 256), F32),
        ((ext, dm), BF16), ((length, 1), F32), ((ext, 256), F32), ((ext, 256), F32), ((length, 256), BF16),
        ((2,) + sq, F32), ((4,) + sq, F32), ((3,) + sq, F32), ((128, 128), F32), ((length, 384), F32),
    ]
    late_front = (8, 9, 10, 13, 15)
    (
        info, taps, gain, skip, wdt_all, wbc, taps_bc, normed, rs, bcm, dsl, maps, tab_a, tab_b, tab_c, dpt, sig,
    ) = pl.pallas_call(
        functools.partial(front_kernel, length, hl),
        out_shape=[sds((8,), jnp.int32)]
        + [pltpu.HBM(*v) if k in late_front else sds(*v) for k, v in enumerate(front_shapes)],
        in_specs=[SMEM] + [VMEM] * 7,
        out_specs=[SMEM] + [HBM if k in late_front else VMEM for k in range(len(front_shapes))],
        scratch_shapes=[
            pltpu.VMEM((ext, 256), jnp.int32), pltpu.VMEM((ext, 256), F32), pltpu.VMEM((128, 128), F32),
            pltpu.VMEM((ext, dm), BF16),
        ]
        + [pltpu.VMEM(*front_shapes[k]) for k in late_front]
        + [pltpu.SemaphoreType.DMA((len(late_front),))],
        compiler_params=params(False, 14),
        cost_estimate=cost(6),
        name="front",
    )(starts, live, x, pre_gain.reshape(1, dm), w_bc, conv_bc, small_own, small_other)

    wv_over_x = flip(wv_first, 2, wide)

    def states(first):
        return pl.BlockSpec((1, nb + 1, 128, 128), lambda j: (j + first, 0, 0, 0))

    bnd_spec = pl.BlockSpec((1, 64, 128), lambda j: (j, 0, 0))
    state_shape = sds((pairs, nb + 1, 128, 128), BF16)
    bnd_shape = sds((hp, 64, 128), BF16)
    act_shape = sds((length, chans), BF16)
    def twin(rows, first):
        return pl.BlockSpec((rows, 256), lambda j: (0, first + j))

    def vals(other, weights, before):
        steps = hp // 2
        first = steps if other else 0
        specs = [SMEM, whole((ext, dm), 1)]
        specs += [whole((quarter, dm), 1)] * 4 if other else [pl.BlockSpec((4, 2 * HD + 2, dm), lambda j: (j, 0, 0))]
        specs += [twin(8, first), whole((2,) + sq, 1), whole((128, 128), 1)] + [ANY] * len(before)
        return pl.pallas_call(
            functools.partial(vals_kernel, length, other),
            grid=(steps,),
            out_shape=[act_shape, sds((ext, chans), BF16), act_shape, state_shape, bnd_shape] + [sds((ch, dm), BF16)] * other,
            in_specs=specs,
            out_specs=[
                twin(length, first), twin(ext, first), twin(length, first),
                pl.BlockSpec((2, nb + 1, 128, 128), lambda j: (j + first, 0, 0, 0)),
                pl.BlockSpec((2, 64, 128), lambda j: (j, 0, 0)),
            ] + [whole((ch, dm), 1)] * other,
            scratch_shapes=[pltpu.VMEM((ext, 128), F32), pltpu.VMEM((ext, 128), F32), pltpu.VMEM((ext, 128), jnp.int32)],
            input_output_aliases={len(specs) - len(before) + i: i for i in range(len(before))},
            compiler_params=params(True, 10),
            cost_estimate=cost(9),
            name="vals_other" if other else "vals_own",
        )(info, normed, *weights, taps, tab_a, dpt, *before)

    *own_vals, bnd_own = vals(False, (w_turned,), ())
    wv_pieces = wv_first, wv_over_x, flip(wv_first, 1, wide), flip(wv_over_x, 1, wide)
    xc, vm, ds, s_loc, bnd_other, wv_other = vals(True, wv_pieces, own_vals)

    def aliases(specs, before):
        return {len(specs) - len(before) + i: i for i in range(len(before))}

    def scan(first, s0, before):
        specs = [
            SMEM, columns(length, first), states(first), bnd_spec, whole((128, 128), 1), whole((4,) + sq, 1), columns(8, first),
        ] + [ANY] * len(before)
        return pl.pallas_call(
            functools.partial(scan_kernel, length, first),
            grid=(hp,),
            out_shape=[act_shape, state_shape],
            in_specs=specs,
            out_specs=[columns(length, first), states(first)],
            input_output_aliases=aliases(specs, before),
            compiler_params=params(True, 5),
            cost_estimate=cost(10),
            name="scan_other" if first else "scan_own",
        )(info, xc, s_loc, s0, dpt, tab_b, skip, *before)

    y, s_true = scan(0, swap(bnd_other), scan(hp, swap(bnd_own), ()))

    out, gy, ggate, hn, ggain, wg_other, gs_loc, gbnd = pl.pallas_call(
        functools.partial(gate_kernel, nb),
        out_shape=[
            pltpu.HBM((length, dm), BF16), act_shape, act_shape, act_shape, sds((8, chans), F32), pltpu.HBM((ch, dm), BF16),
            state_shape, sds((pairs, 64, 128), BF16),
        ],
        in_specs=[SMEM] + [VMEM] * 14,
        out_specs=[HBM, VMEM, VMEM, VMEM, VMEM, HBM, VMEM, VMEM],
        scratch_shapes=[pltpu.VMEM((ch, 2 * dm), BF16)]
        + [pltpu.VMEM((BLOCK, chans), F32)] * 4
        + [pltpu.VMEM((nb, BLOCK, chans), F32), pltpu.VMEM((length, dm), BF16), pltpu.SemaphoreType.DMA((2,))],
        compiler_params=params(False, 18),
        cost_estimate=cost(16),
        name="gated",
    )(info, x, g, normed, y, wo, w_turned, *wog_pieces, gain, tab_b, tab_c, dpt)

    gw_shape = (2, dm // 2, dm + ch)
    piece = sds((4, share, dm + ch), BF16)
    a_pieces = pl.pallas_call(
        wsum_kernel,
        out_shape=[piece] * 4,
        in_specs=[VMEM] * 4,
        out_specs=[VMEM] * 4,
        scratch_shapes=[pltpu.VMEM(gw_shape, BF16)] * 3 + [pltpu.SemaphoreType.DMA((2, 2))] * 2,
        compiler_params=pltpu.CompilerParams(collective_id=1, has_side_effects=True, vmem_limit_bytes=16 * 2**20),
        cost_estimate=cost(7),
        name="wsum",
    )(g, normed, hn, ggate)

    mine, to_x, to_y, to_d = a_pieces
    got_d = cross(to_d, 2, wide)

    def table(k):
        return pl.BlockSpec((None,) + sq, lambda j: (k, 0, 0, 0))

    sums = [whole(sq, 1), whole(sq, 1), whole(sq, 1), whole(pos, 1), whole(sq, 1)]
    gmix, ggt, gb, gct, ksum, rsum, phi, gskip, edge = pl.pallas_call(
        functools.partial(gscan_kernel, length),
        grid=(pairs,),
        out_shape=[
            act_shape, sds(sq, F32), sds(sq, F32), sds(sq, F32), sds(pos, F32), sds(sq, F32), sds((16, chans), F32),
            sds((8, chans), F32), sds((HALO, chans), BF16),
        ],
        in_specs=[
            SMEM, columns(length), columns(length), columns(length), states(0), states(0),
            pl.BlockSpec((1, 64, 128), lambda j: ((j + hp) % pairs, 0, 0)), whole((128, 128), 1), table(1), table(0), table(0),
            whole((3,) + sq, 1), columns(8),
        ],
        out_specs=[columns(length)] + sums + [columns(16), columns(8), columns(HALO)],
        scratch_shapes=[pltpu.VMEM((nb + 1, 128, 128), BF16)],
        compiler_params=params(True, 8),
        cost_estimate=cost(22),
        name="gscan",
    )(info, xc, ds, gy, s_true, gs_loc, swap(gbnd), dpt, tab_b, tab_a, tab_b, tab_c, skip)
    edge = swap(edge)

    gmix, ggt, got_d = lax.optimization_barrier((gmix, ggt, got_d))
    a_plane = total(mine, flip(to_x, 2, wide), swap(to_y), got_d).astype(BF16)

    gmb, gv, small, edge_bc = pl.pallas_call(
        functools.partial(join_kernel, length, heads),
        out_shape=[sds((ext, 256), F32), sds(pos, BF16), sds((16, 128), F32), sds((HALO, 256), F32)],
        in_specs=[SMEM] + [VMEM] * 9,
        out_specs=[VMEM] * 4,
        scratch_shapes=[pltpu.VMEM((ext, 128), F32), pltpu.VMEM((ext, 256), F32)],
        compiler_params=params(False, 6),
        cost_estimate=cost(6),
        name="join",
    )(info, ggt, gb, gct, ksum, rsum, phi, maps, dsl, sig)

    edge_bc = swap(edge_bc)
    sum_shape = (2, dm // 2, ch)
    gvals, keep_v, send_v, tiny = pl.pallas_call(
        functools.partial(back_kernel, length, pairs // 2),
        out_shape=[act_shape, sds(sum_shape, BF16), sds(sum_shape, BF16), sds((2, 16, ch), F32)],
        in_specs=[SMEM] + [VMEM] * 7,
        out_specs=[VMEM] * 4,
        scratch_shapes=[
            pltpu.VMEM((ext, 128), F32), pltpu.VMEM((ext, 128), jnp.int32), pltpu.VMEM((dm, length), BF16),
        ],
        compiler_params=params(False, 10),
        cost_estimate=cost(12),
        name="back",
    )(info, gmix, edge, vm, normed, taps, ggain, gskip)

    def buffers(cols, cut):
        rest = cols - cut
        return (
            [pltpu.VMEM((4, 2, 2 * share, cols), BF16), pltpu.VMEM((4, 2, share, cut), F32), pltpu.VMEM((4, 2, share, rest), F32)]
            + [pltpu.VMEM((4, 2, share, cut), BF16)] * 2
            + [pltpu.VMEM((4, 2, share, rest), BF16)] * 2
            + [pltpu.VMEM((4, share, cut), BF16)] * 2
            + [pltpu.VMEM((4, share, rest), BF16)] * 2
            + [pltpu.VMEM((3, share, cols), BF16)] * 2
        )

    cols = ch + 384
    wb, tiny, wa, grad_in = pl.pallas_call(
        functools.partial(collect_kernel, length, hl),
        out_shape=[sds((share, cols), F32), sds((16, ch), F32), sds((share, dm + ch), F32), sds((length, dm), F32)],
        in_specs=[SMEM] + [VMEM] * 22,
        out_specs=[VMEM] * 4,
        scratch_shapes=[
            pltpu.VMEM((ext, 128), F32), pltpu.VMEM((ext, 128), jnp.int32),
            pltpu.VMEM((2, dm // 2, 384), BF16), pltpu.VMEM((2, dm // 2, 384), BF16), pltpu.VMEM((2, 16, ch), F32),
            pltpu.VMEM((length, dm), F32),
        ]
        + buffers(ch, ch // 2)
        + buffers(384, 256)
        + [
            pltpu.VMEM((2, 16, ch), F32),
            pltpu.VMEM((2, 16, ch), F32),
            pltpu.VMEM((3, 16, ch), F32),
            pltpu.VMEM((16, ch), F32),
            pltpu.VMEM((3, 16, ch), F32),
            pltpu.VMEM((3, share, dm + ch), BF16),
        ]
        + [pltpu.SemaphoreType.DMA(v) for v in ((9,), (2, 4, 2), (2, 4, 2), (3,), (4, 3)) * 2],
        compiler_params=pltpu.CompilerParams(collective_id=0, has_side_effects=True, vmem_limit_bytes=24 * 2**20),
        name="collect",
    )(
        info, gvals, ggate, w_turned, wv_other, wg_other, normed, gmb, edge_bc, bcm, taps_bc, gv, wdt_all, wbc, x, g, rs,
        pre_gain.reshape(1, dm), small, tiny, keep_v, send_v, a_plane,
    )

    g_w_heads, g_w_out, g_w_bc, g_conv_x, g_conv_bc, g_pre, g_bias, g_rate, g_skip, g_gain = pl.pallas_call(
        functools.partial(finish_kernel, hl),
        out_shape=[
            sds((hl, share, 2 * HD + 2), F32), sds((hl, share, HD), F32), sds((share, 256), F32), sds((7, HD // wide, hl), F32),
            sds((7, 256 // wide), F32), sds((1, share), F32), sds((2, hl), F32), sds((1, hl), F32), sds((1, hl), F32),
            sds((HD // wide, hl), F32),
        ],
        in_specs=[VMEM] * 3,
        out_specs=[VMEM] * 10,
        compiler_params=params(False, 8),
        name="finish",
    )(tiny, wa, wb)
    return (
        out[None],
        grad_in[None],
        g_pre[0],
        jnp.transpose(g_w_heads, (1, 0, 2)),
        g_w_bc,
        jnp.transpose(g_conv_x, (0, 2, 1)),
        g_conv_bc,
        g_bias.T,
        g_rate[0],
        g_skip[0],
        g_gain.T,
        jnp.transpose(g_w_out, (0, 2, 1)),
    )


def solution(mesh):
    body = shards
    if mesh.shape["narrow"] == 2 and mesh.shape["wide"] == 16:
        body = functools.partial(split_positions, mesh.shape["wide"])
    return jax.shard_map(
        body,
        mesh=mesh,
        in_specs=(
            P("wide", "narrow", None),
            P(),
            P(None, "narrow", None),
            P(),
            P(None, "narrow", None),
            P(),
            P("narrow", None),
            P("narrow"),
            P("narrow"),
            P("narrow", None),
            P("narrow", None, None),
            P("wide", "narrow", None),
            P("wide", None),
            P("wide", None),
        ),
        out_specs=(
            P("wide", "narrow", None),
            P("wide", "narrow", None),
            P("wide"),
            P("wide", "narrow", None),
            P("wide", None),
            P(None, "narrow", "wide"),
            P(None, "wide"),
            P("narrow", None),
            P("narrow"),
            P("narrow"),
            P("narrow", "wide"),
            P("narrow", None, "wide"),
        ),
        check_vma=False,
    )
```
